32 devices in a mesh: head: 4 (over y, x), dp: 8 (over z, core).
Axes of the slice: x: 2, y: 2, z: 4, core: 2. Of those that a mesh axis runs over, the one named last changes fastest.
Arguments:
- inputs: bfloat16 [12288, 1024], P('dp', 'head'), may hold values from -7 to 7
- cotangent: bfloat16 [12288, 1024], P('dp', 'head'), may hold values from -6 to 6
- lengths: int32 [24], P('dp'), may hold values from 128 to 512, as said below
- owner_slots: int32 [3141], replicated, may hold values from 0 to 4711, as said below
- table: float32 [4, 4712, 1024], P('head', 'dp'), may hold values from -1.5 to 1.5
- table_m: float32 [4, 4712, 1024], P('head', 'dp'), may hold values from -15.5191752 to 15.5191752
- table_v: float32 [4, 4712, 1024], P('head', 'dp'), may hold values from 6.144 to 245.76
- gains: float32 [3, 1024], replicated, may hold values from 0.5 to 1.5
- gains_m: float32 [3, 1024], replicated, may hold values from -28 to 28
- gains_v: float32 [3, 1024], replicated, may hold values from 81.1008 to 319.488
Outputs:
- outputs: bfloat16 [12288, 1024], P('dp', 'head')
- input_grad: float32 [12288, 1024], P('dp', 'head')
- table_new: float32 [4, 4712, 1024], P('head', 'dp')
- table_m_new: float32 [4, 4712, 1024], P('head', 'dp')
- table_v_new: float32 [4, 4712, 1024], P('head', 'dp')
- gains_new: float32 [3, 1024], replicated
- gains_m_new: float32 [3, 1024], replicated
- gains_v_new: float32 [3, 1024], replicated
- rms_stats: float32 [3], replicated
The draws below stay inside these ranges and needn't reach their ends.
Inputs may be any that keep to these rules, and one draw needn't show every extreme that they name: The valid tokens of a sequence are the first lengths entries of its 512 positions; the rest is padding. `owner_slots`: distinct entries. Slot s belongs to index s // 589 of dp; some index of dp holds rows in all of its 589 slots.
All inputs are finite; a program needn't handle non-finite values.
Results may differ from the reference program's by a relative error of at most 0.012.
The reference program's roundings to bfloat16 on the way count: a program that leaves them out, or rounds other values in their place, can miss the bound.
Values may be sent and summed in bfloat16 or wider, within the bound.
A program may use at most 192 MiB of HBM per device.

```python
import math
import jax
import jax.numpy as jnp
from jax import lax

MODEL_WIDTH = 1024
FF = 2816
HEADS = 8
DK = 128
KCONV = 4
BLOCK = 64
MIN_LEN = 128
STEP = 10
SLOT = 512
SEQ_DEV = 3
SEQS = 24
TOKENS = 12288
HEAD_SHARDS = 4
HDL = 256
FFL = 704
HL = 2
CROWS = 3
ROWS = 3141
SLOTS_PER_RANK = 589
TOTAL_SLOTS = 4712


def owner_map(key):
    key = jax.random.fold_in(key, 100)
    first, second_moment, third = jax.random.split(key, 3)
    owner_ranks = TOTAL_SLOTS // SLOTS_PER_RANK
    complete_owner_map = jax.random.randint(first, (), 0, owner_ranks)
    slot_index = jnp.arange(TOTAL_SLOTS, dtype=jnp.int32)
    random_noise = jax.random.randint(second_moment, (TOTAL_SLOTS,), 0, 2 ** 18)
    ranking_score = jnp.where(slot_index // SLOTS_PER_RANK == complete_owner_map, slot_index, (random_noise + 1) * TOTAL_SLOTS + slot_index)
    order = jnp.argsort(ranking_score)
    chosen = order[:ROWS].astype(jnp.int32)
    return chosen[jax.random.permutation(third, ROWS)]


def category_values(value_entries):
    slot_index = jnp.arange(ROWS)
    bounds = [3 * HDL, 4 * HDL, 4 * HDL + 2 * FFL, 4 * HDL + 3 * FFL, 4 * HDL + 3 * FFL + HL]
    result = jnp.full((ROWS,), value_entries[5], jnp.float32)
    for bound, value in reversed(list(zip(bounds, value_entries[:5]))):
        result = jnp.where(slot_index < bound, value, result)
    return result


def slot_values(table_slots, value_entries, padding_value):
    return jnp.full((TOTAL_SLOTS,), padding_value, jnp.float32).at[table_slots].set(category_values(value_entries))


def grad_sizes():
    root = (TOKENS / 2.0) ** 0.5
    return tuple((factor * root for factor in (0.15, 0.4, 0.4, 0.3, 0.15, 0.15)))


def draw_owner_slots(key, part):
    table_slots = owner_map(key)
    key = jax.random.fold_in(key, 2)
    return table_slots


def draw_table(key, part):
    table_slots = owner_map(key)
    key = jax.random.fold_in(key, 3)
    scales = slot_values(table_slots, (MODEL_WIDTH ** (-0.5), (HEADS * DK) ** (-0.5), MODEL_WIDTH ** (-0.5), FF ** (-0.5), MODEL_WIDTH ** (-0.5), 0.5), MODEL_WIDTH ** (-0.5))
    tensor_shape = (HEAD_SHARDS, TOTAL_SLOTS, MODEL_WIDTH)
    base = jax.random.truncated_normal(key, -3.0, 3.0, tensor_shape, jnp.float32)
    return base * scales[None, :, None]


def draw_table_m(key, part):
    table_slots = owner_map(key)
    key = jax.random.fold_in(key, 4)
    sizes = grad_sizes()
    scales = slot_values(table_slots, tuple((0.111 * value for value in sizes)), 0.111 * sizes[2])
    tensor_shape = (HEAD_SHARDS, TOTAL_SLOTS, MODEL_WIDTH)
    base = jax.random.truncated_normal(key, -3.0, 3.0, tensor_shape, jnp.float32)
    return base * scales[None, :, None]


def draw_table_v(key, part):
    table_slots = owner_map(key)
    key = jax.random.fold_in(key, 5)
    sizes = grad_sizes()
    scales = slot_values(table_slots, tuple((0.0527 * value * value for value in sizes)), 0.0527 * sizes[2] * sizes[2])
    tensor_shape = (HEAD_SHARDS, TOTAL_SLOTS, MODEL_WIDTH)
    factor = jax.random.uniform(key, tensor_shape, jnp.float32, 1.0, 4.0)
    return factor * scales[None, :, None]


def draw_inputs(key, part):
    key = jax.random.fold_in(key, 6)
    columns = jnp.sqrt(1.0 + 2.0 * jnp.arange(MODEL_WIDTH, dtype=jnp.float32) / (MODEL_WIDTH - 1))
    tensor_shape = (TOKENS, MODEL_WIDTH)
    base = jax.random.truncated_normal(key, -4.0, 4.0, tensor_shape, jnp.float32)
    return (base * columns[None, :]).astype(jnp.bfloat16)


def draw_lengths(key, part):
    key = jax.random.fold_in(key, 7)
    groups = SEQS // SEQ_DEV
    device = jnp.arange(SEQS, dtype=jnp.int32) // SEQ_DEV
    top = SLOT * (groups - 1 + 2 * device) // (3 * (groups - 1))
    bottom = jnp.maximum(MIN_LEN, top // 2)
    random_noise = jax.random.randint(key, (SEQS,), 0, 1 << 20)
    result = bottom + random_noise % (top - bottom + 1)
    result = result.at[0].set(MIN_LEN).at[SEQS - 1].set(SLOT)
    return result.astype(jnp.int32)


def steps_of(key, extent, cuts, low, largest):
    factor_of, own = 1.0, jax.random.fold_in(key, 6)
    for position, parts in cuts:
        heights = jnp.exp(jax.random.uniform(jax.random.fold_in(own, position), (parts,), jnp.float32, low / len(cuts), largest / len(cuts)))
        factor_of = factor_of * jnp.repeat(heights, extent[position] // parts).reshape([-1 if axis == position else 1 for axis in range(len(extent))])
    return factor_of


def centred(stream_key, extent, scale, reach, cuts=(), kind=jnp.bfloat16):
    loudness = steps_of(stream_key, extent, cuts, -0.22, 0.18) if cuts else 1.0
    values = jax.random.normal(stream_key, extent, jnp.float32) * scale * loudness
    return jnp.minimum(jnp.maximum(values, -reach), reach).astype(kind)


def setup_inputs(seed: int = 0) -> dict:
    key_list = jax.random.split(jax.random.key(seed), 11)
    return {
        "inputs": draw_inputs(jax.random.fold_in(key_list[10], 71), 0),
        "cotangent": centred(key_list[1], (TOKENS, MODEL_WIDTH), 1.0, 6.0, ((0, 8), (1, 4))),
        "lengths": draw_lengths(jax.random.fold_in(key_list[10], 71), 0),
        "owner_slots": draw_owner_slots(jax.random.fold_in(key_list[10], 71), 0),
        "table": draw_table(jax.random.fold_in(key_list[10], 71), 0),
        "table_m": draw_table_m(jax.random.fold_in(key_list[10], 71), 0),
        "table_v": draw_table_v(jax.random.fold_in(key_list[10], 71), 0),
        "gains": jnp.clip(1.0 + 0.1 * jax.random.normal(key_list[7], (3, MODEL_WIDTH), jnp.float32), 0.5, 1.5),
        "gains_m": centred(key_list[8], (3, MODEL_WIDTH), (0.04 * TOKENS ** 0.5), 28.0, (), jnp.float32),
        "gains_v": jnp.clip(jax.random.uniform(key_list[9], (3, MODEL_WIDTH), jnp.float32, 81.1008, 319.488), 81.1008, 319.488),
    }


norm_eps = 1e-06
adam_eps = 1e-08
beta_one = 0.9
beta_two = 0.95
weight_rate = 0.02
gain_rate = 0.6
weight_decay = 0.1
highest = lax.Precision.HIGHEST

@jax.custom_vjp
def low(v):
    return lax.optimization_barrier(v.astype(jnp.bfloat16)).astype(jnp.float32)

@jax.custom_vjp
def low_back(v):
    return v

def low_keep(v):
    return (low(v), None)

def low_pass(kept, grad):
    return (grad,)

def back_keep(v):
    return (v, None)

def back_low(kept, grad):
    return (low(grad),)
low.defvjp(low_keep, low_pass)
low_back.defvjp(back_keep, back_low)

def matmul_rows(left, right_rows):
    return jnp.dot(left, right_rows.T, precision=highest)

def mixer(projected, beta_logit, conv_taps, out_gain):
    seqs_here, length, width = projected.shape
    heads_here = width // (3 * DK)
    blocks = length // BLOCK
    padded = jnp.pad(projected, ((0, 0), (KCONV - 1, 0), (0, 0)))
    convolved = conv_taps[0] * padded[:, 0:length, :]
    for offset in range(1, KCONV):
        convolved = convolved + conv_taps[offset] * padded[:, offset:offset + length, :]
    activated = jax.nn.silu(convolved).reshape(seqs_here, length, 3, heads_here, DK)
    query = activated[:, :, 0]
    keys = activated[:, :, 1]
    value_entries = activated[:, :, 2]
    query = query * lax.rsqrt(lax.optimization_barrier(jnp.sum(query * query, -1, keepdims=True)) + norm_eps) * DK ** (-0.5)
    keys = keys * lax.rsqrt(lax.optimization_barrier(jnp.sum(keys * keys, -1, keepdims=True)) + norm_eps)
    strength = jax.nn.sigmoid(beta_logit)

    def to_blocks(tensor):
        return tensor.reshape(seqs_here, blocks, BLOCK, heads_here, DK).transpose(0, 3, 1, 2, 4)
    query_b = to_blocks(query)
    keys_b = to_blocks(keys)
    values_b = to_blocks(value_entries)
    strength_b = strength.reshape(seqs_here, blocks, BLOCK, heads_here).transpose(0, 3, 1, 2)
    gram = jnp.einsum('nhbcd,nhbed->nhbce', keys_b, keys_b, precision=highest)
    lower_part = jnp.tril(gram * strength_b[..., :, None], -1)
    identity = jnp.eye(BLOCK, dtype=jnp.float32)
    weighting = jax.scipy.linalg.solve_triangular(identity + lower_part, identity * strength_b[..., :, None], lower=True, unit_diagonal=True)
    keys_w = jnp.einsum('nhbce,nhbed->nhbcd', weighting, keys_b, precision=highest)
    values_u = jnp.einsum('nhbce,nhbed->nhbcd', weighting, values_b, precision=highest)
    scores = jnp.tril(jnp.einsum('nhbcd,nhbed->nhbce', query_b, keys_b, precision=highest))

    def advance(state, pieces):
        query_p, keys_p, keys_wp, values_up, scores_p = pieces
        fresh = values_up - jnp.einsum('nhcd,nhde->nhce', keys_wp, state, precision=highest)
        output = jnp.einsum('nhcd,nhde->nhce', query_p, state, precision=highest)
        output = output + jnp.einsum('nhce,nhef->nhcf', scores_p, fresh, precision=highest)
        state = state + jnp.einsum('nhcd,nhce->nhde', keys_p, fresh, precision=highest)
        return (state, output)
    pieces = tuple((jnp.moveaxis(tensor, 2, 0) for tensor in (query_b, keys_b, keys_w, values_u, scores)))
    initial = jnp.zeros((seqs_here, heads_here, DK, DK), jnp.float32)
    final_state, outputs = lax.scan(jax.checkpoint(advance), initial, pieces)
    outputs = outputs.transpose(1, 0, 3, 2, 4).reshape(seqs_here, length, heads_here, DK)
    scaled = outputs * lax.rsqrt(lax.optimization_barrier(jnp.mean(outputs * outputs, -1, keepdims=True)) + norm_eps)
    scaled = scaled * out_gain.reshape(heads_here, DK)
    return scaled.reshape(seqs_here * length, heads_here * DK)

def layer(tokens_in, weights, gain_values):
    count = tokens_in.shape[0] // SLOT
    end_qkv = 3 * HDL
    end_out = 4 * HDL
    end_gate = end_out + FFL
    end_up = end_gate + FFL
    end_down = end_up + FFL
    end_beta = end_down + HL
    end_conv = end_beta + CROWS
    normed_one = low(tokens_in * lax.rsqrt(lax.optimization_barrier(jnp.mean(tokens_in * tokens_in, -1, keepdims=True)) + norm_eps) * gain_values[0])
    attn_sum = jnp.zeros_like(tokens_in)
    for shard in range(HEAD_SHARDS):
        shard_rows = weights[shard]
        projected = low_back(matmul_rows(normed_one, shard_rows[0:end_qkv]))
        beta_logit = low_back(matmul_rows(normed_one, shard_rows[end_down:end_beta]))
        taps = shard_rows[end_beta:end_conv].reshape(KCONV, 3 * HDL)
        out_gain = gain_values[2, shard * HDL:(shard + 1) * HDL]
        mixed = low(mixer(projected.reshape(count, SLOT, 3 * HDL), beta_logit.reshape(count, SLOT, HL), taps, out_gain))
        attn_sum = attn_sum + jnp.dot(mixed, shard_rows[end_qkv:end_out], precision=highest)
    attn_out = low_back(attn_sum)
    hidden_in = tokens_in + attn_out
    normed_two = low(hidden_in * lax.rsqrt(lax.optimization_barrier(jnp.mean(hidden_in * hidden_in, -1, keepdims=True)) + norm_eps) * gain_values[1])
    mlp_sum = jnp.zeros_like(tokens_in)
    for shard in range(HEAD_SHARDS):
        shard_rows = weights[shard]
        gate_value = low_back(matmul_rows(normed_two, shard_rows[end_out:end_gate]))
        up_value = low_back(matmul_rows(normed_two, shard_rows[end_gate:end_up]))
        hidden = low(jax.nn.silu(gate_value) * up_value)
        mlp_sum = mlp_sum + jnp.dot(hidden, shard_rows[end_up:end_down], precision=highest)
    mlp_out = low_back(mlp_sum)
    return (hidden_in + mlp_out, attn_out, mlp_out)

def adam_step(param, first, second_moment, grad, rate, decay):
    first = beta_one * first + (1.0 - beta_one) * grad
    second_moment = beta_two * second_moment + (1.0 - beta_two) * grad * grad
    denom = jnp.sqrt(second_moment / (1.0 - beta_two ** STEP)) + adam_eps
    param = param - rate / (1.0 - beta_one ** STEP) * first / denom - rate * decay * param
    return (param, first, second_moment)

def reference(inputs, cotangent, lengths, owner_slots, table, table_m, table_v, gains, gains_m, gains_v):
    group = math.gcd(SEQS, max(1, 4096 // SLOT))
    master_rows = table[:, owner_slots, :]

    def forward(flat_inputs, rows_master, gain_values):
        weights = low(rows_master)

        def one_group(group_inputs):
            return layer(group_inputs, weights, gain_values)
        full_out, attn_part, mlp_part = lax.map(jax.checkpoint(one_group), flat_inputs.reshape(SEQS // group, group * SLOT, MODEL_WIDTH))
        return (full_out.reshape(TOKENS, MODEL_WIDTH), (attn_part.reshape(TOKENS, MODEL_WIDTH), mlp_part.reshape(TOKENS, MODEL_WIDTH)))
    full_out, pullback, branches = jax.vjp(forward, inputs.astype(jnp.float32), master_rows, gains, has_aux=True)
    attn_out, mlp_out = branches
    valid = (jnp.arange(SLOT)[None, :] < lengths[:, None]).reshape(TOKENS).astype(jnp.float32)
    input_grad, rows_grad, gains_grad = pullback(cotangent.astype(jnp.float32) * valid[:, None])
    grad_table = jnp.zeros(table.shape, jnp.float32).at[:, owner_slots, :].set(rows_grad)
    table_new, table_m_new, table_v_new = adam_step(table, table_m, table_v, grad_table, weight_rate, weight_decay)
    gains_new, gains_m_new, gains_v_new = adam_step(gains, gains_m, gains_v, gains_grad, gain_rate, 0.0)
    squares = jnp.stack([jnp.sum(valid[:, None] * full_out * full_out), jnp.sum(valid[:, None] * attn_out * attn_out), jnp.sum(valid[:, None] * mlp_out * mlp_out)])
    entries = jnp.sum(valid) * MODEL_WIDTH
    rms_stats = jnp.sqrt(squares / entries)
    return (full_out.astype(jnp.bfloat16), input_grad, table_new, table_m_new, table_v_new, gains_new, gains_m_new, gains_v_new, rms_stats)
```

```python
import functools

import jax
import jax.numpy as jnp
from jax import lax
from jax.experimental import pallas as pl
from jax.experimental.pallas import tpu as pltpu
from jax.sharding import PartitionSpec as P

MODEL_WIDTH = 1024
FF = 2816
HEADS = 8
DK = 128
KCONV = 4
STEP = 10
C = 128

norm_eps = 1e-06
adam_eps = 1e-08
beta_one = 0.9
beta_two = 0.95
weight_rate = 0.02
gain_rate = 0.6
weight_decay = 0.1
f32 = jnp.float32
bf16 = jnp.bfloat16
MESH = pl.DeviceIdType.MESH
VM = functools.partial(pl.BlockSpec, memory_space=pltpu.VMEM)
DMA = pltpu.SemaphoreType.DMA

def dot(a,b): return lax.dot_general(a,b,(((1,),(0,)),((),())),preferred_element_type=f32)
def dot_t(a,b): return lax.dot_general(a,b,(((1,),(1,)),((),())),preferred_element_type=f32)
def tdot(a,b): return lax.dot_general(a,b,(((0,),(0,)),((),())),preferred_element_type=f32)

def shifted(x, prev, j):
    if j==0: return x
    r=pltpu.roll(x,j,0)
    p=pltpu.roll(prev,j,0)
    row=lax.broadcasted_iota(jnp.int32,(8,x.shape[1]),0)
    top=jnp.where(row<j,p,r[0:8])
    return jnp.concatenate([top,r[8:]],0)

def conv_silu(x,prev,taps):
    conv=taps[3:4]*x
    for j in range(1,4):
        conv=conv+taps[3-j:4-j]*shifted(x,prev,j)
    sg=jax.nn.sigmoid(conv)
    return conv,sg

def masks():
    i=lax.broadcasted_iota(jnp.int32,(C,C),0); j=lax.broadcasted_iota(jnp.int32,(C,C),1)
    return i,j

def fwd_kernel(x_ref,lg_ref,taps_ref,gain_ref,a_ref,q_s,k_s,u_s,t_s,p_s,g_s,r_s,s_s,o_s,l_w,*,heads,chunks):
    i,j=masks()
    low=j<=i; slow=j<i; xr=jnp.bitwise_xor(i,j)
    zero8=jnp.zeros((8,DK),f32)
    every=[(c,h) for c in range(chunks) for h in range(heads)]
    beta={}
    for c,h in every:
        rows=slice(c*C,(c+1)*C)
        pre={}
        for n,off in (("q",0),("k",heads*DK),("v",2*heads*DK)):
            cols=slice(off+h*DK,off+(h+1)*DK)
            x=x_ref[rows,cols]
            prev=zero8 if c==0 else x_ref[c*C-8:c*C,cols]
            conv,sg=conv_silu(x,prev,taps_ref[:,cols])
            pre[n]=conv*sg
        q=pre["q"]; q=q*(lax.rsqrt(jnp.sum(q*q,-1,keepdims=True)+norm_eps)*DK**-0.5)
        k=pre["k"]; k=k*lax.rsqrt(jnp.sum(k*k,-1,keepdims=True)+norm_eps)
        qb=q.astype(bf16); kb=k.astype(bf16)
        beta[c,h]=jax.nn.sigmoid(lg_ref[rows,h:h+1])
        sc=dot_t(jnp.concatenate([qb,kb],0),kb)
        G=sc[C:]
        Lw=jnp.where(slow,G*beta[c,h],0.0).astype(bf16)
        q_s[h,rows]=qb; k_s[h,rows]=kb; p_s[h,rows]=jnp.where(low,sc[0:C],0.0).astype(bf16); g_s[h,rows]=G.astype(bf16)
        r_s[h,rows]=pre["v"].astype(bf16)
        l_w[h,rows]=Lw
        t_s[h,rows]=jnp.where(xr==0,1.0,jnp.where(xr==1,-Lw.astype(f32),0.0)).astype(bf16)
    s=2
    while s<C:
        part=(xr>=s)&(xr<2*s)
        half=[dot(t_s[h,c*C:(c+1)*C],jnp.where(part,l_w[h,c*C:(c+1)*C],jnp.zeros((C,C),bf16))).astype(bf16) for c,h in every]
        for (c,h),y in zip(every,half):
            rows=slice(c*C,(c+1)*C)
            X=t_s[h,rows]
            t_s[h,rows]=X-dot(y,X).astype(bf16)
        s*=2
    S=[jnp.zeros((DK,DK),f32) for _ in range(heads)]
    for c in range(chunks):
        rows=slice(c*C,(c+1)*C)
        Sb=[S[h].astype(bf16) for h in range(heads)]
        m=[dot(jnp.concatenate([k_s[h,rows],q_s[h,rows]],0),Sb[h]) for h in range(heads)]
        R=[r_s[h,rows].astype(f32)-m[h][0:C] for h in range(heads)]
        ub=[dot(t_s[h,rows],(R[h]*beta[c,h]).astype(bf16)).astype(bf16) for h in range(heads)]
        S=[S[h]+tdot(k_s[h,rows],ub[h]) for h in range(heads)]
        for h in range(heads):
            s_s[h,rows]=Sb[h]; r_s[h,rows]=R[h].astype(bf16); u_s[h,rows]=ub[h]
            o=m[h][C:]+dot(p_s[h,rows],ub[h])
            o_s[h,rows]=o
            a=o*lax.rsqrt(jnp.mean(o*o,-1,keepdims=True)+norm_eps)*gain_ref[0:1,h*DK:(h+1)*DK]
            a_ref[rows,h*DK:(h+1)*DK]=a.astype(bf16)

def mixer_fwd(x,lg,taps,gain,seqs):
    T=x.shape[0]; L=T//seqs; W=x.shape[1]; heads=W//(3*DK)
    blk=lambda: pl.BlockSpec((heads,L,DK),lambda s:(0,s,0))
    sav=lambda dt: jax.ShapeDtypeStruct((heads,T,DK),dt)
    return pl.pallas_call(functools.partial(fwd_kernel,heads=heads,chunks=L//C),
        grid=(seqs,),
        in_specs=[pl.BlockSpec((L,W),lambda s:(s,0)),pl.BlockSpec((L,lg.shape[1]),lambda s:(s,0)),pl.BlockSpec(taps.shape,lambda s:(0,0)),pl.BlockSpec(gain.shape,lambda s:(0,0))],
        out_specs=[pl.BlockSpec((L,heads*DK),lambda s:(s,0))]+[blk() for _ in range(9)],
        out_shape=[jax.ShapeDtypeStruct((T,heads*DK),bf16)]+[sav(bf16) for _ in range(8)]+[sav(f32)],
        scratch_shapes=[pltpu.VMEM((heads,L,DK),bf16)],
        compiler_params=pltpu.CompilerParams(vmem_limit_bytes=56<<20),
        cost_estimate=pl.CostEstimate(flops=2*24*20*C*C*C,bytes_accessed=15<<20,transcendentals=0),
        name="mixer_fwd")(x,lg,taps,gain)

def bwd_kernel(x_ref,lg_ref,taps_ref,gain_ref,da_ref,q_s,k_s,u_s,t_s,p_s,g_s,r_s,s_s,o_s,dx_ref,dlg_ref,dt_ref,dg_ref,dc,*,heads,chunks):
    i,j=masks()
    low=j<=i; slow=j<i
    zero8=jnp.zeros((8,DK),f32)
    seq=pl.program_id(0)
    @pl.when(seq==0)
    def _():
        dt_ref[...]=jnp.zeros_like(dt_ref); dg_ref[...]=jnp.zeros_like(dg_ref)
    dS=[jnp.zeros((DK,DK),f32) for _ in range(heads)]
    W=heads*DK
    lane=lax.broadcasted_iota(jnp.int32,(C,128),1)
    dc[chunks*C:chunks*C+8]=jnp.zeros((8,3*W),f32)
    for c in reversed(range(chunks)):
        rows=slice(c*C,(c+1)*C)
        dlg=jnp.zeros((C,128),f32)
        for h in range(heads):
            hc=slice(h*DK,(h+1)*DK)
            o=o_s[h,rows]
            ro=lax.rsqrt(jnp.mean(o*o,-1,keepdims=True)+norm_eps)
            da=da_ref[rows,hc]
            on=o*ro
            dg_ref[0:1,hc]+=jnp.sum(da*on,0,keepdims=True)
            t=da*gain_ref[0:1,hc]
            do=(ro*(t-on*jnp.mean(t*on,-1,keepdims=True))).astype(bf16)
            qb=q_s[h,rows]; kb=k_s[h,rows]; ub=u_s[h,rows]; Tb=t_s[h,rows]; Pb=p_s[h,rows]; Sb=s_s[h,rows]
            G=g_s[h,rows].astype(f32); R=r_s[h,rows].astype(f32)
            beta=jax.nn.sigmoid(lg_ref[rows,h:h+1])
            dSb=dS[h].astype(bf16)
            du=tdot(Pb,do)+dot(kb,dSb)
            e=tdot(Tb,du.astype(bf16))
            eb=e.astype(bf16)
            be=beta*e; beb=be.astype(bf16)
            pe=dot_t(jnp.concatenate([do,eb],0),ub)
            dP=jnp.where(low,pe[0:C],0.0).astype(bf16)
            dL=jnp.where(slow,-pe[C:],0.0)
            dG=beta*dL
            ds=dot_t(jnp.concatenate([do,beb],0),Sb)
            dq=ds[0:C]+dot(dP,kb)
            dGb=dG.astype(bf16)
            dk=tdot(dP,qb)+dot_t(ub,dSb)-ds[C:]+dot(dGb,kb)+tdot(dGb,kb)
            db=jnp.sum(e*R+dL*G,-1,keepdims=True)
            dlg=jnp.where(lane==h,db*beta*(1.0-beta),dlg)
            dS[h]=dS[h]+tdot(qb,do)-tdot(kb,beb)
            for n,off in (("q",0),("k",W),("v",2*W)):
                cols=slice(off+h*DK,off+(h+1)*DK)
                x=x_ref[rows,cols]
                prev=zero8 if c==0 else x_ref[c*C-8:c*C,cols]
                conv,sg=conv_silu(x,prev,taps_ref[:,cols])
                act=conv*sg
                if n=="v": d=be
                else:
                    r=lax.rsqrt(jnp.sum(act*act,-1,keepdims=True)+norm_eps)
                    g_=dq*DK**-0.5 if n=="q" else dk
                    an=act*r
                    d=r*(g_-an*jnp.sum(g_*an,-1,keepdims=True))
                dconv=d*(sg*(1.0+conv*(1.0-sg)))
                dc[rows,cols]=dconv
                for jj in range(4):
                    dt_ref[jj:jj+1,cols]+=jnp.sum(dconv*shifted(x,prev,3-jj),0,keepdims=True)
                nxt=dc[(c+1)*C:(c+1)*C+8,cols]
                tp=taps_ref[:,cols]
                dx=tp[3:4]*dconv
                row8=lax.broadcasted_iota(jnp.int32,(8,DK),0)
                for jj in range(1,4):
                    r=pltpu.roll(dconv,C-jj,0)
                    pn=pltpu.roll(nxt,8-jj,0)
                    bot=jnp.where(row8>=8-jj,pn,r[C-8:])
                    dx=dx+tp[3-jj:4-jj]*jnp.concatenate([r[:C-8],bot],0)
                dx_ref[rows,cols]=dx.astype(bf16)
        dlg_ref[rows]=dlg.astype(bf16)

def mixer_bwd(x,lg,taps,gain,da,saved,seqs):
    T=x.shape[0]; L=T//seqs; W=x.shape[1]; heads=W//(3*DK)
    blk=lambda: pl.BlockSpec((heads,L,DK),lambda s:(0,s,0))
    return pl.pallas_call(functools.partial(bwd_kernel,heads=heads,chunks=L//C),
        grid=(seqs,),
        in_specs=[pl.BlockSpec((L,W),lambda s:(s,0)),pl.BlockSpec((L,lg.shape[1]),lambda s:(s,0)),pl.BlockSpec(taps.shape,lambda s:(0,0)),pl.BlockSpec(gain.shape,lambda s:(0,0)),pl.BlockSpec((L,heads*DK),lambda s:(s,0))]+[blk() for _ in range(9)],
        out_specs=[pl.BlockSpec((L,W),lambda s:(s,0)),pl.BlockSpec((L,128),lambda s:(s,0)),pl.BlockSpec((8,W),lambda s:(0,0)),pl.BlockSpec((8,heads*DK),lambda s:(0,0))],
        out_shape=[jax.ShapeDtypeStruct((T,W),bf16),jax.ShapeDtypeStruct((T,128),bf16),jax.ShapeDtypeStruct((8,W),f32),jax.ShapeDtypeStruct((8,heads*DK),f32)],
        scratch_shapes=[pltpu.VMEM((L+8,W),f32)],
        compiler_params=pltpu.CompilerParams(vmem_limit_bytes=56<<20),
        cost_estimate=pl.CostEstimate(flops=2*24*20*C*C*C,bytes_accessed=15<<20,transcendentals=0),
        name="mixer_bwd")(x,lg,taps,gain,da,*saved)


def meet(partners):
    b=pltpu.get_barrier_semaphore()
    for p in partners:
        pl.semaphore_signal(b,inc=1,device_id=p,device_id_type=MESH)
    pl.semaphore_wait(b,len(partners))

def ag_kernel(*refs,count,parts):
    ins=refs[:count]; outs=refs[count:2*count]; ss,rs,ls=refs[2*count:]
    h=lax.axis_index("head"); d=lax.axis_index("dp")
    meet([(jnp.bitwise_xor(h,1),d),(jnp.bitwise_xor(h,2),d)])
    def copy(src,dst,to,k):
        return pltpu.make_async_remote_copy(src,dst,ss.at[to-1,k],rs.at[to-1,k],device_id=(jnp.bitwise_xor(h,to),d),device_id_type=MESH)
    first={}; second=[]; local=[]
    for n in range(count):
        x,o=ins[n],outs[n]
        T,Wd=x.shape; R=T//(2*parts); base=n*3*parts
        def col(b): return pl.ds(pl.multiple_of(b*Wd,Wd),Wd)
        for i in range(2*parts):
            r1=pl.ds(i*R,R); j=(i+parts)%(2*parts); r2=pl.ds(j*R,R)
            first[n,1,i]=copy(x.at[r1],o.at[r1,col(h)],1,base+i); first[n,1,i].start()
            first[n,2,j]=copy(x.at[r2],o.at[r2,col(h)],2,base+j); first[n,2,j].start()
        l=pltpu.make_async_copy(x,o.at[:,col(h)],ls.at[n]); l.start(); local.append(l)
    for n in range(count):
        x,o=ins[n],outs[n]
        T,Wd=x.shape; R=T//(2*parts); base=n*3*parts
        def col(b): return pl.ds(pl.multiple_of(b*Wd,Wd),Wd)
        for i in range(parts):
            ra=pl.ds(i*R,R); rb=pl.ds((i+parts)*R,R)
            ca=col(jnp.bitwise_xor(h,1)); cb=col(jnp.bitwise_xor(h,2))
            first[n,1,i].wait_recv()
            c=copy(o.at[ra,ca],o.at[ra,ca],2,base+2*parts+i); c.start(); second.append(c)
            first[n,2,i+parts].wait_recv()
            c=copy(o.at[rb,cb],o.at[rb,cb],1,base+2*parts+i); c.start(); second.append(c)
    for n in range(count):
        for i in range(parts):
            first[n,1,i+parts].wait_recv(); first[n,2,i].wait_recv()
    for c in second: c.wait()
    for c in first.values(): c.wait_send()
    for l in local: l.wait()

def gather_columns(arrays,parts,cid):
    n=len(arrays)
    return pl.pallas_call(functools.partial(ag_kernel,count=n,parts=parts),
        in_specs=[VM()]*n,out_specs=[VM()]*n,
        out_shape=[jax.ShapeDtypeStruct((a.shape[0],4*a.shape[1]),a.dtype) for a in arrays],
        scratch_shapes=[DMA((2,3*parts*n)),DMA((2,3*parts*n)),DMA((n,))],
        compiler_params=pltpu.CompilerParams(collective_id=cid,has_side_effects=True,vmem_limit_bytes=56<<20),name="gather_columns")(*arrays)

def rs_kernel(*refs,count,parts):
    ins=refs[:count]; outs=refs[count:2*count]; fb,db,cb,sb,ss,rs=refs[2*count:]
    h=lax.axis_index("head"); d=lax.axis_index("dp")
    h1,h2,h3=[jnp.bitwise_xor(h,k) for k in (1,2,3)]
    meet([(h1,d),(h2,d)])
    T=ins[0].shape[0]; Wd=ins[0].shape[1]//4; half=T//2; R=half//parts
    def col(b): return pl.ds(pl.multiple_of(b*Wd,Wd),Wd)
    def copy(src,dst,to,k):
        return pltpu.make_async_remote_copy(src,dst,ss.at[to-1,k],rs.at[to-1,k],device_id=(jnp.bitwise_xor(h,to),d),device_id_type=MESH)
    K=lambda n,p,kind: (n*parts+p)*3+kind
    fw={}; dr={}; cm={}
    for n in range(count):
        x=ins[n]
        for p in range(parts):
            for side,to,nb in ((0,1,h1),(1,2,h2)):
                r=pl.ds(side*half+p*R,R); q=pl.ds(p*R,R)
                fw[n,p,side]=copy(x.at[r,col(h3)],fb.at[n,side,q],to,K(n,p,0)); fw[n,p,side].start()
            for side,to,nb in ((0,1,h1),(1,2,h2)):
                r=pl.ds(side*half+p*R,R); q=pl.ds(p*R,R)
                dr[n,p,side]=copy(x.at[r,col(nb)],db.at[n,side,q],to,K(n,p,1)); dr[n,p,side].start()
    for n in range(count):
        x=ins[n]
        for p in range(parts):
            for side,to,nb in ((0,2,h2),(1,1,h1)):
                r=pl.ds(side*half+p*R,R); q=pl.ds(p*R,R)
                fw[n,p,side].wait_recv()
                sb[n,side,q]=(fb[n,side,q].astype(f32)+x[r,col(nb)].astype(f32)).astype(bf16)
                cm[n,p,side]=copy(sb.at[n,side,q],cb.at[n,side,q],to,K(n,p,2)); cm[n,p,side].start()
    for n in range(count):
        x,o=ins[n],outs[n]
        for p in range(parts):
            for side in (0,1):
                r=pl.ds(side*half+p*R,R); q=pl.ds(p*R,R)
                dr[n,p,side].wait_recv()
                cm[n,p,side].wait_recv()
                o[r]=x[r,col(h)].astype(f32)+db[n,side,q].astype(f32)+cb[n,side,q].astype(f32)
    for g in (fw,dr,cm):
        for c in g.values(): c.wait_send()

def scatter_columns(arrays,parts,cid):
    n=len(arrays); T=arrays[0].shape[0]; Wd=arrays[0].shape[1]//4
    buf=pltpu.VMEM((n,2,T//2,Wd),bf16)
    return pl.pallas_call(functools.partial(rs_kernel,count=n,parts=parts),
        in_specs=[VM()]*n,out_specs=[VM()]*n,
        out_shape=[jax.ShapeDtypeStruct((T,Wd),f32) for a in arrays],
        scratch_shapes=[buf]*4+[DMA((2,3*parts*n)),DMA((2,3*parts*n))],
        compiler_params=pltpu.CompilerParams(collective_id=cid,has_side_effects=True,vmem_limit_bytes=60<<20),name="scatter_columns")(*arrays)

def scan_kernel(own,out,oth,rb,lb,rst,lst,xs,xr,fs,fr,ss,rs,*,chunk,skew):
    h=lax.axis_index("head"); d=lax.axis_index("dp"); n=lax.axis_size("dp")//2
    z=d//2; core=lax.rem(d,2)
    mate=(h,jnp.bitwise_xor(d,1)); right=(h,d+2); left=(h,d-2)
    rows=own.shape[0]; Wd=own.shape[1]//2; nc=rows//chunk
    b=pltpu.get_barrier_semaphore()
    pl.semaphore_signal(b,inc=1,device_id=mate,device_id_type=MESH)
    @pl.when(z>0)
    def _(): pl.semaphore_signal(b,inc=1,device_id=left,device_id_type=MESH)
    @pl.when(z<n-1)
    def _(): pl.semaphore_signal(b,inc=1,device_id=right,device_id_type=MESH)
    pl.semaphore_wait(b,1+(z>0).astype(jnp.int32)+(z<n-1).astype(jnp.int32))
    mine=pl.ds(pl.multiple_of(core*Wd,Wd),Wd); other=pl.ds(pl.multiple_of((1-core)*Wd,Wd),Wd)
    def at(c): return pl.ds(pl.multiple_of(c*chunk,chunk),chunk)
    def remote(src,dst,s,r,dev): return pltpu.make_async_remote_copy(src,dst,s,r,device_id=dev,device_id_type=MESH)
    def swap(c): return remote(own.at[at(c),other],oth.at[at(c)],xs.at[c],xr.at[c],mate)
    def give(c): return remote(out.at[at(c),mine],out.at[at(c),mine],fs.at[c],fr.at[c],mate)
    def goR(c): return remote(rst.at[at(c)],rb.at[at(c)],ss.at[0,c],rs.at[0,c],right)
    def goL(c): return remote(lst.at[at(c)],lb.at[at(c)],ss.at[1,c],rs.at[1,c],left)
    def issue(c,carry):
        swap(c).start(); return carry
    lax.fori_loop(0,nc,issue,0)
    last=skew*jnp.maximum(z,n-1-z)
    def step(t,carry):
        @pl.when(t<nc)
        def _():
            swap(t).wait_recv()
            oth[at(t)]=(oth[at(t)].astype(f32)+own[at(t),mine].astype(f32)).astype(bf16)
        c=t-skew*z
        @pl.when((c>=0)&(c<nc))
        def _():
            @pl.when(z>0)
            def _(): goR(c).wait_recv()
            @pl.when(z<n-1)
            def _():
                @pl.when(z==0)
                def _(): rst[at(c)]=oth[at(c)]
                @pl.when(z>0)
                def _(): rst[at(c)]=(oth[at(c)].astype(f32)+rb[at(c)].astype(f32)).astype(bf16)
                goR(c).start()
        e=t-skew*(n-1-z)
        @pl.when((e>=0)&(e<nc))
        def _():
            @pl.when(z<n-1)
            def _(): goL(e).wait_recv()
            @pl.when(z>0)
            def _():
                @pl.when(z==n-1)
                def _(): lst[at(e)]=oth[at(e)]
                @pl.when(z<n-1)
                def _(): lst[at(e)]=(oth[at(e)].astype(f32)+lb[at(e)].astype(f32)).astype(bf16)
                goL(e).start()
        g=t-last
        @pl.when((g>=0)&(g<nc))
        def _():
            @pl.when(z==0)
            def _(): out[at(g),mine]=(oth[at(g)].astype(f32)+lb[at(g)].astype(f32)).astype(bf16)
            @pl.when(z==n-1)
            def _(): out[at(g),mine]=(oth[at(g)].astype(f32)+rb[at(g)].astype(f32)).astype(bf16)
            @pl.when((z>0)&(z<n-1))
            def _(): out[at(g),mine]=(oth[at(g)].astype(f32)+rb[at(g)].astype(f32)+lb[at(g)].astype(f32)).astype(bf16)
            give(g).start()
        return carry
    lax.fori_loop(0,nc+skew*(n-1),step,0)
    def drain(c,carry):
        give(c).wait()
        swap(c).wait_send()
        @pl.when(z<n-1)
        def _(): goR(c).wait_send()
        @pl.when(z>0)
        def _(): goL(c).wait_send()
        return carry
    lax.fori_loop(0,nc,drain,0)

def sum_rows(own,chunk,cid,skew=2):
    rows,wd=own.shape; nc=rows//chunk
    buf=pltpu.VMEM((rows,wd//2),bf16)
    return pl.pallas_call(functools.partial(scan_kernel,chunk=chunk,skew=skew),
        in_specs=[VM()],out_specs=VM(),out_shape=jax.ShapeDtypeStruct((rows,wd),bf16),
        scratch_shapes=[buf]*5+[DMA((nc,))]*4+[DMA((2,nc))]*2,
        compiler_params=pltpu.CompilerParams(collective_id=cid,has_side_effects=True,vmem_limit_bytes=60<<20),name="sum_rows")(own)


class Spread:
    def __init__(self, src, dst, first, second, ss, rs, base):
        self.h, self.d = lax.axis_index("head"), lax.axis_index("dp")
        self.src, self.dst, self.first, self.second = src, dst, first, second
        self.ss, self.rs, self.base, self.n = ss, rs, base, len(first)

    def copy(self, src, dst, to, k):
        return pltpu.make_async_remote_copy(
            src, dst, self.ss.at[to - 1, self.base + k], self.rs.at[to - 1, self.base + k],
            device_id=(jnp.bitwise_xor(self.h, to), self.d), device_id_type=MESH,
        )

    def direct(self, to, i):
        rows = (self.first + self.second)[i]
        return self.copy(self.src(rows), self.dst(rows, self.h), to, i)

    def passed(self, to, i):
        rows = (self.second if to == 1 else self.first)[i]
        ref = self.dst(rows, jnp.bitwise_xor(self.h, 3 - to))
        return self.copy(ref, ref, to, 2 * self.n + i)

    def start(self):
        n = self.n
        for i in range(2 * n):
            self.direct(1, i).start()
            self.direct(2, (i + n) % (2 * n)).start()

    def forward(self, i):
        self.direct(1, i).wait_recv()
        self.passed(2, i).start()
        self.direct(2, self.n + i).wait_recv()
        self.passed(1, i).start()

    def arrived(self):
        for i in range(self.n):
            self.direct(1, self.n + i).wait_recv()
            self.direct(2, i).wait_recv()
            self.passed(1, i).wait_recv()
            self.passed(2, i).wait_recv()

    def sent(self):
        for to in (1, 2):
            for i in range(2 * self.n):
                self.direct(to, i).wait_send()
            for i in range(self.n):
                self.passed(to, i).wait_send()


def fwd_conv(x_ref, lg_ref, taps_ref, q_s, k_s, p_s, g_s, r_s, t_s, l_w, heads, chunks):
    i, j = masks()
    low = j <= i
    slow = j < i
    xr = jnp.bitwise_xor(i, j)
    zero8 = jnp.zeros((8, DK), f32)
    for c in range(chunks):
        for h in range(heads):
            rows = slice(c * C, (c + 1) * C)
            pre = {}
            for n, off in (("q", 0), ("k", heads * DK), ("v", 2 * heads * DK)):
                cols = slice(off + h * DK, off + (h + 1) * DK)
                x = x_ref[rows, cols]
                prev = zero8 if c == 0 else x_ref[c * C - 8 : c * C, cols]
                conv, sg = conv_silu(x, prev, taps_ref[:, cols])
                pre[n] = conv * sg
            q, k = pre["q"], pre["k"]
            q = q * (lax.rsqrt(jnp.sum(q * q, -1, keepdims=True) + norm_eps) * DK**-0.5)
            k = k * lax.rsqrt(jnp.sum(k * k, -1, keepdims=True) + norm_eps)
            qb, kb = q.astype(bf16), k.astype(bf16)
            beta = jax.nn.sigmoid(lg_ref[rows, h : h + 1])
            sc = dot_t(jnp.concatenate([qb, kb], 0), kb)
            G = sc[C:]
            Lw = jnp.where(slow, G * beta, 0.0).astype(bf16)
            q_s[h, rows] = qb
            k_s[h, rows] = kb
            p_s[h, rows] = jnp.where(low, sc[0:C], 0.0).astype(bf16)
            g_s[h, rows] = G.astype(bf16)
            r_s[h, rows] = pre["v"].astype(bf16)
            l_w[h, rows] = Lw
            t_s[h, rows] = jnp.where(xr == 0, 1.0, jnp.where(xr == 1, -Lw.astype(f32), 0.0)).astype(bf16)


def fwd_inverse(t_s, l_w, heads, chunks):
    i, j = masks()
    xr = jnp.bitwise_xor(i, j)
    every = [(c, h) for c in range(chunks) for h in range(heads)]
    s = 2
    while s < C:
        part = (xr >= s) & (xr < 2 * s)
        half = [
            dot(t_s[h, c * C : (c + 1) * C], jnp.where(part, l_w[h, c * C : (c + 1) * C], jnp.zeros((C, C), bf16))).astype(bf16)
            for c, h in every
        ]
        for (c, h), y in zip(every, half):
            rows = slice(c * C, (c + 1) * C)
            X = t_s[h, rows]
            t_s[h, rows] = X - dot(y, X).astype(bf16)
        s *= 2


def fwd_states(lg_ref, gain_ref, a_ref, q_s, k_s, u_s, t_s, p_s, r_s, s_s, o_s, heads, chunks):
    S = [jnp.zeros((DK, DK), f32) for _ in range(heads)]
    for c in range(chunks):
        rows = slice(c * C, (c + 1) * C)
        Sb = [S[h].astype(bf16) for h in range(heads)]
        m = [dot(jnp.concatenate([k_s[h, rows], q_s[h, rows]], 0), Sb[h]) for h in range(heads)]
        R = [r_s[h, rows].astype(f32) - m[h][0:C] for h in range(heads)]
        beta = [jax.nn.sigmoid(lg_ref[rows, h : h + 1]) for h in range(heads)]
        ub = [dot(t_s[h, rows], (R[h] * beta[h]).astype(bf16)).astype(bf16) for h in range(heads)]
        S = [S[h] + tdot(k_s[h, rows], ub[h]) for h in range(heads)]
        for h in range(heads):
            s_s[h, rows] = Sb[h]
            r_s[h, rows] = R[h].astype(bf16)
            u_s[h, rows] = ub[h]
            o = m[h][C:] + dot(p_s[h, rows], ub[h])
            o_s[h, rows] = o
            a = o * lax.rsqrt(jnp.mean(o * o, -1, keepdims=True) + norm_eps) * gain_ref[0:1, h * DK : (h + 1) * DK]
            a_ref[rows, h * DK : (h + 1) * DK] = a.astype(bf16)


CH = 128
SKEW = 2


def front_kernel(
    table, order, gain, gout, x, cot,
    w, xf, cf, af, of, qkv_o, lg_o, q_o, k_o, u_o, t_o, p_o, g_o, r_o, s_o, o_o,
    own, oth, rb, lb, wv, xv, qv, lv, tp, av, q_s, k_s, u_s, t_s, p_s, g_s, r_s, s_s, o_s, l_w,
    xs, xr_, gl, fs, fr, ss, rs, as_, ar_, ls, sv,
    *, seqs, heads, lead, at_out, at_gate, hl, small,
):
    h = lax.axis_index("head")
    d = lax.axis_index("dp")
    n = lax.axis_size("dp") // 2
    z = d // 2
    core = lax.rem(d, 2)
    mate = (h, jnp.bitwise_xor(d, 1))
    h1, h2 = jnp.bitwise_xor(h, 1), jnp.bitwise_xor(h, 2)
    T, Wd = x.shape
    L = T // seqs
    rows_all, width = own.shape
    half = width // 2
    nc = rows_all // CH
    early = wv.shape[0] // CH
    chunks = L // C

    b = pltpu.get_barrier_semaphore()
    for p in (mate, (h1, d), (h2, d)):
        pl.semaphore_signal(b, inc=1, device_id=p, device_id_type=MESH)
    @pl.when(z > 0)
    def _():
        pl.semaphore_signal(b, inc=1, device_id=(h, d - 2), device_id_type=MESH)
    @pl.when(z < n - 1)
    def _():
        pl.semaphore_signal(b, inc=1, device_id=(h, d + 2), device_id_type=MESH)
    pl.semaphore_wait(b, 3 + (z > 0).astype(jnp.int32) + (z < n - 1).astype(jnp.int32))

    def col(i, size=Wd):
        return pl.ds(pl.multiple_of(i * size, size), size)

    def at(c):
        return pl.ds(pl.multiple_of(c * CH, CH), CH)

    parts = 3
    R = T // (2 * parts)
    A = [pl.ds(i * R, R) for i in range(parts)]
    B = [pl.ds((i + parts) * R, R) for i in range(parts)]
    spread_x = Spread(lambda r: x.at[r], lambda r, i: xv.at[r, col(i)], A, B, as_, ar_, 0)
    spread_c = Spread(lambda r: cot.at[r], lambda r, i: cf.at[r, col(i)], A, B, as_, ar_, 9)
    spread_a = [
        Spread(
            lambda r: av.at[r], lambda r, i: af.at[r, col(i)],
            [pl.ds(s * L, L // 2)], [pl.ds(s * L + L // 2, L // 2)], as_, ar_, 18 + 3 * s,
        )
        for s in range(seqs)
    ]
    hw = at_gate - at_out
    spread_o = Spread(
        lambda r: w.at[pl.ds(at_out + r[0], r[1])],
        lambda r, i: of.at[pl.ds(pl.multiple_of(i * hw, hw) + r[0], r[1])],
        [(0, hw // 2)], [(hw // 2, hw // 2)], as_, ar_, 18 + 3 * seqs,
    )
    spread_x.start()
    own_x = pltpu.make_async_copy(x, xv.at[:, col(h)], ls.at[0])
    own_x.start()

    mine, other = col(core, half), col(1 - core, half)

    def remote(src, dst, s, r, dev):
        return pltpu.make_async_remote_copy(src, dst, s, r, device_id=dev, device_id_type=MESH)

    def swap(c):
        return remote(own.at[at(c), other], oth.at[at(c)], xs.at[c], xr_.at[c], mate)

    def to_right(c):
        return remote(rb.at[at(c)], rb.at[at(c)], ss.at[0, c], rs.at[0, c], (h, d + 2))

    def to_left(c):
        return remote(lb.at[at(c)], lb.at[at(c)], ss.at[1, c], rs.at[1, c], (h, d - 2))

    def give(c, dst):
        return remote(oth.at[at(c)], dst.at[at(c), mine], fs.at[c], fr.at[c], mate)

    def keep(c, dst):
        return pltpu.make_async_copy(oth.at[at(c)], dst.at[at(c), mine], gl.at[c])

    def pick(c):
        place = lax.broadcasted_iota(jnp.int32, (CH, table.shape[0]), 1)
        hot = jnp.where(order[at(c), 0:1] == place, 1.0, 0.0).astype(bf16)
        own[at(c)] = dot(hot, table[...]).astype(bf16)
        swap(c).start()

    pick(0)
    pick(1)
    last = SKEW * jnp.maximum(z, n - 1 - z)

    def step(t, carry):
        @pl.when(t + 2 < nc)
        def _():
            pick(t + 2)

        @pl.when(t < nc)
        def _():
            swap(t).wait_recv()
            oth[at(t)] = oth[at(t)] + own[at(t), mine]

        c = t - SKEW * z
        @pl.when((c >= 0) & (c < nc))
        def _():
            @pl.when(z > 0)
            def _():
                to_right(c).wait_recv()
                rb[at(c)] = rb[at(c)] + oth[at(c)]
            @pl.when(z == 0)
            def _():
                rb[at(c)] = oth[at(c)]
            @pl.when(z < n - 1)
            def _():
                to_right(c).start()

        e = t - SKEW * (n - 1 - z)
        @pl.when((e >= 0) & (e < nc))
        def _():
            @pl.when(z < n - 1)
            def _():
                to_left(e).wait_recv()
                lb[at(e)] = lb[at(e)] + oth[at(e)]
            @pl.when(z == n - 1)
            def _():
                lb[at(e)] = oth[at(e)]
            @pl.when(z > 0)
            def _():
                to_left(e).start()

        g = t - last
        @pl.when((g >= 0) & (g < nc))
        def _():
            oth[at(g)] = rb[at(g)] + lb[at(g)] - oth[at(g)]
            @pl.when(g < early)
            def _():
                give(g, wv).start()
                keep(g, wv).start()
            @pl.when(g >= early)
            def _():
                give(g, w).start()
                keep(g, w).start()
        return carry

    def steps(lo, hi):
        lax.fori_loop(lo, hi, step, 0)

    steps(0, 2)
    for i in range(parts):
        spread_x.forward(i)
        steps(2 + i, 3 + i)
    spread_c.start()
    own_c = pltpu.make_async_copy(cot, cf.at[:, col(h)], ls.at[1])
    own_c.start()
    t = early + SKEW * (n - 1)
    steps(2 + parts, t)
    for c in range(early):
        keep(c, wv).wait()
        give(c, wv).wait_recv()
    save_w = pltpu.make_async_copy(wv, w.at[pl.ds(0, early * CH)], ls.at[2])
    save_w.start()
    spread_x.arrived()
    own_x.wait()
    save_x = pltpu.make_async_copy(xv, xf, ls.at[3])
    save_x.start()

    taps3 = wv[0:16].astype(f32)
    flat = [taps3[hl + i : hl + i + 1] for i in range(small - hl)]
    line = 3 * heads * DK
    joined = jnp.concatenate(flat, 1)
    for j in range(KCONV):
        tp[j : j + 1] = joined[:, j * line : (j + 1) * line]

    saves = []
    for s in range(seqs):
        rows = pl.ds(s * L, L)
        for i in range(2):
            r = pl.ds(s * L + i * (L // 2), L // 2)
            xx = xv[r].astype(f32)
            n1 = (xx * lax.rsqrt(jnp.mean(xx * xx, -1, keepdims=True) + norm_eps) * gain[0:1]).astype(bf16)
            lv[r] = dot_t(n1, wv[0:lead])
            qv[r] = dot_t(n1, wv[lead:at_out])
        if s == 0:
            spread_c.forward(0)
        steps(t, t + 1)
        sub = lambda ref: ref.at[:, rows]
        fwd_conv(qv.at[rows], lv.at[rows], tp, sub(q_s), sub(k_s), sub(p_s), sub(g_s), sub(r_s), sub(t_s), l_w, heads, chunks)
        if s == 0:
            spread_c.forward(1)
        else:
            spread_a[s - 1].forward(0)
        steps(t + 1, t + 2)
        fwd_inverse(sub(t_s), l_w, heads, chunks)
        if s == 0:
            spread_c.forward(2)
        steps(t + 2, t + 3)
        fwd_states(lv.at[rows], gout, av.at[rows], sub(q_s), sub(k_s), sub(u_s), sub(t_s), sub(p_s), sub(r_s), sub(s_s), sub(o_s), heads, chunks)
        spread_a[s].start()
        saves.append(pltpu.make_async_copy(av.at[rows], af.at[rows, col(h)], sv.at[s, 0]))
        pairs = [(qv.at[rows], qkv_o.at[rows]), (lv.at[rows], lg_o.at[rows])]
        for src, dst in ((q_s, q_o), (k_s, k_o), (u_s, u_o), (t_s, t_o), (p_s, p_o), (g_s, g_o), (r_s, r_o), (s_s, s_o), (o_s, o_o)):
            pairs.append((src.at[:, rows], dst.at[:, rows]))
        for k, (src, dst) in enumerate(pairs):
            saves.append(pltpu.make_async_copy(src, dst, sv.at[s, 1 + k]))
        for cp in saves[-12:]:
            cp.start()
        steps(t + 3, t + 4)
        t += 4
        if s == 1:
            save_w.wait()
            for c in range(early, -(-at_gate // CH)):
                keep(c, w).wait()
                give(c, w).wait_recv()
            spread_o.start()
            own_o = pltpu.make_async_copy(w.at[pl.ds(at_out, hw)], of.at[col(h, hw)], ls.at[4])
            own_o.start()
    steps(t, t + 2)
    spread_a[seqs - 1].forward(0)
    spread_o.forward(0)
    steps(t + 2, nc + SKEW * (n - 1))

    own_c.wait()
    own_o.wait()
    save_x.wait()
    for cp in saves:
        cp.wait()
    for sp in [spread_c, *spread_a, spread_o]:
        sp.arrived()
    for sp in [spread_x, spread_c, *spread_a, spread_o]:
        sp.sent()

    def drain(c, carry):
        swap(c).wait_send()
        @pl.when(c < early)
        def _():
            give(c, wv).wait_send()
        @pl.when(c >= early)
        def _():
            give(c, w).wait_send()
        @pl.when(c >= -(-at_gate // CH))
        def _():
            keep(c, w).wait()
            give(c, w).wait_recv()
        @pl.when(z < n - 1)
        def _():
            to_right(c).wait_send()
        @pl.when(z > 0)
        def _():
            to_left(c).wait_send()
        return carry

    lax.fori_loop(0, nc, drain, 0)


def front(table, order, gain, gout, x, cot, seqs, heads, lead, at_out, at_gate, hl, small, cid):
    T, Wd = x.shape
    rows = order.shape[0]
    width = table.shape[1]
    half = width // 2
    nc = rows // CH
    early = -(-at_out // CH)
    L = T // seqs
    hbm = pl.BlockSpec(memory_space=pl.ANY)
    S = jax.ShapeDtypeStruct
    sav = [S((heads, T, DK), bf16)] * 8 + [S((heads, T, DK), f32)]
    outs = [
        S((rows, width), bf16), S((T, width), bf16), S((T, width), bf16), S((T, width), bf16),
        S((4 * (at_gate - at_out), width), bf16), S((T, at_out - lead), f32), S((T, lead), f32), *sav,
    ]
    V = pltpu.VMEM
    piece = V((rows, half), bf16)
    return pl.pallas_call(
        functools.partial(
            front_kernel, seqs=seqs, heads=heads, lead=lead, at_out=at_out, at_gate=at_gate, hl=hl, small=small
        ),
        in_specs=[VM()] * 4 + [hbm] * 2,
        out_specs=[hbm] * len(outs),
        out_shape=outs,
        scratch_shapes=[
            V((rows, width), bf16), piece, piece, piece, V((early * CH, width), bf16), V((T, width), bf16),
            V((T, at_out - lead), f32), V((T, lead), f32), V((8, at_out - lead), f32), V((T, heads * DK), bf16),
            *[V((heads, T, DK), bf16)] * 8, V((heads, T, DK), f32), V((heads, L, DK), bf16),
            DMA((nc,)), DMA((nc,)), DMA((nc,)), DMA((nc,)), DMA((nc,)), DMA((2, nc)), DMA((2, nc)),
            DMA((2, 21 + 3 * seqs)), DMA((2, 21 + 3 * seqs)), DMA((5,)), DMA((seqs, 12)),
        ],
        compiler_params=pltpu.CompilerParams(collective_id=cid, has_side_effects=True, vmem_limit_bytes=60 << 20),
        name="front",
    )(table, order, gain, gout, x, cot)


def bwd_blocks(da_ref, gain_ref, o_s, q_s, k_s, u_s, p_s, s_s, dg_ref, do_w, w_w, dq_w, dk_w, qd_w, heads, chunks):
    i, j = masks()
    low = j <= i
    for c in range(chunks):
        for h in range(heads):
            rows = slice(c * C, (c + 1) * C)
            hc = slice(h * DK, (h + 1) * DK)
            o = o_s[h, rows]
            ro = lax.rsqrt(jnp.mean(o * o, -1, keepdims=True) + norm_eps)
            da = da_ref[rows, hc]
            on = o * ro
            dg_ref[0:1, hc] += jnp.sum(da * on, 0, keepdims=True)
            t = da * gain_ref[0:1, hc]
            do = (ro * (t - on * jnp.mean(t * on, -1, keepdims=True))).astype(bf16)
            qb, kb = q_s[h, rows], k_s[h, rows]
            dP = jnp.where(low, dot_t(do, u_s[h, rows]), 0.0).astype(bf16)
            do_w[h, rows] = do
            w_w[h, rows] = tdot(p_s[h, rows], do)
            dq_w[h, rows] = dot_t(do, s_s[h, rows]) + dot(dP, kb)
            dk_w[h, rows] = tdot(dP, qb)
            qd_w[h, rows] = tdot(qb, do)


def bwd_states(lg_ref, k_s, t_s, w_w, qd_w, ds_w, heads, chunks):
    dS = [jnp.zeros((DK, DK), f32) for _ in range(heads)]
    for c in reversed(range(chunks)):
        rows = slice(c * C, (c + 1) * C)
        kb = [k_s[h, rows] for h in range(heads)]
        dSb = [dS[h].astype(bf16) for h in range(heads)]
        du = [(w_w[h, rows] + dot(kb[h], dSb[h])).astype(bf16) for h in range(heads)]
        e = [tdot(t_s[h, rows], du[h]) for h in range(heads)]
        beta = [jax.nn.sigmoid(lg_ref[rows, h : h + 1]) for h in range(heads)]
        dS = [dS[h] + qd_w[h, rows] - tdot(kb[h], (beta[h] * e[h]).astype(bf16)) for h in range(heads)]
        for h in range(heads):
            w_w[h, rows] = e[h]
            ds_w[h, rows] = dSb[h]


def bwd_conv(x_ref, lg_ref, taps_ref, q_s, k_s, u_s, g_s, r_s, s_s, w_w, dq_w, dk_w, ds_w, dc, dx_ref, dlg_ref, dt_ref, heads, chunks):
    i, j = masks()
    slow = j < i
    zero8 = jnp.zeros((8, DK), f32)
    W = heads * DK
    lane = lax.broadcasted_iota(jnp.int32, (C, dlg_ref.shape[1]), 1)
    row8 = lax.broadcasted_iota(jnp.int32, (8, DK), 0)
    dc[chunks * C : chunks * C + 8] = jnp.zeros((8, 3 * W), f32)
    for c in reversed(range(chunks)):
        rows = slice(c * C, (c + 1) * C)
        dlg = jnp.zeros(lane.shape, f32)
        for h in range(heads):
            e = w_w[h, rows]
            eb = e.astype(bf16)
            beta = jax.nn.sigmoid(lg_ref[rows, h : h + 1])
            be = beta * e
            ub, kb = u_s[h, rows], k_s[h, rows]
            dL = jnp.where(slow, -dot_t(eb, ub), 0.0)
            dGb = (beta * dL).astype(bf16)
            dk = (
                dk_w[h, rows] + dot_t(ub, ds_w[h, rows]) - dot_t(be.astype(bf16), s_s[h, rows])
                + dot(dGb, kb) + tdot(dGb, kb)
            )
            db = jnp.sum(e * r_s[h, rows].astype(f32) + dL * g_s[h, rows].astype(f32), -1, keepdims=True)
            dlg = jnp.where(lane == h, db * beta * (1.0 - beta), dlg)
            for n, off in (("q", 0), ("k", W), ("v", 2 * W)):
                cols = slice(off + h * DK, off + (h + 1) * DK)
                tp = taps_ref[:, cols]
                x = x_ref[rows, cols]
                prev = zero8 if c == 0 else x_ref[c * C - 8 : c * C, cols]
                moved = [shifted(x, prev, 3 - jj) for jj in range(4)]
                conv = tp[3:4] * moved[3]
                for jj in range(3):
                    conv = conv + tp[jj : jj + 1] * moved[jj]
                sg = jax.nn.sigmoid(conv)
                act = conv * sg
                if n == "v":
                    dd = be
                else:
                    r = lax.rsqrt(jnp.sum(act * act, -1, keepdims=True) + norm_eps)
                    g = dq_w[h, rows] * DK**-0.5 if n == "q" else dk
                    an = act * r
                    dd = r * (g - an * jnp.sum(g * an, -1, keepdims=True))
                dconv = dd * (sg + act * (1.0 - sg))
                dc[rows, cols] = dconv
                for jj in range(4):
                    dt_ref[jj : jj + 1, cols] += jnp.sum(dconv * moved[jj], 0, keepdims=True)
                nxt = dc[(c + 1) * C : (c + 1) * C + 8, cols]
                dx = tp[3:4] * dconv
                for jj in range(1, 4):
                    r = pltpu.roll(dconv, C - jj, 0)
                    bot = jnp.where(row8 >= 8 - jj, pltpu.roll(nxt, 8 - jj, 0), r[C - 8 :])
                    dx = dx + tp[3 - jj : 4 - jj] * jnp.concatenate([r[: C - 8], bot], 0)
                dx_ref[rows, cols] = dx.astype(bf16)
        dlg_ref[rows] = dlg.astype(bf16)


class Scatter:
    def __init__(self, part, beside, rows, bufs, slot, ss, rs, base):
        self.h, self.d = lax.axis_index("head"), lax.axis_index("dp")
        self.part, self.beside, self.slot = part, beside, slot
        self.fb, self.db, self.cb = bufs
        self.half = rows.size // 2
        self.rows = [pl.ds(rows.start + i * self.half, self.half) for i in range(2)]
        self.ss, self.rs, self.base = ss, rs, base

    def col(self, k):
        w = self.part.shape[1] // 4
        return pl.ds(pl.multiple_of(jnp.bitwise_xor(self.h, k) * w, w), w)

    def copy(self, src, dst, to, k):
        return pltpu.make_async_remote_copy(
            src, dst, self.ss.at[to - 1, self.base + k], self.rs.at[to - 1, self.base + k],
            device_id=(jnp.bitwise_xor(self.h, to), self.d), device_id_type=MESH,
        )

    def far(self, side):
        return self.copy(self.part.at[self.rows[side], self.col(3)], self.fb.at[self.slot, side], side + 1, 0)

    def near(self, side):
        return self.copy(self.part.at[self.rows[side], self.col(side + 1)], self.db.at[self.slot, side], side + 1, 1)

    def both(self, side):
        return self.copy(self.fb.at[self.slot, side], self.cb.at[self.slot, side], 2 - side, 2)

    def one(self):
        for side in (0, 1):
            self.far(side).start()
        for side in (0, 1):
            self.near(side).start()

    def two(self):
        for side in (0, 1):
            self.far(side).wait_recv()
            got = self.fb[self.slot, side].astype(f32) + self.beside(side).astype(f32)
            self.fb[self.slot, side] = got.astype(bf16)
            self.both(side).start()

    def three(self):
        got = []
        for side in (0, 1):
            self.near(side).wait_recv()
            self.both(side).wait_recv()
            got.append(self.db[self.slot, side].astype(f32) + self.cb[self.slot, side].astype(f32))
            self.far(side).wait_send()
            self.near(side).wait_send()
            self.both(side).wait_send()
        return got


RING = 4
SLOTS = 4


def back_kernel(
    gain, gout, taps, stat_in, valid, order,
    da_part, h1_part, mlp_part, da_own, dh_own, mlp_own, h1_own, xf, af, w, g_ffn, qkv, lg, q_i, k_i, u_i, t_i, p_i, g_i, r_i, s_i, o_i,
    y_o, ig_o, stat_o, g_o,
    own, oth, rb, lb, rst, lst, qv, lv, q_s, k_s, u_s, t_s, p_s, g_s, r_s, s_s, o_s,
    do_w, w_w, dq_w, dk_w, qd_w, ds_w, dc, xv, wv, nb, da_f, dh_f, mlp_f, h1_f, xp, fb, db, cb, gq, gs, n1_w, dx_w, dlg_w, dt_w, dg_w, g1_w, st_w, go_w,
    xs, xr_, gl, fs, fr, ss, rs, as_, ar_, ls, lds, a2s, a2r, sts, str_,
    *, seqs, heads, lead, n_ffn, hl, small,
):
    h = lax.axis_index("head")
    d = lax.axis_index("dp")
    n = lax.axis_size("dp") // 2
    z = d // 2
    core = lax.rem(d, 2)
    mate = (h, jnp.bitwise_xor(d, 1))
    T = xf.shape[0]
    L = T // seqs
    rows_all, width = own.shape
    half = width // 2
    Wd = width // 4
    nc = rows_all // CH
    chunks = L // C
    hd = heads * DK
    at_qkv, at_out = n_ffn, n_ffn + 3 * hd
    at_small = at_out + hd

    bits = []
    k = 2
    while k < 2 * n:
        bits.append(k)
        k *= 2
    b = pltpu.get_barrier_semaphore()
    peers = [mate] + [(jnp.bitwise_xor(h, k), d) for k in (1, 2, 3)] + [(h, jnp.bitwise_xor(d, k)) for k in bits]
    for p in peers:
        pl.semaphore_signal(b, inc=1, device_id=p, device_id_type=MESH)
    @pl.when(z > 0)
    def _():
        pl.semaphore_signal(b, inc=1, device_id=(h, d - 2), device_id_type=MESH)
    @pl.when(z < n - 1)
    def _():
        pl.semaphore_signal(b, inc=1, device_id=(h, d + 2), device_id_type=MESH)
    pl.semaphore_wait(b, len(peers) + (z > 0).astype(jnp.int32) + (z < n - 1).astype(jnp.int32))

    def col(i, size=Wd):
        return pl.ds(pl.multiple_of(i * size, size), size)

    def at(c):
        return pl.ds(pl.multiple_of(c * CH, CH), CH)

    seq_rows = [pl.ds(s * L, L) for s in range(seqs)]
    bufs = (fb, db, cb)
    jobs = []
    for kind, part in enumerate((da_part, h1_part, mlp_part, xp)):
        for s in range(seqs):
            if kind < 3:
                def beside(side, kind=kind, s=s):
                    return nb[kind, s, side]
            else:
                def beside(side, s=s):
                    r = pl.ds(s * L + side * (L // 2), L // 2)
                    return xp[r, col(jnp.bitwise_xor(h, 2 - side))]
            k = len(jobs)
            jobs.append(Scatter(part, beside, seq_rows[s], bufs, k % SLOTS, as_, ar_, 3 * k))
    jobs[0].one()

    def load(src, dst, k):
        cp = pltpu.make_async_copy(src, dst, ls.at[k])
        cp.start()
        return cp

    first = load(g_ffn, own.at[pl.ds(0, n_ffn)], 0)
    nbs = []
    for kind, part in enumerate((da_part, h1_part, mlp_part)):
        for s in range(seqs):
            for side in (0, 1):
                r = pl.ds(s * L + side * (L // 2), L // 2)
                nbs.append(load(part.at[r, col(jnp.bitwise_xor(h, 2 - side))], nb.at[kind, s, side], 8 + len(nbs)))
    load_da = load(da_own, da_f, 1)
    ins = (q_i, k_i, u_i, t_i, p_i, g_i, r_i, s_i, o_i)
    scr = (q_s, k_s, u_s, t_s, p_s, g_s, r_s, s_s, o_s)

    def fetch(s):
        sl = s % 2
        cps = [pltpu.make_async_copy(qkv.at[seq_rows[s]], qv.at[sl], lds.at[sl, 9]),
               pltpu.make_async_copy(lg.at[seq_rows[s]], lv.at[sl], lds.at[sl, 10])]
        for k, (i, o) in enumerate(zip(ins, scr)):
            cps.append(pltpu.make_async_copy(i.at[:, seq_rows[s]], o.at[sl], lds.at[sl, k]))
        return cps

    for cp in fetch(0):
        cp.start()
    load_w = load(w.at[pl.ds(0, lead + 3 * hd)], wv, 2)
    load_x = load(xf, xv, 3)
    load_dh = load(dh_own, dh_f, 4)
    load_m = load(mlp_own, mlp_f, 5)
    load_h = load(h1_own, h1_f, 6)

    mine, other = col(core, half), col(1 - core, half)

    def remote(src, dst, s, r, dev):
        return pltpu.make_async_remote_copy(src, dst, s, r, device_id=dev, device_id_type=MESH)

    def ring(c):
        return pl.ds(pl.multiple_of(lax.rem(c, RING) * CH, CH), CH)

    def swap(c):
        return remote(own.at[at(c), other], oth.at[at(c)], xs.at[c], xr_.at[c], mate)

    def to_right(c):
        return remote(rst.at[ring(c)], rb.at[at(c)], ss.at[0, c], rs.at[0, c], (h, d + 2))

    def to_left(c):
        return remote(lst.at[ring(c)], lb.at[at(c)], ss.at[1, c], rs.at[1, c], (h, d - 2))

    def give(c):
        return remote(oth.at[at(c)], g_o.at[at(c), mine], fs.at[c], fr.at[c], mate)

    def keep(c):
        return pltpu.make_async_copy(oth.at[at(c)], g_o.at[at(c), mine], gl.at[c])

    def swaps(lo, hi):
        def body(c, carry):
            swap(c).start()
            return carry
        lax.fori_loop(lo, hi, body, 0)

    last = SKEW * jnp.maximum(z, n - 1 - z)

    def step(t, carry):
        @pl.when(t < nc)
        def _():
            swap(t).wait_recv()
            oth[at(t)] = (oth[at(t)].astype(f32) + own[at(t), mine].astype(f32)).astype(bf16)

        c = t - SKEW * z
        @pl.when((c >= 0) & (c < nc))
        def _():
            @pl.when(z > 0)
            def _():
                to_right(c).wait_recv()
            @pl.when(z < n - 1)
            def _():
                @pl.when(c >= RING)
                def _():
                    to_right(c - RING).wait_send()
                @pl.when(z == 0)
                def _():
                    rst[ring(c)] = oth[at(c)]
                @pl.when(z > 0)
                def _():
                    rst[ring(c)] = (oth[at(c)].astype(f32) + rb[at(c)].astype(f32)).astype(bf16)
                to_right(c).start()

        e = t - SKEW * (n - 1 - z)
        @pl.when((e >= 0) & (e < nc))
        def _():
            @pl.when(z < n - 1)
            def _():
                to_left(e).wait_recv()
            @pl.when(z > 0)
            def _():
                @pl.when(e >= RING)
                def _():
                    to_left(e - RING).wait_send()
                @pl.when(z == n - 1)
                def _():
                    lst[ring(e)] = oth[at(e)]
                @pl.when(z < n - 1)
                def _():
                    lst[ring(e)] = (oth[at(e)].astype(f32) + lb[at(e)].astype(f32)).astype(bf16)
                to_left(e).start()

        g = t - last
        @pl.when((g >= 0) & (g < nc))
        def _():
            @pl.when(z == 0)
            def _():
                oth[at(g)] = (oth[at(g)].astype(f32) + lb[at(g)].astype(f32)).astype(bf16)
            @pl.when(z == n - 1)
            def _():
                oth[at(g)] = (oth[at(g)].astype(f32) + rb[at(g)].astype(f32)).astype(bf16)
            @pl.when((z > 0) & (z < n - 1))
            def _():
                oth[at(g)] = (oth[at(g)].astype(f32) + rb[at(g)].astype(f32) + lb[at(g)].astype(f32)).astype(bf16)
            give(g).start()
            keep(g).start()
        return carry

    now = [0]
    end = nc + SKEW * (n - 1)

    def advance(k):
        hi = min(now[0] + k, end)
        if hi > now[0]:
            lax.fori_loop(now[0], hi, step, 0)
        now[0] = hi

    first.wait()
    swaps(0, at_qkv // CH)
    for ref in (dt_w, dg_w, g1_w, gq, gs):
        ref[...] = jnp.zeros_like(ref)
    advance(1)
    for cp in nbs:
        cp.wait()
    jobs[0].two()
    jobs[1].one()
    advance(1)
    load_da.wait()

    def finish(k):
        kind, s = k // seqs, k % seqs
        got = jobs[k].three()
        for side in (0, 1):
            r = pl.ds(s * L + side * (L // 2), L // 2)
            if kind == 0:
                da_f[r] += got[side]
            elif kind == 1:
                dh_f[r] += got[side]
            elif kind == 2:
                m = mlp_f[r] + got[side]
                y = h1_f[r] + m
                y_o[r] = y.astype(bf16)
                v = valid[r, 0:1]
                lane = lax.broadcasted_iota(jnp.int32, (1, width), 1)
                sy = jnp.sum(jnp.sum(v * y * y, -1, keepdims=True), 0, keepdims=True)
                sm = jnp.sum(jnp.sum(v * m * m, -1, keepdims=True), 0, keepdims=True)
                st_w[0, 3:4] += jnp.where(lane == 0, sy, jnp.where(lane == 2, sm, 0.0))
            else:
                ig_o[r] = dh_f[r] + xp[r, col(h)].astype(f32) + got[side]

    turn = [1]

    def relay():
        k = turn[0]
        if k < len(jobs):
            jobs[k].two()
        if k + 1 < len(jobs):
            jobs[k + 1].one()
        if k - 1 < len(jobs):
            finish(k - 1)
        turn[0] += 1

    st_w[0] = stat_in[...]
    advance(1)
    for s in range(seqs):
        sl = s % 2
        for cp in fetch(s):
            cp.wait()
        if s + 1 < seqs:
            for cp in fetch(s + 1):
                cp.start()
        if s == 0:
            finish0 = True
            relay()
        sub = [ref.at[sl] for ref in scr]
        q_, k_, u_, t_, p_, g_, r_, s_, o_ = sub
        x_, l_ = qv.at[sl], lv.at[sl]
        bwd_blocks(da_f.at[seq_rows[s]], gout, o_, q_, k_, u_, p_, s_, dg_w, do_w, w_w, dq_w, dk_w, qd_w, heads, chunks)
        advance(1)
        if s > 0:
            relay()
        bwd_states(l_, k_, t_, w_w, qd_w, ds_w, heads, chunks)
        advance(1)
        bwd_conv(x_, l_, taps, q_, k_, u_, g_, r_, s_, w_w, dq_w, dk_w, ds_w, dc, dx_w, dlg_w, dt_w, heads, chunks)
        advance(1)
        relay()
        if s == 0:
            load_w.wait()
            load_x.wait()
            load_dh.wait()
            load_m.wait()
            load_h.wait()
        for i in range(2):
            lo = i * (L // 2)
            r = pl.ds(s * L + lo, L // 2)
            here = pl.ds(lo, L // 2)
            xx = xv[r].astype(f32)
            r1 = lax.rsqrt(jnp.mean(xx * xx, -1, keepdims=True) + norm_eps)
            xn = xx * r1
            n1_w[here] = (xn * gain[0:1]).astype(bf16)
            dn = dot(dx_w[here], wv[lead:]) + dot(dlg_w[here], wv[0:lead])
            g1_w[0:1] += jnp.sum(dn * xn, 0, keepdims=True)
            gd = dn * gain[0:1]
            xp[r] = (r1 * (gd - xn * jnp.mean(gd * xn, -1, keepdims=True))).astype(bf16)
        gq[...] += tdot(dx_w[...], n1_w[...])
        gs[...] += tdot(dlg_w[...], n1_w[...])
        if s + 1 < seqs:
            advance(1)
    load_a = pltpu.make_async_copy(af, xv, ls.at[7])
    load_a.start()
    own[pl.ds(at_qkv, 3 * hd)] = gq[...].astype(bf16)
    swaps(at_qkv // CH, at_out // CH)
    advance(1)
    while turn[0] <= 2 * seqs:
        relay()
        advance(1)
    load_a.wait()
    go_w[...] = tdot(xv[...], dh_f[...].astype(bf16)).astype(bf16)
    ex = []
    for k in (1, 2, 3):
        p = jnp.bitwise_xor(h, k)
        cp = remote(go_w.at[col(p, hd)], own.at[pl.ds(at_out, hd), col(h)], a2s.at[k - 1], a2r.at[k - 1], (p, d))
        cp.start()
        ex.append(cp)
    own[pl.ds(at_out, hd), col(h)] = go_w[col(h, hd)]
    line = 3 * hd
    dt = jnp.concatenate([dt_w[j : j + 1] for j in range(KCONV)], 1)
    row = lax.broadcasted_iota(jnp.int32, (lead, width), 0)
    tail = gs[...]
    for i in range(small - hl):
        tail = jnp.where(row == hl + i, dt[:, i * width : (i + 1) * width], tail)
    tail = jnp.where(row < small, tail, 0.0)
    own[pl.ds(at_small, lead)] = tail.astype(bf16)
    advance(1)
    relay()
    for cp in ex:
        cp.wait()
    swaps(at_out // CH, nc)
    lane = lax.broadcasted_iota(jnp.int32, (1, width), 1)
    three = jnp.concatenate([dg_w[0:1]] * 4, 1)
    st_w[0, 0:1] = g1_w[0:1]
    st_w[0, 2:3] = jnp.where((lane >= h * Wd) & (lane < (h + 1) * Wd), three, 0.0)
    advance(2)
    while turn[0] <= 3 * seqs:
        relay()
        advance(2)
    rounds = [(jnp.bitwise_xor(h, k), d) for k in (1, 2)] + [mate] + [(h, jnp.bitwise_xor(d, k)) for k in bits]
    sent = []
    for i, p in enumerate(rounds):
        cp = remote(st_w.at[i], str_.at[i], sts.at[0, i], sts.at[1, i], p)
        cp.start()
        sent.append(cp)
        if turn[0] <= len(jobs):
            relay()
        advance(2)
        cp.wait_recv()
        st_w[i + 1] = st_w[i] + str_[i]
    stat_o[...] = st_w[len(rounds)]
    while turn[0] <= len(jobs):
        relay()
        advance(2)
    advance(end)
    for cp in sent:
        cp.wait_send()

    def drain(c, carry):
        swap(c).wait_send()
        give(c).wait()
        keep(c).wait()
        @pl.when(c >= nc - RING)
        def _():
            @pl.when(z < n - 1)
            def _():
                to_right(c).wait_send()
            @pl.when(z > 0)
            def _():
                to_left(c).wait_send()
        return carry

    lax.fori_loop(0, nc, drain, 0)


def back(gain, gout, taps, stat_in, valid, order, parts, owns, xf, af, w, g_ffn, qkv, lg, saved, seqs, heads, lead, hl, small, cid):
    T, width = xf.shape
    Wd = width // 4
    half = width // 2
    L = T // seqs
    hd = heads * DK
    n_ffn = g_ffn.shape[0]
    rows = n_ffn + 4 * hd + lead
    nc = rows // CH
    hbm = pl.BlockSpec(memory_space=pl.ANY)
    S = jax.ShapeDtypeStruct
    V = pltpu.VMEM
    n = lax.axis_size("dp") // 2
    rounds = 2 + 1 + max(n.bit_length() - 1, 0)
    piece, ringbuf = V((rows, half), bf16), V((RING * CH, half), bf16)
    blk = lambda dt: V((2, heads, L, DK), dt)
    wk = lambda dt: V((heads, L, DK), dt)
    rsb = V((SLOTS, 2, L // 2, Wd), bf16)
    njobs = 4 * seqs
    return pl.pallas_call(
        functools.partial(back_kernel, seqs=seqs, heads=heads, lead=lead, n_ffn=n_ffn, hl=hl, small=small),
        in_specs=[VM()] * 6 + [hbm] * 22,
        out_specs=[VM(), VM(), VM(), hbm],
        out_shape=[S((T, Wd), bf16), S((T, Wd), f32), S((8, width), f32), S((rows, width), bf16)],
        scratch_shapes=[
            V((rows, width), bf16), piece, piece, piece, ringbuf, ringbuf,
            V((2, L, 3 * hd), f32), V((2, L, lead), f32), *[blk(bf16)] * 8, blk(f32),
            wk(bf16), wk(f32), wk(f32), wk(f32), wk(f32), wk(bf16), V((L + 8, 3 * hd), f32),
            V((T, width), bf16), V((lead + 3 * hd, width), bf16), V((3, seqs, 2, L // 2, Wd), bf16),
            V((T, Wd), f32), V((T, Wd), f32), V((T, Wd), f32), V((T, Wd), f32), V((T, width), bf16), rsb, rsb, rsb,
            V((3 * hd, width), f32), V((lead, width), f32), V((L, width), bf16), V((L, 3 * hd), bf16), V((L, lead), bf16),
            V((8, 3 * hd), f32), V((8, hd), f32), V((8, width), f32), V((rounds + 1, 8, width), f32), V((4 * hd, Wd), bf16),
            DMA((nc,)), DMA((nc,)), DMA((nc,)), DMA((nc,)), DMA((nc,)), DMA((2, nc)), DMA((2, nc)),
            DMA((2, 3 * njobs)), DMA((2, 3 * njobs)), DMA((8 + 6 * seqs,)), DMA((2, 11)), DMA((3,)), DMA((3,)),
            DMA((2, rounds)), V((rounds, 8, width), f32),
        ],
        compiler_params=pltpu.CompilerParams(collective_id=cid, has_side_effects=True, vmem_limit_bytes=63 << 20),
        name="back",
    )(gain, gout, taps, stat_in, valid, order, *parts, *owns, xf, af, w, g_ffn, qkv, lg, *saved)


def cols_of(x, rows):
    return lax.dot_general(x, rows, (((1,), (1,)), ((), ())), preferred_element_type=f32)


def over_tokens(left, right):
    return lax.dot_general(left, right, (((0,), (0,)), ((), ())), preferred_element_type=f32)


def adam_step(param, first, second_moment, grad, rate, decay):
    first = beta_one * first + (1.0 - beta_one) * grad
    second_moment = beta_two * second_moment + (1.0 - beta_two) * grad * grad
    denom = jnp.sqrt(second_moment / (1.0 - beta_two**STEP)) + adam_eps
    param = param - rate / (1.0 - beta_one**STEP) * first / denom - rate * decay * param
    return (param, first, second_moment)


def on_device(
    inputs, cotangent, lengths, owner_slots, table, table_m, table_v, gains, gains_m, gains_v
):
    shards = lax.axis_size("head")
    width = inputs.shape[1]
    tokens = inputs.shape[0]
    seqs = lengths.shape[0]
    slot_len = tokens // seqs
    hd = HEADS * DK // shards
    ffl = FF // shards
    hl = HEADS // shards
    taps_rows = KCONV * 3 * hd // MODEL_WIDTH
    capacity = table.shape[1]
    first_col = lax.axis_index("head") * width
    small = hl + taps_rows
    lead = 64
    at_out = lead + 3 * hd
    at_gate = at_out + hd
    at_up = at_gate + ffl
    at_down = at_up + ffl
    total = at_down + ffl
    n_qkv, n_body = 3 * hd, 4 * hd + 3 * ffl
    order = jnp.concatenate(
        [owner_slots[n_body:], jnp.full((lead - small,), -1, jnp.int32), owner_slots[:n_body]]
    )
    mine = order - lax.axis_index("dp") * capacity
    padded = -(-capacity // 128) * 128
    tab = jnp.pad(table[0].astype(bf16), ((0, padded - capacity), (0, 0)))
    valid = (jnp.arange(slot_len)[None, :] < lengths[:, None]).reshape(tokens, 1).astype(f32)
    masked = (cotangent.astype(f32) * valid).astype(bf16)
    gain_out = lax.dynamic_slice_in_dim(gains[2], first_col, width)[None]
    weights, x_full, cot_full, a_full, out_full, qkv, logit, *saved = front(
        tab, mine[:, None], gains, gain_out, inputs, masked, seqs, hl, lead, at_out, at_gate, hl, small, 1
    )
    taps = weights[hl:small].astype(f32).reshape(KCONV, 3 * hd)
    x32 = x_full.astype(f32)

    attn = jnp.dot(a_full, out_full, preferred_element_type=f32)
    h1 = x32 + attn
    r2 = lax.rsqrt(jnp.mean(h1 * h1, -1, keepdims=True) + norm_eps)
    n2 = (h1 * r2 * gains[1]).astype(bf16)
    w_gu = weights[at_gate:at_down]
    w_down = weights[at_down:]
    gu = cols_of(n2, w_gu)
    gate, up = gu[:, :ffl], gu[:, ffl:]
    sig = jax.nn.sigmoid(gate)
    act = gate * sig
    hidden = (act * up).astype(bf16)
    mlp_part = jnp.dot(hidden, w_down, preferred_element_type=f32)
    d_hidden = cols_of(cot_full, w_down)
    d_gate = d_hidden * up * sig * (1.0 + gate * (1.0 - sig))
    d_up = d_hidden * act
    d_gu = jnp.concatenate([d_gate, d_up], 1).astype(bf16)
    dn2 = jnp.dot(d_gu, w_gu, preferred_element_type=f32)
    g_dn2 = dn2 * gains[1]
    h1_part = r2 * g_dn2 - h1 * (r2**3 * jnp.sum(g_dn2 * h1, -1, keepdims=True) / MODEL_WIDTH)
    gain_two = jnp.sum(dn2 * h1 * r2, 0)
    h1_low = h1_part.astype(bf16)
    da_part = cols_of(h1_low, out_full)

    def mine_of(t):
        return lax.dynamic_slice_in_dim(t, first_col, width, 1)

    da_own = mine_of(da_part) + cols_of(cot_full, weights[at_out:at_gate])
    dh_own = masked.astype(f32) + mine_of(h1_part)
    mlp_own = mine_of(mlp_part)
    attn_loc = mine_of(attn)
    h1_own = inputs.astype(f32) + attn_loc
    g_ffn = jnp.concatenate(
        [over_tokens(d_gu, n2).astype(bf16), over_tokens(hidden, cot_full).astype(bf16)], 0
    )
    stat_in = jnp.zeros((8, MODEL_WIDTH), f32).at[1].set(gain_two)
    stat_in = stat_in.at[3, 1].set(jnp.sum(valid * attn_loc * attn_loc))
    stat_in = stat_in.at[3, 3].set(jnp.sum(valid) * width)
    y, input_grad, stats, g_total = back(
        gains, gain_out, taps, stat_in, valid, mine.reshape(-1, 128),
        [da_part.astype(bf16), h1_low, mlp_part.astype(bf16)], [da_own, dh_own, mlp_own, h1_own],
        x_full, a_full, weights, g_ffn, qkv, logit, saved, seqs, hl, lead, hl, small, 2,
    )
    mine = jnp.concatenate([mine[at_gate:], mine[lead:at_gate], mine[:lead]])
    pick = (mine[:, None] == jnp.arange(capacity, dtype=jnp.int32)[None, :]).astype(bf16)
    owned = lax.dot_general(
        pick, g_total, (((0,), (0,)), ((), ())), preferred_element_type=f32
    )
    table_new, table_m_new, table_v_new = adam_step(
        table[0], table_m[0], table_v[0], owned, weight_rate, weight_decay
    )

    gains_grad, total_squares, total_entries = stats[0:3], stats[3, 0:3], stats[3, 3]
    gains_new, gains_m_new, gains_v_new = adam_step(
        gains, gains_m, gains_v, gains_grad, gain_rate, 0.0
    )
    rms_stats = jnp.sqrt(total_squares / total_entries)
    return (
        y,
        input_grad,
        table_new[None],
        table_m_new[None],
        table_v_new[None],
        gains_new,
        gains_m_new,
        gains_v_new,
        rms_stats,
    )


def solution(mesh):
    tok, tab = P("dp", "head"), P("head", "dp", None)
    return jax.shard_map(
        on_device,
        mesh=mesh,
        in_specs=(tok, tok, P("dp"), P(), tab, tab, tab, P(), P(), P()),
        out_specs=(tok, tok, tab, tab, tab, P(), P(), P(), P()),
        check_vma=False,
    )
```

```python
import functools

import jax
import jax.numpy as jnp
from jax import lax
from jax.experimental import pallas as pl
from jax.experimental.pallas import tpu as pltpu
from jax.sharding import PartitionSpec as P

MODEL_WIDTH = 1024
FF = 2816
HEADS = 8
DK = 128
KCONV = 4
STEP = 10
C = 128

norm_eps = 1e-06
adam_eps = 1e-08
beta_one = 0.9
beta_two = 0.95
weight_rate = 0.02
gain_rate = 0.6
weight_decay = 0.1
f32 = jnp.float32
bf16 = jnp.bfloat16
MESH = pl.DeviceIdType.MESH
VM = functools.partial(pl.BlockSpec, memory_space=pltpu.VMEM)
DMA = pltpu.SemaphoreType.DMA

def dot(a,b): return lax.dot_general(a,b,(((1,),(0,)),((),())),preferred_element_type=f32)
def dot_t(a,b): return lax.dot_general(a,b,(((1,),(1,)),((),())),preferred_element_type=f32)
def tdot(a,b): return lax.dot_general(a,b,(((0,),(0,)),((),())),preferred_element_type=f32)

def shifted(x, prev, j):
    if j==0: return x
    r=pltpu.roll(x,j,0)
    p=pltpu.roll(prev,j,0)
    row=lax.broadcasted_iota(jnp.int32,(8,x.shape[1]),0)
    top=jnp.where(row<j,p,r[0:8])
    return jnp.concatenate([top,r[8:]],0)

def conv_silu(x,prev,taps):
    conv=taps[3:4]*x
    for j in range(1,4):
        conv=conv+taps[3-j:4-j]*shifted(x,prev,j)
    sg=jax.nn.sigmoid(conv)
    return conv,sg

def masks():
    i=lax.broadcasted_iota(jnp.int32,(C,C),0); j=lax.broadcasted_iota(jnp.int32,(C,C),1)
    return i,j

def fwd_kernel(x_ref,lg_ref,taps_ref,gain_ref,a_ref,q_s,k_s,u_s,t_s,p_s,g_s,r_s,s_s,o_s,l_w,*,heads,chunks):
    i,j=masks()
    low=j<=i; slow=j<i; xr=jnp.bitwise_xor(i,j)
    zero8=jnp.zeros((8,DK),f32)
    every=[(c,h) for c in range(chunks) for h in range(heads)]
    beta={}
    for c,h in every:
        rows=slice(c*C,(c+1)*C)
        pre={}
        for n,off in (("q",0),("k",heads*DK),("v",2*heads*DK)):
            cols=slice(off+h*DK,off+(h+1)*DK)
            x=x_ref[rows,cols]
            prev=zero8 if c==0 else x_ref[c*C-8:c*C,cols]
            conv,sg=conv_silu(x,prev,taps_ref[:,cols])
            pre[n]=conv*sg
        q=pre["q"]; q=q*(lax.rsqrt(jnp.sum(q*q,-1,keepdims=True)+norm_eps)*DK**-0.5)
        k=pre["k"]; k=k*lax.rsqrt(jnp.sum(k*k,-1,keepdims=True)+norm_eps)
        qb=q.astype(bf16); kb=k.astype(bf16)
        beta[c,h]=jax.nn.sigmoid(lg_ref[rows,h:h+1])
        sc=dot_t(jnp.concatenate([qb,kb],0),kb)
        G=sc[C:]
        Lw=jnp.where(slow,G*beta[c,h],0.0).astype(bf16)
        q_s[h,rows]=qb; k_s[h,rows]=kb; p_s[h,rows]=jnp.where(low,sc[0:C],0.0).astype(bf16); g_s[h,rows]=G.astype(bf16)
        r_s[h,rows]=pre["v"].astype(bf16)
        l_w[h,rows]=Lw
        t_s[h,rows]=jnp.where(xr==0,1.0,jnp.where(xr==1,-Lw.astype(f32),0.0)).astype(bf16)
    s=2
    while s<C:
        part=(xr>=s)&(xr<2*s)
        half=[dot(t_s[h,c*C:(c+1)*C],jnp.where(part,l_w[h,c*C:(c+1)*C],jnp.zeros((C,C),bf16))).astype(bf16) for c,h in every]
        for (c,h),y in zip(every,half):
            rows=slice(c*C,(c+1)*C)
            X=t_s[h,rows]
            t_s[h,rows]=X-dot(y,X).astype(bf16)
        s*=2
    S=[jnp.zeros((DK,DK),f32) for _ in range(heads)]
    for c in range(chunks):
        rows=slice(c*C,(c+1)*C)
        Sb=[S[h].astype(bf16) for h in range(heads)]
        m=[dot(jnp.concatenate([k_s[h,rows],q_s[h,rows]],0),Sb[h]) for h in range(heads)]
        R=[r_s[h,rows].astype(f32)-m[h][0:C] for h in range(heads)]
        ub=[dot(t_s[h,rows],(R[h]*beta[c,h]).astype(bf16)).astype(bf16) for h in range(heads)]
        S=[S[h]+tdot(k_s[h,rows],ub[h]) for h in range(heads)]
        for h in range(heads):
            s_s[h,rows]=Sb[h]; r_s[h,rows]=R[h].astype(bf16); u_s[h,rows]=ub[h]
            o=m[h][C:]+dot(p_s[h,rows],ub[h])
            o_s[h,rows]=o
            a=o*lax.rsqrt(jnp.mean(o*o,-1,keepdims=True)+norm_eps)*gain_ref[0:1,h*DK:(h+1)*DK]
            a_ref[rows,h*DK:(h+1)*DK]=a.astype(bf16)

def mixer_fwd(x,lg,taps,gain,seqs):
    T=x.shape[0]; L=T//seqs; W=x.shape[1]; heads=W//(3*DK)
    blk=lambda: pl.BlockSpec((heads,L,DK),lambda s:(0,s,0))
    sav=lambda dt: jax.ShapeDtypeStruct((heads,T,DK),dt)
    return pl.pallas_call(functools.partial(fwd_kernel,heads=heads,chunks=L//C),
        grid=(seqs,),
        in_specs=[pl.BlockSpec((L,W),lambda s:(s,0)),pl.BlockSpec((L,lg.shape[1]),lambda s:(s,0)),pl.BlockSpec(taps.shape,lambda s:(0,0)),pl.BlockSpec(gain.shape,lambda s:(0,0))],
        out_specs=[pl.BlockSpec((L,heads*DK),lambda s:(s,0))]+[blk() for _ in range(9)],
        out_shape=[jax.ShapeDtypeStruct((T,heads*DK),bf16)]+[sav(bf16) for _ in range(8)]+[sav(f32)],
        scratch_shapes=[pltpu.VMEM((heads,L,DK),bf16)],
        compiler_params=pltpu.CompilerParams(vmem_limit_bytes=56<<20),
        cost_estimate=pl.CostEstimate(flops=2*24*20*C*C*C,bytes_accessed=15<<20,transcendentals=0),
        name="mixer_fwd")(x,lg,taps,gain)

def bwd_kernel(x_ref,lg_ref,taps_ref,gain_ref,da_ref,q_s,k_s,u_s,t_s,p_s,g_s,r_s,s_s,o_s,dx_ref,dlg_ref,dt_ref,dg_ref,dc,*,heads,chunks):
    i,j=masks()
    low=j<=i; slow=j<i
    zero8=jnp.zeros((8,DK),f32)
    seq=pl.program_id(0)
    @pl.when(seq==0)
    def _():
        dt_ref[...]=jnp.zeros_like(dt_ref); dg_ref[...]=jnp.zeros_like(dg_ref)
    dS=[jnp.zeros((DK,DK),f32) for _ in range(heads)]
    W=heads*DK
    lane=lax.broadcasted_iota(jnp.int32,(C,128),1)
    dc[chunks*C:chunks*C+8]=jnp.zeros((8,3*W),f32)
    for c in reversed(range(chunks)):
        rows=slice(c*C,(c+1)*C)
        dlg=jnp.zeros((C,128),f32)
        for h in range(heads):
            hc=slice(h*DK,(h+1)*DK)
            o=o_s[h,rows]
            ro=lax.rsqrt(jnp.mean(o*o,-1,keepdims=True)+norm_eps)
            da=da_ref[rows,hc]
            on=o*ro
            dg_ref[0:1,hc]+=jnp.sum(da*on,0,keepdims=True)
            t=da*gain_ref[0:1,hc]
            do=(ro*(t-on*jnp.mean(t*on,-1,keepdims=True))).astype(bf16)
            qb=q_s[h,rows]; kb=k_s[h,rows]; ub=u_s[h,rows]; Tb=t_s[h,rows]; Pb=p_s[h,rows]; Sb=s_s[h,rows]
            G=g_s[h,rows].astype(f32); R=r_s[h,rows].astype(f32)
            beta=jax.nn.sigmoid(lg_ref[rows,h:h+1])
            dSb=dS[h].astype(bf16)
            du=tdot(Pb,do)+dot(kb,dSb)
            e=tdot(Tb,du.astype(bf16))
            eb=e.astype(bf16)
            be=beta*e; beb=be.astype(bf16)
            pe=dot_t(jnp.concatenate([do,eb],0),ub)
            dP=jnp.where(low,pe[0:C],0.0).astype(bf16)
            dL=jnp.where(slow,-pe[C:],0.0)
            dG=beta*dL
            ds=dot_t(jnp.concatenate([do,beb],0),Sb)
            dq=ds[0:C]+dot(dP,kb)
            dGb=dG.astype(bf16)
            dk=tdot(dP,qb)+dot_t(ub,dSb)-ds[C:]+dot(dGb,kb)+tdot(dGb,kb)
            db=jnp.sum(e*R+dL*G,-1,keepdims=True)
            dlg=jnp.where(lane==h,db*beta*(1.0-beta),dlg)
            dS[h]=dS[h]+tdot(qb,do)-tdot(kb,beb)
            for n,off in (("q",0),("k",W),("v",2*W)):
                cols=slice(off+h*DK,off+(h+1)*DK)
                x=x_ref[rows,cols]
                prev=zero8 if c==0 else x_ref[c*C-8:c*C,cols]
                conv,sg=conv_silu(x,prev,taps_ref[:,cols])
                act=conv*sg
                if n=="v": d=be
                else:
                    r=lax.rsqrt(jnp.sum(act*act,-1,keepdims=True)+norm_eps)
                    g_=dq*DK**-0.5 if n=="q" else dk
                    an=act*r
                    d=r*(g_-an*jnp.sum(g_*an,-1,keepdims=True))
                dconv=d*(sg*(1.0+conv*(1.0-sg)))
                dc[rows,cols]=dconv
                for jj in range(4):
                    dt_ref[jj:jj+1,cols]+=jnp.sum(dconv*shifted(x,prev,3-jj),0,keepdims=True)
                nxt=dc[(c+1)*C:(c+1)*C+8,cols]
                tp=taps_ref[:,cols]
                dx=tp[3:4]*dconv
                row8=lax.broadcasted_iota(jnp.int32,(8,DK),0)
                for jj in range(1,4):
                    r=pltpu.roll(dconv,C-jj,0)
                    pn=pltpu.roll(nxt,8-jj,0)
                    bot=jnp.where(row8>=8-jj,pn,r[C-8:])
                    dx=dx+tp[3-jj:4-jj]*jnp.concatenate([r[:C-8],bot],0)
                dx_ref[rows,cols]=dx.astype(bf16)
        dlg_ref[rows]=dlg.astype(bf16)

def mixer_bwd(x,lg,taps,gain,da,saved,seqs):
    T=x.shape[0]; L=T//seqs; W=x.shape[1]; heads=W//(3*DK)
    blk=lambda: pl.BlockSpec((heads,L,DK),lambda s:(0,s,0))
    return pl.pallas_call(functools.partial(bwd_kernel,heads=heads,chunks=L//C),
        grid=(seqs,),
        in_specs=[pl.BlockSpec((L,W),lambda s:(s,0)),pl.BlockSpec((L,lg.shape[1]),lambda s:(s,0)),pl.BlockSpec(taps.shape,lambda s:(0,0)),pl.BlockSpec(gain.shape,lambda s:(0,0)),pl.BlockSpec((L,heads*DK),lambda s:(s,0))]+[blk() for _ in range(9)],
        out_specs=[pl.BlockSpec((L,W),lambda s:(s,0)),pl.BlockSpec((L,128),lambda s:(s,0)),pl.BlockSpec((8,W),lambda s:(0,0)),pl.BlockSpec((8,heads*DK),lambda s:(0,0))],
        out_shape=[jax.ShapeDtypeStruct((T,W),bf16),jax.ShapeDtypeStruct((T,128),bf16),jax.ShapeDtypeStruct((8,W),f32),jax.ShapeDtypeStruct((8,heads*DK),f32)],
        scratch_shapes=[pltpu.VMEM((L+8,W),f32)],
        compiler_params=pltpu.CompilerParams(vmem_limit_bytes=56<<20),
        cost_estimate=pl.CostEstimate(flops=2*24*20*C*C*C,bytes_accessed=15<<20,transcendentals=0),
        name="mixer_bwd")(x,lg,taps,gain,da,*saved)


def meet(partners):
    b=pltpu.get_barrier_semaphore()
    for p in partners:
        pl.semaphore_signal(b,inc=1,device_id=p,device_id_type=MESH)
    pl.semaphore_wait(b,len(partners))

def ag_kernel(*refs,count,parts):
    ins=refs[:count]; outs=refs[count:2*count]; ss,rs,ls=refs[2*count:]
    h=lax.axis_index("head"); d=lax.axis_index("dp")
    meet([(jnp.bitwise_xor(h,1),d),(jnp.bitwise_xor(h,2),d)])
    def copy(src,dst,to,k):
        return pltpu.make_async_remote_copy(src,dst,ss.at[to-1,k],rs.at[to-1,k],device_id=(jnp.bitwise_xor(h,to),d),device_id_type=MESH)
    first={}; second=[]; local=[]
    for n in range(count):
        x,o=ins[n],outs[n]
        T,Wd=x.shape; R=T//(2*parts); base=n*3*parts
        def col(b): return pl.ds(pl.multiple_of(b*Wd,Wd),Wd)
        for i in range(2*parts):
            r1=pl.ds(i*R,R); j=(i+parts)%(2*parts); r2=pl.ds(j*R,R)
            first[n,1,i]=copy(x.at[r1],o.at[r1,col(h)],1,base+i); first[n,1,i].start()
            first[n,2,j]=copy(x.at[r2],o.at[r2,col(h)],2,base+j); first[n,2,j].start()
        l=pltpu.make_async_copy(x,o.at[:,col(h)],ls.at[n]); l.start(); local.append(l)
    for n in range(count):
        x,o=ins[n],outs[n]
        T,Wd=x.shape; R=T//(2*parts); base=n*3*parts
        def col(b): return pl.ds(pl.multiple_of(b*Wd,Wd),Wd)
        for i in range(parts):
            ra=pl.ds(i*R,R); rb=pl.ds((i+parts)*R,R)
            ca=col(jnp.bitwise_xor(h,1)); cb=col(jnp.bitwise_xor(h,2))
            first[n,1,i].wait_recv()
            c=copy(o.at[ra,ca],o.at[ra,ca],2,base+2*parts+i); c.start(); second.append(c)
            first[n,2,i+parts].wait_recv()
            c=copy(o.at[rb,cb],o.at[rb,cb],1,base+2*parts+i); c.start(); second.append(c)
    for n in range(count):
        for i in range(parts):
            first[n,1,i+parts].wait_recv(); first[n,2,i].wait_recv()
    for c in second: c.wait()
    for c in first.values(): c.wait_send()
    for l in local: l.wait()

def gather_columns(arrays,parts,cid):
    n=len(arrays)
    return pl.pallas_call(functools.partial(ag_kernel,count=n,parts=parts),
        in_specs=[VM()]*n,out_specs=[VM()]*n,
        out_shape=[jax.ShapeDtypeStruct((a.shape[0],4*a.shape[1]),a.dtype) for a in arrays],
        scratch_shapes=[DMA((2,3*parts*n)),DMA((2,3*parts*n)),DMA((n,))],
        compiler_params=pltpu.CompilerParams(collective_id=cid,has_side_effects=True,vmem_limit_bytes=56<<20),name="gather_columns")(*arrays)

def rs_kernel(*refs,count,parts):
    ins=refs[:count]; outs=refs[count:2*count]; fb,db,cb,sb,ss,rs=refs[2*count:]
    h=lax.axis_index("head"); d=lax.axis_index("dp")
    h1,h2,h3=[jnp.bitwise_xor(h,k) for k in (1,2,3)]
    meet([(h1,d),(h2,d)])
    T=ins[0].shape[0]; Wd=ins[0].shape[1]//4; half=T//2; R=half//parts
    def col(b): return pl.ds(pl.multiple_of(b*Wd,Wd),Wd)
    def copy(src,dst,to,k):
        return pltpu.make_async_remote_copy(src,dst,ss.at[to-1,k],rs.at[to-1,k],device_id=(jnp.bitwise_xor(h,to),d),device_id_type=MESH)
    K=lambda n,p,kind: (n*parts+p)*3+kind
    fw={}; dr={}; cm={}
    for n in range(count):
        x=ins[n]
        for p in range(parts):
            for side,to,nb in ((0,1,h1),(1,2,h2)):
                r=pl.ds(side*half+p*R,R); q=pl.ds(p*R,R)
                fw[n,p,side]=copy(x.at[r,col(h3)],fb.at[n,side,q],to,K(n,p,0)); fw[n,p,side].start()
            for side,to,nb in ((0,1,h1),(1,2,h2)):
                r=pl.ds(side*half+p*R,R); q=pl.ds(p*R,R)
                dr[n,p,side]=copy(x.at[r,col(nb)],db.at[n,side,q],to,K(n,p,1)); dr[n,p,side].start()
    for n in range(count):
        x=ins[n]
        for p in range(parts):
            for side,to,nb in ((0,2,h2),(1,1,h1)):
                r=pl.ds(side*half+p*R,R); q=pl.ds(p*R,R)
                fw[n,p,side].wait_recv()
                sb[n,side,q]=(fb[n,side,q].astype(f32)+x[r,col(nb)].astype(f32)).astype(bf16)
                cm[n,p,side]=copy(sb.at[n,side,q],cb.at[n,side,q],to,K(n,p,2)); cm[n,p,side].start()
    for n in range(count):
        x,o=ins[n],outs[n]
        for p in range(parts):
            for side in (0,1):
                r=pl.ds(side*half+p*R,R); q=pl.ds(p*R,R)
                dr[n,p,side].wait_recv()
                cm[n,p,side].wait_recv()
                o[r]=x[r,col(h)].astype(f32)+db[n,side,q].astype(f32)+cb[n,side,q].astype(f32)
    for g in (fw,dr,cm):
        for c in g.values(): c.wait_send()

def scatter_columns(arrays,parts,cid):
    n=len(arrays); T=arrays[0].shape[0]; Wd=arrays[0].shape[1]//4
    buf=pltpu.VMEM((n,2,T//2,Wd),bf16)
    return pl.pallas_call(functools.partial(rs_kernel,count=n,parts=parts),
        in_specs=[VM()]*n,out_specs=[VM()]*n,
        out_shape=[jax.ShapeDtypeStruct((T,Wd),f32) for a in arrays],
        scratch_shapes=[buf]*4+[DMA((2,3*parts*n)),DMA((2,3*parts*n))],
        compiler_params=pltpu.CompilerParams(collective_id=cid,has_side_effects=True,vmem_limit_bytes=60<<20),name="scatter_columns")(*arrays)

def scan_kernel(own,out,oth,rb,lb,rst,lst,xs,xr,fs,fr,ss,rs,*,chunk,skew):
    h=lax.axis_index("head"); d=lax.axis_index("dp"); n=lax.axis_size("dp")//2
    z=d//2; core=lax.rem(d,2)
    mate=(h,jnp.bitwise_xor(d,1)); right=(h,d+2); left=(h,d-2)
    rows=own.shape[0]; Wd=own.shape[1]//2; nc=rows//chunk
    b=pltpu.get_barrier_semaphore()
    pl.semaphore_signal(b,inc=1,device_id=mate,device_id_type=MESH)
    @pl.when(z>0)
    def _(): pl.semaphore_signal(b,inc=1,device_id=left,device_id_type=MESH)
    @pl.when(z<n-1)
    def _(): pl.semaphore_signal(b,inc=1,device_id=right,device_id_type=MESH)
    pl.semaphore_wait(b,1+(z>0).astype(jnp.int32)+(z<n-1).astype(jnp.int32))
    mine=pl.ds(pl.multiple_of(core*Wd,Wd),Wd); other=pl.ds(pl.multiple_of((1-core)*Wd,Wd),Wd)
    def at(c): return pl.ds(pl.multiple_of(c*chunk,chunk),chunk)
    def remote(src,dst,s,r,dev): return pltpu.make_async_remote_copy(src,dst,s,r,device_id=dev,device_id_type=MESH)
    def swap(c): return remote(own.at[at(c),other],oth.at[at(c)],xs.at[c],xr.at[c],mate)
    def give(c): return remote(out.at[at(c),mine],out.at[at(c),mine],fs.at[c],fr.at[c],mate)
    def goR(c): return remote(rst.at[at(c)],rb.at[at(c)],ss.at[0,c],rs.at[0,c],right)
    def goL(c): return remote(lst.at[at(c)],lb.at[at(c)],ss.at[1,c],rs.at[1,c],left)
    def issue(c,carry):
        swap(c).start(); return carry
    lax.fori_loop(0,nc,issue,0)
    last=skew*jnp.maximum(z,n-1-z)
    def step(t,carry):
        @pl.when(t<nc)
        def _():
            swap(t).wait_recv()
            oth[at(t)]=(oth[at(t)].astype(f32)+own[at(t),mine].astype(f32)).astype(bf16)
        c=t-skew*z
        @pl.when((c>=0)&(c<nc))
        def _():
            @pl.when(z>0)
            def _(): goR(c).wait_recv()
            @pl.when(z<n-1)
            def _():
                @pl.when(z==0)
                def _(): rst[at(c)]=oth[at(c)]
                @pl.when(z>0)
                def _(): rst[at(c)]=(oth[at(c)].astype(f32)+rb[at(c)].astype(f32)).astype(bf16)
                goR(c).start()
        e=t-skew*(n-1-z)
        @pl.when((e>=0)&(e<nc))
        def _():
            @pl.when(z<n-1)
            def _(): goL(e).wait_recv()
            @pl.when(z>0)
            def _():
                @pl.when(z==n-1)
                def _(): lst[at(e)]=oth[at(e)]
                @pl.when(z<n-1)
                def _(): lst[at(e)]=(oth[at(e)].astype(f32)+lb[at(e)].astype(f32)).astype(bf16)
                goL(e).start()
        g=t-last
        @pl.when((g>=0)&(g<nc))
        def _():
            @pl.when(z==0)
            def _(): out[at(g),mine]=(oth[at(g)].astype(f32)+lb[at(g)].astype(f32)).astype(bf16)
            @pl.when(z==n-1)
            def _(): out[at(g),mine]=(oth[at(g)].astype(f32)+rb[at(g)].astype(f32)).astype(bf16)
            @pl.when((z>0)&(z<n-1))
            def _(): out[at(g),mine]=(oth[at(g)].astype(f32)+rb[at(g)].astype(f32)+lb[at(g)].astype(f32)).astype(bf16)
            give(g).start()
        return carry
    lax.fori_loop(0,nc+skew*(n-1),step,0)
    def drain(c,carry):
        give(c).wait()
        swap(c).wait_send()
        @pl.when(z<n-1)
        def _(): goR(c).wait_send()
        @pl.when(z>0)
        def _(): goL(c).wait_send()
        return carry
    lax.fori_loop(0,nc,drain,0)

def sum_rows(own,chunk,cid,skew=2):
    rows,wd=own.shape; nc=rows//chunk
    buf=pltpu.VMEM((rows,wd//2),bf16)
    return pl.pallas_call(functools.partial(scan_kernel,chunk=chunk,skew=skew),
        in_specs=[VM()],out_specs=VM(),out_shape=jax.ShapeDtypeStruct((rows,wd),bf16),
        scratch_shapes=[buf]*5+[DMA((nc,))]*4+[DMA((2,nc))]*2,
        compiler_params=pltpu.CompilerParams(collective_id=cid,has_side_effects=True,vmem_limit_bytes=60<<20),name="sum_rows")(own)


class Spread:
    def __init__(self, src, dst, first, second, ss, rs, base):
        self.h, self.d = lax.axis_index("head"), lax.axis_index("dp")
        self.src, self.dst, self.first, self.second = src, dst, first, second
        self.ss, self.rs, self.base, self.n = ss, rs, base, len(first)

    def copy(self, src, dst, to, k):
        return pltpu.make_async_remote_copy(
            src, dst, self.ss.at[to - 1, self.base + k], self.rs.at[to - 1, self.base + k],
            device_id=(jnp.bitwise_xor(self.h, to), self.d), device_id_type=MESH,
        )

    def direct(self, to, i):
        rows = (self.first + self.second)[i]
        return self.copy(self.src(rows), self.dst(rows, self.h), to, i)

    def passed(self, to, i):
        rows = (self.second if to == 1 else self.first)[i]
        ref = self.dst(rows, jnp.bitwise_xor(self.h, 3 - to))
        return self.copy(ref, ref, to, 2 * self.n + i)

    def start(self):
        n = self.n
        for i in range(2 * n):
            self.direct(1, i).start()
            self.direct(2, (i + n) % (2 * n)).start()

    def forward(self, i):
        self.direct(1, i).wait_recv()
        self.passed(2, i).start()
        self.direct(2, self.n + i).wait_recv()
        self.passed(1, i).start()

    def arrived(self):
        for i in range(self.n):
            self.direct(1, self.n + i).wait_recv()
            self.direct(2, i).wait_recv()
            self.passed(1, i).wait_recv()
            self.passed(2, i).wait_recv()

    def sent(self):
        for to in (1, 2):
            for i in range(2 * self.n):
                self.direct(to, i).wait_send()
            for i in range(self.n):
                self.passed(to, i).wait_send()


def fwd_conv(x_ref, lg_ref, taps_ref, q_s, k_s, p_s, g_s, r_s, t_s, l_w, heads, chunks):
    i, j = masks()
    low = j <= i
    slow = j < i
    xr = jnp.bitwise_xor(i, j)
    zero8 = jnp.zeros((8, DK), f32)
    for c in range(chunks):
        for h in range(heads):
            rows = slice(c * C, (c + 1) * C)
            pre = {}
            for n, off in (("q", 0), ("k", heads * DK), ("v", 2 * heads * DK)):
                cols = slice(off + h * DK, off + (h + 1) * DK)
                x = x_ref[rows, cols]
                prev = zero8 if c == 0 else x_ref[c * C - 8 : c * C, cols]
                conv, sg = conv_silu(x, prev, taps_ref[:, cols])
                pre[n] = conv * sg
            q, k = pre["q"], pre["k"]
            q = q * (lax.rsqrt(jnp.sum(q * q, -1, keepdims=True) + norm_eps) * DK**-0.5)
            k = k * lax.rsqrt(jnp.sum(k * k, -1, keepdims=True) + norm_eps)
            qb, kb = q.astype(bf16), k.astype(bf16)
            beta = jax.nn.sigmoid(lg_ref[rows, h : h + 1])
            sc = dot_t(jnp.concatenate([qb, kb], 0), kb)
            G = sc[C:]
            Lw = jnp.where(slow, G * beta, 0.0).astype(bf16)
            q_s[h, rows] = qb
            k_s[h, rows] = kb
            p_s[h, rows] = jnp.where(low, sc[0:C], 0.0).astype(bf16)
            g_s[h, rows] = G.astype(bf16)
            r_s[h, rows] = pre["v"].astype(bf16)
            l_w[h, rows] = Lw
            t_s[h, rows] = jnp.where(xr == 0, 1.0, jnp.where(xr == 1, -Lw.astype(f32), 0.0)).astype(bf16)


def fwd_inverse(t_s, l_w, heads, chunks):
    i, j = masks()
    xr = jnp.bitwise_xor(i, j)
    every = [(c, h) for c in range(chunks) for h in range(heads)]
    s = 2
    while s < C:
        part = (xr >= s) & (xr < 2 * s)
        half = [
            dot(t_s[h, c * C : (c + 1) * C], jnp.where(part, l_w[h, c * C : (c + 1) * C], jnp.zeros((C, C), bf16))).astype(bf16)
            for c, h in every
        ]
        for (c, h), y in zip(every, half):
            rows = slice(c * C, (c + 1) * C)
            X = t_s[h, rows]
            t_s[h, rows] = X - dot(y, X).astype(bf16)
        s *= 2


def fwd_states(lg_ref, gain_ref, a_ref, q_s, k_s, u_s, t_s, p_s, r_s, s_s, o_s, heads, chunks):
    S = [jnp.zeros((DK, DK), f32) for _ in range(heads)]
    for c in range(chunks):
        rows = slice(c * C, (c + 1) * C)
        Sb = [S[h].astype(bf16) for h in range(heads)]
        m = [dot(jnp.concatenate([k_s[h, rows], q_s[h, rows]], 0), Sb[h]) for h in range(heads)]
        R = [r_s[h, rows].astype(f32) - m[h][0:C] for h in range(heads)]
        beta = [jax.nn.sigmoid(lg_ref[rows, h : h + 1]) for h in range(heads)]
        ub = [dot(t_s[h, rows], (R[h] * beta[h]).astype(bf16)).astype(bf16) for h in range(heads)]
        S = [S[h] + tdot(k_s[h, rows], ub[h]) for h in range(heads)]
        for h in range(heads):
            s_s[h, rows] = Sb[h]
            r_s[h, rows] = R[h].astype(bf16)
            u_s[h, rows] = ub[h]
            o = m[h][C:] + dot(p_s[h, rows], ub[h])
            o_s[h, rows] = o
            a = o * lax.rsqrt(jnp.mean(o * o, -1, keepdims=True) + norm_eps) * gain_ref[0:1, h * DK : (h + 1) * DK]
            a_ref[rows, h * DK : (h + 1) * DK] = a.astype(bf16)


CH = 128
SKEW = 2


def front_kernel(
    table, order, gain, lengths, x, cot,
    w, xf, cf, af, of, qkv_o, lg_o, q_o, k_o, u_o, t_o, p_o, g_o, r_o, s_o, o_o,
    own, oth, rb, lb, wv, xv, qv, lv, tp, av, q_s, k_s, u_s, t_s, p_s, g_s, r_s, s_s, o_s, l_w, cv, go,
    xs, xr_, gl, fs, fr, ss, rs, as_, ar_, ls, sv,
    *, seqs, heads, lead, at_out, at_gate, hl, small, capacity,
):
    h = lax.axis_index("head")
    d = lax.axis_index("dp")
    n = lax.axis_size("dp") // 2
    z = d // 2
    core = lax.rem(d, 2)
    mate = (h, jnp.bitwise_xor(d, 1))
    h1, h2 = jnp.bitwise_xor(h, 1), jnp.bitwise_xor(h, 2)
    T, Wd = x.shape
    L = T // seqs
    rows_all, width = own.shape
    half = width // 2
    nc = rows_all // CH
    early = wv.shape[0] // CH
    chunks = L // C

    b = pltpu.get_barrier_semaphore()
    for p in (mate, (h1, d), (h2, d)):
        pl.semaphore_signal(b, inc=1, device_id=p, device_id_type=MESH)
    @pl.when(z > 0)
    def _():
        pl.semaphore_signal(b, inc=1, device_id=(h, d - 2), device_id_type=MESH)
    @pl.when(z < n - 1)
    def _():
        pl.semaphore_signal(b, inc=1, device_id=(h, d + 2), device_id_type=MESH)
    pl.semaphore_wait(b, 3 + (z > 0).astype(jnp.int32) + (z < n - 1).astype(jnp.int32))

    def col(i, size=Wd):
        return pl.ds(pl.multiple_of(i * size, size), size)

    def at(c):
        return pl.ds(pl.multiple_of(c * CH, CH), CH)

    parts = 3
    R = T // (2 * parts)
    A = [pl.ds(i * R, R) for i in range(parts)]
    B = [pl.ds((i + parts) * R, R) for i in range(parts)]
    spread_x = Spread(lambda r: x.at[r], lambda r, i: xv.at[r, col(i)], A, B, as_, ar_, 0)
    spread_c = Spread(lambda r: cv.at[r], lambda r, i: cf.at[r, col(i)], A, B, as_, ar_, 9)
    spread_a = [
        Spread(
            lambda r: av.at[r], lambda r, i: af.at[r, col(i)],
            [pl.ds(s * L, L // 2)], [pl.ds(s * L + L // 2, L // 2)], as_, ar_, 18 + 3 * s,
        )
        for s in range(seqs)
    ]
    hw = at_gate - at_out
    spread_o = Spread(
        lambda r: w.at[pl.ds(at_out + r[0], r[1])],
        lambda r, i: of.at[pl.ds(pl.multiple_of(i * hw, hw) + r[0], r[1])],
        [(0, hw // 2)], [(hw // 2, hw // 2)], as_, ar_, 18 + 3 * seqs,
    )
    spread_x.start()
    own_x = pltpu.make_async_copy(x, xv.at[:, col(h)], ls.at[0])
    own_x.start()
    load_c = pltpu.make_async_copy(cot, cv, ls.at[5])
    load_c.start()

    mine, other = col(core, half), col(1 - core, half)

    def remote(src, dst, s, r, dev):
        return pltpu.make_async_remote_copy(src, dst, s, r, device_id=dev, device_id_type=MESH)

    def swap(c):
        return remote(own.at[at(c), other], oth.at[at(c)], xs.at[c], xr_.at[c], mate)

    def to_right(c):
        return remote(rb.at[at(c)], rb.at[at(c)], ss.at[0, c], rs.at[0, c], (h, d + 2))

    def to_left(c):
        return remote(lb.at[at(c)], lb.at[at(c)], ss.at[1, c], rs.at[1, c], (h, d - 2))

    def give(c, dst):
        return remote(oth.at[at(c)], dst.at[at(c), mine], fs.at[c], fr.at[c], mate)

    def keep(c, dst):
        return pltpu.make_async_copy(oth.at[at(c)], dst.at[at(c), mine], gl.at[c])

    def pick(c):
        place = lax.broadcasted_iota(jnp.int32, (table.shape[0], CH), 0) + base
        hot = jnp.where(order[pl.ds(c, 1)] == place, 1.0, 0.0).astype(bf16)
        own[at(c)] = tdot(hot, table[...]).astype(bf16)
        swap(c).start()

    base = d * capacity
    pick(0)
    pick(1)
    last = SKEW * jnp.maximum(z, n - 1 - z)

    def step(t, carry):
        @pl.when(t + 2 < nc)
        def _():
            pick(t + 2)

        @pl.when(t < nc)
        def _():
            swap(t).wait_recv()
            oth[at(t)] = oth[at(t)] + own[at(t), mine]

        c = t - SKEW * z
        @pl.when((c >= 0) & (c < nc))
        def _():
            @pl.when(z > 0)
            def _():
                to_right(c).wait_recv()
                rb[at(c)] = rb[at(c)] + oth[at(c)]
            @pl.when(z == 0)
            def _():
                rb[at(c)] = oth[at(c)]
            @pl.when(z < n - 1)
            def _():
                to_right(c).start()

        e = t - SKEW * (n - 1 - z)
        @pl.when((e >= 0) & (e < nc))
        def _():
            @pl.when(z < n - 1)
            def _():
                to_left(e).wait_recv()
                lb[at(e)] = lb[at(e)] + oth[at(e)]
            @pl.when(z == n - 1)
            def _():
                lb[at(e)] = oth[at(e)]
            @pl.when(z > 0)
            def _():
                to_left(e).start()

        g = t - last
        @pl.when((g >= 0) & (g < nc))
        def _():
            oth[at(g)] = rb[at(g)] + lb[at(g)] - oth[at(g)]
            @pl.when(g < early)
            def _():
                give(g, wv).start()
                keep(g, wv).start()
            @pl.when(g >= early)
            def _():
                give(g, w).start()
                keep(g, w).start()
        return carry

    def steps(lo, hi):
        lax.fori_loop(lo, hi, step, 0)

    steps(0, 1)
    load_c.wait()
    place = lax.broadcasted_iota(jnp.int32, (L, Wd), 0)
    for s in range(seqs):
        r = pl.ds(s * L, L)
        cv[r] = jnp.where(place < lengths[s], cv[r], jnp.zeros((L, Wd), bf16))
    steps(1, 2)
    for i in range(parts):
        spread_x.forward(i)
        steps(2 + i, 3 + i)
    spread_c.start()
    own_c = pltpu.make_async_copy(cv, cf.at[:, col(h)], ls.at[1])
    own_c.start()
    t = early + SKEW * (n - 1)
    steps(2 + parts, t)
    for c in range(early):
        keep(c, wv).wait()
        give(c, wv).wait_recv()
    save_w = pltpu.make_async_copy(wv, w.at[pl.ds(0, early * CH)], ls.at[2])
    save_w.start()
    spread_x.arrived()
    own_x.wait()
    save_x = pltpu.make_async_copy(xv, xf, ls.at[3])
    save_x.start()

    taps3 = wv[0:16].astype(f32)
    flat = [taps3[hl + i : hl + i + 1] for i in range(small - hl)]
    line = 3 * heads * DK
    joined = jnp.concatenate(flat, 1)
    for j in range(KCONV):
        tp[j : j + 1] = joined[:, j * line : (j + 1) * line]

    go[0:1] = gain[2:3, col(h)]
    saves = []
    for s in range(seqs):
        rows = pl.ds(s * L, L)
        for i in range(2):
            r = pl.ds(s * L + i * (L // 2), L // 2)
            xx = xv[r].astype(f32)
            n1 = (xx * lax.rsqrt(jnp.mean(xx * xx, -1, keepdims=True) + norm_eps) * gain[0:1]).astype(bf16)
            lv[r] = dot_t(n1, wv[0:lead])
            qv[r] = dot_t(n1, wv[lead:at_out])
        if s == 0:
            spread_c.forward(0)
        steps(t, t + 1)
        sub = lambda ref: ref.at[:, rows]
        fwd_conv(qv.at[rows], lv.at[rows], tp, sub(q_s), sub(k_s), sub(p_s), sub(g_s), sub(r_s), sub(t_s), l_w, heads, chunks)
        if s == 0:
            spread_c.forward(1)
        else:
            spread_a[s - 1].forward(0)
        steps(t + 1, t + 2)
        fwd_inverse(sub(t_s), l_w, heads, chunks)
        if s == 0:
            spread_c.forward(2)
        steps(t + 2, t + 3)
        fwd_states(lv.at[rows], go, av.at[rows], sub(q_s), sub(k_s), sub(u_s), sub(t_s), sub(p_s), sub(r_s), sub(s_s), sub(o_s), heads, chunks)
        spread_a[s].start()
        saves.append(pltpu.make_async_copy(av.at[rows], af.at[rows, col(h)], sv.at[s, 0]))
        pairs = [(qv.at[rows], qkv_o.at[rows]), (lv.at[rows], lg_o.at[rows])]
        for src, dst in ((q_s, q_o), (k_s, k_o), (u_s, u_o), (t_s, t_o), (p_s, p_o), (g_s, g_o), (r_s, r_o), (s_s, s_o), (o_s, o_o)):
            pairs.append((src.at[:, rows], dst.at[:, rows]))
        for k, (src, dst) in enumerate(pairs):
            saves.append(pltpu.make_async_copy(src, dst, sv.at[s, 1 + k]))
        for cp in saves[-12:]:
            cp.start()
        steps(t + 3, t + 4)
        t += 4
        if s == 1:
            save_w.wait()
            for c in range(early, -(-at_gate // CH)):
                keep(c, w).wait()
                give(c, w).wait_recv()
            spread_o.start()
            own_o = pltpu.make_async_copy(w.at[pl.ds(at_out, hw)], of.at[col(h, hw)], ls.at[4])
            own_o.start()
    steps(t, t + 2)
    spread_a[seqs - 1].forward(0)
    spread_o.forward(0)
    steps(t + 2, nc + SKEW * (n - 1))

    own_c.wait()
    own_o.wait()
    save_x.wait()
    for cp in saves:
        cp.wait()
    for sp in [spread_c, *spread_a, spread_o]:
        sp.arrived()
    for sp in [spread_x, spread_c, *spread_a, spread_o]:
        sp.sent()

    def drain(c, carry):
        swap(c).wait_send()
        @pl.when(c < early)
        def _():
            give(c, wv).wait_send()
        @pl.when(c >= early)
        def _():
            give(c, w).wait_send()
        @pl.when(c >= -(-at_gate // CH))
        def _():
            keep(c, w).wait()
            give(c, w).wait_recv()
        @pl.when(z < n - 1)
        def _():
            to_right(c).wait_send()
        @pl.when(z > 0)
        def _():
            to_left(c).wait_send()
        return carry

    lax.fori_loop(0, nc, drain, 0)


def front(table, order, gain, lengths, x, cot, seqs, heads, lead, at_out, at_gate, hl, small, capacity, cid):
    T, Wd = x.shape
    rows = order.shape[0] * order.shape[1]
    width = table.shape[1]
    half = width // 2
    nc = rows // CH
    early = -(-at_out // CH)
    L = T // seqs
    hbm = pl.BlockSpec(memory_space=pl.ANY)
    S = jax.ShapeDtypeStruct
    sav = [S((heads, T, DK), bf16)] * 8 + [S((heads, T, DK), f32)]
    outs = [
        S((rows, width), bf16), S((T, width), bf16), S((T, width), bf16), S((T, width), bf16),
        S((4 * (at_gate - at_out), width), bf16), S((T, at_out - lead), f32), S((T, lead), f32), *sav,
    ]
    V = pltpu.VMEM
    piece = V((rows, half), bf16)
    return pl.pallas_call(
        functools.partial(
            front_kernel, seqs=seqs, heads=heads, lead=lead, at_out=at_out, at_gate=at_gate, hl=hl, small=small, capacity=capacity
        ),
        in_specs=[VM()] * 3 + [pl.BlockSpec(memory_space=pltpu.SMEM)] + [hbm] * 2,
        out_specs=[hbm] * len(outs),
        out_shape=outs,
        scratch_shapes=[
            V((rows, width), bf16), piece, piece, piece, V((early * CH, width), bf16), V((T, width), bf16),
            V((T, at_out - lead), f32), V((T, lead), f32), V((8, at_out - lead), f32), V((T, heads * DK), bf16),
            *[V((heads, T, DK), bf16)] * 8, V((heads, T, DK), f32), V((heads, L, DK), bf16), V((T, Wd), bf16), V((8, Wd), f32),
            DMA((nc,)), DMA((nc,)), DMA((nc,)), DMA((nc,)), DMA((nc,)), DMA((2, nc)), DMA((2, nc)),
            DMA((2, 21 + 3 * seqs)), DMA((2, 21 + 3 * seqs)), DMA((6,)), DMA((seqs, 12)),
        ],
        compiler_params=pltpu.CompilerParams(collective_id=cid, has_side_effects=True, vmem_limit_bytes=60 << 20),
        name="front",
    )(table, order, gain, lengths, x, cot)


def bwd_blocks(da_ref, gain_ref, o_s, q_s, k_s, u_s, p_s, s_s, dg_ref, do_w, w_w, dq_w, dk_w, qd_w, heads, chunks):
    i, j = masks()
    low = j <= i
    for c in range(chunks):
        for h in range(heads):
            rows = slice(c * C, (c + 1) * C)
            hc = slice(h * DK, (h + 1) * DK)
            o = o_s[h, rows]
            ro = lax.rsqrt(jnp.mean(o * o, -1, keepdims=True) + norm_eps)
            da = da_ref[rows, hc]
            on = o * ro
            dg_ref[0:1, hc] += jnp.sum(da * on, 0, keepdims=True)
            t = da * gain_ref[0:1, hc]
            do = (ro * (t - on * jnp.mean(t * on, -1, keepdims=True))).astype(bf16)
            qb, kb = q_s[h, rows], k_s[h, rows]
            dP = jnp.where(low, dot_t(do, u_s[h, rows]), 0.0).astype(bf16)
            do_w[h, rows] = do
            w_w[h, rows] = tdot(p_s[h, rows], do)
            dq_w[h, rows] = dot_t(do, s_s[h, rows]) + dot(dP, kb)
            dk_w[h, rows] = tdot(dP, qb)
            qd_w[h, rows] = tdot(qb, do)


def bwd_states(lg_ref, k_s, t_s, w_w, qd_w, ds_w, heads, chunks):
    dS = [jnp.zeros((DK, DK), f32) for _ in range(heads)]
    for c in reversed(range(chunks)):
        rows = slice(c * C, (c + 1) * C)
        kb = [k_s[h, rows] for h in range(heads)]
        dSb = [dS[h].astype(bf16) for h in range(heads)]
        du = [(w_w[h, rows] + dot(kb[h], dSb[h])).astype(bf16) for h in range(heads)]
        e = [tdot(t_s[h, rows], du[h]) for h in range(heads)]
        beta = [jax.nn.sigmoid(lg_ref[rows, h : h + 1]) for h in range(heads)]
        dS = [dS[h] + qd_w[h, rows] - tdot(kb[h], (beta[h] * e[h]).astype(bf16)) for h in range(heads)]
        for h in range(heads):
            w_w[h, rows] = e[h]
            ds_w[h, rows] = dSb[h]


def bwd_conv(x_ref, lg_ref, taps_ref, q_s, k_s, u_s, g_s, r_s, s_s, w_w, dq_w, dk_w, ds_w, dc, dx_ref, dlg_ref, dt_ref, heads, chunks):
    i, j = masks()
    slow = j < i
    zero8 = jnp.zeros((8, DK), f32)
    W = heads * DK
    lane = lax.broadcasted_iota(jnp.int32, (C, dlg_ref.shape[1]), 1)
    row8 = lax.broadcasted_iota(jnp.int32, (8, DK), 0)
    dc[chunks * C : chunks * C + 8] = jnp.zeros((8, 3 * W), f32)
    for c in reversed(range(chunks)):
        rows = slice(c * C, (c + 1) * C)
        dlg = jnp.zeros(lane.shape, f32)
        for h in range(heads):
            e = w_w[h, rows]
            eb = e.astype(bf16)
            beta = jax.nn.sigmoid(lg_ref[rows, h : h + 1])
            be = beta * e
            ub, kb = u_s[h, rows], k_s[h, rows]
            dL = jnp.where(slow, -dot_t(eb, ub), 0.0)
            dGb = (beta * dL).astype(bf16)
            dk = (
                dk_w[h, rows] + dot_t(ub, ds_w[h, rows]) - dot_t(be.astype(bf16), s_s[h, rows])
                + dot(dGb, kb) + tdot(dGb, kb)
            )
            db = jnp.sum(e * r_s[h, rows].astype(f32) + dL * g_s[h, rows].astype(f32), -1, keepdims=True)
            dlg = jnp.where(lane == h, db * beta * (1.0 - beta), dlg)
            for n, off in (("q", 0), ("k", W), ("v", 2 * W)):
                cols = slice(off + h * DK, off + (h + 1) * DK)
                tp = taps_ref[:, cols]
                x = x_ref[rows, cols]
                prev = zero8 if c == 0 else x_ref[c * C - 8 : c * C, cols]
                moved = [shifted(x, prev, 3 - jj) for jj in range(4)]
                conv = tp[3:4] * moved[3]
                for jj in range(3):
                    conv = conv + tp[jj : jj + 1] * moved[jj]
                sg = jax.nn.sigmoid(conv)
                act = conv * sg
                if n == "v":
                    dd = be
                else:
                    r = lax.rsqrt(jnp.sum(act * act, -1, keepdims=True) + norm_eps)
                    g = dq_w[h, rows] * DK**-0.5 if n == "q" else dk
                    an = act * r
                    dd = r * (g - an * jnp.sum(g * an, -1, keepdims=True))
                dconv = dd * (sg + act * (1.0 - sg))
                dc[rows, cols] = dconv
                for jj in range(4):
                    dt_ref[jj : jj + 1, cols] += jnp.sum(dconv * moved[jj], 0, keepdims=True)
                nxt = dc[(c + 1) * C : (c + 1) * C + 8, cols]
                dx = tp[3:4] * dconv
                for jj in range(1, 4):
                    r = pltpu.roll(dconv, C - jj, 0)
                    bot = jnp.where(row8 >= 8 - jj, pltpu.roll(nxt, 8 - jj, 0), r[C - 8 :])
                    dx = dx + tp[3 - jj : 4 - jj] * jnp.concatenate([r[: C - 8], bot], 0)
                dx_ref[rows, cols] = dx.astype(bf16)
        dlg_ref[rows] = dlg.astype(bf16)


class Scatter:
    def __init__(self, part, beside, rows, bufs, slot, ss, rs, base):
        self.h, self.d = lax.axis_index("head"), lax.axis_index("dp")
        self.part, self.beside, self.slot = part, beside, slot
        self.fb, self.db, self.cb = bufs
        self.half = rows.size // 2
        self.rows = [pl.ds(rows.start + i * self.half, self.half) for i in range(2)]
        self.ss, self.rs, self.base = ss, rs, base

    def col(self, k):
        w = self.part.shape[1] // 4
        return pl.ds(pl.multiple_of(jnp.bitwise_xor(self.h, k) * w, w), w)

    def copy(self, src, dst, to, k):
        return pltpu.make_async_remote_copy(
            src, dst, self.ss.at[to - 1, self.base + k], self.rs.at[to - 1, self.base + k],
            device_id=(jnp.bitwise_xor(self.h, to), self.d), device_id_type=MESH,
        )

    def far(self, side):
        return self.copy(self.part.at[self.rows[side], self.col(3)], self.fb.at[self.slot, side], side + 1, 0)

    def near(self, side):
        return self.copy(self.part.at[self.rows[side], self.col(side + 1)], self.db.at[self.slot, side], side + 1, 1)

    def both(self, side):
        return self.copy(self.fb.at[self.slot, side], self.cb.at[self.slot, side], 2 - side, 2)

    def one(self):
        for side in (0, 1):
            self.far(side).start()
        for side in (0, 1):
            self.near(side).start()

    def two(self):
        for side in (0, 1):
            self.far(side).wait_recv()
            got = self.fb[self.slot, side].astype(f32) + self.beside(side).astype(f32)
            self.fb[self.slot, side] = got.astype(bf16)
            self.both(side).start()

    def three(self):
        got = []
        for side in (0, 1):
            self.near(side).wait_recv()
            self.both(side).wait_recv()
            got.append(self.db[self.slot, side].astype(f32) + self.cb[self.slot, side].astype(f32))
            self.far(side).wait_send()
            self.near(side).wait_send()
            self.both(side).wait_send()
        return got


RING = 4
SLOTS = 4


def back_kernel(
    gain, stat_in, lengths,
    h1_part, mlp_part, da_in, dh_own, mlp_own, h1_own, xf, af, w, g_ffn, qkv, lg, q_i, k_i, u_i, t_i, p_i, g_i, r_i, s_i, o_i,
    y_o, ig_o, stat_o, g_o,
    own, oth, rb, lb, rst, lst, qv, lv, q_s, k_s, u_s, t_s, p_s, g_s, r_s, s_s, o_s,
    do_w, w_w, dq_w, dk_w, qd_w, ds_w, dc, xv, wv, nb, da_f, dh_f, mlp_f, h1_f, xp, fb, db, cb, gq, gs, n1_w, dx_w, dlg_w, dt_w, dg_w, g1_w, st_w, go_w, tp, gout,
    xs, xr_, gl, fs, fr, ss, rs, as_, ar_, ls, lds, a2s, a2r, sts, str_,
    *, seqs, heads, lead, n_ffn, hl, small,
):
    h = lax.axis_index("head")
    d = lax.axis_index("dp")
    n = lax.axis_size("dp") // 2
    z = d // 2
    core = lax.rem(d, 2)
    mate = (h, jnp.bitwise_xor(d, 1))
    T = xf.shape[0]
    L = T // seqs
    rows_all, width = own.shape
    half = width // 2
    Wd = width // 4
    nc = rows_all // CH
    chunks = L // C
    hd = heads * DK
    at_qkv, at_out, at_ffn = lead, lead + 3 * hd, lead + 4 * hd

    bits = []
    k = 2
    while k < 2 * n:
        bits.append(k)
        k *= 2
    b = pltpu.get_barrier_semaphore()
    peers = [mate] + [(jnp.bitwise_xor(h, k), d) for k in (1, 2, 3)] + [(h, jnp.bitwise_xor(d, k)) for k in bits]
    for p in peers:
        pl.semaphore_signal(b, inc=1, device_id=p, device_id_type=MESH)
    @pl.when(z > 0)
    def _():
        pl.semaphore_signal(b, inc=1, device_id=(h, d - 2), device_id_type=MESH)
    @pl.when(z < n - 1)
    def _():
        pl.semaphore_signal(b, inc=1, device_id=(h, d + 2), device_id_type=MESH)
    pl.semaphore_wait(b, len(peers) + (z > 0).astype(jnp.int32) + (z < n - 1).astype(jnp.int32))

    def col(i, size=Wd):
        return pl.ds(pl.multiple_of(i * size, size), size)

    def at(c):
        return pl.ds(pl.multiple_of((nc - 1 - c) * CH, CH), CH)

    seq_rows = [pl.ds(s * L, L) for s in range(seqs)]
    bufs = (fb, db, cb)
    jobs = []
    for kind, part in enumerate((h1_part, mlp_part, xp)):
        for s in range(seqs):
            if kind < 2:
                def beside(side, kind=kind, s=s):
                    return nb[kind, s, side]
            else:
                def beside(side, s=s):
                    r = pl.ds(s * L + side * (L // 2), L // 2)
                    return xp[r, col(jnp.bitwise_xor(h, 2 - side))]
            k = len(jobs)
            jobs.append(Scatter(part, beside, seq_rows[s], bufs, k % SLOTS, as_, ar_, 3 * k))
    jobs[0].one()

    def load(src, dst, k):
        cp = pltpu.make_async_copy(src, dst, ls.at[k])
        cp.start()
        return cp

    first = load(g_ffn, own.at[pl.ds(at_ffn, n_ffn)], 0)
    nbs = []
    for kind, part in enumerate((h1_part, mlp_part)):
        for s in range(seqs):
            for side in (0, 1):
                r = pl.ds(s * L + side * (L // 2), L // 2)
                nbs.append(load(part.at[r, col(jnp.bitwise_xor(h, 2 - side))], nb.at[kind, s, side], 8 + len(nbs)))
    load_da = load(da_in, da_f, 1)
    ins = (q_i, k_i, u_i, t_i, p_i, g_i, r_i, s_i, o_i)
    scr = (q_s, k_s, u_s, t_s, p_s, g_s, r_s, s_s, o_s)

    def fetch(s):
        sl = s % 2
        cps = [pltpu.make_async_copy(qkv.at[seq_rows[s]], qv.at[sl], lds.at[sl, 9]),
               pltpu.make_async_copy(lg.at[seq_rows[s]], lv.at[sl], lds.at[sl, 10])]
        for k, (i, o) in enumerate(zip(ins, scr)):
            cps.append(pltpu.make_async_copy(i.at[:, seq_rows[s]], o.at[sl], lds.at[sl, k]))
        return cps

    for cp in fetch(0):
        cp.start()
    load_w = load(w.at[pl.ds(0, lead + 3 * hd)], wv, 2)
    load_x = load(xf, xv, 3)
    load_dh = load(dh_own, dh_f, 4)
    load_m = load(mlp_own, mlp_f, 5)
    load_h = load(h1_own, h1_f, 6)

    mine, other = col(core, half), col(1 - core, half)

    def remote(src, dst, s, r, dev):
        return pltpu.make_async_remote_copy(src, dst, s, r, device_id=dev, device_id_type=MESH)

    def ring(c):
        return pl.ds(pl.multiple_of(lax.rem(c, RING) * CH, CH), CH)

    def swap(c):
        return remote(own.at[at(c), other], oth.at[at(c)], xs.at[c], xr_.at[c], mate)

    def to_right(c):
        return remote(rst.at[ring(c)], rb.at[at(c)], ss.at[0, c], rs.at[0, c], (h, d + 2))

    def to_left(c):
        return remote(lst.at[ring(c)], lb.at[at(c)], ss.at[1, c], rs.at[1, c], (h, d - 2))

    def give(c):
        return remote(oth.at[at(c)], g_o.at[at(c), mine], fs.at[c], fr.at[c], mate)

    def keep(c):
        return pltpu.make_async_copy(oth.at[at(c)], g_o.at[at(c), mine], gl.at[c])

    def swaps(lo, hi):
        def body(c, carry):
            swap(c).start()
            return carry
        lax.fori_loop(lo, hi, body, 0)

    last = SKEW * jnp.maximum(z, n - 1 - z)

    def step(t, carry):
        @pl.when(t < nc)
        def _():
            swap(t).wait_recv()
            oth[at(t)] = (oth[at(t)].astype(f32) + own[at(t), mine].astype(f32)).astype(bf16)

        c = t - SKEW * z
        @pl.when((c >= 0) & (c < nc))
        def _():
            @pl.when(z > 0)
            def _():
                to_right(c).wait_recv()
            @pl.when(z < n - 1)
            def _():
                @pl.when(c >= RING)
                def _():
                    to_right(c - RING).wait_send()
                @pl.when(z == 0)
                def _():
                    rst[ring(c)] = oth[at(c)]
                @pl.when(z > 0)
                def _():
                    rst[ring(c)] = (oth[at(c)].astype(f32) + rb[at(c)].astype(f32)).astype(bf16)
                to_right(c).start()

        e = t - SKEW * (n - 1 - z)
        @pl.when((e >= 0) & (e < nc))
        def _():
            @pl.when(z < n - 1)
            def _():
                to_left(e).wait_recv()
            @pl.when(z > 0)
            def _():
                @pl.when(e >= RING)
                def _():
                    to_left(e - RING).wait_send()
                @pl.when(z == n - 1)
                def _():
                    lst[ring(e)] = oth[at(e)]
                @pl.when(z < n - 1)
                def _():
                    lst[ring(e)] = (oth[at(e)].astype(f32) + lb[at(e)].astype(f32)).astype(bf16)
                to_left(e).start()

        g = t - last
        @pl.when((g >= 0) & (g < nc))
        def _():
            @pl.when(z == 0)
            def _():
                oth[at(g)] = (oth[at(g)].astype(f32) + lb[at(g)].astype(f32)).astype(bf16)
            @pl.when(z == n - 1)
            def _():
                oth[at(g)] = (oth[at(g)].astype(f32) + rb[at(g)].astype(f32)).astype(bf16)
            @pl.when((z > 0) & (z < n - 1))
            def _():
                oth[at(g)] = (oth[at(g)].astype(f32) + rb[at(g)].astype(f32) + lb[at(g)].astype(f32)).astype(bf16)
            give(g).start()
            keep(g).start()
        return carry

    now = [0]
    end = nc + SKEW * (n - 1)

    def advance(k):
        hi = min(now[0] + k, end)
        if hi > now[0]:
            lax.fori_loop(now[0], hi, step, 0)
        now[0] = hi

    first.wait()
    swaps(0, n_ffn // CH)
    for ref in (dt_w, dg_w, g1_w, gq, gs):
        ref[...] = jnp.zeros_like(ref)
    advance(1)
    for cp in nbs:
        cp.wait()
    jobs[0].two()
    jobs[1].one()
    advance(1)
    load_da.wait()

    def finish(k):
        kind, s = k // seqs, k % seqs
        got = jobs[k].three()
        for side in (0, 1):
            r = pl.ds(s * L + side * (L // 2), L // 2)
            if kind == 0:
                dh_f[r] += got[side]
            elif kind == 1:
                m = mlp_f[r] + got[side]
                y = h1_f[r] + m
                y_o[r] = y.astype(bf16)
                place = lax.broadcasted_iota(jnp.int32, (L // 2, Wd), 0) + side * (L // 2)
                keep_ = place < lengths[s]
                lane = lax.broadcasted_iota(jnp.int32, (1, width), 1)
                sy = jnp.sum(jnp.sum(jnp.where(keep_, y * y, 0.0), -1, keepdims=True), 0, keepdims=True)
                sm = jnp.sum(jnp.sum(jnp.where(keep_, m * m, 0.0), -1, keepdims=True), 0, keepdims=True)
                st_w[0, 3:4] += jnp.where(lane == 0, sy, jnp.where(lane == 2, sm, 0.0))
            else:
                ig_o[r] = dh_f[r] + xp[r, col(h)].astype(f32) + got[side]

    turn = [1]

    def relay():
        k = turn[0]
        if k < len(jobs):
            jobs[k].two()
        if k + 1 < len(jobs):
            jobs[k + 1].one()
        if k - 1 < len(jobs):
            finish(k - 1)
        turn[0] += 1

    st_w[0] = stat_in[...]
    load_w.wait()
    taps3 = wv[0:16].astype(f32)
    joined = jnp.concatenate([taps3[hl + i : hl + i + 1] for i in range(small - hl)], 1)
    for j in range(KCONV):
        tp[j : j + 1] = joined[:, j * 3 * hd : (j + 1) * 3 * hd]
    gout[0:1] = gain[2:3, col(h)]
    for s in range(seqs):
        sl = s % 2
        for cp in fetch(s):
            cp.wait()
        if s + 1 < seqs:
            for cp in fetch(s + 1):
                cp.start()
        if s == 0:
            for cp in (load_x, load_dh, load_m, load_h):
                cp.wait()
        sub = [ref.at[sl] for ref in scr]
        q_, k_, u_, t_, p_, g_, r_, s_, o_ = sub
        x_, l_ = qv.at[sl], lv.at[sl]
        bwd_blocks(da_f.at[seq_rows[s]], gout, o_, q_, k_, u_, p_, s_, dg_w, do_w, w_w, dq_w, dk_w, qd_w, heads, chunks)
        advance(1)
        bwd_states(l_, k_, t_, w_w, qd_w, ds_w, heads, chunks)
        advance(1)
        relay()
        bwd_conv(x_, l_, tp, q_, k_, u_, g_, r_, s_, w_w, dq_w, dk_w, ds_w, dc, dx_w, dlg_w, dt_w, heads, chunks)
        advance(1)
        for i in range(2):
            lo = i * (L // 2)
            r = pl.ds(s * L + lo, L // 2)
            here = pl.ds(lo, L // 2)
            xx = xv[r].astype(f32)
            r1 = lax.rsqrt(jnp.mean(xx * xx, -1, keepdims=True) + norm_eps)
            xn = xx * r1
            n1_w[here] = (xn * gain[0:1]).astype(bf16)
            dn = dot(dx_w[here], wv[lead:]) + dot(dlg_w[here], wv[0:lead])
            g1_w[0:1] += jnp.sum(dn * xn, 0, keepdims=True)
            gd = dn * gain[0:1]
            xp[r] = (r1 * (gd - xn * jnp.mean(gd * xn, -1, keepdims=True))).astype(bf16)
        gq[...] += tdot(dx_w[...], n1_w[...])
        gs[...] += tdot(dlg_w[...], n1_w[...])
        if s == seqs - 1:
            relay()
        else:
            advance(1)
    load_a = pltpu.make_async_copy(af, xv, ls.at[7])
    load_a.start()
    line = 3 * hd
    dt = jnp.concatenate([dt_w[j : j + 1] for j in range(KCONV)], 1)
    row = lax.broadcasted_iota(jnp.int32, (lead, width), 0)
    tail = gs[...]
    for i in range(small - hl):
        tail = jnp.where(row == hl + i, dt[:, i * width : (i + 1) * width], tail)
    tail = jnp.where(row < small, tail, 0.0)
    own[pl.ds(0, lead)] = tail.astype(bf16)
    own[pl.ds(at_qkv, 3 * hd)] = gq[...].astype(bf16)
    advance(1)
    while turn[0] <= seqs:
        relay()
        advance(1)
    load_a.wait()
    go_w[...] = tdot(xv[...], dh_f[...].astype(bf16)).astype(bf16)
    ex = []
    for k in (1, 2, 3):
        p = jnp.bitwise_xor(h, k)
        cp = remote(go_w.at[col(p, hd)], own.at[pl.ds(at_out, hd), col(h)], a2s.at[k - 1], a2r.at[k - 1], (p, d))
        cp.start()
        ex.append(cp)
    own[pl.ds(at_out, hd), col(h)] = go_w[col(h, hd)]
    advance(1)
    relay()
    for cp in ex:
        cp.wait()
    swaps(n_ffn // CH, nc)
    lane = lax.broadcasted_iota(jnp.int32, (1, width), 1)
    three = jnp.concatenate([dg_w[0:1]] * 4, 1)
    st_w[0, 0:1] = g1_w[0:1]
    st_w[0, 2:3] = jnp.where((lane >= h * Wd) & (lane < (h + 1) * Wd), three, 0.0)
    advance(2)
    while turn[0] <= 2 * seqs:
        relay()
        advance(2)
    rounds = [(jnp.bitwise_xor(h, k), d) for k in (1, 2)] + [mate] + [(h, jnp.bitwise_xor(d, k)) for k in bits]
    sent = []
    for i, p in enumerate(rounds):
        cp = remote(st_w.at[i], str_.at[i], sts.at[0, i], sts.at[1, i], p)
        cp.start()
        sent.append(cp)
        if turn[0] <= len(jobs):
            relay()
        advance(2)
        cp.wait_recv()
        st_w[i + 1] = st_w[i] + str_[i]
    stat_o[...] = st_w[len(rounds)]
    while turn[0] <= len(jobs):
        relay()
        advance(2)
    advance(end)
    for cp in sent:
        cp.wait_send()

    def drain(c, carry):
        swap(c).wait_send()
        give(c).wait()
        keep(c).wait()
        @pl.when(c >= nc - RING)
        def _():
            @pl.when(z < n - 1)
            def _():
                to_right(c).wait_send()
            @pl.when(z > 0)
            def _():
                to_left(c).wait_send()
        return carry

    lax.fori_loop(0, nc, drain, 0)


def back(gain, stat_in, lengths, h1_part, mlp_part, owns, xf, af, w, g_ffn, qkv, lg, saved, seqs, heads, lead, hl, small, cid):
    T, width = xf.shape
    Wd = width // 4
    half = width // 2
    L = T // seqs
    hd = heads * DK
    n_ffn = g_ffn.shape[0]
    rows = n_ffn + 4 * hd + lead
    nc = rows // CH
    hbm = pl.BlockSpec(memory_space=pl.ANY)
    S = jax.ShapeDtypeStruct
    V = pltpu.VMEM
    n = lax.axis_size("dp") // 2
    rounds = 2 + 1 + max(n.bit_length() - 1, 0)
    piece, ringbuf = V((rows, half), bf16), V((RING * CH, half), bf16)
    blk = lambda dt: V((2, heads, L, DK), dt)
    wk = lambda dt: V((heads, L, DK), dt)
    rsb = V((SLOTS, 2, L // 2, Wd), bf16)
    njobs = 3 * seqs
    return pl.pallas_call(
        functools.partial(back_kernel, seqs=seqs, heads=heads, lead=lead, n_ffn=n_ffn, hl=hl, small=small),
        in_specs=[VM(), VM(), pl.BlockSpec(memory_space=pltpu.SMEM)] + [hbm] * 21,
        out_specs=[VM(), VM(), VM(), hbm],
        out_shape=[S((T, Wd), bf16), S((T, Wd), f32), S((8, width), f32), S((rows, width), bf16)],
        scratch_shapes=[
            V((rows, width), bf16), piece, piece, piece, ringbuf, ringbuf,
            V((2, L, 3 * hd), f32), V((2, L, lead), f32), *[blk(bf16)] * 8, blk(f32),
            wk(bf16), wk(f32), wk(f32), wk(f32), wk(f32), wk(bf16), V((L + 8, 3 * hd), f32),
            V((T, width), bf16), V((lead + 3 * hd, width), bf16), V((2, seqs, 2, L // 2, Wd), bf16),
            V((T, Wd), f32), V((T, Wd), f32), V((T, Wd), f32), V((T, Wd), f32), V((T, width), bf16), rsb, rsb, rsb,
            V((3 * hd, width), f32), V((lead, width), f32), V((L, width), bf16), V((L, 3 * hd), bf16), V((L, lead), bf16),
            V((8, 3 * hd), f32), V((8, hd), f32), V((8, width), f32), V((rounds + 1, 8, width), f32), V((4 * hd, Wd), bf16),
            V((8, 3 * hd), f32), V((8, Wd), f32),
            DMA((nc,)), DMA((nc,)), DMA((nc,)), DMA((nc,)), DMA((nc,)), DMA((2, nc)), DMA((2, nc)),
            DMA((2, 3 * njobs)), DMA((2, 3 * njobs)), DMA((8 + 4 * seqs,)), DMA((2, 11)), DMA((3,)), DMA((3,)),
            DMA((2, rounds)), V((rounds, 8, width), f32),
        ],
        compiler_params=pltpu.CompilerParams(collective_id=cid, has_side_effects=True, vmem_limit_bytes=63 << 20),
        name="back",
    )(gain, stat_in, lengths, h1_part, mlp_part, *owns, xf, af, w, g_ffn, qkv, lg, *saved)


RT = 256


def ffn_kernel(
    gain, lengths, af, xf, cf, of, w,
    mlp_o, h1p_o, da_o, dh_o, mo_o, h1_o, g_o, stat_o,
    ov, wg, wu, wd, wo, a_v, x_v, c_v, n2_s, hid_s, dg_s, du_s, h1_w, t_w, mlp_s, h1p_s, da_s, fb, db, cb,
    lw, lt, sv, as_, ar_,
    *, seqs, at_out, at_gate,
):
    h = lax.axis_index("head")
    d = lax.axis_index("dp")
    T, width = xf.shape
    Wd = width // 4
    L = T // seqs
    ffl = wg.shape[0]
    n = T // RT
    b = pltpu.get_barrier_semaphore()
    for k in (1, 2):
        pl.semaphore_signal(b, inc=1, device_id=(jnp.bitwise_xor(h, k), d), device_id_type=MESH)
    pl.semaphore_wait(b, 2)

    def col(k):
        return pl.ds(pl.multiple_of(jnp.bitwise_xor(h, k) * Wd, Wd), Wd)

    def rows(i):
        return pl.ds(pl.multiple_of(i * RT, RT), RT)

    def slot(i):
        return lax.rem(i, 2)

    def fetch(i):
        return [
            pltpu.make_async_copy(src.at[rows(i)], dst.at[slot(i)], lt.at[slot(i), k])
            for k, (src, dst) in enumerate(((af, a_v), (xf, x_v)))
        ]

    loads = [pltpu.make_async_copy(of, ov, lw.at[0])]
    for k, (lo, dst) in enumerate(((at_gate, wg), (at_gate + ffl, wu), (at_gate + 2 * ffl, wd), (at_out, wo))):
        loads.append(pltpu.make_async_copy(w.at[pl.ds(lo, dst.shape[0])], dst, lw.at[1 + k]))
    loads.append(pltpu.make_async_copy(cf, c_v, lw.at[5]))
    loads[0].start()
    for cp in fetch(0):
        cp.start()
    for cp in loads[1:]:
        cp.start()
    stat_o[...] = jnp.zeros_like(stat_o)

    def job(i):
        def beside(side):
            start = pl.multiple_of(i * RT + side * (RT // 2), RT // 2)
            return da_s[pl.ds(start, RT // 2), col(2 - side)]

        return Scatter(da_s, beside, rows(i), (fb, db, cb), lax.rem(i, SLOTS), as_, ar_, 3 * i)

    def finish(i):
        got = job(i).three()
        for side in (0, 1):
            start = pl.multiple_of(i * RT + side * (RT // 2), RT // 2)
            da_o[pl.ds(start, RT // 2)] += got[side]

    def saves(i):
        return [
            pltpu.make_async_copy(src.at[slot(i)], dst.at[rows(i)], sv.at[slot(i), k])
            for k, (src, dst) in enumerate(((mlp_s, mlp_o), (h1p_s, h1p_o)))
        ]

    loads[0].wait()

    def tile(i, carry):
        @pl.when(i + 1 < n)
        def _():
            for cp in fetch(i + 1):
                cp.start()

        @pl.when(i >= 2)
        def _():
            for cp in saves(i - 2):
                cp.wait()

        for cp in fetch(i):
            cp.wait()
        r, s = rows(i), slot(i)
        t_w[...] = dot(a_v[s], ov[...])
        attn = t_w[:, col(0)]
        place = lax.broadcasted_iota(jnp.int32, (RT, Wd), 0) + lax.rem(i * RT, L)
        good = place < lengths[i * RT // L]
        lane = lax.broadcasted_iota(jnp.int32, (1, width), 1)
        sa = jnp.sum(jnp.sum(jnp.where(good, attn * attn, 0.0), -1, keepdims=True), 0, keepdims=True)
        count = jnp.sum(jnp.sum(jnp.where(good, 1.0, 0.0), -1, keepdims=True), 0, keepdims=True)
        stat_o[3:4] += jnp.where(lane == 1, sa, jnp.where(lane == 3, count, 0.0))
        h1 = x_v[s].astype(f32) + t_w[...]
        h1_w[...] = h1
        h1_o[r] = h1_w[:, col(0)]
        r2 = lax.rsqrt(jnp.mean(h1 * h1, -1, keepdims=True) + norm_eps)
        n2 = (h1 * r2 * gain[1:2]).astype(bf16)
        n2_s[r] = n2

        @pl.when(i == 0)
        def _():
            for cp in loads[1:]:
                cp.wait()

        cot = c_v[r]
        gate = dot_t(n2, wg[...])
        up = dot_t(n2, wu[...])
        sig = jax.nn.sigmoid(gate)
        act = gate * sig
        hid = (act * up).astype(bf16)
        hid_s[r] = hid
        t_w[...] = dot(hid, wd[...])
        mo_o[r] = t_w[:, col(0)]
        mlp_s[s] = t_w[...].astype(bf16)
        dh = dot_t(cot, wd[...])
        dg = (dh * up * (sig + act * (1.0 - sig))).astype(bf16)
        du = (dh * act).astype(bf16)
        dg_s[r] = dg
        du_s[r] = du
        dn2 = dot(dg, wg[...]) + dot(du, wu[...])
        h1 = h1_w[...]
        hr = h1 * r2
        stat_o[1:2] += jnp.sum(dn2 * hr, 0, keepdims=True)
        gd = dn2 * gain[1:2]
        part = r2 * (gd - hr * jnp.mean(gd * hr, -1, keepdims=True))
        t_w[...] = part
        dh_o[r] = t_w[:, col(0)] + c_v[r, col(0)].astype(f32)
        low = part.astype(bf16)
        h1p_s[s] = low
        for cp in saves(i):
            cp.start()
        t_w[...] = dot_t(low, ov[...])
        da_s[r] = t_w[...].astype(bf16)
        da_o[r] = t_w[:, col(0)] + dot_t(cot, wo[...])

        @pl.when(i >= 2)
        def _():
            finish(i - 2)

        @pl.when(i >= 1)
        def _():
            job(i - 1).two()

        job(i).one()
        return carry

    lax.fori_loop(0, n, tile, 0)
    g_o[pl.ds(0, ffl)] = tdot(dg_s[...], n2_s[...]).astype(bf16)
    job(n - 1).two()
    finish(n - 2)
    g_o[pl.ds(ffl, ffl)] = tdot(du_s[...], n2_s[...]).astype(bf16)
    g_o[pl.ds(2 * ffl, ffl)] = tdot(hid_s[...], c_v[...]).astype(bf16)
    finish(n - 1)
    for i in (n - 2, n - 1):
        for cp in saves(i):
            cp.wait()


def ffn(gain, lengths, af, xf, cf, of, w, seqs, at_out, at_gate, ffl, cid):
    T, width = xf.shape
    Wd = width // 4
    hd = at_gate - at_out
    n = T // RT
    hbm = pl.BlockSpec(memory_space=pl.ANY)
    S = jax.ShapeDtypeStruct
    V = pltpu.VMEM
    slots = V((SLOTS, 2, RT // 2, Wd), bf16)
    pair = V((2, RT, width), bf16)
    own = S((T, Wd), f32)
    return pl.pallas_call(
        functools.partial(ffn_kernel, seqs=seqs, at_out=at_out, at_gate=at_gate),
        in_specs=[VM(), pl.BlockSpec(memory_space=pltpu.SMEM)] + [hbm] * 5,
        out_specs=[hbm, hbm] + [VM()] * 6,
        out_shape=[
            S((T, width), bf16), S((T, width), bf16), own, own, own, own,
            S((3 * ffl, width), bf16), S((8, width), f32),
        ],
        scratch_shapes=[
            V((width, width), bf16), V((ffl, width), bf16), V((ffl, width), bf16), V((ffl, width), bf16), V((hd, width), bf16),
            pair, pair, V((T, width), bf16), V((T, width), bf16), V((T, ffl), bf16), V((T, ffl), bf16), V((T, ffl), bf16),
            V((RT, width), f32), V((RT, width), f32), pair, pair, V((T, width), bf16), slots, slots, slots,
            DMA((6,)), DMA((2, 2)), DMA((2, 2)), DMA((2, 3 * n)), DMA((2, 3 * n)),
        ],
        compiler_params=pltpu.CompilerParams(collective_id=cid, has_side_effects=True, vmem_limit_bytes=63 << 20),
        name="feed_forward",
    )(gain, lengths, af, xf, cf, of, w)


SB = 128


def tail_kernel(order, g, stats, gain, gain_m, gain_v, p, m, v, p_o, m_o, v_o, gain_o, gm_o, gv_o, rms_o, w, *, capacity):
    i = pl.program_id(0)
    base = lax.axis_index("dp") * capacity + i * SB
    place = lax.broadcasted_iota(jnp.int32, (SB, CH), 0) + base
    hot = jnp.concatenate(
        [jnp.where(order[c : c + 1] == place, 1.0, 0.0).astype(bf16) for c in range(order.shape[0])], 1
    )
    grad = dot(hot, g[...])
    for j in range(8):
        w[:, j, :] = grad[:, j * 128 : (j + 1) * 128]
    p_o[...], m_o[...], v_o[...] = adam_step(p[...], m[...], v[...], w[...], weight_rate, weight_decay)

    @pl.when(i == 0)
    def _():
        gain_o[...], gm_o[...], gv_o[...] = adam_step(gain[...], gain_m[...], gain_v[...], stats[0:3], gain_rate, 0.0)
        rms_o[...] = jnp.sqrt(stats[3:4, 0:128] / stats[3:4, 3:4])


def tail(order, g, stats, gain, gain_m, gain_v, p, m, v):
    capacity = p.shape[0]
    S = jax.ShapeDtypeStruct
    whole = lambda a: pl.BlockSpec(a.shape, lambda i: (0,) * a.ndim)
    blk = pl.BlockSpec((SB, 8, 128), lambda i: (i, 0, 0))
    like = S(p.shape, f32)
    small = S(gain.shape, f32)
    return pl.pallas_call(
        functools.partial(tail_kernel, capacity=capacity),
        grid=(-(-capacity // SB),),
        in_specs=[whole(a) for a in (order, g, stats, gain, gain_m, gain_v)] + [blk] * 3,
        out_specs=[blk] * 3 + [whole(gain)] * 3 + [pl.BlockSpec((1, 128), lambda i: (0, 0))],
        out_shape=[like] * 3 + [small] * 3 + [S((1, 128), f32)],
        scratch_shapes=[pltpu.VMEM((SB, 8, 128), f32)],
        compiler_params=pltpu.CompilerParams(vmem_limit_bytes=56 << 20),
        name="owners_step",
    )(order, g, stats, gain, gain_m, gain_v, p, m, v)


def adam_step(param, first, second_moment, grad, rate, decay):
    first = beta_one * first + (1.0 - beta_one) * grad
    second_moment = beta_two * second_moment + (1.0 - beta_two) * grad * grad
    denom = jnp.sqrt(second_moment / (1.0 - beta_two**STEP)) + adam_eps
    param = param - rate / (1.0 - beta_one**STEP) * first / denom - rate * decay * param
    return (param, first, second_moment)


def on_device(
    inputs, cotangent, lengths, owner_slots, table, table_m, table_v, gains, gains_m, gains_v
):
    shards = lax.axis_size("head")
    seqs = lengths.shape[0]
    hd = HEADS * DK // shards
    ffl = FF // shards
    hl = HEADS // shards
    taps_rows = KCONV * 3 * hd // MODEL_WIDTH
    capacity = table.shape[1]
    small = hl + taps_rows
    lead = 64
    at_out = lead + 3 * hd
    at_gate = at_out + hd
    n_body = 4 * hd + 3 * ffl
    order = jnp.concatenate(
        [owner_slots[n_body:], jnp.full((lead - small,), -1, jnp.int32), owner_slots[:n_body]]
    ).reshape(-1, CH)
    padded = -(-capacity // 128) * 128
    tab = jnp.pad(table[0].astype(bf16), ((0, padded - capacity), (0, 0)))
    weights, x_full, cot_full, a_full, out_full, qkv, logit, *saved = front(
        tab, order, gains, lengths, inputs, cotangent, seqs, hl, lead, at_out, at_gate, hl, small, capacity, 0
    )
    mlp_part, h1_part, da, dh_own, mlp_own, h1_own, g_ffn, stat_in = ffn(
        gains, lengths, a_full, x_full, cot_full, out_full, weights, seqs, at_out, at_gate, ffl, 1
    )
    y, input_grad, stats, g_total = back(
        gains, stat_in, lengths, h1_part, mlp_part, [da, dh_own, mlp_own, h1_own],
        x_full, a_full, weights, g_ffn, qkv, logit, saved, seqs, hl, lead, hl, small, 2,
    )
    split = lambda t: t[0].reshape(capacity, 8, 128)
    table_new, table_m_new, table_v_new, gains_new, gains_m_new, gains_v_new, rms = tail(
        order, g_total, stats, gains, gains_m, gains_v, split(table), split(table_m), split(table_v)
    )
    return (
        y,
        input_grad,
        table_new.reshape(table.shape),
        table_m_new.reshape(table.shape),
        table_v_new.reshape(table.shape),
        gains_new,
        gains_m_new,
        gains_v_new,
        rms[0, 0:3],
    )


def solution(mesh):
    tok, tab = P("dp", "head"), P("head", "dp", None)
    return jax.shard_map(
        on_device,
        mesh=mesh,
        in_specs=(tok, tok, P("dp"), P(), tab, tab, tab, P(), P(), P()),
        out_specs=(tok, tok, tab, tab, tab, P(), P(), P(), P()),
        check_vma=False,
    )
```

```python
import functools

import jax
import jax.numpy as jnp
from jax import lax
from jax.experimental import pallas as pl
from jax.experimental.pallas import tpu as pltpu
from jax.sharding import PartitionSpec as P

MODEL_WIDTH = 1024
FF = 2816
HEADS = 8
DK = 128
KCONV = 4
STEP = 10
C = 128

norm_eps = 1e-06
adam_eps = 1e-08
beta_one = 0.9
beta_two = 0.95
weight_rate = 0.02
gain_rate = 0.6
weight_decay = 0.1
f32 = jnp.float32
bf16 = jnp.bfloat16
MESH = pl.DeviceIdType.MESH
VM = functools.partial(pl.BlockSpec, memory_space=pltpu.VMEM)
DMA = pltpu.SemaphoreType.DMA

def dot(a,b): return lax.dot_general(a,b,(((1,),(0,)),((),())),preferred_element_type=f32)
def dot_t(a,b): return lax.dot_general(a,b,(((1,),(1,)),((),())),preferred_element_type=f32)
def tdot(a,b): return lax.dot_general(a,b,(((0,),(0,)),((),())),preferred_element_type=f32)

def shifted(x, prev, j):
    if j==0: return x
    r=pltpu.roll(x,j,0)
    p=pltpu.roll(prev,j,0)
    row=lax.broadcasted_iota(jnp.int32,(8,x.shape[1]),0)
    top=jnp.where(row<j,p,r[0:8])
    return jnp.concatenate([top,r[8:]],0)

def conv_silu(x,prev,taps):
    conv=taps[3:4]*x
    for j in range(1,4):
        conv=conv+taps[3-j:4-j]*shifted(x,prev,j)
    sg=jax.nn.sigmoid(conv)
    return conv,sg

def masks():
    i=lax.broadcasted_iota(jnp.int32,(C,C),0); j=lax.broadcasted_iota(jnp.int32,(C,C),1)
    return i,j

def fwd_kernel(x_ref,lg_ref,taps_ref,gain_ref,a_ref,q_s,k_s,u_s,t_s,p_s,g_s,r_s,s_s,o_s,l_w,*,heads,chunks):
    i,j=masks()
    low=j<=i; slow=j<i; xr=jnp.bitwise_xor(i,j)
    zero8=jnp.zeros((8,DK),f32)
    every=[(c,h) for c in range(chunks) for h in range(heads)]
    beta={}
    for c,h in every:
        rows=slice(c*C,(c+1)*C)
        pre={}
        for n,off in (("q",0),("k",heads*DK),("v",2*heads*DK)):
            cols=slice(off+h*DK,off+(h+1)*DK)
            x=x_ref[rows,cols]
            prev=zero8 if c==0 else x_ref[c*C-8:c*C,cols]
            conv,sg=conv_silu(x,prev,taps_ref[:,cols])
            pre[n]=conv*sg
        q=pre["q"]; q=q*(lax.rsqrt(jnp.sum(q*q,-1,keepdims=True)+norm_eps)*DK**-0.5)
        k=pre["k"]; k=k*lax.rsqrt(jnp.sum(k*k,-1,keepdims=True)+norm_eps)
        qb=q.astype(bf16); kb=k.astype(bf16)
        beta[c,h]=jax.nn.sigmoid(lg_ref[rows,h:h+1])
        sc=dot_t(jnp.concatenate([qb,kb],0),kb)
        G=sc[C:]
        Lw=jnp.where(slow,G*beta[c,h],0.0).astype(bf16)
        q_s[h,rows]=qb; k_s[h,rows]=kb; p_s[h,rows]=jnp.where(low,sc[0:C],0.0).astype(bf16); g_s[h,rows]=G.astype(bf16)
        r_s[h,rows]=pre["v"].astype(bf16)
        l_w[h,rows]=Lw
        t_s[h,rows]=jnp.where(xr==0,1.0,jnp.where(xr==1,-Lw.astype(f32),0.0)).astype(bf16)
    s=2
    while s<C:
        part=(xr>=s)&(xr<2*s)
        half=[dot(t_s[h,c*C:(c+1)*C],jnp.where(part,l_w[h,c*C:(c+1)*C],jnp.zeros((C,C),bf16))).astype(bf16) for c,h in every]
        for (c,h),y in zip(every,half):
            rows=slice(c*C,(c+1)*C)
            X=t_s[h,rows]
            t_s[h,rows]=X-dot(y,X).astype(bf16)
        s*=2
    S=[jnp.zeros((DK,DK),f32) for _ in range(heads)]
    for c in range(chunks):
        rows=slice(c*C,(c+1)*C)
        Sb=[S[h].astype(bf16) for h in range(heads)]
        m=[dot(jnp.concatenate([k_s[h,rows],q_s[h,rows]],0),Sb[h]) for h in range(heads)]
        R=[r_s[h,rows].astype(f32)-m[h][0:C] for h in range(heads)]
        ub=[dot(t_s[h,rows],(R[h]*beta[c,h]).astype(bf16)).astype(bf16) for h in range(heads)]
        S=[S[h]+tdot(k_s[h,rows],ub[h]) for h in range(heads)]
        for h in range(heads):
            s_s[h,rows]=Sb[h]; r_s[h,rows]=R[h].astype(bf16); u_s[h,rows]=ub[h]
            o=m[h][C:]+dot(p_s[h,rows],ub[h])
            o_s[h,rows]=o
            a=o*lax.rsqrt(jnp.mean(o*o,-1,keepdims=True)+norm_eps)*gain_ref[0:1,h*DK:(h+1)*DK]
            a_ref[rows,h*DK:(h+1)*DK]=a.astype(bf16)

def mixer_fwd(x,lg,taps,gain,seqs):
    T=x.shape[0]; L=T//seqs; W=x.shape[1]; heads=W//(3*DK)
    blk=lambda: pl.BlockSpec((heads,L,DK),lambda s:(0,s,0))
    sav=lambda dt: jax.ShapeDtypeStruct((heads,T,DK),dt)
    return pl.pallas_call(functools.partial(fwd_kernel,heads=heads,chunks=L//C),
        grid=(seqs,),
        in_specs=[pl.BlockSpec((L,W),lambda s:(s,0)),pl.BlockSpec((L,lg.shape[1]),lambda s:(s,0)),pl.BlockSpec(taps.shape,lambda s:(0,0)),pl.BlockSpec(gain.shape,lambda s:(0,0))],
        out_specs=[pl.BlockSpec((L,heads*DK),lambda s:(s,0))]+[blk() for _ in range(9)],
        out_shape=[jax.ShapeDtypeStruct((T,heads*DK),bf16)]+[sav(bf16) for _ in range(8)]+[sav(f32)],
        scratch_shapes=[pltpu.VMEM((heads,L,DK),bf16)],
        compiler_params=pltpu.CompilerParams(vmem_limit_bytes=56<<20),
        cost_estimate=pl.CostEstimate(flops=2*24*20*C*C*C,bytes_accessed=15<<20,transcendentals=0),
        name="mixer_fwd")(x,lg,taps,gain)

def bwd_kernel(x_ref,lg_ref,taps_ref,gain_ref,da_ref,q_s,k_s,u_s,t_s,p_s,g_s,r_s,s_s,o_s,dx_ref,dlg_ref,dt_ref,dg_ref,dc,*,heads,chunks):
    i,j=masks()
    low=j<=i; slow=j<i
    zero8=jnp.zeros((8,DK),f32)
    seq=pl.program_id(0)
    @pl.when(seq==0)
    def _():
        dt_ref[...]=jnp.zeros_like(dt_ref); dg_ref[...]=jnp.zeros_like(dg_ref)
    dS=[jnp.zeros((DK,DK),f32) for _ in range(heads)]
    W=heads*DK
    lane=lax.broadcasted_iota(jnp.int32,(C,128),1)
    dc[chunks*C:chunks*C+8]=jnp.zeros((8,3*W),f32)
    for c in reversed(range(chunks)):
        rows=slice(c*C,(c+1)*C)
        dlg=jnp.zeros((C,128),f32)
        for h in range(heads):
            hc=slice(h*DK,(h+1)*DK)
            o=o_s[h,rows]
            ro=lax.rsqrt(jnp.mean(o*o,-1,keepdims=True)+norm_eps)
            da=da_ref[rows,hc]
            on=o*ro
            dg_ref[0:1,hc]+=jnp.sum(da*on,0,keepdims=True)
            t=da*gain_ref[0:1,hc]
            do=(ro*(t-on*jnp.mean(t*on,-1,keepdims=True))).astype(bf16)
            qb=q_s[h,rows]; kb=k_s[h,rows]; ub=u_s[h,rows]; Tb=t_s[h,rows]; Pb=p_s[h,rows]; Sb=s_s[h,rows]
            G=g_s[h,rows].astype(f32); R=r_s[h,rows].astype(f32)
            beta=jax.nn.sigmoid(lg_ref[rows,h:h+1])
            dSb=dS[h].astype(bf16)
            du=tdot(Pb,do)+dot(kb,dSb)
            e=tdot(Tb,du.astype(bf16))
            eb=e.astype(bf16)
            be=beta*e; beb=be.astype(bf16)
            pe=dot_t(jnp.concatenate([do,eb],0),ub)
            dP=jnp.where(low,pe[0:C],0.0).astype(bf16)
            dL=jnp.where(slow,-pe[C:],0.0)
            dG=beta*dL
            ds=dot_t(jnp.concatenate([do,beb],0),Sb)
            dq=ds[0:C]+dot(dP,kb)
            dGb=dG.astype(bf16)
            dk=tdot(dP,qb)+dot_t(ub,dSb)-ds[C:]+dot(dGb,kb)+tdot(dGb,kb)
            db=jnp.sum(e*R+dL*G,-1,keepdims=True)
            dlg=jnp.where(lane==h,db*beta*(1.0-beta),dlg)
            dS[h]=dS[h]+tdot(qb,do)-tdot(kb,beb)
            for n,off in (("q",0),("k",W),("v",2*W)):
                cols=slice(off+h*DK,off+(h+1)*DK)
                x=x_ref[rows,cols]
                prev=zero8 if c==0 else x_ref[c*C-8:c*C,cols]
                conv,sg=conv_silu(x,prev,taps_ref[:,cols])
                act=conv*sg
                if n=="v": d=be
                else:
                    r=lax.rsqrt(jnp.sum(act*act,-1,keepdims=True)+norm_eps)
                    g_=dq*DK**-0.5 if n=="q" else dk
                    an=act*r
                    d=r*(g_-an*jnp.sum(g_*an,-1,keepdims=True))
                dconv=d*(sg*(1.0+conv*(1.0-sg)))
                dc[rows,cols]=dconv
                for jj in range(4):
                    dt_ref[jj:jj+1,cols]+=jnp.sum(dconv*shifted(x,prev,3-jj),0,keepdims=True)
                nxt=dc[(c+1)*C:(c+1)*C+8,cols]
                tp=taps_ref[:,cols]
                dx=tp[3:4]*dconv
                row8=lax.broadcasted_iota(jnp.int32,(8,DK),0)
                for jj in range(1,4):
                    r=pltpu.roll(dconv,C-jj,0)
                    pn=pltpu.roll(nxt,8-jj,0)
                    bot=jnp.where(row8>=8-jj,pn,r[C-8:])
                    dx=dx+tp[3-jj:4-jj]*jnp.concatenate([r[:C-8],bot],0)
                dx_ref[rows,cols]=dx.astype(bf16)
        dlg_ref[rows]=dlg.astype(bf16)

def mixer_bwd(x,lg,taps,gain,da,saved,seqs):
    T=x.shape[0]; L=T//seqs; W=x.shape[1]; heads=W//(3*DK)
    blk=lambda: pl.BlockSpec((heads,L,DK),lambda s:(0,s,0))
    return pl.pallas_call(functools.partial(bwd_kernel,heads=heads,chunks=L//C),
        grid=(seqs,),
        in_specs=[pl.BlockSpec((L,W),lambda s:(s,0)),pl.BlockSpec((L,lg.shape[1]),lambda s:(s,0)),pl.BlockSpec(taps.shape,lambda s:(0,0)),pl.BlockSpec(gain.shape,lambda s:(0,0)),pl.BlockSpec((L,heads*DK),lambda s:(s,0))]+[blk() for _ in range(9)],
        out_specs=[pl.BlockSpec((L,W),lambda s:(s,0)),pl.BlockSpec((L,128),lambda s:(s,0)),pl.BlockSpec((8,W),lambda s:(0,0)),pl.BlockSpec((8,heads*DK),lambda s:(0,0))],
        out_shape=[jax.ShapeDtypeStruct((T,W),bf16),jax.ShapeDtypeStruct((T,128),bf16),jax.ShapeDtypeStruct((8,W),f32),jax.ShapeDtypeStruct((8,heads*DK),f32)],
        scratch_shapes=[pltpu.VMEM((L+8,W),f32)],
        compiler_params=pltpu.CompilerParams(vmem_limit_bytes=56<<20),
        cost_estimate=pl.CostEstimate(flops=2*24*20*C*C*C,bytes_accessed=15<<20,transcendentals=0),
        name="mixer_bwd")(x,lg,taps,gain,da,*saved)


def meet(partners):
    b=pltpu.get_barrier_semaphore()
    for p in partners:
        pl.semaphore_signal(b,inc=1,device_id=p,device_id_type=MESH)
    pl.semaphore_wait(b,len(partners))

def ag_kernel(*refs,count,parts):
    ins=refs[:count]; outs=refs[count:2*count]; ss,rs,ls=refs[2*count:]
    h=lax.axis_index("head"); d=lax.axis_index("dp")
    meet([(jnp.bitwise_xor(h,1),d),(jnp.bitwise_xor(h,2),d)])
    def copy(src,dst,to,k):
        return pltpu.make_async_remote_copy(src,dst,ss.at[to-1,k],rs.at[to-1,k],device_id=(jnp.bitwise_xor(h,to),d),device_id_type=MESH)
    first={}; second=[]; local=[]
    for n in range(count):
        x,o=ins[n],outs[n]
        T,Wd=x.shape; R=T//(2*parts); base=n*3*parts
        def col(b): return pl.ds(pl.multiple_of(b*Wd,Wd),Wd)
        for i in range(2*parts):
            r1=pl.ds(i*R,R); j=(i+parts)%(2*parts); r2=pl.ds(j*R,R)
            first[n,1,i]=copy(x.at[r1],o.at[r1,col(h)],1,base+i); first[n,1,i].start()
            first[n,2,j]=copy(x.at[r2],o.at[r2,col(h)],2,base+j); first[n,2,j].start()
        l=pltpu.make_async_copy(x,o.at[:,col(h)],ls.at[n]); l.start(); local.append(l)
    for n in range(count):
        x,o=ins[n],outs[n]
        T,Wd=x.shape; R=T//(2*parts); base=n*3*parts
        def col(b): return pl.ds(pl.multiple_of(b*Wd,Wd),Wd)
        for i in range(parts):
            ra=pl.ds(i*R,R); rb=pl.ds((i+parts)*R,R)
            ca=col(jnp.bitwise_xor(h,1)); cb=col(jnp.bitwise_xor(h,2))
            first[n,1,i].wait_recv()
            c=copy(o.at[ra,ca],o.at[ra,ca],2,base+2*parts+i); c.start(); second.append(c)
            first[n,2,i+parts].wait_recv()
            c=copy(o.at[rb,cb],o.at[rb,cb],1,base+2*parts+i); c.start(); second.append(c)
    for n in range(count):
        for i in range(parts):
            first[n,1,i+parts].wait_recv(); first[n,2,i].wait_recv()
    for c in second: c.wait()
    for c in first.values(): c.wait_send()
    for l in local: l.wait()

def gather_columns(arrays,parts,cid):
    n=len(arrays)
    return pl.pallas_call(functools.partial(ag_kernel,count=n,parts=parts),
        in_specs=[VM()]*n,out_specs=[VM()]*n,
        out_shape=[jax.ShapeDtypeStruct((a.shape[0],4*a.shape[1]),a.dtype) for a in arrays],
        scratch_shapes=[DMA((2,3*parts*n)),DMA((2,3*parts*n)),DMA((n,))],
        compiler_params=pltpu.CompilerParams(collective_id=cid,has_side_effects=True,vmem_limit_bytes=56<<20),name="gather_columns")(*arrays)

def rs_kernel(*refs,count,parts):
    ins=refs[:count]; outs=refs[count:2*count]; fb,db,cb,sb,ss,rs=refs[2*count:]
    h=lax.axis_index("head"); d=lax.axis_index("dp")
    h1,h2,h3=[jnp.bitwise_xor(h,k) for k in (1,2,3)]
    meet([(h1,d),(h2,d)])
    T=ins[0].shape[0]; Wd=ins[0].shape[1]//4; half=T//2; R=half//parts
    def col(b): return pl.ds(pl.multiple_of(b*Wd,Wd),Wd)
    def copy(src,dst,to,k):
        return pltpu.make_async_remote_copy(src,dst,ss.at[to-1,k],rs.at[to-1,k],device_id=(jnp.bitwise_xor(h,to),d),device_id_type=MESH)
    K=lambda n,p,kind: (n*parts+p)*3+kind
    fw={}; dr={}; cm={}
    for n in range(count):
        x=ins[n]
        for p in range(parts):
            for side,to,nb in ((0,1,h1),(1,2,h2)):
                r=pl.ds(side*half+p*R,R); q=pl.ds(p*R,R)
                fw[n,p,side]=copy(x.at[r,col(h3)],fb.at[n,side,q],to,K(n,p,0)); fw[n,p,side].start()
            for side,to,nb in ((0,1,h1),(1,2,h2)):
                r=pl.ds(side*half+p*R,R); q=pl.ds(p*R,R)
                dr[n,p,side]=copy(x.at[r,col(nb)],db.at[n,side,q],to,K(n,p,1)); dr[n,p,side].start()
    for n in range(count):
        x=ins[n]
        for p in range(parts):
            for side,to,nb in ((0,2,h2),(1,1,h1)):
                r=pl.ds(side*half+p*R,R); q=pl.ds(p*R,R)
                fw[n,p,side].wait_recv()
                sb[n,side,q]=(fb[n,side,q].astype(f32)+x[r,col(nb)].astype(f32)).astype(bf16)
                cm[n,p,side]=copy(sb.at[n,side,q],cb.at[n,side,q],to,K(n,p,2)); cm[n,p,side].start()
    for n in range(count):
        x,o=ins[n],outs[n]
        for p in range(parts):
            for side in (0,1):
                r=pl.ds(side*half+p*R,R); q=pl.ds(p*R,R)
                dr[n,p,side].wait_recv()
                cm[n,p,side].wait_recv()
                o[r]=x[r,col(h)].astype(f32)+db[n,side,q].astype(f32)+cb[n,side,q].astype(f32)
    for g in (fw,dr,cm):
        for c in g.values(): c.wait_send()

def scatter_columns(arrays,parts,cid):
    n=len(arrays); T=arrays[0].shape[0]; Wd=arrays[0].shape[1]//4
    buf=pltpu.VMEM((n,2,T//2,Wd),bf16)
    return pl.pallas_call(functools.partial(rs_kernel,count=n,parts=parts),
        in_specs=[VM()]*n,out_specs=[VM()]*n,
        out_shape=[jax.ShapeDtypeStruct((T,Wd),f32) for a in arrays],
        scratch_shapes=[buf]*4+[DMA((2,3*parts*n)),DMA((2,3*parts*n))],
        compiler_params=pltpu.CompilerParams(collective_id=cid,has_side_effects=True,vmem_limit_bytes=60<<20),name="scatter_columns")(*arrays)

def scan_kernel(own,out,oth,rb,lb,rst,lst,xs,xr,fs,fr,ss,rs,*,chunk,skew):
    h=lax.axis_index("head"); d=lax.axis_index("dp"); n=lax.axis_size("dp")//2
    z=d//2; core=lax.rem(d,2)
    mate=(h,jnp.bitwise_xor(d,1)); right=(h,d+2); left=(h,d-2)
    rows=own.shape[0]; Wd=own.shape[1]//2; nc=rows//chunk
    b=pltpu.get_barrier_semaphore()
    pl.semaphore_signal(b,inc=1,device_id=mate,device_id_type=MESH)
    @pl.when(z>0)
    def _(): pl.semaphore_signal(b,inc=1,device_id=left,device_id_type=MESH)
    @pl.when(z<n-1)
    def _(): pl.semaphore_signal(b,inc=1,device_id=right,device_id_type=MESH)
    pl.semaphore_wait(b,1+(z>0).astype(jnp.int32)+(z<n-1).astype(jnp.int32))
    mine=pl.ds(pl.multiple_of(core*Wd,Wd),Wd); other=pl.ds(pl.multiple_of((1-core)*Wd,Wd),Wd)
    def at(c): return pl.ds(pl.multiple_of(c*chunk,chunk),chunk)
    def remote(src,dst,s,r,dev): return pltpu.make_async_remote_copy(src,dst,s,r,device_id=dev,device_id_type=MESH)
    def swap(c): return remote(own.at[at(c),other],oth.at[at(c)],xs.at[c],xr.at[c],mate)
    def give(c): return remote(out.at[at(c),mine],out.at[at(c),mine],fs.at[c],fr.at[c],mate)
    def goR(c): return remote(rst.at[at(c)],rb.at[at(c)],ss.at[0,c],rs.at[0,c],right)
    def goL(c): return remote(lst.at[at(c)],lb.at[at(c)],ss.at[1,c],rs.at[1,c],left)
    def issue(c,carry):
        swap(c).start(); return carry
    lax.fori_loop(0,nc,issue,0)
    last=skew*jnp.maximum(z,n-1-z)
    def step(t,carry):
        @pl.when(t<nc)
        def _():
            swap(t).wait_recv()
            oth[at(t)]=(oth[at(t)].astype(f32)+own[at(t),mine].astype(f32)).astype(bf16)
        c=t-skew*z
        @pl.when((c>=0)&(c<nc))
        def _():
            @pl.when(z>0)
            def _(): goR(c).wait_recv()
            @pl.when(z<n-1)
            def _():
                @pl.when(z==0)
                def _(): rst[at(c)]=oth[at(c)]
                @pl.when(z>0)
                def _(): rst[at(c)]=(oth[at(c)].astype(f32)+rb[at(c)].astype(f32)).astype(bf16)
                goR(c).start()
        e=t-skew*(n-1-z)
        @pl.when((e>=0)&(e<nc))
        def _():
            @pl.when(z<n-1)
            def _(): goL(e).wait_recv()
            @pl.when(z>0)
            def _():
                @pl.when(z==n-1)
                def _(): lst[at(e)]=oth[at(e)]
                @pl.when(z<n-1)
                def _(): lst[at(e)]=(oth[at(e)].astype(f32)+lb[at(e)].astype(f32)).astype(bf16)
                goL(e).start()
        g=t-last
        @pl.when((g>=0)&(g<nc))
        def _():
            @pl.when(z==0)
            def _(): out[at(g),mine]=(oth[at(g)].astype(f32)+lb[at(g)].astype(f32)).astype(bf16)
            @pl.when(z==n-1)
            def _(): out[at(g),mine]=(oth[at(g)].astype(f32)+rb[at(g)].astype(f32)).astype(bf16)
            @pl.when((z>0)&(z<n-1))
            def _(): out[at(g),mine]=(oth[at(g)].astype(f32)+rb[at(g)].astype(f32)+lb[at(g)].astype(f32)).astype(bf16)
            give(g).start()
        return carry
    lax.fori_loop(0,nc+skew*(n-1),step,0)
    def drain(c,carry):
        give(c).wait()
        swap(c).wait_send()
        @pl.when(z<n-1)
        def _(): goR(c).wait_send()
        @pl.when(z>0)
        def _(): goL(c).wait_send()
        return carry
    lax.fori_loop(0,nc,drain,0)

def sum_rows(own,chunk,cid,skew=2):
    rows,wd=own.shape; nc=rows//chunk
    buf=pltpu.VMEM((rows,wd//2),bf16)
    return pl.pallas_call(functools.partial(scan_kernel,chunk=chunk,skew=skew),
        in_specs=[VM()],out_specs=VM(),out_shape=jax.ShapeDtypeStruct((rows,wd),bf16),
        scratch_shapes=[buf]*5+[DMA((nc,))]*4+[DMA((2,nc))]*2,
        compiler_params=pltpu.CompilerParams(collective_id=cid,has_side_effects=True,vmem_limit_bytes=60<<20),name="sum_rows")(own)


class Spread:
    def __init__(self, src, dst, first, second, ss, rs, base):
        self.h, self.d = lax.axis_index("head"), lax.axis_index("dp")
        self.src, self.dst, self.first, self.second = src, dst, first, second
        self.ss, self.rs, self.base, self.n = ss, rs, base, len(first)

    def copy(self, src, dst, to, k):
        return pltpu.make_async_remote_copy(
            src, dst, self.ss.at[to - 1, self.base + k], self.rs.at[to - 1, self.base + k],
            device_id=(jnp.bitwise_xor(self.h, to), self.d), device_id_type=MESH,
        )

    def direct(self, to, i):
        rows = (self.first + self.second)[i]
        return self.copy(self.src(rows), self.dst(rows, self.h), to, i)

    def passed(self, to, i):
        rows = (self.second if to == 1 else self.first)[i]
        ref = self.dst(rows, jnp.bitwise_xor(self.h, 3 - to))
        return self.copy(ref, ref, to, 2 * self.n + i)

    def start(self):
        n = self.n
        for i in range(2 * n):
            self.direct(1, i).start()
            self.direct(2, (i + n) % (2 * n)).start()

    def forward(self, i):
        self.direct(1, i).wait_recv()
        self.passed(2, i).start()
        self.direct(2, self.n + i).wait_recv()
        self.passed(1, i).start()

    def arrived(self):
        for i in range(self.n):
            self.direct(1, self.n + i).wait_recv()
            self.direct(2, i).wait_recv()
            self.passed(1, i).wait_recv()
            self.passed(2, i).wait_recv()

    def sent(self):
        for to in (1, 2):
            for i in range(2 * self.n):
                self.direct(to, i).wait_send()
            for i in range(self.n):
                self.passed(to, i).wait_send()


def fwd_conv(x_ref, lg_ref, taps_ref, q_s, k_s, p_s, g_s, r_s, t_s, l_w, heads, chunks):
    i, j = masks()
    low = j <= i
    slow = j < i
    xr = jnp.bitwise_xor(i, j)
    zero8 = jnp.zeros((8, DK), f32)
    for c in range(chunks):
        for h in range(heads):
            rows = slice(c * C, (c + 1) * C)
            pre = {}
            for n, off in (("q", 0), ("k", heads * DK), ("v", 2 * heads * DK)):
                cols = slice(off + h * DK, off + (h + 1) * DK)
                x = x_ref[rows, cols]
                prev = zero8 if c == 0 else x_ref[c * C - 8 : c * C, cols]
                conv, sg = conv_silu(x, prev, taps_ref[:, cols])
                pre[n] = conv * sg
            q, k = pre["q"], pre["k"]
            q = q * (lax.rsqrt(jnp.sum(q * q, -1, keepdims=True) + norm_eps) * DK**-0.5)
            k = k * lax.rsqrt(jnp.sum(k * k, -1, keepdims=True) + norm_eps)
            qb, kb = q.astype(bf16), k.astype(bf16)
            beta = jax.nn.sigmoid(lg_ref[rows, h : h + 1])
            sc = dot_t(jnp.concatenate([qb, kb], 0), kb)
            G = sc[C:]
            Lw = jnp.where(slow, G * beta, 0.0).astype(bf16)
            q_s[h, rows] = qb
            k_s[h, rows] = kb
            p_s[h, rows] = jnp.where(low, sc[0:C], 0.0).astype(bf16)
            g_s[h, rows] = G.astype(bf16)
            r_s[h, rows] = pre["v"].astype(bf16)
            l_w[h, rows] = Lw
            t_s[h, rows] = jnp.where(xr == 0, 1.0, jnp.where(xr == 1, -Lw.astype(f32), 0.0)).astype(bf16)


def fwd_inverse(t_s, l_w, heads, chunks):
    i, j = masks()
    xr = jnp.bitwise_xor(i, j)
    every = [(c, h) for c in range(chunks) for h in range(heads)]
    s = 2
    while s < C:
        part = (xr >= s) & (xr < 2 * s)
        half = [
            dot(t_s[h, c * C : (c + 1) * C], jnp.where(part, l_w[h, c * C : (c + 1) * C], jnp.zeros((C, C), bf16))).astype(bf16)
            for c, h in every
        ]
        for (c, h), y in zip(every, half):
            rows = slice(c * C, (c + 1) * C)
            X = t_s[h, rows]
            t_s[h, rows] = X - dot(y, X).astype(bf16)
        s *= 2


def fwd_states(lg_ref, gain_ref, a_ref, q_s, k_s, u_s, t_s, p_s, r_s, s_s, o_s, heads, chunks):
    S = [jnp.zeros((DK, DK), f32) for _ in range(heads)]
    for c in range(chunks):
        rows = slice(c * C, (c + 1) * C)
        Sb = [S[h].astype(bf16) for h in range(heads)]
        m = [dot(jnp.concatenate([k_s[h, rows], q_s[h, rows]], 0), Sb[h]) for h in range(heads)]
        R = [r_s[h, rows].astype(f32) - m[h][0:C] for h in range(heads)]
        beta = [jax.nn.sigmoid(lg_ref[rows, h : h + 1]) for h in range(heads)]
        ub = [dot(t_s[h, rows], (R[h] * beta[h]).astype(bf16)).astype(bf16) for h in range(heads)]
        S = [S[h] + tdot(k_s[h, rows], ub[h]) for h in range(heads)]
        for h in range(heads):
            s_s[h, rows] = Sb[h]
            r_s[h, rows] = R[h].astype(bf16)
            u_s[h, rows] = ub[h]
            o = m[h][C:] + dot(p_s[h, rows], ub[h])
            o_s[h, rows] = o
            a = o * lax.rsqrt(jnp.mean(o * o, -1, keepdims=True) + norm_eps) * gain_ref[0:1, h * DK : (h + 1) * DK]
            a_ref[rows, h * DK : (h + 1) * DK] = a.astype(bf16)


CH = 128
SKEW = 2


def front_kernel(
    order, gain, lengths, slots, x, cot,
    w, xf, cf, af, of, qkv_o, lg_o, q_o, k_o, u_o, t_o, p_o, g_o, r_o, s_o, o_o,
    own, oth, rb, lb, wv, xv, qv, lv, tp, av, q_s, k_s, u_s, t_s, p_s, g_s, r_s, s_s, o_s, l_w, cv, go, slots_v, table,
    xs, xr_, gl, fs, fr, ss, rs, as_, ar_, ls, sv,
    *, seqs, heads, lead, at_out, at_gate, hl, small, capacity,
):
    h = lax.axis_index("head")
    d = lax.axis_index("dp")
    n = lax.axis_size("dp") // 2
    z = d // 2
    core = lax.rem(d, 2)
    mate = (h, jnp.bitwise_xor(d, 1))
    h1, h2 = jnp.bitwise_xor(h, 1), jnp.bitwise_xor(h, 2)
    T, Wd = x.shape
    L = T // seqs
    rows_all, width = own.shape
    half = width // 2
    nc = rows_all // CH
    early = wv.shape[0] // CH
    chunks = L // C

    load_t = pltpu.make_async_copy(slots, slots_v.at[pl.ds(0, capacity)], ls.at[6])
    load_t.start()
    b = pltpu.get_barrier_semaphore()
    for p in (mate, (h1, d), (h2, d)):
        pl.semaphore_signal(b, inc=1, device_id=p, device_id_type=MESH)
    @pl.when(z > 0)
    def _():
        pl.semaphore_signal(b, inc=1, device_id=(h, d - 2), device_id_type=MESH)
    @pl.when(z < n - 1)
    def _():
        pl.semaphore_signal(b, inc=1, device_id=(h, d + 2), device_id_type=MESH)
    pl.semaphore_wait(b, 3 + (z > 0).astype(jnp.int32) + (z < n - 1).astype(jnp.int32))

    def col(i, size=Wd):
        return pl.ds(pl.multiple_of(i * size, size), size)

    def at(c):
        return pl.ds(pl.multiple_of(c * CH, CH), CH)

    parts = 3
    R = T // (2 * parts)
    A = [pl.ds(i * R, R) for i in range(parts)]
    B = [pl.ds((i + parts) * R, R) for i in range(parts)]
    spread_x = Spread(lambda r: x.at[r], lambda r, i: xv.at[r, col(i)], A, B, as_, ar_, 0)
    spread_c = Spread(lambda r: cv.at[r], lambda r, i: cf.at[r, col(i)], A, B, as_, ar_, 9)
    spread_a = [
        Spread(
            lambda r: av.at[r], lambda r, i: af.at[r, col(i)],
            [pl.ds(s * L, L // 2)], [pl.ds(s * L + L // 2, L // 2)], as_, ar_, 18 + 3 * s,
        )
        for s in range(seqs)
    ]
    hw = at_gate - at_out
    spread_o = Spread(
        lambda r: w.at[pl.ds(at_out + r[0], r[1])],
        lambda r, i: of.at[pl.ds(pl.multiple_of(i * hw, hw) + r[0], r[1])],
        [(0, hw // 2)], [(hw // 2, hw // 2)], as_, ar_, 18 + 3 * seqs,
    )
    spread_x.start()
    own_x = pltpu.make_async_copy(x, xv.at[:, col(h)], ls.at[0])
    own_x.start()
    load_c = pltpu.make_async_copy(cot, cv, ls.at[5])
    load_c.start()

    mine, other = col(core, half), col(1 - core, half)

    def remote(src, dst, s, r, dev):
        return pltpu.make_async_remote_copy(src, dst, s, r, device_id=dev, device_id_type=MESH)

    def swap(c):
        return remote(own.at[at(c), other], oth.at[at(c)], xs.at[c], xr_.at[c], mate)

    def to_right(c):
        return remote(rb.at[at(c)], rb.at[at(c)], ss.at[0, c], rs.at[0, c], (h, d + 2))

    def to_left(c):
        return remote(lb.at[at(c)], lb.at[at(c)], ss.at[1, c], rs.at[1, c], (h, d - 2))

    def give(c, dst):
        return remote(oth.at[at(c)], dst.at[at(c), mine], fs.at[c], fr.at[c], mate)

    def keep(c, dst):
        return pltpu.make_async_copy(oth.at[at(c)], dst.at[at(c), mine], gl.at[c])

    def pick(c):
        place = lax.broadcasted_iota(jnp.int32, (table.shape[0], CH), 0) + base
        hot = jnp.where(order[pl.ds(c, 1)] == place, 1.0, 0.0).astype(bf16)
        own[at(c)] = tdot(hot, table[...]).astype(bf16)
        swap(c).start()

    base = d * capacity
    spare = slots_v.shape[0] - capacity
    if spare:
        slots_v[pl.ds(capacity, spare)] = jnp.zeros((spare, 8, width // 8), f32)
    load_t.wait()
    for j in range(8):
        table[:, j * (width // 8) : (j + 1) * (width // 8)] = slots_v[:, j, :].astype(bf16)
    pick(0)
    pick(1)
    last = SKEW * jnp.maximum(z, n - 1 - z)

    def step(t, carry):
        @pl.when(t + 2 < nc)
        def _():
            pick(t + 2)

        @pl.when(t < nc)
        def _():
            swap(t).wait_recv()
            oth[at(t)] = oth[at(t)] + own[at(t), mine]

        c = t - SKEW * z
        @pl.when((c >= 0) & (c < nc))
        def _():
            @pl.when(z > 0)
            def _():
                to_right(c).wait_recv()
                rb[at(c)] = rb[at(c)] + oth[at(c)]
            @pl.when(z == 0)
            def _():
                rb[at(c)] = oth[at(c)]
            @pl.when(z < n - 1)
            def _():
                to_right(c).start()

        e = t - SKEW * (n - 1 - z)
        @pl.when((e >= 0) & (e < nc))
        def _():
            @pl.when(z < n - 1)
            def _():
                to_left(e).wait_recv()
                lb[at(e)] = lb[at(e)] + oth[at(e)]
            @pl.when(z == n - 1)
            def _():
                lb[at(e)] = oth[at(e)]
            @pl.when(z > 0)
            def _():
                to_left(e).start()

        g = t - last
        @pl.when((g >= 0) & (g < nc))
        def _():
            oth[at(g)] = rb[at(g)] + lb[at(g)] - oth[at(g)]
            @pl.when(g < early)
            def _():
                give(g, wv).start()
                keep(g, wv).start()
            @pl.when(g >= early)
            def _():
                give(g, w).start()
                keep(g, w).start()
        return carry

    def steps(lo, hi):
        lax.fori_loop(lo, hi, step, 0)

    steps(0, 1)
    load_c.wait()
    place = lax.broadcasted_iota(jnp.int32, (L, Wd), 0)
    for s in range(seqs):
        r = pl.ds(s * L, L)
        cv[r] = jnp.where(place < lengths[s], cv[r], jnp.zeros((L, Wd), bf16))
    steps(1, 2)
    for i in range(parts):
        spread_x.forward(i)
        steps(2 + i, 3 + i)
    spread_c.start()
    own_c = pltpu.make_async_copy(cv, cf.at[:, col(h)], ls.at[1])
    own_c.start()
    t = early + SKEW * (n - 1)
    steps(2 + parts, t)
    for c in range(early):
        keep(c, wv).wait()
        give(c, wv).wait_recv()
    save_w = pltpu.make_async_copy(wv, w.at[pl.ds(0, early * CH)], ls.at[2])
    save_w.start()
    spread_x.arrived()
    own_x.wait()
    save_x = pltpu.make_async_copy(xv, xf, ls.at[3])
    save_x.start()

    taps3 = wv[0:16].astype(f32)
    flat = [taps3[hl + i : hl + i + 1] for i in range(small - hl)]
    line = 3 * heads * DK
    joined = jnp.concatenate(flat, 1)
    for j in range(KCONV):
        tp[j : j + 1] = joined[:, j * line : (j + 1) * line]

    go[0:1] = gain[2:3, col(h)]
    saves = []
    for s in range(seqs):
        rows = pl.ds(s * L, L)
        for i in range(2):
            r = pl.ds(s * L + i * (L // 2), L // 2)
            xx = xv[r].astype(f32)
            n1 = (xx * lax.rsqrt(jnp.mean(xx * xx, -1, keepdims=True) + norm_eps) * gain[0:1]).astype(bf16)
            lv[r] = dot_t(n1, wv[0:lead])
            qv[r] = dot_t(n1, wv[lead:at_out])
        if s == 0:
            spread_c.forward(0)
        steps(t, t + 1)
        sub = lambda ref: ref.at[:, rows]
        fwd_conv(qv.at[rows], lv.at[rows], tp, sub(q_s), sub(k_s), sub(p_s), sub(g_s), sub(r_s), sub(t_s), l_w, heads, chunks)
        if s == 0:
            spread_c.forward(1)
        else:
            spread_a[s - 1].forward(0)
        steps(t + 1, t + 2)
        fwd_inverse(sub(t_s), l_w, heads, chunks)
        if s == 0:
            spread_c.forward(2)
        steps(t + 2, t + 3)
        fwd_states(lv.at[rows], go, av.at[rows], sub(q_s), sub(k_s), sub(u_s), sub(t_s), sub(p_s), sub(r_s), sub(s_s), sub(o_s), heads, chunks)
        spread_a[s].start()
        saves.append(pltpu.make_async_copy(av.at[rows], af.at[rows, col(h)], sv.at[s, 0]))
        pairs = [(qv.at[rows], qkv_o.at[rows]), (lv.at[rows], lg_o.at[rows])]
        for src, dst in ((q_s, q_o), (k_s, k_o), (u_s, u_o), (t_s, t_o), (p_s, p_o), (g_s, g_o), (r_s, r_o), (s_s, s_o), (o_s, o_o)):
            pairs.append((src.at[:, rows], dst.at[:, rows]))
        for k, (src, dst) in enumerate(pairs):
            saves.append(pltpu.make_async_copy(src, dst, sv.at[s, 1 + k]))
        for cp in saves[-12:]:
            cp.start()
        steps(t + 3, t + 4)
        t += 4
        if s == 1:
            save_w.wait()
            for c in range(early, -(-at_gate // CH)):
                keep(c, w).wait()
                give(c, w).wait_recv()
            spread_o.start()
            own_o = pltpu.make_async_copy(w.at[pl.ds(at_out, hw)], of.at[col(h, hw)], ls.at[4])
            own_o.start()
    steps(t, t + 2)
    spread_a[seqs - 1].forward(0)
    spread_o.forward(0)
    steps(t + 2, nc + SKEW * (n - 1))

    own_c.wait()
    own_o.wait()
    save_x.wait()
    for cp in saves:
        cp.wait()
    for sp in [spread_c, *spread_a, spread_o]:
        sp.arrived()
    for sp in [spread_x, spread_c, *spread_a, spread_o]:
        sp.sent()

    def drain(c, carry):
        swap(c).wait_send()
        @pl.when(c < early)
        def _():
            give(c, wv).wait_send()
        @pl.when(c >= early)
        def _():
            give(c, w).wait_send()
        @pl.when(c >= -(-at_gate // CH))
        def _():
            keep(c, w).wait()
            give(c, w).wait_recv()
        @pl.when(z < n - 1)
        def _():
            to_right(c).wait_send()
        @pl.when(z > 0)
        def _():
            to_left(c).wait_send()
        return carry

    lax.fori_loop(0, nc, drain, 0)


def front(slots, order, gain, lengths, x, cot, seqs, heads, lead, at_out, at_gate, hl, small, capacity, cid):
    T, Wd = x.shape
    rows = order.shape[0] * order.shape[1]
    width = slots.shape[1] * slots.shape[2]
    padded = -(-capacity // 128) * 128
    half = width // 2
    nc = rows // CH
    early = -(-at_out // CH)
    L = T // seqs
    hbm = pl.BlockSpec(memory_space=pl.ANY)
    S = jax.ShapeDtypeStruct
    sav = [S((heads, T, DK), bf16)] * 8 + [S((heads, T, DK), f32)]
    outs = [
        S((rows, width), bf16), S((T, width), bf16), S((T, width), bf16), S((T, width), bf16),
        S((4 * (at_gate - at_out), width), bf16), S((T, at_out - lead), f32), S((T, lead), f32), *sav,
    ]
    V = pltpu.VMEM
    piece = V((rows, half), bf16)
    return pl.pallas_call(
        functools.partial(
            front_kernel, seqs=seqs, heads=heads, lead=lead, at_out=at_out, at_gate=at_gate, hl=hl, small=small, capacity=capacity
        ),
        in_specs=[VM()] * 2 + [pl.BlockSpec(memory_space=pltpu.SMEM)] + [hbm] * 3,
        out_specs=[hbm] * len(outs),
        out_shape=outs,
        scratch_shapes=[
            V((rows, width), bf16), piece, piece, piece, V((early * CH, width), bf16), V((T, width), bf16),
            V((T, at_out - lead), f32), V((T, lead), f32), V((8, at_out - lead), f32), V((T, heads * DK), bf16),
            *[V((heads, T, DK), bf16)] * 8, V((heads, T, DK), f32), V((heads, L, DK), bf16), V((T, Wd), bf16), V((8, Wd), f32),
            V((padded, 8, width // 8), f32), V((padded, width), bf16),
            DMA((nc,)), DMA((nc,)), DMA((nc,)), DMA((nc,)), DMA((nc,)), DMA((2, nc)), DMA((2, nc)),
            DMA((2, 21 + 3 * seqs)), DMA((2, 21 + 3 * seqs)), DMA((7,)), DMA((seqs, 12)),
        ],
        compiler_params=pltpu.CompilerParams(collective_id=cid, has_side_effects=True, vmem_limit_bytes=60 << 20),
        name="front",
    )(order, gain, lengths, slots, x, cot)


def bwd_blocks(da_ref, gain_ref, o_s, q_s, k_s, u_s, p_s, s_s, dg_ref, do_w, w_w, dq_w, dk_w, qd_w, heads, chunks):
    i, j = masks()
    low = j <= i
    for c in range(chunks):
        for h in range(heads):
            rows = slice(c * C, (c + 1) * C)
            hc = slice(h * DK, (h + 1) * DK)
            o = o_s[h, rows]
            ro = lax.rsqrt(jnp.mean(o * o, -1, keepdims=True) + norm_eps)
            da = da_ref[rows, hc]
            on = o * ro
            dg_ref[0:1, hc] += jnp.sum(da * on, 0, keepdims=True)
            t = da * gain_ref[0:1, hc]
            do = (ro * (t - on * jnp.mean(t * on, -1, keepdims=True))).astype(bf16)
            qb, kb = q_s[h, rows], k_s[h, rows]
            dP = jnp.where(low, dot_t(do, u_s[h, rows]), 0.0).astype(bf16)
            do_w[h, rows] = do
            w_w[h, rows] = tdot(p_s[h, rows], do)
            dq_w[h, rows] = dot_t(do, s_s[h, rows]) + dot(dP, kb)
            dk_w[h, rows] = tdot(dP, qb)
            qd_w[h, rows] = tdot(qb, do)


def bwd_states(lg_ref, k_s, t_s, w_w, qd_w, ds_w, heads, chunks):
    dS = [jnp.zeros((DK, DK), f32) for _ in range(heads)]
    for c in reversed(range(chunks)):
        rows = slice(c * C, (c + 1) * C)
        kb = [k_s[h, rows] for h in range(heads)]
        dSb = [dS[h].astype(bf16) for h in range(heads)]
        du = [(w_w[h, rows] + dot(kb[h], dSb[h])).astype(bf16) for h in range(heads)]
        e = [tdot(t_s[h, rows], du[h]) for h in range(heads)]
        beta = [jax.nn.sigmoid(lg_ref[rows, h : h + 1]) for h in range(heads)]
        dS = [dS[h] + qd_w[h, rows] - tdot(kb[h], (beta[h] * e[h]).astype(bf16)) for h in range(heads)]
        for h in range(heads):
            w_w[h, rows] = e[h]
            ds_w[h, rows] = dSb[h]


def bwd_conv(x_ref, lg_ref, taps_ref, q_s, k_s, u_s, g_s, r_s, s_s, w_w, dq_w, dk_w, ds_w, dc, dx_ref, dlg_ref, dt_ref, heads, chunks):
    i, j = masks()
    slow = j < i
    zero8 = jnp.zeros((8, DK), f32)
    W = heads * DK
    lane = lax.broadcasted_iota(jnp.int32, (C, dlg_ref.shape[1]), 1)
    row8 = lax.broadcasted_iota(jnp.int32, (8, DK), 0)
    dc[chunks * C : chunks * C + 8] = jnp.zeros((8, 3 * W), f32)
    for c in reversed(range(chunks)):
        rows = slice(c * C, (c + 1) * C)
        dlg = jnp.zeros(lane.shape, f32)
        for h in range(heads):
            e = w_w[h, rows]
            eb = e.astype(bf16)
            beta = jax.nn.sigmoid(lg_ref[rows, h : h + 1])
            be = beta * e
            ub, kb = u_s[h, rows], k_s[h, rows]
            dL = jnp.where(slow, -dot_t(eb, ub), 0.0)
            dGb = (beta * dL).astype(bf16)
            dk = (
                dk_w[h, rows] + dot_t(ub, ds_w[h, rows]) - dot_t(be.astype(bf16), s_s[h, rows])
                + dot(dGb, kb) + tdot(dGb, kb)
            )
            db = jnp.sum(e * r_s[h, rows].astype(f32) + dL * g_s[h, rows].astype(f32), -1, keepdims=True)
            dlg = jnp.where(lane == h, db * beta * (1.0 - beta), dlg)
            for n, off in (("q", 0), ("k", W), ("v", 2 * W)):
                cols = slice(off + h * DK, off + (h + 1) * DK)
                tp = taps_ref[:, cols]
                x = x_ref[rows, cols]
                prev = zero8 if c == 0 else x_ref[c * C - 8 : c * C, cols]
                moved = [shifted(x, prev, 3 - jj) for jj in range(4)]
                conv = tp[3:4] * moved[3]
                for jj in range(3):
                    conv = conv + tp[jj : jj + 1] * moved[jj]
                sg = jax.nn.sigmoid(conv)
                act = conv * sg
                if n == "v":
                    dd = be
                else:
                    r = lax.rsqrt(jnp.sum(act * act, -1, keepdims=True) + norm_eps)
                    g = dq_w[h, rows] * DK**-0.5 if n == "q" else dk
                    an = act * r
                    dd = r * (g - an * jnp.sum(g * an, -1, keepdims=True))
                dconv = dd * (sg + act * (1.0 - sg))
                dc[rows, cols] = dconv
                for jj in range(4):
                    dt_ref[jj : jj + 1, cols] += jnp.sum(dconv * moved[jj], 0, keepdims=True)
                nxt = dc[(c + 1) * C : (c + 1) * C + 8, cols]
                dx = tp[3:4] * dconv
                for jj in range(1, 4):
                    r = pltpu.roll(dconv, C - jj, 0)
                    bot = jnp.where(row8 >= 8 - jj, pltpu.roll(nxt, 8 - jj, 0), r[C - 8 :])
                    dx = dx + tp[3 - jj : 4 - jj] * jnp.concatenate([r[: C - 8], bot], 0)
                dx_ref[rows, cols] = dx.astype(bf16)
        dlg_ref[rows] = dlg.astype(bf16)


class Scatter:
    def __init__(self, part, beside, rows, bufs, slot, ss, rs, base):
        self.h, self.d = lax.axis_index("head"), lax.axis_index("dp")
        self.part, self.beside, self.slot = part, beside, slot
        self.fb, self.db, self.cb = bufs
        self.half = rows.size // 2
        self.rows = [pl.ds(rows.start + i * self.half, self.half) for i in range(2)]
        self.ss, self.rs, self.base = ss, rs, base

    def col(self, k):
        w = self.part.shape[1] // 4
        return pl.ds(pl.multiple_of(jnp.bitwise_xor(self.h, k) * w, w), w)

    def copy(self, src, dst, to, k):
        return pltpu.make_async_remote_copy(
            src, dst, self.ss.at[to - 1, self.base + k], self.rs.at[to - 1, self.base + k],
            device_id=(jnp.bitwise_xor(self.h, to), self.d), device_id_type=MESH,
        )

    def far(self, side):
        return self.copy(self.part.at[self.rows[side], self.col(3)], self.fb.at[self.slot, side], side + 1, 0)

    def near(self, side):
        return self.copy(self.part.at[self.rows[side], self.col(side + 1)], self.db.at[self.slot, side], side + 1, 1)

    def both(self, side):
        return self.copy(self.fb.at[self.slot, side], self.cb.at[self.slot, side], 2 - side, 2)

    def one(self):
        for side in (0, 1):
            self.far(side).start()
        for side in (0, 1):
            self.near(side).start()

    def two(self):
        for side in (0, 1):
            self.far(side).wait_recv()
            got = self.fb[self.slot, side].astype(f32) + self.beside(side).astype(f32)
            self.fb[self.slot, side] = got.astype(bf16)
            self.both(side).start()

    def three(self):
        got = []
        for side in (0, 1):
            self.near(side).wait_recv()
            self.both(side).wait_recv()
            got.append(self.db[self.slot, side].astype(f32) + self.cb[self.slot, side].astype(f32))
            self.far(side).wait_send()
            self.near(side).wait_send()
            self.both(side).wait_send()
        return got


RING = 4
SLOTS = 4


def back_kernel(
    gain, stat_in, lengths,
    h1_part, mlp_part, da_in, dh_own, mlp_own, h1_own, xf, af, w, g_ffn, qkv, lg, q_i, k_i, u_i, t_i, p_i, g_i, r_i, s_i, o_i,
    y_o, ig_o, stat_o, g_o,
    own, oth, rb, lb, rst, lst, qv, lv, q_s, k_s, u_s, t_s, p_s, g_s, r_s, s_s, o_s,
    do_w, w_w, dq_w, dk_w, qd_w, ds_w, dc, xv, wv, nb, da_f, dh_f, mlp_f, h1_f, xp, fb, db, cb, gq, gs, n1_w, dx_w, dlg_w, dt_w, dg_w, g1_w, st_w, go_w, tp, gout, av,
    xs, xr_, gl, fs, fr, ss, rs, as_, ar_, ls, lds, a2s, a2r, sts, str_,
    *, seqs, heads, lead, n_ffn, hl, small,
):
    h = lax.axis_index("head")
    d = lax.axis_index("dp")
    n = lax.axis_size("dp") // 2
    z = d // 2
    core = lax.rem(d, 2)
    mate = (h, jnp.bitwise_xor(d, 1))
    T = xf.shape[0]
    L = T // seqs
    rows_all, width = own.shape
    half = width // 2
    Wd = width // 4
    nc = rows_all // CH
    chunks = L // C
    hd = heads * DK
    at_qkv, at_out, at_ffn = lead, lead + 3 * hd, lead + 4 * hd

    bits = []
    k = 2
    while k < 2 * n:
        bits.append(k)
        k *= 2
    b = pltpu.get_barrier_semaphore()
    peers = [mate] + [(jnp.bitwise_xor(h, k), d) for k in (1, 2, 3)] + [(h, jnp.bitwise_xor(d, k)) for k in bits]
    for p in peers:
        pl.semaphore_signal(b, inc=1, device_id=p, device_id_type=MESH)
    @pl.when(z > 0)
    def _():
        pl.semaphore_signal(b, inc=1, device_id=(h, d - 2), device_id_type=MESH)
    @pl.when(z < n - 1)
    def _():
        pl.semaphore_signal(b, inc=1, device_id=(h, d + 2), device_id_type=MESH)
    pl.semaphore_wait(b, len(peers) + (z > 0).astype(jnp.int32) + (z < n - 1).astype(jnp.int32))

    def col(i, size=Wd):
        return pl.ds(pl.multiple_of(i * size, size), size)

    def at(c):
        return pl.ds(pl.multiple_of((nc - 1 - c) * CH, CH), CH)

    seq_rows = [pl.ds(s * L, L) for s in range(seqs)]
    bufs = (fb, db, cb)
    jobs = []
    kinds = []
    for kind, part in enumerate((h1_part, mlp_part, xp)):
        for s in range(EARLY if kind == 0 else 0, seqs):
            kinds.append((kind, s))
            if kind < 2:
                def beside(side, kind=kind, s=s):
                    return nb[kind, s, side]
            else:
                def beside(side, s=s):
                    r = pl.ds(s * L + side * (L // 2), L // 2)
                    return xp[r, col(jnp.bitwise_xor(h, 2 - side))]
            k = len(jobs)
            jobs.append(Scatter(part, beside, seq_rows[s], bufs, k % SLOTS, as_, ar_, 3 * k))
    jobs[0].one()

    def load(src, dst, k):
        cp = pltpu.make_async_copy(src, dst, ls.at[k])
        cp.start()
        return cp

    first = load(g_ffn, own.at[pl.ds(at_ffn, n_ffn)], 0)
    nbs = []
    for kind, part in enumerate((h1_part, mlp_part)):
        for s in range(EARLY if kind == 0 else 0, seqs):
            for side in (0, 1):
                r = pl.ds(s * L + side * (L // 2), L // 2)
                nbs.append(load(part.at[r, col(jnp.bitwise_xor(h, 2 - side))], nb.at[kind, s, side], 8 + len(nbs)))
    load_da = load(da_in, da_f, 1)
    ins = (q_i, k_i, u_i, t_i, p_i, g_i, r_i, s_i, o_i)
    scr = (q_s, k_s, u_s, t_s, p_s, g_s, r_s, s_s, o_s)

    def fetch(s):
        sl = s % 2
        cps = [pltpu.make_async_copy(qkv.at[seq_rows[s]], qv.at[sl], lds.at[sl, 9]),
               pltpu.make_async_copy(lg.at[seq_rows[s]], lv.at[sl], lds.at[sl, 10])]
        for k, (i, o) in enumerate(zip(ins, scr)):
            cps.append(pltpu.make_async_copy(i.at[:, seq_rows[s]], o.at[sl], lds.at[sl, k]))
        return cps

    for cp in fetch(0):
        cp.start()
    load_w = load(w.at[pl.ds(0, lead + 3 * hd)], wv, 2)
    load_x = load(xf, xv, 3)
    load_dh = load(dh_own, dh_f, 4)
    load_m = load(mlp_own, mlp_f, 5)
    load_h = load(h1_own, h1_f, 6)

    mine, other = col(core, half), col(1 - core, half)

    def remote(src, dst, s, r, dev):
        return pltpu.make_async_remote_copy(src, dst, s, r, device_id=dev, device_id_type=MESH)

    def ring(c):
        return pl.ds(pl.multiple_of(lax.rem(c, RING) * CH, CH), CH)

    def swap(c):
        return remote(own.at[at(c), other], oth.at[at(c)], xs.at[c], xr_.at[c], mate)

    def to_right(c):
        return remote(rst.at[ring(c)], rb.at[at(c)], ss.at[0, c], rs.at[0, c], (h, d + 2))

    def to_left(c):
        return remote(lst.at[ring(c)], lb.at[at(c)], ss.at[1, c], rs.at[1, c], (h, d - 2))

    def give(c):
        return remote(oth.at[at(c)], g_o.at[at(c), mine], fs.at[c], fr.at[c], mate)

    def keep(c):
        return pltpu.make_async_copy(oth.at[at(c)], g_o.at[at(c), mine], gl.at[c])

    def swaps(lo, hi):
        def body(c, carry):
            swap(c).start()
            return carry
        lax.fori_loop(lo, hi, body, 0)

    last = SKEW * jnp.maximum(z, n - 1 - z)

    def step(t, carry):
        @pl.when(t < nc)
        def _():
            swap(t).wait_recv()
            oth[at(t)] = oth[at(t)] + own[at(t), mine]

        c = t - SKEW * z
        @pl.when((c >= 0) & (c < nc))
        def _():
            @pl.when(z > 0)
            def _():
                to_right(c).wait_recv()
            @pl.when(z < n - 1)
            def _():
                @pl.when(c >= RING)
                def _():
                    to_right(c - RING).wait_send()
                @pl.when(z == 0)
                def _():
                    rst[ring(c)] = oth[at(c)]
                @pl.when(z > 0)
                def _():
                    rst[ring(c)] = oth[at(c)] + rb[at(c)]
                to_right(c).start()

        e = t - SKEW * (n - 1 - z)
        @pl.when((e >= 0) & (e < nc))
        def _():
            @pl.when(z < n - 1)
            def _():
                to_left(e).wait_recv()
            @pl.when(z > 0)
            def _():
                @pl.when(e >= RING)
                def _():
                    to_left(e - RING).wait_send()
                @pl.when(z == n - 1)
                def _():
                    lst[ring(e)] = oth[at(e)]
                @pl.when(z < n - 1)
                def _():
                    lst[ring(e)] = oth[at(e)] + lb[at(e)]
                to_left(e).start()

        g = t - last
        @pl.when((g >= 0) & (g < nc))
        def _():
            @pl.when(z == 0)
            def _():
                oth[at(g)] = oth[at(g)] + lb[at(g)]
            @pl.when(z == n - 1)
            def _():
                oth[at(g)] = oth[at(g)] + rb[at(g)]
            @pl.when((z > 0) & (z < n - 1))
            def _():
                oth[at(g)] = (oth[at(g)].astype(f32) + rb[at(g)].astype(f32) + lb[at(g)].astype(f32)).astype(bf16)
            give(g).start()
            keep(g).start()
        return carry

    now = [0]
    end = nc + SKEW * (n - 1)

    def advance(k):
        hi = min(now[0] + k, end)
        if hi > now[0]:
            lax.fori_loop(now[0], hi, step, 0)
        now[0] = hi

    first.wait()
    swaps(0, n_ffn // CH)
    for ref in (dt_w, dg_w, g1_w, gq, gs):
        ref[...] = jnp.zeros_like(ref)
    advance(1)
    for cp in nbs:
        cp.wait()
    jobs[0].two()
    jobs[1].one()
    advance(1)
    load_da.wait()

    def finish(k):
        kind, s = kinds[k]
        got = jobs[k].three()
        for side in (0, 1):
            r = pl.ds(s * L + side * (L // 2), L // 2)
            if kind == 0:
                dh_f[r] += got[side]
            elif kind == 1:
                m = mlp_f[r] + got[side]
                y = h1_f[r] + m
                y_o[r] = y.astype(bf16)
                place = lax.broadcasted_iota(jnp.int32, (L // 2, Wd), 0) + side * (L // 2)
                keep_ = place < lengths[s]
                lane = lax.broadcasted_iota(jnp.int32, (1, width), 1)
                sy = jnp.sum(jnp.sum(jnp.where(keep_, y * y, 0.0), -1, keepdims=True), 0, keepdims=True)
                sm = jnp.sum(jnp.sum(jnp.where(keep_, m * m, 0.0), -1, keepdims=True), 0, keepdims=True)
                st_w[0, 3:4] += jnp.where(lane == 0, sy, jnp.where(lane == 2, sm, 0.0))
            else:
                ig_o[r] = dh_f[r] + xp[r, col(h)].astype(f32) + got[side]

    turn = [1]
    done = [0]

    def relay():
        k = turn[0]
        if k + 1 < len(jobs) and kinds[k + 1][0] == 2:
            assert kinds[k + 1][1] < done[0]
        if k < len(jobs):
            jobs[k].two()
        if k + 1 < len(jobs):
            jobs[k + 1].one()
        if k - 1 < len(jobs):
            finish(k - 1)
        turn[0] += 1

    st_w[0] = stat_in[...]
    load_w.wait()
    taps3 = wv[0:16].astype(f32)
    joined = jnp.concatenate([taps3[hl + i : hl + i + 1] for i in range(small - hl)], 1)
    for j in range(KCONV):
        tp[j : j + 1] = joined[:, j * 3 * hd : (j + 1) * 3 * hd]
    gout[0:1] = gain[2:3, col(h)]
    ex = []
    load_a = load(af, av, 7)

    def output_rows():
        if ex or turn[0] < 1 + sum(kind == 0 for kind, _ in kinds):
            return
        load_a.wait()
        go_w[...] = tdot(av[...], dh_f[...].astype(bf16)).astype(bf16)
        for k in (1, 2, 3):
            p = jnp.bitwise_xor(h, k)
            cp = remote(go_w.at[col(p, hd)], own.at[pl.ds(at_out, hd), col(h)], a2s.at[k - 1], a2r.at[k - 1], (p, d))
            cp.start()
            ex.append(cp)
        own[pl.ds(at_out, hd), col(h)] = go_w[col(h, hd)]

    for s in range(seqs):
        sl = s % 2
        for cp in fetch(s):
            cp.wait()
        if s + 1 < seqs:
            for cp in fetch(s + 1):
                cp.start()
        if s == 0:
            for cp in (load_x, load_dh, load_m, load_h):
                cp.wait()
        sub = [ref.at[sl] for ref in scr]
        q_, k_, u_, t_, p_, g_, r_, s_, o_ = sub
        x_, l_ = qv.at[sl], lv.at[sl]
        bwd_blocks(da_f.at[seq_rows[s]], gout, o_, q_, k_, u_, p_, s_, dg_w, do_w, w_w, dq_w, dk_w, qd_w, heads, chunks)
        advance(1)
        bwd_states(l_, k_, t_, w_w, qd_w, ds_w, heads, chunks)
        if s > 0:
            relay()
            output_rows()
        advance(1)
        bwd_conv(x_, l_, tp, q_, k_, u_, g_, r_, s_, w_w, dq_w, dk_w, ds_w, dc, dx_w, dlg_w, dt_w, heads, chunks)
        advance(1)
        if s == 0:
            relay()
            output_rows()
        for i in range(2):
            lo = i * (L // 2)
            r = pl.ds(s * L + lo, L // 2)
            here = pl.ds(lo, L // 2)
            xx = xv[r].astype(f32)
            r1 = lax.rsqrt(jnp.mean(xx * xx, -1, keepdims=True) + norm_eps)
            xn = xx * r1
            n1_w[here] = (xn * gain[0:1]).astype(bf16)
            dn = dot(dx_w[here], wv[lead:]) + dot(dlg_w[here], wv[0:lead])
            g1_w[0:1] += jnp.sum(dn * xn, 0, keepdims=True)
            gd = dn * gain[0:1]
            xp[r] = (r1 * (gd - xn * jnp.mean(gd * xn, -1, keepdims=True))).astype(bf16)
            if i == 0:
                advance(1)
        done[0] += 1
        gq[...] += tdot(dx_w[...], n1_w[...])
        gs[...] += tdot(dlg_w[...], n1_w[...])
        if 0 < s < seqs - 1:
            relay()
            output_rows()
        if s + 1 < seqs:
            advance(1)
    line = 3 * hd
    dt = jnp.concatenate([dt_w[j : j + 1] for j in range(KCONV)], 1)
    row = lax.broadcasted_iota(jnp.int32, (lead, width), 0)
    tail = gs[...]
    for i in range(small - hl):
        tail = jnp.where(row == hl + i, dt[:, i * width : (i + 1) * width], tail)
    tail = jnp.where(row < small, tail, 0.0)
    own[pl.ds(0, lead)] = tail.astype(bf16)
    own[pl.ds(at_qkv, 3 * hd)] = gq[...].astype(bf16)
    for cp in ex:
        cp.wait()
    assert now[0] <= n_ffn // CH
    swaps(n_ffn // CH, nc)
    lane = lax.broadcasted_iota(jnp.int32, (1, width), 1)
    three = jnp.concatenate([dg_w[0:1]] * 4, 1)
    st_w[0, 0:1] = g1_w[0:1]
    st_w[0, 2:3] = jnp.where((lane >= h * Wd) & (lane < (h + 1) * Wd), three, 0.0)
    assert ex
    advance(1)
    while turn[0] <= len(jobs) - seqs:
        relay()
        advance(3)
    rounds = [(jnp.bitwise_xor(h, k), d) for k in (1, 2)] + [mate] + [(h, jnp.bitwise_xor(d, k)) for k in bits]
    sent = []
    for i, p in enumerate(rounds):
        cp = remote(st_w.at[i], str_.at[i], sts.at[0, i], sts.at[1, i], p)
        cp.start()
        sent.append(cp)
        if turn[0] <= len(jobs) and i % 2 == 1:
            relay()
        advance(2)
        cp.wait_recv()
        st_w[i + 1] = st_w[i] + str_[i]
    stat_o[...] = st_w[len(rounds)]
    while turn[0] <= len(jobs):
        relay()
        advance(2)
    advance(end)
    for cp in sent:
        cp.wait_send()

    def drain(c, carry):
        swap(c).wait_send()
        give(c).wait()
        keep(c).wait()
        @pl.when(c >= nc - RING)
        def _():
            @pl.when(z < n - 1)
            def _():
                to_right(c).wait_send()
            @pl.when(z > 0)
            def _():
                to_left(c).wait_send()
        return carry

    lax.fori_loop(0, nc, drain, 0)


def back(gain, stat_in, lengths, h1_part, mlp_part, owns, xf, af, w, g_ffn, qkv, lg, saved, seqs, heads, lead, hl, small, cid):
    T, width = xf.shape
    Wd = width // 4
    half = width // 2
    L = T // seqs
    hd = heads * DK
    n_ffn = g_ffn.shape[0]
    rows = n_ffn + 4 * hd + lead
    nc = rows // CH
    hbm = pl.BlockSpec(memory_space=pl.ANY)
    S = jax.ShapeDtypeStruct
    V = pltpu.VMEM
    n = lax.axis_size("dp") // 2
    rounds = 2 + 1 + max(n.bit_length() - 1, 0)
    piece, ringbuf = V((rows, half), bf16), V((RING * CH, half), bf16)
    blk = lambda dt: V((2, heads, L, DK), dt)
    wk = lambda dt: V((heads, L, DK), dt)
    rsb = V((SLOTS, 2, L // 2, Wd), bf16)
    njobs = 3 * seqs - EARLY
    return pl.pallas_call(
        functools.partial(back_kernel, seqs=seqs, heads=heads, lead=lead, n_ffn=n_ffn, hl=hl, small=small),
        in_specs=[VM(), VM(), pl.BlockSpec(memory_space=pltpu.SMEM)] + [hbm] * 21,
        out_specs=[VM(), VM(), VM(), hbm],
        out_shape=[S((T, Wd), bf16), S((T, Wd), f32), S((8, width), f32), S((rows, width), bf16)],
        scratch_shapes=[
            V((rows, width), bf16), piece, piece, piece, ringbuf, ringbuf,
            V((2, L, 3 * hd), f32), V((2, L, lead), f32), *[blk(bf16)] * 8, blk(f32),
            wk(bf16), wk(f32), wk(f32), wk(f32), wk(f32), wk(bf16), V((L + 8, 3 * hd), f32),
            V((T, width), bf16), V((lead + 3 * hd, width), bf16), V((2, seqs, 2, L // 2, Wd), bf16),
            V((T, Wd), f32), V((T, Wd), f32), V((T, Wd), f32), V((T, Wd), f32), V((T, width), bf16), rsb, rsb, rsb,
            V((3 * hd, width), f32), V((lead, width), f32), V((L, width), bf16), V((L, 3 * hd), bf16), V((L, lead), bf16),
            V((8, 3 * hd), f32), V((8, hd), f32), V((8, width), f32), V((rounds + 1, 8, width), f32), V((4 * hd, Wd), bf16),
            V((8, 3 * hd), f32), V((8, Wd), f32), V((T, width), bf16),
            DMA((nc,)), DMA((nc,)), DMA((nc,)), DMA((nc,)), DMA((nc,)), DMA((2, nc)), DMA((2, nc)),
            DMA((2, 3 * njobs)), DMA((2, 3 * njobs)), DMA((8 + 4 * seqs,)), DMA((2, 11)), DMA((3,)), DMA((3,)),
            DMA((2, rounds)), V((rounds, 8, width), f32),
        ],
        compiler_params=pltpu.CompilerParams(collective_id=cid, has_side_effects=True, vmem_limit_bytes=63 << 20),
        name="back",
    )(gain, stat_in, lengths, h1_part, mlp_part, *owns, xf, af, w, g_ffn, qkv, lg, *saved)


RT = 256
RC = 32
EARLY = 0


def ffn_kernel(
    gain, lengths, af, xf, cf, of, w,
    mlp_o, h1p_o, da_o, dh_o, mo_o, h1_o, g_o, stat_o,
    ov, wgu, wd, wo, a_v, x_v, c_v, n2_s, hid_s, dgu_s, h1_w, t_w, g2_w, gate_w, up_w, dh_w, mlp_s, h1p_s, da_s, fb, db, cb, hb, kb, lb, dav, dhv, mov, h1v, gv,
    lw, lt, sv, as_, ar_, hs, hr_, og,
    *, seqs, at_out, at_gate,
):
    h = lax.axis_index("head")
    d = lax.axis_index("dp")
    T, width = xf.shape
    Wd = width // 4
    L = T // seqs
    ffl, ffp = wd.shape[0], wgu.shape[0] // 2
    n = T // RT
    b = pltpu.get_barrier_semaphore()
    for k in (1, 2):
        pl.semaphore_signal(b, inc=1, device_id=(jnp.bitwise_xor(h, k), d), device_id_type=MESH)
    pl.semaphore_wait(b, 2)

    def col(k):
        return pl.ds(pl.multiple_of(jnp.bitwise_xor(h, k) * Wd, Wd), Wd)

    def rows(i):
        return pl.ds(pl.multiple_of(i * RT, RT), RT)

    def slot(i):
        return lax.rem(i, 2)

    def fetch(i):
        return [
            pltpu.make_async_copy(src.at[rows(i)], dst.at[slot(i)], lt.at[slot(i), k])
            for k, (src, dst) in enumerate(((af, a_v), (xf, x_v)))
        ]

    loads = [pltpu.make_async_copy(of, ov, lw.at[0])]
    dsts = (wgu.at[pl.ds(0, ffl)], wgu.at[pl.ds(ffp, ffl)], wd, wo)
    for k, (lo, dst) in enumerate(zip((at_gate, at_gate + ffl, at_gate + 2 * ffl, at_out), dsts)):
        loads.append(pltpu.make_async_copy(w.at[pl.ds(lo, dst.shape[0])], dst, lw.at[1 + k]))
    loads.append(pltpu.make_async_copy(cf, c_v, lw.at[5]))
    loads[0].start()
    for cp in fetch(0):
        cp.start()
    for cp in loads[1:]:
        cp.start()
    stat_o[...] = jnp.zeros_like(stat_o)
    for lo in (ffl, ffp + ffl):
        wgu[pl.ds(lo, ffp - ffl)] = jnp.zeros((ffp - ffl, width), bf16)
        dgu_s[:, lo : lo + ffp - ffl] = jnp.zeros((T, ffp - ffl), bf16)

    def job(i):
        def beside(side):
            start = pl.multiple_of(i * RT + side * (RT // 2), RT // 2)
            return da_s[pl.ds(start, RT // 2), col(2 - side)]

        return Scatter(da_s, beside, rows(i), (fb, db, cb), lax.rem(i, SLOTS), as_, ar_, 3 * i)

    more = EARLY * L // RT

    def job2(i):
        def beside(side):
            start = pl.multiple_of(i * RT + side * (RT // 2), RT // 2)
            return h1p_s[pl.ds(start, RT // 2), col(2 - side)]

        return Scatter(h1p_s, beside, rows(i), (hb, kb, lb), lax.rem(i, SLOTS), hs, hr_, 3 * i)

    def out(k, i):
        src, dst = ((dav, da_o), (dhv, dh_o), (mov, mo_o), (h1v, h1_o))[k]
        return pltpu.make_async_copy(src.at[rows(i)], dst.at[rows(i)], og.at[k, i])

    def finish(i):
        got = job(i).three()
        for side in (0, 1):
            start = pl.multiple_of(i * RT + side * (RT // 2), RT // 2)
            dav[pl.ds(start, RT // 2)] += got[side]
        out(0, i).start()

    def finish2(i):
        got = job2(i).three()
        for side in (0, 1):
            start = pl.multiple_of(i * RT + side * (RT // 2), RT // 2)
            dhv[pl.ds(start, RT // 2)] += got[side]
        out(1, i).start()

    def saves(i):
        return [
            pltpu.make_async_copy(mlp_s.at[slot(i)], mlp_o.at[rows(i)], sv.at[slot(i), 0]),
            pltpu.make_async_copy(h1p_s.at[rows(i)], h1p_o.at[rows(i)], sv.at[slot(i), 1]),
        ]

    loads[0].wait()

    def tile(i, carry):
        @pl.when(i + 1 < n)
        def _():
            for cp in fetch(i + 1):
                cp.start()

        @pl.when(i >= 2)
        def _():
            for cp in saves(i - 2):
                cp.wait()

        for cp in fetch(i):
            cp.wait()
        r, s = rows(i), slot(i)

        def part_of(k):
            return pl.ds(pl.multiple_of(i * RT + k, RC), RC), slice(k, k + RC)

        t_w[...] = dot(a_v[s], ov[...])
        place = lax.broadcasted_iota(jnp.int32, (RT, Wd), 0) + lax.rem(i * RT, L)
        good = place < lengths[i * RT // L]
        lane = lax.broadcasted_iota(jnp.int32, (1, width), 1)
        attn = t_w[:, col(0)]
        sa = jnp.sum(jnp.sum(jnp.where(good, attn * attn, 0.0), 0, keepdims=True), -1, keepdims=True)
        count = jnp.sum(jnp.sum(jnp.where(good, 1.0, 0.0), 0, keepdims=True), -1, keepdims=True)
        stat_o[3:4] += jnp.where(lane == 1, sa, jnp.where(lane == 3, count, 0.0))
        for k in range(0, RT, RC):
            rk, k_ = part_of(k)
            h1 = x_v[s, k_].astype(f32) + t_w[k_]
            h1_w[k_] = h1
            r2 = lax.rsqrt(jnp.mean(h1 * h1, -1, keepdims=True) + norm_eps)
            n2_s[rk] = (h1 * r2 * gain[1:2]).astype(bf16)
        h1v[r] = h1_w[:, col(0)]
        out(3, i).start()

        @pl.when(i == 0)
        def _():
            for cp in loads[1:]:
                cp.wait()

        cot = c_v[r]
        gate_w[...] = dot_t(n2_s[r], wgu[0:ffl])
        up_w[...] = dot_t(n2_s[r], wgu[ffp : ffp + ffl])
        dh_w[...] = dot_t(cot, wd[...])
        for k in range(0, RT, RC):
            rk, k_ = part_of(k)
            gate, up, dh = gate_w[k_], up_w[k_], dh_w[k_]
            sig = jax.nn.sigmoid(gate)
            act = gate * sig
            hid_s[rk] = (act * up).astype(bf16)
            dgu_s[rk, 0:ffl] = (dh * up * (sig + act * (1.0 - sig))).astype(bf16)
            dgu_s[rk, ffp : ffp + ffl] = (dh * act).astype(bf16)
        t_w[...] = dot(hid_s[r], wd[...])
        mov[r] = t_w[:, col(0)]
        out(2, i).start()
        mlp_s[s] = t_w[...].astype(bf16)
        t_w[...] = dot(dgu_s[r], wgu[...])
        for k in range(0, RT, RC):
            rk, k_ = part_of(k)
            h1, dn2 = h1_w[k_], t_w[k_]
            r2 = lax.rsqrt(jnp.mean(h1 * h1, -1, keepdims=True) + norm_eps)
            hr = h1 * r2
            g2_w[k_] = dn2 * hr
            gd = dn2 * gain[1:2]
            t_w[k_] = r2 * (gd - hr * jnp.mean(gd * hr, -1, keepdims=True))
        stat_o[1:2] += jnp.sum(g2_w[...], 0, keepdims=True)
        dhv[r] = t_w[:, col(0)] + c_v[r, col(0)].astype(f32)
        low = t_w[...].astype(bf16)
        h1p_s[r] = low
        for cp in saves(i):
            cp.start()
        t_w[...] = dot_t(low, ov[...])
        da_s[r] = t_w[...].astype(bf16)
        dav[r] = t_w[:, col(0)] + dot_t(cot, wo[...])

        @pl.when(i >= 2)
        def _():
            finish(i - 2)

        @pl.when((i >= 2) & (i - 2 < more))
        def _():
            finish2(i - 2)

        @pl.when(i >= 1)
        def _():
            job(i - 1).two()

        @pl.when((i >= 1) & (i - 1 < more))
        def _():
            job2(i - 1).two()

        job(i).one()

        @pl.when(i < more)
        def _():
            job2(i).one()

        @pl.when(i >= more)
        def _():
            out(1, i).start()

        return carry

    lax.fori_loop(0, n, tile, 0)

    def grad(k, value):
        gv[pl.ds(k * ffl, ffl)] = value.astype(bf16)
        return pltpu.make_async_copy(gv.at[pl.ds(k * ffl, ffl)], g_o.at[pl.ds(k * ffl, ffl)], lw.at[k])

    g2 = grad(2, tdot(hid_s[...], c_v[...]))
    g2.start()
    job(n - 1).two()
    finish(n - 2)
    g1 = grad(1, tdot(dgu_s[:, ffp:], n2_s[...])[0:ffl])
    g1.start()
    g0 = grad(0, tdot(dgu_s[:, 0:ffp], n2_s[...])[0:ffl])
    g0.start()
    finish(n - 1)
    for cp in (g0, g1, g2):
        cp.wait()
    for i in (n - 2, n - 1):
        for cp in saves(i):
            cp.wait()
    for i in range(n):
        for k in range(4):
            out(k, i).wait()


def ffn(gain, lengths, af, xf, cf, of, w, seqs, at_out, at_gate, ffl, cid):
    T, width = xf.shape
    Wd = width // 4
    hd = at_gate - at_out
    n = T // RT
    ffp = -(-ffl // 128) * 128
    hbm = pl.BlockSpec(memory_space=pl.ANY)
    S = jax.ShapeDtypeStruct
    V = pltpu.VMEM
    slots = V((SLOTS, 2, RT // 2, Wd), bf16)
    pair = V((2, RT, width), bf16)
    own = S((T, Wd), f32)
    return pl.pallas_call(
        functools.partial(ffn_kernel, seqs=seqs, at_out=at_out, at_gate=at_gate),
        in_specs=[VM(), pl.BlockSpec(memory_space=pltpu.SMEM)] + [hbm] * 5,
        out_specs=[hbm] * 7 + [VM()],
        out_shape=[
            S((T, width), bf16), S((T, width), bf16), own, own, own, own,
            S((3 * ffl, width), bf16), S((8, width), f32),
        ],
        scratch_shapes=[
            V((width, width), bf16), V((2 * ffp, width), bf16), V((ffl, width), bf16), V((hd, width), bf16),
            pair, pair, V((T, width), bf16), V((T, width), bf16), V((T, ffl), bf16), V((T, 2 * ffp), bf16),
            V((RT, width), f32), V((RT, width), f32), V((RT, width), f32), *[V((RT, ffl), f32)] * 3, pair, V((T, width), bf16), V((T, width), bf16),
            *[slots] * 6, *[V((T, Wd), f32)] * 4, V((3 * ffl, width), bf16),
            DMA((6,)), DMA((2, 2)), DMA((2, 2)), *[DMA((2, 3 * n))] * 4, DMA((4, n)),
        ],
        compiler_params=pltpu.CompilerParams(collective_id=cid, has_side_effects=True, vmem_limit_bytes=63 << 20),
        name="feed_forward",
    )(gain, lengths, af, xf, cf, of, w)


SB = 128


def tail_kernel(order, g, stats, gain, gain_m, gain_v, y, ig, p, m, v, p_o, m_o, v_o, gain_o, gm_o, gv_o, rms_o, y_o, ig_o, w, sem, *, capacity):
    i = pl.program_id(0)
    through = [pltpu.make_async_copy(a, b, sem.at[k]) for k, (a, b) in enumerate(((y, y_o), (ig, ig_o)))]

    @pl.when(i == 0)
    def _():
        for cp in through:
            cp.start()

    base = lax.axis_index("dp") * capacity + i * SB
    place = lax.broadcasted_iota(jnp.int32, (SB, CH), 0) + base
    hot = jnp.concatenate(
        [jnp.where(order[c : c + 1] == place, 1.0, 0.0).astype(bf16) for c in range(order.shape[0])], 1
    )
    grad = dot(hot, g[...])
    for j in range(8):
        w[:, j, :] = grad[:, j * 128 : (j + 1) * 128]
    p_o[...], m_o[...], v_o[...] = adam_step(p[...], m[...], v[...], w[...], weight_rate, weight_decay)

    @pl.when(i == 0)
    def _():
        gain_o[...], gm_o[...], gv_o[...] = adam_step(gain[...], gain_m[...], gain_v[...], stats[0:3], gain_rate, 0.0)
        lane = lax.broadcasted_iota(jnp.int32, (1, 128), 1)
        rms = jnp.sqrt(stats[3:4, 0:128] / stats[3:4, 3:4])
        for k in range(3):
            rms_o[k] = jnp.sum(jnp.where(lane == k, rms, 0.0))

    @pl.when(i == pl.num_programs(0) - 1)
    def _():
        for cp in through:
            cp.wait()


def tail(order, g, stats, gain, gain_m, gain_v, y, ig, p, m, v):
    capacity = p.shape[0]
    S = jax.ShapeDtypeStruct
    hbm = pl.BlockSpec(memory_space=pl.ANY)
    whole = lambda a: pl.BlockSpec(a.shape, lambda i: (0,) * a.ndim)
    blk = pl.BlockSpec((SB, 8, 128), lambda i: (i, 0, 0))
    like = S(p.shape, f32)
    small = S(gain.shape, f32)
    return pl.pallas_call(
        functools.partial(tail_kernel, capacity=capacity),
        grid=(-(-capacity // SB),),
        in_specs=[whole(a) for a in (order, g, stats, gain, gain_m, gain_v)] + [hbm] * 2 + [blk] * 3,
        out_specs=[blk] * 3 + [whole(gain)] * 3 + [pl.BlockSpec(memory_space=pltpu.SMEM), hbm, hbm],
        out_shape=[like] * 3 + [small] * 3 + [S((3,), f32), S(y.shape, y.dtype), S(ig.shape, ig.dtype)],
        scratch_shapes=[pltpu.VMEM((SB, 8, 128), f32), DMA((2,))],
        compiler_params=pltpu.CompilerParams(vmem_limit_bytes=56 << 20),
        name="owners_step",
    )(order, g, stats, gain, gain_m, gain_v, y, ig, p, m, v)


def adam_step(param, first, second_moment, grad, rate, decay):
    first = beta_one * first + (1.0 - beta_one) * grad
    second_moment = beta_two * second_moment + (1.0 - beta_two) * grad * grad
    denom = jnp.sqrt(second_moment / (1.0 - beta_two**STEP)) + adam_eps
    param = param - rate / (1.0 - beta_one**STEP) * first / denom - rate * decay * param
    return (param, first, second_moment)


def on_device(
    inputs, cotangent, lengths, owner_slots, table, table_m, table_v, gains, gains_m, gains_v
):
    shards = lax.axis_size("head")
    seqs = lengths.shape[0]
    hd = HEADS * DK // shards
    ffl = FF // shards
    hl = HEADS // shards
    taps_rows = KCONV * 3 * hd // MODEL_WIDTH
    capacity = table.shape[1]
    small = hl + taps_rows
    lead = 64
    at_out = lead + 3 * hd
    at_gate = at_out + hd
    n_body = 4 * hd + 3 * ffl
    order = jnp.concatenate(
        [owner_slots[n_body:], jnp.full((lead - small,), -1, jnp.int32), owner_slots[:n_body]]
    ).reshape(-1, CH)
    split = lambda t: t[0].reshape(capacity, 8, MODEL_WIDTH // 8)
    weights, x_full, cot_full, a_full, out_full, qkv, logit, *saved = front(
        split(table), order, gains, lengths, inputs, cotangent, seqs, hl, lead, at_out, at_gate, hl, small, capacity, 0
    )
    mlp_part, h1_part, da, dh_own, mlp_own, h1_own, g_ffn, stat_in = ffn(
        gains, lengths, a_full, x_full, cot_full, out_full, weights, seqs, at_out, at_gate, ffl, 1
    )
    y, input_grad, stats, g_total = back(
        gains, stat_in, lengths, h1_part, mlp_part, [da, dh_own, mlp_own, h1_own],
        x_full, a_full, weights, g_ffn, qkv, logit, saved, seqs, hl, lead, hl, small, 2,
    )
    table_new, table_m_new, table_v_new, gains_new, gains_m_new, gains_v_new, rms, y, input_grad = tail(
        order, g_total, stats, gains, gains_m, gains_v, y, input_grad, split(table), split(table_m), split(table_v)
    )
    return (
        y,
        input_grad,
        table_new.reshape(table.shape),
        table_m_new.reshape(table.shape),
        table_v_new.reshape(table.shape),
        gains_new,
        gains_m_new,
        gains_v_new,
        rms,
    )


def solution(mesh):
    tok, tab = P("dp", "head"), P("head", "dp", None)
    return jax.shard_map(
        on_device,
        mesh=mesh,
        in_specs=(tok, tok, P("dp"), P(), tab, tab, tab, P(), P(), P()),
        out_specs=(tok, tok, tab, tab, tab, P(), P(), P(), P()),
        check_vma=False,
    )
```

```python
import functools

import jax
import jax.numpy as jnp
from jax import lax
from jax.experimental import pallas as pl
from jax.experimental.pallas import tpu as pltpu
from jax.sharding import PartitionSpec as P

MODEL_WIDTH = 1024
FF = 2816
HEADS = 8
DK = 128
KCONV = 4
STEP = 10
C = 128

norm_eps = 1e-06
adam_eps = 1e-08
beta_one = 0.9
beta_two = 0.95
weight_rate = 0.02
gain_rate = 0.6
weight_decay = 0.1
f32 = jnp.float32
bf16 = jnp.bfloat16
MESH = pl.DeviceIdType.MESH
VM = functools.partial(pl.BlockSpec, memory_space=pltpu.VMEM)
DMA = pltpu.SemaphoreType.DMA

def dot(a,b): return lax.dot_general(a,b,(((1,),(0,)),((),())),preferred_element_type=f32)
def dot_t(a,b): return lax.dot_general(a,b,(((1,),(1,)),((),())),preferred_element_type=f32)
def tdot(a,b): return lax.dot_general(a,b,(((0,),(0,)),((),())),preferred_element_type=f32)

def shifted(x, prev, j):
    if j==0: return x
    r=pltpu.roll(x,j,0)
    p=pltpu.roll(prev,j,0)
    row=lax.broadcasted_iota(jnp.int32,(8,x.shape[1]),0)
    top=jnp.where(row<j,p,r[0:8])
    return jnp.concatenate([top,r[8:]],0)

def conv_silu(x,prev,taps):
    conv=taps[3:4]*x
    for j in range(1,4):
        conv=conv+taps[3-j:4-j]*shifted(x,prev,j)
    sg=jax.nn.sigmoid(conv)
    return conv,sg

def masks():
    i=lax.broadcasted_iota(jnp.int32,(C,C),0); j=lax.broadcasted_iota(jnp.int32,(C,C),1)
    return i,j

def fwd_kernel(x_ref,lg_ref,taps_ref,gain_ref,a_ref,q_s,k_s,u_s,t_s,p_s,g_s,r_s,s_s,o_s,l_w,*,heads,chunks):
    i,j=masks()
    low=j<=i; slow=j<i; xr=jnp.bitwise_xor(i,j)
    zero8=jnp.zeros((8,DK),f32)
    every=[(c,h) for c in range(chunks) for h in range(heads)]
    beta={}
    for c,h in every:
        rows=slice(c*C,(c+1)*C)
        pre={}
        for n,off in (("q",0),("k",heads*DK),("v",2*heads*DK)):
            cols=slice(off+h*DK,off+(h+1)*DK)
            x=x_ref[rows,cols]
            prev=zero8 if c==0 else x_ref[c*C-8:c*C,cols]
            conv,sg=conv_silu(x,prev,taps_ref[:,cols])
            pre[n]=conv*sg
        q=pre["q"]; q=q*(lax.rsqrt(jnp.sum(q*q,-1,keepdims=True)+norm_eps)*DK**-0.5)
        k=pre["k"]; k=k*lax.rsqrt(jnp.sum(k*k,-1,keepdims=True)+norm_eps)
        qb=q.astype(bf16); kb=k.astype(bf16)
        beta[c,h]=jax.nn.sigmoid(lg_ref[rows,h:h+1])
        sc=dot_t(jnp.concatenate([qb,kb],0),kb)
        G=sc[C:]
        Lw=jnp.where(slow,G*beta[c,h],0.0).astype(bf16)
        q_s[h,rows]=qb; k_s[h,rows]=kb; p_s[h,rows]=jnp.where(low,sc[0:C],0.0).astype(bf16); g_s[h,rows]=G.astype(bf16)
        r_s[h,rows]=pre["v"].astype(bf16)
        l_w[h,rows]=Lw
        t_s[h,rows]=jnp.where(xr==0,1.0,jnp.where(xr==1,-Lw.astype(f32),0.0)).astype(bf16)
    s=2
    while s<C:
        part=(xr>=s)&(xr<2*s)
        half=[dot(t_s[h,c*C:(c+1)*C],jnp.where(part,l_w[h,c*C:(c+1)*C],jnp.zeros((C,C),bf16))).astype(bf16) for c,h in every]
        for (c,h),y in zip(every,half):
            rows=slice(c*C,(c+1)*C)
            X=t_s[h,rows]
            t_s[h,rows]=X-dot(y,X).astype(bf16)
        s*=2
    S=[jnp.zeros((DK,DK),f32) for _ in range(heads)]
    for c in range(chunks):
        rows=slice(c*C,(c+1)*C)
        Sb=[S[h].astype(bf16) for h in range(heads)]
        m=[dot(jnp.concatenate([k_s[h,rows],q_s[h,rows]],0),Sb[h]) for h in range(heads)]
        R=[r_s[h,rows].astype(f32)-m[h][0:C] for h in range(heads)]
        ub=[dot(t_s[h,rows],(R[h]*beta[c,h]).astype(bf16)).astype(bf16) for h in range(heads)]
        S=[S[h]+tdot(k_s[h,rows],ub[h]) for h in range(heads)]
        for h in range(heads):
            s_s[h,rows]=Sb[h]; r_s[h,rows]=R[h].astype(bf16); u_s[h,rows]=ub[h]
            o=m[h][C:]+dot(p_s[h,rows],ub[h])
            o_s[h,rows]=o
            a=o*lax.rsqrt(jnp.mean(o*o,-1,keepdims=True)+norm_eps)*gain_ref[0:1,h*DK:(h+1)*DK]
            a_ref[rows,h*DK:(h+1)*DK]=a.astype(bf16)

def mixer_fwd(x,lg,taps,gain,seqs):
    T=x.shape[0]; L=T//seqs; W=x.shape[1]; heads=W//(3*DK)
    blk=lambda: pl.BlockSpec((heads,L,DK),lambda s:(0,s,0))
    sav=lambda dt: jax.ShapeDtypeStruct((heads,T,DK),dt)
    return pl.pallas_call(functools.partial(fwd_kernel,heads=heads,chunks=L//C),
        grid=(seqs,),
        in_specs=[pl.BlockSpec((L,W),lambda s:(s,0)),pl.BlockSpec((L,lg.shape[1]),lambda s:(s,0)),pl.BlockSpec(taps.shape,lambda s:(0,0)),pl.BlockSpec(gain.shape,lambda s:(0,0))],
        out_specs=[pl.BlockSpec((L,heads*DK),lambda s:(s,0))]+[blk() for _ in range(9)],
        out_shape=[jax.ShapeDtypeStruct((T,heads*DK),bf16)]+[sav(bf16) for _ in range(8)]+[sav(f32)],
        scratch_shapes=[pltpu.VMEM((heads,L,DK),bf16)],
        compiler_params=pltpu.CompilerParams(vmem_limit_bytes=56<<20),
        cost_estimate=pl.CostEstimate(flops=2*24*20*C*C*C,bytes_accessed=15<<20,transcendentals=0),
        name="mixer_fwd")(x,lg,taps,gain)

def bwd_kernel(x_ref,lg_ref,taps_ref,gain_ref,da_ref,q_s,k_s,u_s,t_s,p_s,g_s,r_s,s_s,o_s,dx_ref,dlg_ref,dt_ref,dg_ref,dc,*,heads,chunks):
    i,j=masks()
    low=j<=i; slow=j<i
    zero8=jnp.zeros((8,DK),f32)
    seq=pl.program_id(0)
    @pl.when(seq==0)
    def _():
        dt_ref[...]=jnp.zeros_like(dt_ref); dg_ref[...]=jnp.zeros_like(dg_ref)
    dS=[jnp.zeros((DK,DK),f32) for _ in range(heads)]
    W=heads*DK
    lane=lax.broadcasted_iota(jnp.int32,(C,128),1)
    dc[chunks*C:chunks*C+8]=jnp.zeros((8,3*W),f32)
    for c in reversed(range(chunks)):
        rows=slice(c*C,(c+1)*C)
        dlg=jnp.zeros((C,128),f32)
        for h in range(heads):
            hc=slice(h*DK,(h+1)*DK)
            o=o_s[h,rows]
            ro=lax.rsqrt(jnp.mean(o*o,-1,keepdims=True)+norm_eps)
            da=da_ref[rows,hc]
            on=o*ro
            dg_ref[0:1,hc]+=jnp.sum(da*on,0,keepdims=True)
            t=da*gain_ref[0:1,hc]
            do=(ro*(t-on*jnp.mean(t*on,-1,keepdims=True))).astype(bf16)
            qb=q_s[h,rows]; kb=k_s[h,rows]; ub=u_s[h,rows]; Tb=t_s[h,rows]; Pb=p_s[h,rows]; Sb=s_s[h,rows]
            G=g_s[h,rows].astype(f32); R=r_s[h,rows].astype(f32)
            beta=jax.nn.sigmoid(lg_ref[rows,h:h+1])
            dSb=dS[h].astype(bf16)
            du=tdot(Pb,do)+dot(kb,dSb)
            e=tdot(Tb,du.astype(bf16))
            eb=e.astype(bf16)
            be=beta*e; beb=be.astype(bf16)
            pe=dot_t(jnp.concatenate([do,eb],0),ub)
            dP=jnp.where(low,pe[0:C],0.0).astype(bf16)
            dL=jnp.where(slow,-pe[C:],0.0)
            dG=beta*dL
            ds=dot_t(jnp.concatenate([do,beb],0),Sb)
            dq=ds[0:C]+dot(dP,kb)
            dGb=dG.astype(bf16)
            dk=tdot(dP,qb)+dot_t(ub,dSb)-ds[C:]+dot(dGb,kb)+tdot(dGb,kb)
            db=jnp.sum(e*R+dL*G,-1,keepdims=True)
            dlg=jnp.where(lane==h,db*beta*(1.0-beta),dlg)
            dS[h]=dS[h]+tdot(qb,do)-tdot(kb,beb)
            for n,off in (("q",0),("k",W),("v",2*W)):
                cols=slice(off+h*DK,off+(h+1)*DK)
                x=x_ref[rows,cols]
                prev=zero8 if c==0 else x_ref[c*C-8:c*C,cols]
                conv,sg=conv_silu(x,prev,taps_ref[:,cols])
                act=conv*sg
                if n=="v": d=be
                else:
                    r=lax.rsqrt(jnp.sum(act*act,-1,keepdims=True)+norm_eps)
                    g_=dq*DK**-0.5 if n=="q" else dk
                    an=act*r
                    d=r*(g_-an*jnp.sum(g_*an,-1,keepdims=True))
                dconv=d*(sg*(1.0+conv*(1.0-sg)))
                dc[rows,cols]=dconv
                for jj in range(4):
                    dt_ref[jj:jj+1,cols]+=jnp.sum(dconv*shifted(x,prev,3-jj),0,keepdims=True)
                nxt=dc[(c+1)*C:(c+1)*C+8,cols]
                tp=taps_ref[:,cols]
                dx=tp[3:4]*dconv
                row8=lax.broadcasted_iota(jnp.int32,(8,DK),0)
                for jj in range(1,4):
                    r=pltpu.roll(dconv,C-jj,0)
                    pn=pltpu.roll(nxt,8-jj,0)
                    bot=jnp.where(row8>=8-jj,pn,r[C-8:])
                    dx=dx+tp[3-jj:4-jj]*jnp.concatenate([r[:C-8],bot],0)
                dx_ref[rows,cols]=dx.astype(bf16)
        dlg_ref[rows]=dlg.astype(bf16)

def mixer_bwd(x,lg,taps,gain,da,saved,seqs):
    T=x.shape[0]; L=T//seqs; W=x.shape[1]; heads=W//(3*DK)
    blk=lambda: pl.BlockSpec((heads,L,DK),lambda s:(0,s,0))
    return pl.pallas_call(functools.partial(bwd_kernel,heads=heads,chunks=L//C),
        grid=(seqs,),
        in_specs=[pl.BlockSpec((L,W),lambda s:(s,0)),pl.BlockSpec((L,lg.shape[1]),lambda s:(s,0)),pl.BlockSpec(taps.shape,lambda s:(0,0)),pl.BlockSpec(gain.shape,lambda s:(0,0)),pl.BlockSpec((L,heads*DK),lambda s:(s,0))]+[blk() for _ in range(9)],
        out_specs=[pl.BlockSpec((L,W),lambda s:(s,0)),pl.BlockSpec((L,128),lambda s:(s,0)),pl.BlockSpec((8,W),lambda s:(0,0)),pl.BlockSpec((8,heads*DK),lambda s:(0,0))],
        out_shape=[jax.ShapeDtypeStruct((T,W),bf16),jax.ShapeDtypeStruct((T,128),bf16),jax.ShapeDtypeStruct((8,W),f32),jax.ShapeDtypeStruct((8,heads*DK),f32)],
        scratch_shapes=[pltpu.VMEM((L+8,W),f32)],
        compiler_params=pltpu.CompilerParams(vmem_limit_bytes=56<<20),
        cost_estimate=pl.CostEstimate(flops=2*24*20*C*C*C,bytes_accessed=15<<20,transcendentals=0),
        name="mixer_bwd")(x,lg,taps,gain,da,*saved)


def meet(partners):
    b=pltpu.get_barrier_semaphore()
    for p in partners:
        pl.semaphore_signal(b,inc=1,device_id=p,device_id_type=MESH)
    pl.semaphore_wait(b,len(partners))

def ag_kernel(*refs,count,parts):
    ins=refs[:count]; outs=refs[count:2*count]; ss,rs,ls=refs[2*count:]
    h=lax.axis_index("head"); d=lax.axis_index("dp")
    meet([(jnp.bitwise_xor(h,1),d),(jnp.bitwise_xor(h,2),d)])
    def copy(src,dst,to,k):
        return pltpu.make_async_remote_copy(src,dst,ss.at[to-1,k],rs.at[to-1,k],device_id=(jnp.bitwise_xor(h,to),d),device_id_type=MESH)
    first={}; second=[]; local=[]
    for n in range(count):
        x,o=ins[n],outs[n]
        T,Wd=x.shape; R=T//(2*parts); base=n*3*parts
        def col(b): return pl.ds(pl.multiple_of(b*Wd,Wd),Wd)
        for i in range(2*parts):
            r1=pl.ds(i*R,R); j=(i+parts)%(2*parts); r2=pl.ds(j*R,R)
            first[n,1,i]=copy(x.at[r1],o.at[r1,col(h)],1,base+i); first[n,1,i].start()
            first[n,2,j]=copy(x.at[r2],o.at[r2,col(h)],2,base+j); first[n,2,j].start()
        l=pltpu.make_async_copy(x,o.at[:,col(h)],ls.at[n]); l.start(); local.append(l)
    for n in range(count):
        x,o=ins[n],outs[n]
        T,Wd=x.shape; R=T//(2*parts); base=n*3*parts
        def col(b): return pl.ds(pl.multiple_of(b*Wd,Wd),Wd)
        for i in range(parts):
            ra=pl.ds(i*R,R); rb=pl.ds((i+parts)*R,R)
            ca=col(jnp.bitwise_xor(h,1)); cb=col(jnp.bitwise_xor(h,2))
            first[n,1,i].wait_recv()
            c=copy(o.at[ra,ca],o.at[ra,ca],2,base+2*parts+i); c.start(); second.append(c)
            first[n,2,i+parts].wait_recv()
            c=copy(o.at[rb,cb],o.at[rb,cb],1,base+2*parts+i); c.start(); second.append(c)
    for n in range(count):
        for i in range(parts):
            first[n,1,i+parts].wait_recv(); first[n,2,i].wait_recv()
    for c in second: c.wait()
    for c in first.values(): c.wait_send()
    for l in local: l.wait()

def gather_columns(arrays,parts,cid):
    n=len(arrays)
    return pl.pallas_call(functools.partial(ag_kernel,count=n,parts=parts),
        in_specs=[VM()]*n,out_specs=[VM()]*n,
        out_shape=[jax.ShapeDtypeStruct((a.shape[0],4*a.shape[1]),a.dtype) for a in arrays],
        scratch_shapes=[DMA((2,3*parts*n)),DMA((2,3*parts*n)),DMA((n,))],
        compiler_params=pltpu.CompilerParams(collective_id=cid,has_side_effects=True,vmem_limit_bytes=56<<20),name="gather_columns")(*arrays)

def rs_kernel(*refs,count,parts):
    ins=refs[:count]; outs=refs[count:2*count]; fb,db,cb,sb,ss,rs=refs[2*count:]
    h=lax.axis_index("head"); d=lax.axis_index("dp")
    h1,h2,h3=[jnp.bitwise_xor(h,k) for k in (1,2,3)]
    meet([(h1,d),(h2,d)])
    T=ins[0].shape[0]; Wd=ins[0].shape[1]//4; half=T//2; R=half//parts
    def col(b): return pl.ds(pl.multiple_of(b*Wd,Wd),Wd)
    def copy(src,dst,to,k):
        return pltpu.make_async_remote_copy(src,dst,ss.at[to-1,k],rs.at[to-1,k],device_id=(jnp.bitwise_xor(h,to),d),device_id_type=MESH)
    K=lambda n,p,kind: (n*parts+p)*3+kind
    fw={}; dr={}; cm={}
    for n in range(count):
        x=ins[n]
        for p in range(parts):
            for side,to,nb in ((0,1,h1),(1,2,h2)):
                r=pl.ds(side*half+p*R,R); q=pl.ds(p*R,R)
                fw[n,p,side]=copy(x.at[r,col(h3)],fb.at[n,side,q],to,K(n,p,0)); fw[n,p,side].start()
            for side,to,nb in ((0,1,h1),(1,2,h2)):
                r=pl.ds(side*half+p*R,R); q=pl.ds(p*R,R)
                dr[n,p,side]=copy(x.at[r,col(nb)],db.at[n,side,q],to,K(n,p,1)); dr[n,p,side].start()
    for n in range(count):
        x=ins[n]
        for p in range(parts):
            for side,to,nb in ((0,2,h2),(1,1,h1)):
                r=pl.ds(side*half+p*R,R); q=pl.ds(p*R,R)
                fw[n,p,side].wait_recv()
                sb[n,side,q]=(fb[n,side,q].astype(f32)+x[r,col(nb)].astype(f32)).astype(bf16)
                cm[n,p,side]=copy(sb.at[n,side,q],cb.at[n,side,q],to,K(n,p,2)); cm[n,p,side].start()
    for n in range(count):
        x,o=ins[n],outs[n]
        for p in range(parts):
            for side in (0,1):
                r=pl.ds(side*half+p*R,R); q=pl.ds(p*R,R)
                dr[n,p,side].wait_recv()
                cm[n,p,side].wait_recv()
                o[r]=x[r,col(h)].astype(f32)+db[n,side,q].astype(f32)+cb[n,side,q].astype(f32)
    for g in (fw,dr,cm):
        for c in g.values(): c.wait_send()

def scatter_columns(arrays,parts,cid):
    n=len(arrays); T=arrays[0].shape[0]; Wd=arrays[0].shape[1]//4
    buf=pltpu.VMEM((n,2,T//2,Wd),bf16)
    return pl.pallas_call(functools.partial(rs_kernel,count=n,parts=parts),
        in_specs=[VM()]*n,out_specs=[VM()]*n,
        out_shape=[jax.ShapeDtypeStruct((T,Wd),f32) for a in arrays],
        scratch_shapes=[buf]*4+[DMA((2,3*parts*n)),DMA((2,3*parts*n))],
        compiler_params=pltpu.CompilerParams(collective_id=cid,has_side_effects=True,vmem_limit_bytes=60<<20),name="scatter_columns")(*arrays)

def scan_kernel(own,out,oth,rb,lb,rst,lst,xs,xr,fs,fr,ss,rs,*,chunk,skew):
    h=lax.axis_index("head"); d=lax.axis_index("dp"); n=lax.axis_size("dp")//2
    z=d//2; core=lax.rem(d,2)
    mate=(h,jnp.bitwise_xor(d,1)); right=(h,d+2); left=(h,d-2)
    rows=own.shape[0]; Wd=own.shape[1]//2; nc=rows//chunk
    b=pltpu.get_barrier_semaphore()
    pl.semaphore_signal(b,inc=1,device_id=mate,device_id_type=MESH)
    @pl.when(z>0)
    def _(): pl.semaphore_signal(b,inc=1,device_id=left,device_id_type=MESH)
    @pl.when(z<n-1)
    def _(): pl.semaphore_signal(b,inc=1,device_id=right,device_id_type=MESH)
    pl.semaphore_wait(b,1+(z>0).astype(jnp.int32)+(z<n-1).astype(jnp.int32))
    mine=pl.ds(pl.multiple_of(core*Wd,Wd),Wd); other=pl.ds(pl.multiple_of((1-core)*Wd,Wd),Wd)
    def at(c): return pl.ds(pl.multiple_of(c*chunk,chunk),chunk)
    def remote(src,dst,s,r,dev): return pltpu.make_async_remote_copy(src,dst,s,r,device_id=dev,device_id_type=MESH)
    def swap(c): return remote(own.at[at(c),other],oth.at[at(c)],xs.at[c],xr.at[c],mate)
    def give(c): return remote(out.at[at(c),mine],out.at[at(c),mine],fs.at[c],fr.at[c],mate)
    def goR(c): return remote(rst.at[at(c)],rb.at[at(c)],ss.at[0,c],rs.at[0,c],right)
    def goL(c): return remote(lst.at[at(c)],lb.at[at(c)],ss.at[1,c],rs.at[1,c],left)
    def issue(c,carry):
        swap(c).start(); return carry
    lax.fori_loop(0,nc,issue,0)
    last=skew*jnp.maximum(z,n-1-z)
    def step(t,carry):
        @pl.when(t<nc)
        def _():
            swap(t).wait_recv()
            oth[at(t)]=(oth[at(t)].astype(f32)+own[at(t),mine].astype(f32)).astype(bf16)
        c=t-skew*z
        @pl.when((c>=0)&(c<nc))
        def _():
            @pl.when(z>0)
            def _(): goR(c).wait_recv()
            @pl.when(z<n-1)
            def _():
                @pl.when(z==0)
                def _(): rst[at(c)]=oth[at(c)]
                @pl.when(z>0)
                def _(): rst[at(c)]=(oth[at(c)].astype(f32)+rb[at(c)].astype(f32)).astype(bf16)
                goR(c).start()
        e=t-skew*(n-1-z)
        @pl.when((e>=0)&(e<nc))
        def _():
            @pl.when(z<n-1)
            def _(): goL(e).wait_recv()
            @pl.when(z>0)
            def _():
                @pl.when(z==n-1)
                def _(): lst[at(e)]=oth[at(e)]
                @pl.when(z<n-1)
                def _(): lst[at(e)]=(oth[at(e)].astype(f32)+lb[at(e)].astype(f32)).astype(bf16)
                goL(e).start()
        g=t-last
        @pl.when((g>=0)&(g<nc))
        def _():
            @pl.when(z==0)
            def _(): out[at(g),mine]=(oth[at(g)].astype(f32)+lb[at(g)].astype(f32)).astype(bf16)
            @pl.when(z==n-1)
            def _(): out[at(g),mine]=(oth[at(g)].astype(f32)+rb[at(g)].astype(f32)).astype(bf16)
            @pl.when((z>0)&(z<n-1))
            def _(): out[at(g),mine]=(oth[at(g)].astype(f32)+rb[at(g)].astype(f32)+lb[at(g)].astype(f32)).astype(bf16)
            give(g).start()
        return carry
    lax.fori_loop(0,nc+skew*(n-1),step,0)
    def drain(c,carry):
        give(c).wait()
        swap(c).wait_send()
        @pl.when(z<n-1)
        def _(): goR(c).wait_send()
        @pl.when(z>0)
        def _(): goL(c).wait_send()
        return carry
    lax.fori_loop(0,nc,drain,0)

def sum_rows(own,chunk,cid,skew=2):
    rows,wd=own.shape; nc=rows//chunk
    buf=pltpu.VMEM((rows,wd//2),bf16)
    return pl.pallas_call(functools.partial(scan_kernel,chunk=chunk,skew=skew),
        in_specs=[VM()],out_specs=VM(),out_shape=jax.ShapeDtypeStruct((rows,wd),bf16),
        scratch_shapes=[buf]*5+[DMA((nc,))]*4+[DMA((2,nc))]*2,
        compiler_params=pltpu.CompilerParams(collective_id=cid,has_side_effects=True,vmem_limit_bytes=60<<20),name="sum_rows")(own)


class Spread:
    def __init__(self, src, dst, first, second, ss, rs, base):
        self.h, self.d = lax.axis_index("head"), lax.axis_index("dp")
        self.src, self.dst, self.first, self.second = src, dst, first, second
        self.ss, self.rs, self.base, self.n = ss, rs, base, len(first)

    def copy(self, src, dst, to, k):
        return pltpu.make_async_remote_copy(
            src, dst, self.ss.at[to - 1, self.base + k], self.rs.at[to - 1, self.base + k],
            device_id=(jnp.bitwise_xor(self.h, to), self.d), device_id_type=MESH,
        )

    def direct(self, to, i):
        rows = (self.first + self.second)[i]
        return self.copy(self.src(rows), self.dst(rows, self.h), to, i)

    def passed(self, to, i):
        rows = (self.second if to == 1 else self.first)[i]
        ref = self.dst(rows, jnp.bitwise_xor(self.h, 3 - to))
        return self.copy(ref, ref, to, 2 * self.n + i)

    def start(self):
        n = self.n
        for i in range(2 * n):
            self.direct(1, i).start()
            self.direct(2, (i + n) % (2 * n)).start()

    def forward(self, i):
        self.direct(1, i).wait_recv()
        self.passed(2, i).start()
        self.direct(2, self.n + i).wait_recv()
        self.passed(1, i).start()

    def arrived(self):
        for i in range(self.n):
            self.direct(1, self.n + i).wait_recv()
            self.direct(2, i).wait_recv()
            self.passed(1, i).wait_recv()
            self.passed(2, i).wait_recv()

    def sent(self):
        for to in (1, 2):
            for i in range(2 * self.n):
                self.direct(to, i).wait_send()
            for i in range(self.n):
                self.passed(to, i).wait_send()


def fwd_conv(x_ref, lg_ref, taps_ref, q_s, k_s, p_s, g_s, r_s, t_s, l_w, heads, chunks):
    i, j = masks()
    low = j <= i
    slow = j < i
    xr = jnp.bitwise_xor(i, j)
    zero8 = jnp.zeros((8, DK), f32)
    for c in range(chunks):
        for h in range(heads):
            rows = slice(c * C, (c + 1) * C)
            pre = {}
            for n, off in (("q", 0), ("k", heads * DK), ("v", 2 * heads * DK)):
                cols = slice(off + h * DK, off + (h + 1) * DK)
                x = x_ref[rows, cols]
                prev = zero8 if c == 0 else x_ref[c * C - 8 : c * C, cols]
                conv, sg = conv_silu(x, prev, taps_ref[:, cols])
                pre[n] = conv * sg
            q, k = pre["q"], pre["k"]
            q = q * (lax.rsqrt(jnp.sum(q * q, -1, keepdims=True) + norm_eps) * DK**-0.5)
            k = k * lax.rsqrt(jnp.sum(k * k, -1, keepdims=True) + norm_eps)
            qb, kb = q.astype(bf16), k.astype(bf16)
            beta = jax.nn.sigmoid(lg_ref[rows, h : h + 1])
            sc = dot_t(jnp.concatenate([qb, kb], 0), kb)
            G = sc[C:]
            Lw = jnp.where(slow, G * beta, 0.0).astype(bf16)
            q_s[h, rows] = qb
            k_s[h, rows] = kb
            p_s[h, rows] = jnp.where(low, sc[0:C], 0.0).astype(bf16)
            g_s[h, rows] = G.astype(bf16)
            r_s[h, rows] = pre["v"].astype(bf16)
            l_w[h, rows] = Lw
            t_s[h, rows] = jnp.where(xr == 0, 1.0, jnp.where(xr == 1, -Lw.astype(f32), 0.0)).astype(bf16)


def fwd_inverse(t_s, l_w, heads, chunks):
    i, j = masks()
    xr = jnp.bitwise_xor(i, j)
    every = [(c, h) for c in range(chunks) for h in range(heads)]
    s = 2
    while s < C:
        part = (xr >= s) & (xr < 2 * s)
        half = [
            dot(t_s[h, c * C : (c + 1) * C], jnp.where(part, l_w[h, c * C : (c + 1) * C], jnp.zeros((C, C), bf16))).astype(bf16)
            for c, h in every
        ]
        for (c, h), y in zip(every, half):
            rows = slice(c * C, (c + 1) * C)
            X = t_s[h, rows]
            t_s[h, rows] = X - dot(y, X).astype(bf16)
        s *= 2


def fwd_states(lg_ref, gain_ref, a_ref, q_s, k_s, u_s, t_s, p_s, r_s, s_s, o_s, heads, chunks):
    S = [jnp.zeros((DK, DK), f32) for _ in range(heads)]
    for c in range(chunks):
        rows = slice(c * C, (c + 1) * C)
        Sb = [S[h].astype(bf16) for h in range(heads)]
        m = [dot(jnp.concatenate([k_s[h, rows], q_s[h, rows]], 0), Sb[h]) for h in range(heads)]
        R = [r_s[h, rows].astype(f32) - m[h][0:C] for h in range(heads)]
        beta = [jax.nn.sigmoid(lg_ref[rows, h : h + 1]) for h in range(heads)]
        ub = [dot(t_s[h, rows], (R[h] * beta[h]).astype(bf16)).astype(bf16) for h in range(heads)]
        S = [S[h] + tdot(k_s[h, rows], ub[h]) for h in range(heads)]
        for h in range(heads):
            s_s[h, rows] = Sb[h]
            r_s[h, rows] = R[h].astype(bf16)
            u_s[h, rows] = ub[h]
            o = m[h][C:] + dot(p_s[h, rows], ub[h])
            o_s[h, rows] = o
            a = o * lax.rsqrt(jnp.mean(o * o, -1, keepdims=True) + norm_eps) * gain_ref[0:1, h * DK : (h + 1) * DK]
            a_ref[rows, h * DK : (h + 1) * DK] = a.astype(bf16)


CH = 128
SKEW = 2


def front_kernel(
    order, gain, lengths, slots, x, cot,
    w, xf, cf, af, of, qkv_o, lg_o, q_o, k_o, u_o, t_o, p_o, g_o, r_o, s_o, o_o,
    own, oth, rb, lb, wv, xv, qv, lv, tp, av, q_s, k_s, u_s, t_s, p_s, g_s, r_s, s_s, o_s, l_w, cv, go, slots_v, table,
    xs, xr_, gl, fs, fr, ss, rs, as_, ar_, ls, sv,
    *, seqs, heads, lead, at_out, at_gate, hl, small, capacity,
):
    h = lax.axis_index("head")
    d = lax.axis_index("dp")
    n = lax.axis_size("dp") // 2
    z = d // 2
    core = lax.rem(d, 2)
    mate = (h, jnp.bitwise_xor(d, 1))
    h1, h2 = jnp.bitwise_xor(h, 1), jnp.bitwise_xor(h, 2)
    T, Wd = x.shape
    L = T // seqs
    rows_all, width = own.shape
    half = width // 2
    nc = rows_all // CH
    early = wv.shape[0] // CH
    chunks = L // C

    load_t = pltpu.make_async_copy(slots, slots_v.at[pl.ds(0, capacity)], ls.at[6])
    load_t.start()
    b = pltpu.get_barrier_semaphore()
    for p in (mate, (h1, d), (h2, d)):
        pl.semaphore_signal(b, inc=1, device_id=p, device_id_type=MESH)
    @pl.when(z > 0)
    def _():
        pl.semaphore_signal(b, inc=1, device_id=(h, d - 2), device_id_type=MESH)
    @pl.when(z < n - 1)
    def _():
        pl.semaphore_signal(b, inc=1, device_id=(h, d + 2), device_id_type=MESH)
    pl.semaphore_wait(b, 3 + (z > 0).astype(jnp.int32) + (z < n - 1).astype(jnp.int32))

    def col(i, size=Wd):
        return pl.ds(pl.multiple_of(i * size, size), size)

    def at(c):
        return pl.ds(pl.multiple_of(c * CH, CH), CH)

    parts = 3
    R = T // (2 * parts)
    A = [pl.ds(i * R, R) for i in range(parts)]
    B = [pl.ds((i + parts) * R, R) for i in range(parts)]
    spread_x = Spread(lambda r: x.at[r], lambda r, i: xv.at[r, col(i)], A, B, as_, ar_, 0)
    spread_c = Spread(lambda r: cv.at[r], lambda r, i: cf.at[r, col(i)], A, B, as_, ar_, 9)
    spread_a = [
        Spread(
            lambda r: av.at[r], lambda r, i: af.at[r, col(i)],
            [pl.ds(s * L, L // 2)], [pl.ds(s * L + L // 2, L // 2)], as_, ar_, 18 + 3 * s,
        )
        for s in range(seqs)
    ]
    hw = at_gate - at_out
    spread_o = Spread(
        lambda r: w.at[pl.ds(at_out + r[0], r[1])],
        lambda r, i: of.at[pl.ds(pl.multiple_of(i * hw, hw) + r[0], r[1])],
        [(0, hw // 2)], [(hw // 2, hw // 2)], as_, ar_, 18 + 3 * seqs,
    )
    spread_x.start()
    own_x = pltpu.make_async_copy(x, xv.at[:, col(h)], ls.at[0])
    own_x.start()
    load_c = pltpu.make_async_copy(cot, cv, ls.at[5])
    load_c.start()

    mine, other = col(core, half), col(1 - core, half)

    def remote(src, dst, s, r, dev):
        return pltpu.make_async_remote_copy(src, dst, s, r, device_id=dev, device_id_type=MESH)

    def swap(c):
        return remote(own.at[at(c), other], oth.at[at(c)], xs.at[c], xr_.at[c], mate)

    def to_right(c):
        return remote(rb.at[at(c)], rb.at[at(c)], ss.at[0, c], rs.at[0, c], (h, d + 2))

    def to_left(c):
        return remote(lb.at[at(c)], lb.at[at(c)], ss.at[1, c], rs.at[1, c], (h, d - 2))

    def give(c, dst):
        return remote(oth.at[at(c)], dst.at[at(c), mine], fs.at[c], fr.at[c], mate)

    def keep(c, dst):
        return pltpu.make_async_copy(oth.at[at(c)], dst.at[at(c), mine], gl.at[c])

    def pick(c):
        place = lax.broadcasted_iota(jnp.int32, (table.shape[0], CH), 0) + base
        hot = jnp.where(order[pl.ds(c, 1)] == place, 1.0, 0.0).astype(bf16)
        own[at(c)] = tdot(hot, table[...]).astype(bf16)
        swap(c).start()

    base = d * capacity
    spare = slots_v.shape[0] - capacity
    if spare:
        slots_v[pl.ds(capacity, spare)] = jnp.zeros((spare, 8, width // 8), f32)
    load_t.wait()
    for j in range(8):
        table[:, j * (width // 8) : (j + 1) * (width // 8)] = slots_v[:, j, :].astype(bf16)
    pick(0)
    pick(1)
    last = SKEW * jnp.maximum(z, n - 1 - z)

    def step(t, carry):
        @pl.when(t + 2 < nc)
        def _():
            pick(t + 2)

        @pl.when(t < nc)
        def _():
            swap(t).wait_recv()
            oth[at(t)] = oth[at(t)] + own[at(t), mine]

        c = t - SKEW * z
        @pl.when((c >= 0) & (c < nc))
        def _():
            @pl.when(z > 0)
            def _():
                to_right(c).wait_recv()
                rb[at(c)] = rb[at(c)] + oth[at(c)]
            @pl.when(z == 0)
            def _():
                rb[at(c)] = oth[at(c)]
            @pl.when(z < n - 1)
            def _():
                to_right(c).start()

        e = t - SKEW * (n - 1 - z)
        @pl.when((e >= 0) & (e < nc))
        def _():
            @pl.when(z < n - 1)
            def _():
                to_left(e).wait_recv()
                lb[at(e)] = lb[at(e)] + oth[at(e)]
            @pl.when(z == n - 1)
            def _():
                lb[at(e)] = oth[at(e)]
            @pl.when(z > 0)
            def _():
                to_left(e).start()

        g = t - last
        @pl.when((g >= 0) & (g < nc))
        def _():
            oth[at(g)] = rb[at(g)] + lb[at(g)] - oth[at(g)]
            @pl.when(g < early)
            def _():
                give(g, wv).start()
                keep(g, wv).start()
            @pl.when(g >= early)
            def _():
                give(g, w).start()
                keep(g, w).start()
        return carry

    def steps(lo, hi):
        lax.fori_loop(lo, hi, step, 0)

    steps(0, 1)
    load_c.wait()
    place = lax.broadcasted_iota(jnp.int32, (L, Wd), 0)
    for s in range(seqs):
        r = pl.ds(s * L, L)
        cv[r] = jnp.where(place < lengths[s], cv[r], jnp.zeros((L, Wd), bf16))
    steps(1, 2)
    for i in range(parts):
        spread_x.forward(i)
        steps(2 + i, 3 + i)
    spread_c.start()
    own_c = pltpu.make_async_copy(cv, cf.at[:, col(h)], ls.at[1])
    own_c.start()
    t = early + SKEW * (n - 1)
    steps(2 + parts, t)
    for c in range(early):
        keep(c, wv).wait()
        give(c, wv).wait_recv()
    save_w = pltpu.make_async_copy(wv, w.at[pl.ds(0, early * CH)], ls.at[2])
    save_w.start()
    spread_x.arrived()
    own_x.wait()
    save_x = pltpu.make_async_copy(xv, xf, ls.at[3])
    save_x.start()

    taps3 = wv[0:16].astype(f32)
    flat = [taps3[hl + i : hl + i + 1] for i in range(small - hl)]
    line = 3 * heads * DK
    joined = jnp.concatenate(flat, 1)
    for j in range(KCONV):
        tp[j : j + 1] = joined[:, j * line : (j + 1) * line]

    go[0:1] = gain[2:3, col(h)]
    saves = []
    for s in range(seqs):
        rows = pl.ds(s * L, L)
        for i in range(2):
            r = pl.ds(s * L + i * (L // 2), L // 2)
            xx = xv[r].astype(f32)
            n1 = (xx * lax.rsqrt(jnp.mean(xx * xx, -1, keepdims=True) + norm_eps) * gain[0:1]).astype(bf16)
            lv[r] = dot_t(n1, wv[0:lead])
            qv[r] = dot_t(n1, wv[lead:at_out])
        if s == 0:
            spread_c.forward(0)
        steps(t, t + 1)
        sub = lambda ref: ref.at[:, rows]
        fwd_conv(qv.at[rows], lv.at[rows], tp, sub(q_s), sub(k_s), sub(p_s), sub(g_s), sub(r_s), sub(t_s), l_w, heads, chunks)
        if s == 0:
            spread_c.forward(1)
        else:
            spread_a[s - 1].forward(0)
        steps(t + 1, t + 2)
        fwd_inverse(sub(t_s), l_w, heads, chunks)
        if s == 0:
            spread_c.forward(2)
        steps(t + 2, t + 3)
        fwd_states(lv.at[rows], go, av.at[rows], sub(q_s), sub(k_s), sub(u_s), sub(t_s), sub(p_s), sub(r_s), sub(s_s), sub(o_s), heads, chunks)
        spread_a[s].start()
        saves.append(pltpu.make_async_copy(av.at[rows], af.at[rows, col(h)], sv.at[s, 0]))
        pairs = [(qv.at[rows], qkv_o.at[rows]), (lv.at[rows], lg_o.at[rows])]
        for src, dst in ((q_s, q_o), (k_s, k_o), (u_s, u_o), (t_s, t_o), (p_s, p_o), (g_s, g_o), (r_s, r_o), (s_s, s_o), (o_s, o_o)):
            pairs.append((src.at[:, rows], dst.at[:, rows]))
        for k, (src, dst) in enumerate(pairs):
            saves.append(pltpu.make_async_copy(src, dst, sv.at[s, 1 + k]))
        for cp in saves[-12:]:
            cp.start()
        steps(t + 3, t + 4)
        t += 4
        if s == 1:
            save_w.wait()
            for c in range(early, -(-at_gate // CH)):
                keep(c, w).wait()
                give(c, w).wait_recv()
            spread_o.start()
            own_o = pltpu.make_async_copy(w.at[pl.ds(at_out, hw)], of.at[col(h, hw)], ls.at[4])
            own_o.start()
    steps(t, t + 2)
    spread_a[seqs - 1].forward(0)
    spread_o.forward(0)
    steps(t + 2, nc + SKEW * (n - 1))

    own_c.wait()
    own_o.wait()
    save_x.wait()
    for cp in saves:
        cp.wait()
    for sp in [spread_c, *spread_a, spread_o]:
        sp.arrived()
    for sp in [spread_x, spread_c, *spread_a, spread_o]:
        sp.sent()

    def drain(c, carry):
        swap(c).wait_send()
        @pl.when(c < early)
        def _():
            give(c, wv).wait_send()
        @pl.when(c >= early)
        def _():
            give(c, w).wait_send()
        @pl.when(c >= -(-at_gate // CH))
        def _():
            keep(c, w).wait()
            give(c, w).wait_recv()
        @pl.when(z < n - 1)
        def _():
            to_right(c).wait_send()
        @pl.when(z > 0)
        def _():
            to_left(c).wait_send()
        return carry

    lax.fori_loop(0, nc, drain, 0)


def front(slots, order, gain, lengths, x, cot, seqs, heads, lead, at_out, at_gate, hl, small, capacity, cid):
    T, Wd = x.shape
    rows = order.shape[0] * order.shape[1]
    width = slots.shape[1] * slots.shape[2]
    padded = -(-capacity // 128) * 128
    half = width // 2
    nc = rows // CH
    early = -(-at_out // CH)
    L = T // seqs
    hbm = pl.BlockSpec(memory_space=pl.ANY)
    S = jax.ShapeDtypeStruct
    sav = [S((heads, T, DK), bf16)] * 8 + [S((heads, T, DK), f32)]
    outs = [
        S((rows, width), bf16), S((T, width), bf16), S((T, width), bf16), S((T, width), bf16),
        S((4 * (at_gate - at_out), width), bf16), S((T, at_out - lead), f32), S((T, lead), f32), *sav,
    ]
    V = pltpu.VMEM
    piece = V((rows, half), bf16)
    return pl.pallas_call(
        functools.partial(
            front_kernel, seqs=seqs, heads=heads, lead=lead, at_out=at_out, at_gate=at_gate, hl=hl, small=small, capacity=capacity
        ),
        in_specs=[VM()] * 2 + [pl.BlockSpec(memory_space=pltpu.SMEM)] + [hbm] * 3,
        out_specs=[hbm] * len(outs),
        out_shape=outs,
        scratch_shapes=[
            V((rows, width), bf16), piece, piece, piece, V((early * CH, width), bf16), V((T, width), bf16),
            V((T, at_out - lead), f32), V((T, lead), f32), V((8, at_out - lead), f32), V((T, heads * DK), bf16),
            *[V((heads, T, DK), bf16)] * 8, V((heads, T, DK), f32), V((heads, L, DK), bf16), V((T, Wd), bf16), V((8, Wd), f32),
            V((padded, 8, width // 8), f32), V((padded, width), bf16),
            DMA((nc,)), DMA((nc,)), DMA((nc,)), DMA((nc,)), DMA((nc,)), DMA((2, nc)), DMA((2, nc)),
            DMA((2, 21 + 3 * seqs)), DMA((2, 21 + 3 * seqs)), DMA((7,)), DMA((seqs, 12)),
        ],
        compiler_params=pltpu.CompilerParams(collective_id=cid, has_side_effects=True, vmem_limit_bytes=60 << 20),
        name="front",
    )(order, gain, lengths, slots, x, cot)


def bwd_blocks(da_ref, gain_ref, o_s, q_s, k_s, u_s, p_s, s_s, dg_ref, do_w, w_w, dq_w, dk_w, qd_w, heads, chunks):
    i, j = masks()
    low = j <= i
    for c in range(chunks):
        for h in range(heads):
            rows = slice(c * C, (c + 1) * C)
            hc = slice(h * DK, (h + 1) * DK)
            o = o_s[h, rows]
            ro = lax.rsqrt(jnp.mean(o * o, -1, keepdims=True) + norm_eps)
            da = da_ref[rows, hc]
            on = o * ro
            dg_ref[0:1, hc] += jnp.sum(da * on, 0, keepdims=True)
            t = da * gain_ref[0:1, hc]
            do = (ro * (t - on * jnp.mean(t * on, -1, keepdims=True))).astype(bf16)
            qb, kb = q_s[h, rows], k_s[h, rows]
            dP = jnp.where(low, dot_t(do, u_s[h, rows]), 0.0).astype(bf16)
            do_w[h, rows] = do
            w_w[h, rows] = tdot(p_s[h, rows], do)
            dq_w[h, rows] = dot_t(do, s_s[h, rows]) + dot(dP, kb)
            dk_w[h, rows] = tdot(dP, qb)
            qd_w[h, rows] = tdot(qb, do)


def bwd_states(lg_ref, k_s, t_s, w_w, qd_w, ds_w, heads, chunks):
    dS = [jnp.zeros((DK, DK), f32) for _ in range(heads)]
    for c in reversed(range(chunks)):
        rows = slice(c * C, (c + 1) * C)
        kb = [k_s[h, rows] for h in range(heads)]
        dSb = [dS[h].astype(bf16) for h in range(heads)]
        du = [(w_w[h, rows] + dot(kb[h], dSb[h])).astype(bf16) for h in range(heads)]
        e = [tdot(t_s[h, rows], du[h]) for h in range(heads)]
        beta = [jax.nn.sigmoid(lg_ref[rows, h : h + 1]) for h in range(heads)]
        dS = [dS[h] + qd_w[h, rows] - tdot(kb[h], (beta[h] * e[h]).astype(bf16)) for h in range(heads)]
        for h in range(heads):
            w_w[h, rows] = e[h]
            ds_w[h, rows] = dSb[h]


def bwd_conv(x_ref, lg_ref, taps_ref, q_s, k_s, u_s, g_s, r_s, s_s, w_w, dq_w, dk_w, ds_w, dc, dx_ref, dlg_ref, dt_ref, heads, chunks):
    i, j = masks()
    slow = j < i
    zero8 = jnp.zeros((8, DK), f32)
    W = heads * DK
    lane = lax.broadcasted_iota(jnp.int32, (C, dlg_ref.shape[1]), 1)
    row8 = lax.broadcasted_iota(jnp.int32, (8, DK), 0)
    dc[chunks * C : chunks * C + 8] = jnp.zeros((8, 3 * W), f32)
    for c in reversed(range(chunks)):
        rows = slice(c * C, (c + 1) * C)
        dlg = jnp.zeros(lane.shape, f32)
        for h in range(heads):
            e = w_w[h, rows]
            eb = e.astype(bf16)
            beta = jax.nn.sigmoid(lg_ref[rows, h : h + 1])
            be = beta * e
            ub, kb = u_s[h, rows], k_s[h, rows]
            dL = jnp.where(slow, -dot_t(eb, ub), 0.0)
            dGb = (beta * dL).astype(bf16)
            dk = (
                dk_w[h, rows] + dot_t(ub, ds_w[h, rows]) - dot_t(be.astype(bf16), s_s[h, rows])
                + dot(dGb, kb) + tdot(dGb, kb)
            )
            db = jnp.sum(e * r_s[h, rows].astype(f32) + dL * g_s[h, rows].astype(f32), -1, keepdims=True)
            dlg = jnp.where(lane == h, db * beta * (1.0 - beta), dlg)
            for n, off in (("q", 0), ("k", W), ("v", 2 * W)):
                cols = slice(off + h * DK, off + (h + 1) * DK)
                tp = taps_ref[:, cols]
                x = x_ref[rows, cols]
                prev = zero8 if c == 0 else x_ref[c * C - 8 : c * C, cols]
                moved = [shifted(x, prev, 3 - jj) for jj in range(4)]
                conv = tp[3:4] * moved[3]
                for jj in range(3):
                    conv = conv + tp[jj : jj + 1] * moved[jj]
                sg = jax.nn.sigmoid(conv)
                act = conv * sg
                if n == "v":
                    dd = be
                else:
                    r = lax.rsqrt(jnp.sum(act * act, -1, keepdims=True) + norm_eps)
                    g = dq_w[h, rows] * DK**-0.5 if n == "q" else dk
                    an = act * r
                    dd = r * (g - an * jnp.sum(g * an, -1, keepdims=True))
                dconv = dd * (sg + act * (1.0 - sg))
                dc[rows, cols] = dconv
                for jj in range(4):
                    dt_ref[jj : jj + 1, cols] += jnp.sum(dconv * moved[jj], 0, keepdims=True)
                nxt = dc[(c + 1) * C : (c + 1) * C + 8, cols]
                dx = tp[3:4] * dconv
                for jj in range(1, 4):
                    r = pltpu.roll(dconv, C - jj, 0)
                    bot = jnp.where(row8 >= 8 - jj, pltpu.roll(nxt, 8 - jj, 0), r[C - 8 :])
                    dx = dx + tp[3 - jj : 4 - jj] * jnp.concatenate([r[: C - 8], bot], 0)
                dx_ref[rows, cols] = dx.astype(bf16)
        dlg_ref[rows] = dlg.astype(bf16)


class Scatter:
    def __init__(self, part, beside, rows, bufs, slot, ss, rs, base):
        self.h, self.d = lax.axis_index("head"), lax.axis_index("dp")
        self.part, self.beside, self.slot = part, beside, slot
        self.fb, self.db, self.cb = bufs
        self.half = rows.size // 2
        self.rows = [pl.ds(rows.start + i * self.half, self.half) for i in range(2)]
        self.ss, self.rs, self.base = ss, rs, base

    def col(self, k):
        w = self.part.shape[1] // 4
        return pl.ds(pl.multiple_of(jnp.bitwise_xor(self.h, k) * w, w), w)

    def copy(self, src, dst, to, k):
        return pltpu.make_async_remote_copy(
            src, dst, self.ss.at[to - 1, self.base + k], self.rs.at[to - 1, self.base + k],
            device_id=(jnp.bitwise_xor(self.h, to), self.d), device_id_type=MESH,
        )

    def far(self, side):
        return self.copy(self.part.at[self.rows[side], self.col(3)], self.fb.at[self.slot, side], side + 1, 0)

    def near(self, side):
        return self.copy(self.part.at[self.rows[side], self.col(side + 1)], self.db.at[self.slot, side], side + 1, 1)

    def both(self, side):
        return self.copy(self.fb.at[self.slot, side], self.cb.at[self.slot, side], 2 - side, 2)

    def one(self):
        for side in (0, 1):
            self.far(side).start()
        for side in (0, 1):
            self.near(side).start()

    def two(self):
        for side in (0, 1):
            self.far(side).wait_recv()
            got = self.fb[self.slot, side].astype(f32) + self.beside(side).astype(f32)
            self.fb[self.slot, side] = got.astype(bf16)
            self.both(side).start()

    def three(self):
        got = []
        for side in (0, 1):
            self.near(side).wait_recv()
            self.both(side).wait_recv()
            got.append(self.db[self.slot, side].astype(f32) + self.cb[self.slot, side].astype(f32))
            self.far(side).wait_send()
            self.near(side).wait_send()
            self.both(side).wait_send()
        return got


RING = 4
SLOTS = 4


def back_kernel(
    gain, stat_in, order, lengths,
    h1_part, mlp_part, da_in, dh_own, mlp_own, h1_own, xf, af, w, g_ffn, qkv, lg, q_i, k_i, u_i, t_i, p_i, g_i, r_i, s_i, o_i,
    y_o, ig_o, stat_o, own_o,
    own, oth, rb, lb, rst, lst, qv, lv, q_s, k_s, u_s, t_s, p_s, g_s, r_s, s_s, o_s,
    do_w, w_w, dq_w, dk_w, qd_w, ds_w, dc, xv, wv, nb, da_f, dh_f, mlp_f, h1_f, xp, fb, db, cb, gq, gs, n1_w, dx_w, dlg_w, dt_w, dg_w, g1_w, st_w, go_w, tp, gout, av, acc,
    xs, xr_, gl, fs, fr, ss, rs, as_, ar_, ls, lds, a2s, a2r, sts, str_, igs, avs,
    *, seqs, heads, lead, n_ffn, hl, small, capacity,
):
    h = lax.axis_index("head")
    d = lax.axis_index("dp")
    n = lax.axis_size("dp") // 2
    z = d // 2
    core = lax.rem(d, 2)
    mate = (h, jnp.bitwise_xor(d, 1))
    T = xf.shape[0]
    L = T // seqs
    rows_all, width = own.shape
    half = width // 2
    Wd = width // 4
    nc = rows_all // CH
    chunks = L // C
    hd = heads * DK
    at_qkv, at_out, at_ffn = lead, lead + 3 * hd, lead + 4 * hd

    bits = []
    k = 2
    while k < 2 * n:
        bits.append(k)
        k *= 2
    b = pltpu.get_barrier_semaphore()
    peers = [mate] + [(jnp.bitwise_xor(h, k), d) for k in (1, 2, 3)] + [(h, jnp.bitwise_xor(d, k)) for k in bits]
    for p in peers:
        pl.semaphore_signal(b, inc=1, device_id=p, device_id_type=MESH)
    @pl.when(z > 0)
    def _():
        pl.semaphore_signal(b, inc=1, device_id=(h, d - 2), device_id_type=MESH)
    @pl.when(z < n - 1)
    def _():
        pl.semaphore_signal(b, inc=1, device_id=(h, d + 2), device_id_type=MESH)
    pl.semaphore_wait(b, len(peers) + (z > 0).astype(jnp.int32) + (z < n - 1).astype(jnp.int32))

    def col(i, size=Wd):
        return pl.ds(pl.multiple_of(i * size, size), size)

    def at(c):
        return pl.ds(pl.multiple_of((nc - 1 - c) * CH, CH), CH)

    seq_rows = [pl.ds(s * L, L) for s in range(seqs)]
    bufs = (fb, db, cb)
    jobs = []
    kinds = []
    for kind, part in enumerate((h1_part, mlp_part, xp)):
        for s in range(EARLY if kind == 0 else 0, seqs):
            kinds.append((kind, s))
            if kind < 2:
                def beside(side, kind=kind, s=s):
                    return nb[kind, s, side]
            else:
                def beside(side, s=s):
                    r = pl.ds(s * L + side * (L // 2), L // 2)
                    return xp[r, col(jnp.bitwise_xor(h, 2 - side))]
            k = len(jobs)
            jobs.append(Scatter(part, beside, seq_rows[s], bufs, k % SLOTS, as_, ar_, 3 * k))
    jobs[0].one()

    def load(src, dst, k):
        cp = pltpu.make_async_copy(src, dst, ls.at[k])
        cp.start()
        return cp

    first = load(g_ffn, own.at[pl.ds(at_ffn, n_ffn)], 0)
    nbs = []
    for kind, part in enumerate((h1_part, mlp_part)):
        for s in range(EARLY if kind == 0 else 0, seqs):
            for side in (0, 1):
                r = pl.ds(s * L + side * (L // 2), L // 2)
                nbs.append(load(part.at[r, col(jnp.bitwise_xor(h, 2 - side))], nb.at[kind, s, side], 8 + len(nbs)))
    load_da = load(da_in, da_f, 1)
    ins = (q_i, k_i, u_i, t_i, p_i, g_i, r_i, s_i, o_i)
    scr = (q_s, k_s, u_s, t_s, p_s, g_s, r_s, s_s, o_s)

    def fetch(s):
        sl = s % 2
        cps = [pltpu.make_async_copy(qkv.at[seq_rows[s]], qv.at[sl], lds.at[sl, 9]),
               pltpu.make_async_copy(lg.at[seq_rows[s]], lv.at[sl], lds.at[sl, 10])]
        for k, (i, o) in enumerate(zip(ins, scr)):
            cps.append(pltpu.make_async_copy(i.at[:, seq_rows[s]], o.at[sl], lds.at[sl, k]))
        return cps

    for cp in fetch(0):
        cp.start()
    load_w = load(w.at[pl.ds(0, lead + 3 * hd)], wv, 2)
    load_x = load(xf, xv, 3)
    load_dh = load(dh_own, dh_f, 4)
    load_m = load(mlp_own, mlp_f, 5)
    load_h = load(h1_own, h1_f, 6)

    mine, other = col(core, half), col(1 - core, half)

    def remote(src, dst, s, r, dev):
        return pltpu.make_async_remote_copy(src, dst, s, r, device_id=dev, device_id_type=MESH)

    def ring(c):
        return pl.ds(pl.multiple_of(lax.rem(c, RING) * CH, CH), CH)

    def swap(c):
        return remote(own.at[at(c), other], oth.at[at(c)], xs.at[c], xr_.at[c], mate)

    def to_right(c):
        return remote(rst.at[ring(c)], rb.at[at(c)], ss.at[0, c], rs.at[0, c], (h, d + 2))

    def to_left(c):
        return remote(lst.at[ring(c)], lb.at[at(c)], ss.at[1, c], rs.at[1, c], (h, d - 2))

    padded = acc.shape[0] // 2

    def place(first, count):
        rows = pl.ds(pl.multiple_of(first * CH, CH), count * CH)

        def block(i, carry):
            low = i * padded
            slot = lax.broadcasted_iota(jnp.int32, (padded, CH), 0) + low
            slot = jnp.where(slot < padded, slot + d * capacity, slot - padded + jnp.bitwise_xor(d, 1) * capacity)
            hot = [jnp.where(order[pl.ds(first + k, 1)] == slot, 1.0, 0.0).astype(bf16) for k in range(count)]
            hot = jnp.concatenate(hot, 1) if count > 1 else hot[0]
            here = pl.ds(pl.multiple_of(low, padded), padded)
            acc[here] += dot(hot, oth[rows]).astype(bf16)
            return carry

        lax.fori_loop(0, 2, block, 0)

    def swaps(lo, hi):
        def body(c, carry):
            swap(c).start()
            return carry
        lax.fori_loop(lo, hi, body, 0)

    last = SKEW * jnp.maximum(z, n - 1 - z)

    def step(t, carry):
        @pl.when(t < nc)
        def _():
            swap(t).wait_recv()
            oth[at(t)] = oth[at(t)] + own[at(t), mine]

        c = t - SKEW * z
        @pl.when((c >= 0) & (c < nc))
        def _():
            @pl.when(z > 0)
            def _():
                to_right(c).wait_recv()
            @pl.when(z < n - 1)
            def _():
                @pl.when(c >= RING)
                def _():
                    to_right(c - RING).wait_send()
                @pl.when(z == 0)
                def _():
                    rst[ring(c)] = oth[at(c)]
                @pl.when(z > 0)
                def _():
                    rst[ring(c)] = oth[at(c)] + rb[at(c)]
                to_right(c).start()

        e = t - SKEW * (n - 1 - z)
        @pl.when((e >= 0) & (e < nc))
        def _():
            @pl.when(z < n - 1)
            def _():
                to_left(e).wait_recv()
            @pl.when(z > 0)
            def _():
                @pl.when(e >= RING)
                def _():
                    to_left(e - RING).wait_send()
                @pl.when(z == n - 1)
                def _():
                    lst[ring(e)] = oth[at(e)]
                @pl.when(z < n - 1)
                def _():
                    lst[ring(e)] = oth[at(e)] + lb[at(e)]
                to_left(e).start()

        g = t - last
        @pl.when((g >= 0) & (g < nc))
        def _():
            @pl.when(z == 0)
            def _():
                oth[at(g)] = oth[at(g)] + lb[at(g)]
            @pl.when(z == n - 1)
            def _():
                oth[at(g)] = oth[at(g)] + rb[at(g)]
            @pl.when((z > 0) & (z < n - 1))
            def _():
                oth[at(g)] = (oth[at(g)].astype(f32) + rb[at(g)].astype(f32) + lb[at(g)].astype(f32)).astype(bf16)
            @pl.when(lax.rem(g, 2) == 1)
            def _():
                place(nc - 1 - g, 2)
        return carry

    now = [0]
    end = nc + SKEW * (n - 1)

    def advance(k):
        hi = min(now[0] + k, end)
        if hi > now[0]:
            lax.fori_loop(now[0], hi, step, 0)
        now[0] = hi

    first.wait()
    swaps(0, n_ffn // CH)
    for ref in (dt_w, dg_w, g1_w, gq, gs, acc):
        ref[...] = jnp.zeros_like(ref)
    advance(1)
    for cp in nbs:
        cp.wait()
    jobs[0].two()
    jobs[1].one()
    advance(1)
    load_da.wait()

    def save_ig(s):
        return pltpu.make_async_copy(da_f.at[seq_rows[s]], ig_o.at[seq_rows[s]], igs.at[s])

    def finish(k):
        kind, s = kinds[k]
        got = jobs[k].three()
        for side in (0, 1):
            r = pl.ds(s * L + side * (L // 2), L // 2)
            if kind == 0:
                dh_f[r] += got[side]
            elif kind == 1:
                m = mlp_f[r] + got[side]
                y = h1_f[r] + m
                y_o[r] = y.astype(bf16)
                place = lax.broadcasted_iota(jnp.int32, (L // 2, Wd), 0) + side * (L // 2)
                keep_ = place < lengths[s]
                lane = lax.broadcasted_iota(jnp.int32, (1, width), 1)
                sy = jnp.sum(jnp.sum(jnp.where(keep_, y * y, 0.0), -1, keepdims=True), 0, keepdims=True)
                sm = jnp.sum(jnp.sum(jnp.where(keep_, m * m, 0.0), -1, keepdims=True), 0, keepdims=True)
                st_w[0, 3:4] += jnp.where(lane == 0, sy, jnp.where(lane == 2, sm, 0.0))
            else:
                da_f[r] = dh_f[r] + xp[r, col(h)].astype(f32) + got[side]
                if side == 1:
                    save_ig(s).start()

    turn = [1]
    done = [0]

    def relay():
        k = turn[0]
        if k + 1 < len(jobs) and kinds[k + 1][0] == 2:
            assert kinds[k + 1][1] < done[0]
        if k < len(jobs):
            jobs[k].two()
        if k + 1 < len(jobs):
            jobs[k + 1].one()
        if k - 1 < len(jobs):
            finish(k - 1)
        turn[0] += 1

    st_w[0] = stat_in[...]
    load_w.wait()
    taps3 = wv[0:16].astype(f32)
    joined = jnp.concatenate([taps3[hl + i : hl + i + 1] for i in range(small - hl)], 1)
    for j in range(KCONV):
        tp[j : j + 1] = joined[:, j * 3 * hd : (j + 1) * 3 * hd]
    gout[0:1] = gain[2:3, col(h)]
    ex = []
    turns = [jnp.bitwise_xor(h, k) for k in (1, 2, 3, 0)]

    def heads_of(i):
        return pltpu.make_async_copy(af.at[:, col(turns[i])], av.at[i % 2], avs.at[i % 2])

    for i in (0, 1):
        heads_of(i).start()

    def output_rows():
        if ex or turn[0] < 1 + sum(kind == 0 for kind, _ in kinds):
            return
        for i, p in enumerate(turns):
            heads_of(i).wait()
            go_w[col(p, hd)] = tdot(av[i % 2], dh_f[...].astype(bf16)).astype(bf16)
            if i < 2:
                heads_of(i + 2).start()
            if i < 3:
                cp = remote(go_w.at[col(p, hd)], own.at[pl.ds(at_out, hd), col(h)], a2s.at[i], a2r.at[i], (p, d))
                cp.start()
                ex.append(cp)
        own[pl.ds(at_out, hd), col(h)] = go_w[col(h, hd)]

    for s in range(seqs):
        sl = s % 2
        for cp in fetch(s):
            cp.wait()
        if s + 1 < seqs:
            for cp in fetch(s + 1):
                cp.start()
        if s == 0:
            for cp in (load_x, load_dh, load_m, load_h):
                cp.wait()
        sub = [ref.at[sl] for ref in scr]
        q_, k_, u_, t_, p_, g_, r_, s_, o_ = sub
        x_, l_ = qv.at[sl], lv.at[sl]
        bwd_blocks(da_f.at[seq_rows[s]], gout, o_, q_, k_, u_, p_, s_, dg_w, do_w, w_w, dq_w, dk_w, qd_w, heads, chunks)
        advance(1)
        bwd_states(l_, k_, t_, w_w, qd_w, ds_w, heads, chunks)
        if s > 0:
            relay()
            output_rows()
        advance(1)
        bwd_conv(x_, l_, tp, q_, k_, u_, g_, r_, s_, w_w, dq_w, dk_w, ds_w, dc, dx_w, dlg_w, dt_w, heads, chunks)
        advance(1)
        if s == 0:
            relay()
            output_rows()
        for i in range(2):
            lo = i * (L // 2)
            r = pl.ds(s * L + lo, L // 2)
            here = pl.ds(lo, L // 2)
            xx = xv[r].astype(f32)
            r1 = lax.rsqrt(jnp.mean(xx * xx, -1, keepdims=True) + norm_eps)
            xn = xx * r1
            n1_w[here] = (xn * gain[0:1]).astype(bf16)
            dn = dot(dx_w[here], wv[lead:]) + dot(dlg_w[here], wv[0:lead])
            g1_w[0:1] += jnp.sum(dn * xn, 0, keepdims=True)
            gd = dn * gain[0:1]
            xp[r] = (r1 * (gd - xn * jnp.mean(gd * xn, -1, keepdims=True))).astype(bf16)
            if i == 0:
                advance(1)
        done[0] += 1
        gq[...] += tdot(dx_w[...], n1_w[...])
        gs[...] += tdot(dlg_w[...], n1_w[...])
        if 0 < s < seqs - 1:
            relay()
            output_rows()
        if s + 1 < seqs:
            advance(1)
    line = 3 * hd
    dt = jnp.concatenate([dt_w[j : j + 1] for j in range(KCONV)], 1)
    row = lax.broadcasted_iota(jnp.int32, (lead, width), 0)
    tail = gs[...]
    for i in range(small - hl):
        tail = jnp.where(row == hl + i, dt[:, i * width : (i + 1) * width], tail)
    tail = jnp.where(row < small, tail, 0.0)
    own[pl.ds(0, lead)] = tail.astype(bf16)
    own[pl.ds(at_qkv, 3 * hd)] = gq[...].astype(bf16)
    for cp in ex:
        cp.wait()
    assert now[0] <= n_ffn // CH
    swaps(n_ffn // CH, nc)
    lane = lax.broadcasted_iota(jnp.int32, (1, width), 1)
    three = jnp.concatenate([dg_w[0:1]] * 4, 1)
    st_w[0, 0:1] = g1_w[0:1]
    st_w[0, 2:3] = jnp.where((lane >= h * Wd) & (lane < (h + 1) * Wd), three, 0.0)
    assert ex
    advance(1)
    while turn[0] <= len(jobs) - seqs:
        relay()
        advance(3)
    rounds = [(jnp.bitwise_xor(h, k), d) for k in (1, 2)] + [mate] + [(h, jnp.bitwise_xor(d, k)) for k in bits]
    sent = []
    for i, p in enumerate(rounds):
        cp = remote(st_w.at[i], str_.at[i], sts.at[0, i], sts.at[1, i], p)
        cp.start()
        sent.append(cp)
        if turn[0] <= len(jobs) and i % 2 == 1:
            relay()
        advance(2)
        cp.wait_recv()
        st_w[i + 1] = st_w[i] + str_[i]
    stat_o[...] = st_w[len(rounds)]
    while turn[0] <= len(jobs):
        relay()
        advance(2)
    advance(end)
    if nc % 2:
        place(0, 1)
    give = remote(acc.at[pl.ds(padded, padded)], own_o.at[:, mine], fs.at[0], fr.at[0], mate)
    keep = pltpu.make_async_copy(acc.at[pl.ds(0, padded)], own_o.at[:, mine], gl.at[0])
    give.start()
    keep.start()
    for cp in sent:
        cp.wait_send()

    def drain(c, carry):
        swap(c).wait_send()
        @pl.when(c >= nc - RING)
        def _():
            @pl.when(z < n - 1)
            def _():
                to_right(c).wait_send()
            @pl.when(z > 0)
            def _():
                to_left(c).wait_send()
        return carry

    lax.fori_loop(0, nc, drain, 0)
    give.wait()
    keep.wait()
    for s in range(seqs):
        save_ig(s).wait()


def back(gain, stat_in, order, lengths, h1_part, mlp_part, owns, xf, af, w, g_ffn, qkv, lg, saved, seqs, heads, lead, hl, small, capacity, cid):
    T, width = xf.shape
    Wd = width // 4
    half = width // 2
    L = T // seqs
    hd = heads * DK
    n_ffn = g_ffn.shape[0]
    rows = n_ffn + 4 * hd + lead
    nc = rows // CH
    hbm = pl.BlockSpec(memory_space=pl.ANY)
    S = jax.ShapeDtypeStruct
    V = pltpu.VMEM
    n = lax.axis_size("dp") // 2
    rounds = 2 + 1 + max(n.bit_length() - 1, 0)
    piece, ringbuf = V((rows, half), bf16), V((RING * CH, half), bf16)
    blk = lambda dt: V((2, heads, L, DK), dt)
    wk = lambda dt: V((heads, L, DK), dt)
    rsb = V((SLOTS, 2, L // 2, Wd), bf16)
    njobs = 3 * seqs - EARLY
    padded = -(-capacity // 128) * 128
    return pl.pallas_call(
        functools.partial(back_kernel, seqs=seqs, heads=heads, lead=lead, n_ffn=n_ffn, hl=hl, small=small, capacity=capacity),
        in_specs=[VM(), VM(), VM(), pl.BlockSpec(memory_space=pltpu.SMEM)] + [hbm] * 21,
        out_specs=[VM(), hbm, VM(), hbm],
        out_shape=[S((T, Wd), bf16), S((T, Wd), f32), S((8, width), f32), S((padded, width), bf16)],
        scratch_shapes=[
            V((rows, width), bf16), piece, piece, piece, ringbuf, ringbuf,
            V((2, L, 3 * hd), f32), V((2, L, lead), f32), *[blk(bf16)] * 8, blk(f32),
            wk(bf16), wk(f32), wk(f32), wk(f32), wk(f32), wk(bf16), V((L + 8, 3 * hd), f32),
            V((T, width), bf16), V((lead + 3 * hd, width), bf16), V((2, seqs, 2, L // 2, Wd), bf16),
            V((T, Wd), f32), V((T, Wd), f32), V((T, Wd), f32), V((T, Wd), f32), V((T, width), bf16), rsb, rsb, rsb,
            V((3 * hd, width), f32), V((lead, width), f32), V((L, width), bf16), V((L, 3 * hd), bf16), V((L, lead), bf16),
            V((8, 3 * hd), f32), V((8, hd), f32), V((8, width), f32), V((rounds + 1, 8, width), f32), V((4 * hd, Wd), bf16),
            V((8, 3 * hd), f32), V((8, Wd), f32), V((2, T, Wd), bf16), V((2 * padded, half), bf16),
            DMA((nc,)), DMA((nc,)), DMA((1,)), DMA((1,)), DMA((1,)), DMA((2, nc)), DMA((2, nc)),
            DMA((2, 3 * njobs)), DMA((2, 3 * njobs)), DMA((8 + 4 * seqs,)), DMA((2, 11)), DMA((3,)), DMA((3,)),
            DMA((2, rounds)), V((rounds, 8, width), f32), DMA((seqs,)), DMA((2,)),
        ],
        compiler_params=pltpu.CompilerParams(collective_id=cid, has_side_effects=True, vmem_limit_bytes=63 << 20),
        name="back",
    )(gain, stat_in, order, lengths, h1_part, mlp_part, *owns, xf, af, w, g_ffn, qkv, lg, *saved)


RT = 256
RC = 32
EARLY = 0


def ffn_kernel(
    gain, lengths, af, xf, cf, of, w,
    mlp_o, h1p_o, da_o, dh_o, mo_o, h1_o, g_o, stat_o,
    ov, wgu, wd, wo, a_v, x_v, c_v, n2_s, hid_s, dgu_s, h1_w, t_w, g2_w, gate_w, up_w, dh_w, mlp_s, h1p_s, da_s, fb, db, cb, hb, kb, lb, dav, dhv, mov, h1v, gv,
    lw, lt, sv, as_, ar_, hs, hr_, og,
    *, seqs, at_out, at_gate,
):
    h = lax.axis_index("head")
    d = lax.axis_index("dp")
    T, width = xf.shape
    Wd = width // 4
    L = T // seqs
    ffl, ffp = wd.shape[0], wgu.shape[0] // 2
    n = T // RT
    b = pltpu.get_barrier_semaphore()
    for k in (1, 2):
        pl.semaphore_signal(b, inc=1, device_id=(jnp.bitwise_xor(h, k), d), device_id_type=MESH)
    pl.semaphore_wait(b, 2)

    def col(k):
        return pl.ds(pl.multiple_of(jnp.bitwise_xor(h, k) * Wd, Wd), Wd)

    def rows(i):
        return pl.ds(pl.multiple_of(i * RT, RT), RT)

    def slot(i):
        return lax.rem(i, 2)

    def fetch(i):
        return [
            pltpu.make_async_copy(src.at[rows(i)], dst.at[slot(i)], lt.at[slot(i), k])
            for k, (src, dst) in enumerate(((af, a_v), (xf, x_v)))
        ]

    loads = [pltpu.make_async_copy(of, ov, lw.at[0])]
    dsts = (wgu.at[pl.ds(0, ffl)], wgu.at[pl.ds(ffp, ffl)], wd, wo)
    for k, (lo, dst) in enumerate(zip((at_gate, at_gate + ffl, at_gate + 2 * ffl, at_out), dsts)):
        loads.append(pltpu.make_async_copy(w.at[pl.ds(lo, dst.shape[0])], dst, lw.at[1 + k]))
    loads.append(pltpu.make_async_copy(cf, c_v, lw.at[5]))
    loads[0].start()
    for cp in fetch(0):
        cp.start()
    for cp in loads[1:]:
        cp.start()
    stat_o[...] = jnp.zeros_like(stat_o)
    for lo in (ffl, ffp + ffl):
        wgu[pl.ds(lo, ffp - ffl)] = jnp.zeros((ffp - ffl, width), bf16)
        dgu_s[:, lo : lo + ffp - ffl] = jnp.zeros((T, ffp - ffl), bf16)

    def job(i):
        def beside(side):
            start = pl.multiple_of(i * RT + side * (RT // 2), RT // 2)
            return da_s[pl.ds(start, RT // 2), col(2 - side)]

        return Scatter(da_s, beside, rows(i), (fb, db, cb), lax.rem(i, SLOTS), as_, ar_, 3 * i)

    more = EARLY * L // RT

    def job2(i):
        def beside(side):
            start = pl.multiple_of(i * RT + side * (RT // 2), RT // 2)
            return h1p_s[pl.ds(start, RT // 2), col(2 - side)]

        return Scatter(h1p_s, beside, rows(i), (hb, kb, lb), lax.rem(i, SLOTS), hs, hr_, 3 * i)

    def out(k, i):
        src, dst = ((dav, da_o), (dhv, dh_o), (mov, mo_o), (h1v, h1_o))[k]
        return pltpu.make_async_copy(src.at[rows(i)], dst.at[rows(i)], og.at[k, i])

    def finish(i):
        got = job(i).three()
        for side in (0, 1):
            start = pl.multiple_of(i * RT + side * (RT // 2), RT // 2)
            dav[pl.ds(start, RT // 2)] += got[side]
        out(0, i).start()

    def finish2(i):
        got = job2(i).three()
        for side in (0, 1):
            start = pl.multiple_of(i * RT + side * (RT // 2), RT // 2)
            dhv[pl.ds(start, RT // 2)] += got[side]
        out(1, i).start()

    def saves(i):
        return [
            pltpu.make_async_copy(mlp_s.at[slot(i)], mlp_o.at[rows(i)], sv.at[slot(i), 0]),
            pltpu.make_async_copy(h1p_s.at[rows(i)], h1p_o.at[rows(i)], sv.at[slot(i), 1]),
        ]

    loads[0].wait()

    def tile(i, carry):
        @pl.when(i + 1 < n)
        def _():
            for cp in fetch(i + 1):
                cp.start()

        @pl.when(i >= 2)
        def _():
            for cp in saves(i - 2):
                cp.wait()

        for cp in fetch(i):
            cp.wait()
        r, s = rows(i), slot(i)

        def part_of(k):
            return pl.ds(pl.multiple_of(i * RT + k, RC), RC), slice(k, k + RC)

        t_w[...] = dot(a_v[s], ov[...])
        place = lax.broadcasted_iota(jnp.int32, (RT, Wd), 0) + lax.rem(i * RT, L)
        good = place < lengths[i * RT // L]
        lane = lax.broadcasted_iota(jnp.int32, (1, width), 1)
        attn = t_w[:, col(0)]
        sa = jnp.sum(jnp.sum(jnp.where(good, attn * attn, 0.0), 0, keepdims=True), -1, keepdims=True)
        count = jnp.sum(jnp.sum(jnp.where(good, 1.0, 0.0), 0, keepdims=True), -1, keepdims=True)
        stat_o[3:4] += jnp.where(lane == 1, sa, jnp.where(lane == 3, count, 0.0))
        for k in range(0, RT, RC):
            rk, k_ = part_of(k)
            h1 = x_v[s, k_].astype(f32) + t_w[k_]
            h1_w[k_] = h1
            r2 = lax.rsqrt(jnp.mean(h1 * h1, -1, keepdims=True) + norm_eps)
            n2_s[rk] = (h1 * r2 * gain[1:2]).astype(bf16)
        h1v[r] = h1_w[:, col(0)]
        out(3, i).start()

        @pl.when(i == 0)
        def _():
            for cp in loads[1:]:
                cp.wait()

        cot = c_v[r]
        gate_w[...] = dot_t(n2_s[r], wgu[0:ffl])
        up_w[...] = dot_t(n2_s[r], wgu[ffp : ffp + ffl])
        dh_w[...] = dot_t(cot, wd[...])
        for k in range(0, RT, RC):
            rk, k_ = part_of(k)
            gate, up, dh = gate_w[k_], up_w[k_], dh_w[k_]
            sig = jax.nn.sigmoid(gate)
            act = gate * sig
            hid_s[rk] = (act * up).astype(bf16)
            dgu_s[rk, 0:ffl] = (dh * up * (sig + act * (1.0 - sig))).astype(bf16)
            dgu_s[rk, ffp : ffp + ffl] = (dh * act).astype(bf16)
        t_w[...] = dot(hid_s[r], wd[...])
        mov[r] = t_w[:, col(0)]
        out(2, i).start()
        mlp_s[s] = t_w[...].astype(bf16)
        t_w[...] = dot(dgu_s[r], wgu[...])
        for k in range(0, RT, RC):
            rk, k_ = part_of(k)
            h1, dn2 = h1_w[k_], t_w[k_]
            r2 = lax.rsqrt(jnp.mean(h1 * h1, -1, keepdims=True) + norm_eps)
            hr = h1 * r2
            g2_w[k_] = dn2 * hr
            gd = dn2 * gain[1:2]
            t_w[k_] = r2 * (gd - hr * jnp.mean(gd * hr, -1, keepdims=True))
        stat_o[1:2] += jnp.sum(g2_w[...], 0, keepdims=True)
        dhv[r] = t_w[:, col(0)] + c_v[r, col(0)].astype(f32)
        low = t_w[...].astype(bf16)
        h1p_s[r] = low
        for cp in saves(i):
            cp.start()
        t_w[...] = dot_t(low, ov[...])
        da_s[r] = t_w[...].astype(bf16)
        dav[r] = t_w[:, col(0)] + dot_t(cot, wo[...])

        @pl.when(i >= 2)
        def _():
            finish(i - 2)

        @pl.when((i >= 2) & (i - 2 < more))
        def _():
            finish2(i - 2)

        @pl.when(i >= 1)
        def _():
            job(i - 1).two()

        @pl.when((i >= 1) & (i - 1 < more))
        def _():
            job2(i - 1).two()

        job(i).one()

        @pl.when(i < more)
        def _():
            job2(i).one()

        @pl.when(i >= more)
        def _():
            out(1, i).start()

        return carry

    lax.fori_loop(0, n, tile, 0)

    def grad(k, value):
        gv[pl.ds(k * ffl, ffl)] = value.astype(bf16)
        return pltpu.make_async_copy(gv.at[pl.ds(k * ffl, ffl)], g_o.at[pl.ds(k * ffl, ffl)], lw.at[k])

    g2 = grad(2, tdot(hid_s[...], c_v[...]))
    g2.start()
    job(n - 1).two()
    finish(n - 2)
    g1 = grad(1, tdot(dgu_s[:, ffp:], n2_s[...])[0:ffl])
    g1.start()
    g0 = grad(0, tdot(dgu_s[:, 0:ffp], n2_s[...])[0:ffl])
    g0.start()
    finish(n - 1)
    for cp in (g0, g1, g2):
        cp.wait()
    for i in (n - 2, n - 1):
        for cp in saves(i):
            cp.wait()
    for i in range(n):
        for k in range(4):
            out(k, i).wait()


def ffn(gain, lengths, af, xf, cf, of, w, seqs, at_out, at_gate, ffl, cid):
    T, width = xf.shape
    Wd = width // 4
    hd = at_gate - at_out
    n = T // RT
    ffp = -(-ffl // 128) * 128
    hbm = pl.BlockSpec(memory_space=pl.ANY)
    S = jax.ShapeDtypeStruct
    V = pltpu.VMEM
    slots = V((SLOTS, 2, RT // 2, Wd), bf16)
    pair = V((2, RT, width), bf16)
    own = S((T, Wd), f32)
    return pl.pallas_call(
        functools.partial(ffn_kernel, seqs=seqs, at_out=at_out, at_gate=at_gate),
        in_specs=[VM(), pl.BlockSpec(memory_space=pltpu.SMEM)] + [hbm] * 5,
        out_specs=[hbm] * 7 + [VM()],
        out_shape=[
            S((T, width), bf16), S((T, width), bf16), own, own, own, own,
            S((3 * ffl, width), bf16), S((8, width), f32),
        ],
        scratch_shapes=[
            V((width, width), bf16), V((2 * ffp, width), bf16), V((ffl, width), bf16), V((hd, width), bf16),
            pair, pair, V((T, width), bf16), V((T, width), bf16), V((T, ffl), bf16), V((T, 2 * ffp), bf16),
            V((RT, width), f32), V((RT, width), f32), V((RT, width), f32), *[V((RT, ffl), f32)] * 3, pair, V((T, width), bf16), V((T, width), bf16),
            *[slots] * 6, *[V((T, Wd), f32)] * 4, V((3 * ffl, width), bf16),
            DMA((6,)), DMA((2, 2)), DMA((2, 2)), *[DMA((2, 3 * n))] * 4, DMA((4, n)),
        ],
        compiler_params=pltpu.CompilerParams(collective_id=cid, has_side_effects=True, vmem_limit_bytes=63 << 20),
        name="feed_forward",
    )(gain, lengths, af, xf, cf, of, w)


SB = 128


def tail_kernel(g, stats, gain, gain_m, gain_v, y, ig, p, m, v, p_o, m_o, v_o, gain_o, gm_o, gv_o, rms_o, y_o, ig_o, w, yv, iv, sem):
    i = pl.program_id(0)
    come = [pltpu.make_async_copy(a, b, sem.at[0, k]) for k, (a, b) in enumerate(((y, yv), (ig, iv)))]
    go = [pltpu.make_async_copy(a, b, sem.at[1, k]) for k, (a, b) in enumerate(((yv, y_o), (iv, ig_o)))]

    @pl.when(i == 0)
    def _():
        for cp in come:
            cp.start()

    width = g.shape[1] // 8
    for j in range(8):
        w[:, j, :] = g[:, j * width : (j + 1) * width].astype(f32)
    p_o[...], m_o[...], v_o[...] = adam_step(p[...], m[...], v[...], w[...], weight_rate, weight_decay)

    @pl.when(i == 0)
    def _():
        gain_o[...], gm_o[...], gv_o[...] = adam_step(gain[...], gain_m[...], gain_v[...], stats[0:3], gain_rate, 0.0)
        lane = lax.broadcasted_iota(jnp.int32, (1, 128), 1)
        rms = jnp.sqrt(stats[3:4, 0:128] / stats[3:4, 3:4])
        for k in range(3):
            rms_o[k] = jnp.sum(jnp.where(lane == k, rms, 0.0))
        for cp in come:
            cp.wait()
        for cp in go:
            cp.start()

    @pl.when(i == pl.num_programs(0) - 1)
    def _():
        for cp in go:
            cp.wait()


def tail(g, stats, gain, gain_m, gain_v, y, ig, p, m, v):
    capacity = p.shape[0]
    S = jax.ShapeDtypeStruct
    V = pltpu.VMEM
    hbm = pl.BlockSpec(memory_space=pl.ANY)
    whole = lambda a: pl.BlockSpec(a.shape, lambda i: (0,) * a.ndim)
    blk = pl.BlockSpec((SB, *p.shape[1:]), lambda i: (i, 0, 0))
    like = S(p.shape, f32)
    small = S(gain.shape, f32)
    return pl.pallas_call(
        tail_kernel,
        grid=(-(-capacity // SB),),
        in_specs=[pl.BlockSpec((SB, g.shape[1]), lambda i: (i, 0))] + [whole(a) for a in (stats, gain, gain_m, gain_v)] + [hbm] * 2 + [blk] * 3,
        out_specs=[blk] * 3 + [whole(gain)] * 3 + [pl.BlockSpec(memory_space=pltpu.SMEM), hbm, hbm],
        out_shape=[like] * 3 + [small] * 3 + [S((3,), f32), S(y.shape, y.dtype), S(ig.shape, ig.dtype)],
        scratch_shapes=[V((SB, *p.shape[1:]), f32), V(y.shape, y.dtype), V(ig.shape, ig.dtype), DMA((2, 2))],
        compiler_params=pltpu.CompilerParams(vmem_limit_bytes=56 << 20),
        name="owners_step",
    )(g, stats, gain, gain_m, gain_v, y, ig, p, m, v)


def adam_step(param, first, second_moment, grad, rate, decay):
    first = beta_one * first + (1.0 - beta_one) * grad
    second_moment = beta_two * second_moment + (1.0 - beta_two) * grad * grad
    denom = jnp.sqrt(second_moment / (1.0 - beta_two**STEP)) + adam_eps
    param = param - rate / (1.0 - beta_one**STEP) * first / denom - rate * decay * param
    return (param, first, second_moment)


def on_device(
    inputs, cotangent, lengths, owner_slots, table, table_m, table_v, gains, gains_m, gains_v
):
    shards = lax.axis_size("head")
    seqs = lengths.shape[0]
    hd = HEADS * DK // shards
    ffl = FF // shards
    hl = HEADS // shards
    taps_rows = KCONV * 3 * hd // MODEL_WIDTH
    capacity = table.shape[1]
    small = hl + taps_rows
    lead = 64
    at_out = lead + 3 * hd
    at_gate = at_out + hd
    n_body = 4 * hd + 3 * ffl
    order = jnp.concatenate(
        [owner_slots[n_body:], jnp.full((lead - small,), -1, jnp.int32), owner_slots[:n_body]]
    ).reshape(-1, CH)
    split = lambda t: t[0].reshape(capacity, 8, MODEL_WIDTH // 8)
    weights, x_full, cot_full, a_full, out_full, qkv, logit, *saved = front(
        split(table), order, gains, lengths, inputs, cotangent, seqs, hl, lead, at_out, at_gate, hl, small, capacity, 0
    )
    mlp_part, h1_part, da, dh_own, mlp_own, h1_own, g_ffn, stat_in = ffn(
        gains, lengths, a_full, x_full, cot_full, out_full, weights, seqs, at_out, at_gate, ffl, 1
    )
    y, input_grad, stats, owned = back(
        gains, stat_in, order, lengths, h1_part, mlp_part, [da, dh_own, mlp_own, h1_own],
        x_full, a_full, weights, g_ffn, qkv, logit, saved, seqs, hl, lead, hl, small, capacity, 2,
    )
    table_new, table_m_new, table_v_new, gains_new, gains_m_new, gains_v_new, rms, y, input_grad = tail(
        owned, stats, gains, gains_m, gains_v, y, input_grad, split(table), split(table_m), split(table_v)
    )
    return (
        y,
        input_grad,
        table_new.reshape(table.shape),
        table_m_new.reshape(table.shape),
        table_v_new.reshape(table.shape),
        gains_new,
        gains_m_new,
        gains_v_new,
        rms,
    )


def solution(mesh):
    tok, tab = P("dp", "head"), P("head", "dp", None)
    return jax.shard_map(
        on_device,
        mesh=mesh,
        in_specs=(tok, tok, P("dp"), P(), tab, tab, tab, P(), P(), P()),
        out_specs=(tok, tok, tab, tab, tab, P(), P(), P(), P()),
        check_vma=False,
    )
```

```python
import functools

import jax
import jax.numpy as jnp
from jax import lax
from jax.experimental import pallas as pl
from jax.experimental.pallas import tpu as pltpu
from jax.sharding import PartitionSpec as P

MODEL_WIDTH = 1024
FF = 2816
HEADS = 8
DK = 128
KCONV = 4
STEP = 10
C = 128

norm_eps = 1e-06
adam_eps = 1e-08
beta_one = 0.9
beta_two = 0.95
weight_rate = 0.02
gain_rate = 0.6
weight_decay = 0.1
f32 = jnp.float32
bf16 = jnp.bfloat16
MESH = pl.DeviceIdType.MESH
VM = functools.partial(pl.BlockSpec, memory_space=pltpu.VMEM)
DMA = pltpu.SemaphoreType.DMA

def dot(a,b): return lax.dot_general(a,b,(((1,),(0,)),((),())),preferred_element_type=f32)
def dot_t(a,b): return lax.dot_general(a,b,(((1,),(1,)),((),())),preferred_element_type=f32)
def tdot(a,b): return lax.dot_general(a,b,(((0,),(0,)),((),())),preferred_element_type=f32)

def shifted(x, prev, j):
    if j==0: return x
    r=pltpu.roll(x,j,0)
    p=pltpu.roll(prev,j,0)
    row=lax.broadcasted_iota(jnp.int32,(8,x.shape[1]),0)
    top=jnp.where(row<j,p,r[0:8])
    return jnp.concatenate([top,r[8:]],0)

def conv_silu(x,prev,taps):
    conv=taps[3:4]*x
    for j in range(1,4):
        conv=conv+taps[3-j:4-j]*shifted(x,prev,j)
    sg=jax.nn.sigmoid(conv)
    return conv,sg

def masks():
    i=lax.broadcasted_iota(jnp.int32,(C,C),0); j=lax.broadcasted_iota(jnp.int32,(C,C),1)
    return i,j

def fwd_kernel(x_ref,lg_ref,taps_ref,gain_ref,a_ref,q_s,k_s,u_s,t_s,p_s,g_s,r_s,s_s,o_s,l_w,*,heads,chunks):
    i,j=masks()
    low=j<=i; slow=j<i; xr=jnp.bitwise_xor(i,j)
    zero8=jnp.zeros((8,DK),f32)
    every=[(c,h) for c in range(chunks) for h in range(heads)]
    beta={}
    for c,h in every:
        rows=slice(c*C,(c+1)*C)
        pre={}
        for n,off in (("q",0),("k",heads*DK),("v",2*heads*DK)):
            cols=slice(off+h*DK,off+(h+1)*DK)
            x=x_ref[rows,cols]
            prev=zero8 if c==0 else x_ref[c*C-8:c*C,cols]
            conv,sg=conv_silu(x,prev,taps_ref[:,cols])
            pre[n]=conv*sg
        q=pre["q"]; q=q*(lax.rsqrt(jnp.sum(q*q,-1,keepdims=True)+norm_eps)*DK**-0.5)
        k=pre["k"]; k=k*lax.rsqrt(jnp.sum(k*k,-1,keepdims=True)+norm_eps)
        qb=q.astype(bf16); kb=k.astype(bf16)
        beta[c,h]=jax.nn.sigmoid(lg_ref[rows,h:h+1])
        sc=dot_t(jnp.concatenate([qb,kb],0),kb)
        G=sc[C:]
        Lw=jnp.where(slow,G*beta[c,h],0.0).astype(bf16)
        q_s[h,rows]=qb; k_s[h,rows]=kb; p_s[h,rows]=jnp.where(low,sc[0:C],0.0).astype(bf16); g_s[h,rows]=G.astype(bf16)
        r_s[h,rows]=pre["v"].astype(bf16)
        l_w[h,rows]=Lw
        t_s[h,rows]=jnp.where(xr==0,1.0,jnp.where(xr==1,-Lw.astype(f32),0.0)).astype(bf16)
    s=2
    while s<C:
        part=(xr>=s)&(xr<2*s)
        half=[dot(t_s[h,c*C:(c+1)*C],jnp.where(part,l_w[h,c*C:(c+1)*C],jnp.zeros((C,C),bf16))).astype(bf16) for c,h in every]
        for (c,h),y in zip(every,half):
            rows=slice(c*C,(c+1)*C)
            X=t_s[h,rows]
            t_s[h,rows]=X-dot(y,X).astype(bf16)
        s*=2
    S=[jnp.zeros((DK,DK),f32) for _ in range(heads)]
    for c in range(chunks):
        rows=slice(c*C,(c+1)*C)
        Sb=[S[h].astype(bf16) for h in range(heads)]
        m=[dot(jnp.concatenate([k_s[h,rows],q_s[h,rows]],0),Sb[h]) for h in range(heads)]
        R=[r_s[h,rows].astype(f32)-m[h][0:C] for h in range(heads)]
        ub=[dot(t_s[h,rows],(R[h]*beta[c,h]).astype(bf16)).astype(bf16) for h in range(heads)]
        S=[S[h]+tdot(k_s[h,rows],ub[h]) for h in range(heads)]
        for h in range(heads):
            s_s[h,rows]=Sb[h]; r_s[h,rows]=R[h].astype(bf16); u_s[h,rows]=ub[h]
            o=m[h][C:]+dot(p_s[h,rows],ub[h])
            o_s[h,rows]=o
            a=o*lax.rsqrt(jnp.mean(o*o,-1,keepdims=True)+norm_eps)*gain_ref[0:1,h*DK:(h+1)*DK]
            a_ref[rows,h*DK:(h+1)*DK]=a.astype(bf16)

def mixer_fwd(x,lg,taps,gain,seqs):
    T=x.shape[0]; L=T//seqs; W=x.shape[1]; heads=W//(3*DK)
    blk=lambda: pl.BlockSpec((heads,L,DK),lambda s:(0,s,0))
    sav=lambda dt: jax.ShapeDtypeStruct((heads,T,DK),dt)
    return pl.pallas_call(functools.partial(fwd_kernel,heads=heads,chunks=L//C),
        grid=(seqs,),
        in_specs=[pl.BlockSpec((L,W),lambda s:(s,0)),pl.BlockSpec((L,lg.shape[1]),lambda s:(s,0)),pl.BlockSpec(taps.shape,lambda s:(0,0)),pl.BlockSpec(gain.shape,lambda s:(0,0))],
        out_specs=[pl.BlockSpec((L,heads*DK),lambda s:(s,0))]+[blk() for _ in range(9)],
        out_shape=[jax.ShapeDtypeStruct((T,heads*DK),bf16)]+[sav(bf16) for _ in range(8)]+[sav(f32)],
        scratch_shapes=[pltpu.VMEM((heads,L,DK),bf16)],
        compiler_params=pltpu.CompilerParams(vmem_limit_bytes=56<<20),
        cost_estimate=pl.CostEstimate(flops=2*24*20*C*C*C,bytes_accessed=15<<20,transcendentals=0),
        name="mixer_fwd")(x,lg,taps,gain)

def bwd_kernel(x_ref,lg_ref,taps_ref,gain_ref,da_ref,q_s,k_s,u_s,t_s,p_s,g_s,r_s,s_s,o_s,dx_ref,dlg_ref,dt_ref,dg_ref,dc,*,heads,chunks):
    i,j=masks()
    low=j<=i; slow=j<i
    zero8=jnp.zeros((8,DK),f32)
    seq=pl.program_id(0)
    @pl.when(seq==0)
    def _():
        dt_ref[...]=jnp.zeros_like(dt_ref); dg_ref[...]=jnp.zeros_like(dg_ref)
    dS=[jnp.zeros((DK,DK),f32) for _ in range(heads)]
    W=heads*DK
    lane=lax.broadcasted_iota(jnp.int32,(C,128),1)
    dc[chunks*C:chunks*C+8]=jnp.zeros((8,3*W),f32)
    for c in reversed(range(chunks)):
        rows=slice(c*C,(c+1)*C)
        dlg=jnp.zeros((C,128),f32)
        for h in range(heads):
            hc=slice(h*DK,(h+1)*DK)
            o=o_s[h,rows]
            ro=lax.rsqrt(jnp.mean(o*o,-1,keepdims=True)+norm_eps)
            da=da_ref[rows,hc]
            on=o*ro
            dg_ref[0:1,hc]+=jnp.sum(da*on,0,keepdims=True)
            t=da*gain_ref[0:1,hc]
            do=(ro*(t-on*jnp.mean(t*on,-1,keepdims=True))).astype(bf16)
            qb=q_s[h,rows]; kb=k_s[h,rows]; ub=u_s[h,rows]; Tb=t_s[h,rows]; Pb=p_s[h,rows]; Sb=s_s[h,rows]
            G=g_s[h,rows].astype(f32); R=r_s[h,rows].astype(f32)
            beta=jax.nn.sigmoid(lg_ref[rows,h:h+1])
            dSb=dS[h].astype(bf16)
            du=tdot(Pb,do)+dot(kb,dSb)
            e=tdot(Tb,du.astype(bf16))
            eb=e.astype(bf16)
            be=beta*e; beb=be.astype(bf16)
            pe=dot_t(jnp.concatenate([do,eb],0),ub)
            dP=jnp.where(low,pe[0:C],0.0).astype(bf16)
            dL=jnp.where(slow,-pe[C:],0.0)
            dG=beta*dL
            ds=dot_t(jnp.concatenate([do,beb],0),Sb)
            dq=ds[0:C]+dot(dP,kb)
            dGb=dG.astype(bf16)
            dk=tdot(dP,qb)+dot_t(ub,dSb)-ds[C:]+dot(dGb,kb)+tdot(dGb,kb)
            db=jnp.sum(e*R+dL*G,-1,keepdims=True)
            dlg=jnp.where(lane==h,db*beta*(1.0-beta),dlg)
            dS[h]=dS[h]+tdot(qb,do)-tdot(kb,beb)
            for n,off in (("q",0),("k",W),("v",2*W)):
                cols=slice(off+h*DK,off+(h+1)*DK)
                x=x_ref[rows,cols]
                prev=zero8 if c==0 else x_ref[c*C-8:c*C,cols]
                conv,sg=conv_silu(x,prev,taps_ref[:,cols])
                act=conv*sg
                if n=="v": d=be
                else:
                    r=lax.rsqrt(jnp.sum(act*act,-1,keepdims=True)+norm_eps)
                    g_=dq*DK**-0.5 if n=="q" else dk
                    an=act*r
                    d=r*(g_-an*jnp.sum(g_*an,-1,keepdims=True))
                dconv=d*(sg*(1.0+conv*(1.0-sg)))
                dc[rows,cols]=dconv
                for jj in range(4):
                    dt_ref[jj:jj+1,cols]+=jnp.sum(dconv*shifted(x,prev,3-jj),0,keepdims=True)
                nxt=dc[(c+1)*C:(c+1)*C+8,cols]
                tp=taps_ref[:,cols]
                dx=tp[3:4]*dconv
                row8=lax.broadcasted_iota(jnp.int32,(8,DK),0)
                for jj in range(1,4):
                    r=pltpu.roll(dconv,C-jj,0)
                    pn=pltpu.roll(nxt,8-jj,0)
                    bot=jnp.where(row8>=8-jj,pn,r[C-8:])
                    dx=dx+tp[3-jj:4-jj]*jnp.concatenate([r[:C-8],bot],0)
                dx_ref[rows,cols]=dx.astype(bf16)
        dlg_ref[rows]=dlg.astype(bf16)

def mixer_bwd(x,lg,taps,gain,da,saved,seqs):
    T=x.shape[0]; L=T//seqs; W=x.shape[1]; heads=W//(3*DK)
    blk=lambda: pl.BlockSpec((heads,L,DK),lambda s:(0,s,0))
    return pl.pallas_call(functools.partial(bwd_kernel,heads=heads,chunks=L//C),
        grid=(seqs,),
        in_specs=[pl.BlockSpec((L,W),lambda s:(s,0)),pl.BlockSpec((L,lg.shape[1]),lambda s:(s,0)),pl.BlockSpec(taps.shape,lambda s:(0,0)),pl.BlockSpec(gain.shape,lambda s:(0,0)),pl.BlockSpec((L,heads*DK),lambda s:(s,0))]+[blk() for _ in range(9)],
        out_specs=[pl.BlockSpec((L,W),lambda s:(s,0)),pl.BlockSpec((L,128),lambda s:(s,0)),pl.BlockSpec((8,W),lambda s:(0,0)),pl.BlockSpec((8,heads*DK),lambda s:(0,0))],
        out_shape=[jax.ShapeDtypeStruct((T,W),bf16),jax.ShapeDtypeStruct((T,128),bf16),jax.ShapeDtypeStruct((8,W),f32),jax.ShapeDtypeStruct((8,heads*DK),f32)],
        scratch_shapes=[pltpu.VMEM((L+8,W),f32)],
        compiler_params=pltpu.CompilerParams(vmem_limit_bytes=56<<20),
        cost_estimate=pl.CostEstimate(flops=2*24*20*C*C*C,bytes_accessed=15<<20,transcendentals=0),
        name="mixer_bwd")(x,lg,taps,gain,da,*saved)


def meet(partners):
    b=pltpu.get_barrier_semaphore()
    for p in partners:
        pl.semaphore_signal(b,inc=1,device_id=p,device_id_type=MESH)
    pl.semaphore_wait(b,len(partners))

def ag_kernel(*refs,count,parts):
    ins=refs[:count]; outs=refs[count:2*count]; ss,rs,ls=refs[2*count:]
    h=lax.axis_index("head"); d=lax.axis_index("dp")
    meet([(jnp.bitwise_xor(h,1),d),(jnp.bitwise_xor(h,2),d)])
    def copy(src,dst,to,k):
        return pltpu.make_async_remote_copy(src,dst,ss.at[to-1,k],rs.at[to-1,k],device_id=(jnp.bitwise_xor(h,to),d),device_id_type=MESH)
    first={}; second=[]; local=[]
    for n in range(count):
        x,o=ins[n],outs[n]
        T,Wd=x.shape; R=T//(2*parts); base=n*3*parts
        def col(b): return pl.ds(pl.multiple_of(b*Wd,Wd),Wd)
        for i in range(2*parts):
            r1=pl.ds(i*R,R); j=(i+parts)%(2*parts); r2=pl.ds(j*R,R)
            first[n,1,i]=copy(x.at[r1],o.at[r1,col(h)],1,base+i); first[n,1,i].start()
            first[n,2,j]=copy(x.at[r2],o.at[r2,col(h)],2,base+j); first[n,2,j].start()
        l=pltpu.make_async_copy(x,o.at[:,col(h)],ls.at[n]); l.start(); local.append(l)
    for n in range(count):
        x,o=ins[n],outs[n]
        T,Wd=x.shape; R=T//(2*parts); base=n*3*parts
        def col(b): return pl.ds(pl.multiple_of(b*Wd,Wd),Wd)
        for i in range(parts):
            ra=pl.ds(i*R,R); rb=pl.ds((i+parts)*R,R)
            ca=col(jnp.bitwise_xor(h,1)); cb=col(jnp.bitwise_xor(h,2))
            first[n,1,i].wait_recv()
            c=copy(o.at[ra,ca],o.at[ra,ca],2,base+2*parts+i); c.start(); second.append(c)
            first[n,2,i+parts].wait_recv()
            c=copy(o.at[rb,cb],o.at[rb,cb],1,base+2*parts+i); c.start(); second.append(c)
    for n in range(count):
        for i in range(parts):
            first[n,1,i+parts].wait_recv(); first[n,2,i].wait_recv()
    for c in second: c.wait()
    for c in first.values(): c.wait_send()
    for l in local: l.wait()

def gather_columns(arrays,parts,cid):
    n=len(arrays)
    return pl.pallas_call(functools.partial(ag_kernel,count=n,parts=parts),
        in_specs=[VM()]*n,out_specs=[VM()]*n,
        out_shape=[jax.ShapeDtypeStruct((a.shape[0],4*a.shape[1]),a.dtype) for a in arrays],
        scratch_shapes=[DMA((2,3*parts*n)),DMA((2,3*parts*n)),DMA((n,))],
        compiler_params=pltpu.CompilerParams(collective_id=cid,has_side_effects=True,vmem_limit_bytes=56<<20),name="gather_columns")(*arrays)

def rs_kernel(*refs,count,parts):
    ins=refs[:count]; outs=refs[count:2*count]; fb,db,cb,sb,ss,rs=refs[2*count:]
    h=lax.axis_index("head"); d=lax.axis_index("dp")
    h1,h2,h3=[jnp.bitwise_xor(h,k) for k in (1,2,3)]
    meet([(h1,d),(h2,d)])
    T=ins[0].shape[0]; Wd=ins[0].shape[1]//4; half=T//2; R=half//parts
    def col(b): return pl.ds(pl.multiple_of(b*Wd,Wd),Wd)
    def copy(src,dst,to,k):
        return pltpu.make_async_remote_copy(src,dst,ss.at[to-1,k],rs.at[to-1,k],device_id=(jnp.bitwise_xor(h,to),d),device_id_type=MESH)
    K=lambda n,p,kind: (n*parts+p)*3+kind
    fw={}; dr={}; cm={}
    for n in range(count):
        x=ins[n]
        for p in range(parts):
            for side,to,nb in ((0,1,h1),(1,2,h2)):
                r=pl.ds(side*half+p*R,R); q=pl.ds(p*R,R)
                fw[n,p,side]=copy(x.at[r,col(h3)],fb.at[n,side,q],to,K(n,p,0)); fw[n,p,side].start()
            for side,to,nb in ((0,1,h1),(1,2,h2)):
                r=pl.ds(side*half+p*R,R); q=pl.ds(p*R,R)
                dr[n,p,side]=copy(x.at[r,col(nb)],db.at[n,side,q],to,K(n,p,1)); dr[n,p,side].start()
    for n in range(count):
        x=ins[n]
        for p in range(parts):
            for side,to,nb in ((0,2,h2),(1,1,h1)):
                r=pl.ds(side*half+p*R,R); q=pl.ds(p*R,R)
                fw[n,p,side].wait_recv()
                sb[n,side,q]=(fb[n,side,q].astype(f32)+x[r,col(nb)].astype(f32)).astype(bf16)
                cm[n,p,side]=copy(sb.at[n,side,q],cb.at[n,side,q],to,K(n,p,2)); cm[n,p,side].start()
    for n in range(count):
        x,o=ins[n],outs[n]
        for p in range(parts):
            for side in (0,1):
                r=pl.ds(side*half+p*R,R); q=pl.ds(p*R,R)
                dr[n,p,side].wait_recv()
                cm[n,p,side].wait_recv()
                o[r]=x[r,col(h)].astype(f32)+db[n,side,q].astype(f32)+cb[n,side,q].astype(f32)
    for g in (fw,dr,cm):
        for c in g.values(): c.wait_send()

def scatter_columns(arrays,parts,cid):
    n=len(arrays); T=arrays[0].shape[0]; Wd=arrays[0].shape[1]//4
    buf=pltpu.VMEM((n,2,T//2,Wd),bf16)
    return pl.pallas_call(functools.partial(rs_kernel,count=n,parts=parts),
        in_specs=[VM()]*n,out_specs=[VM()]*n,
        out_shape=[jax.ShapeDtypeStruct((T,Wd),f32) for a in arrays],
        scratch_shapes=[buf]*4+[DMA((2,3*parts*n)),DMA((2,3*parts*n))],
        compiler_params=pltpu.CompilerParams(collective_id=cid,has_side_effects=True,vmem_limit_bytes=60<<20),name="scatter_columns")(*arrays)

def scan_kernel(own,out,oth,rb,lb,rst,lst,xs,xr,fs,fr,ss,rs,*,chunk,skew):
    h=lax.axis_index("head"); d=lax.axis_index("dp"); n=lax.axis_size("dp")//2
    z=d//2; core=lax.rem(d,2)
    mate=(h,jnp.bitwise_xor(d,1)); right=(h,d+2); left=(h,d-2)
    rows=own.shape[0]; Wd=own.shape[1]//2; nc=rows//chunk
    b=pltpu.get_barrier_semaphore()
    pl.semaphore_signal(b,inc=1,device_id=mate,device_id_type=MESH)
    @pl.when(z>0)
    def _(): pl.semaphore_signal(b,inc=1,device_id=left,device_id_type=MESH)
    @pl.when(z<n-1)
    def _(): pl.semaphore_signal(b,inc=1,device_id=right,device_id_type=MESH)
    pl.semaphore_wait(b,1+(z>0).astype(jnp.int32)+(z<n-1).astype(jnp.int32))
    mine=pl.ds(pl.multiple_of(core*Wd,Wd),Wd); other=pl.ds(pl.multiple_of((1-core)*Wd,Wd),Wd)
    def at(c): return pl.ds(pl.multiple_of(c*chunk,chunk),chunk)
    def remote(src,dst,s,r,dev): return pltpu.make_async_remote_copy(src,dst,s,r,device_id=dev,device_id_type=MESH)
    def swap(c): return remote(own.at[at(c),other],oth.at[at(c)],xs.at[c],xr.at[c],mate)
    def give(c): return remote(out.at[at(c),mine],out.at[at(c),mine],fs.at[c],fr.at[c],mate)
    def goR(c): return remote(rst.at[at(c)],rb.at[at(c)],ss.at[0,c],rs.at[0,c],right)
    def goL(c): return remote(lst.at[at(c)],lb.at[at(c)],ss.at[1,c],rs.at[1,c],left)
    def issue(c,carry):
        swap(c).start(); return carry
    lax.fori_loop(0,nc,issue,0)
    last=skew*jnp.maximum(z,n-1-z)
    def step(t,carry):
        @pl.when(t<nc)
        def _():
            swap(t).wait_recv()
            oth[at(t)]=(oth[at(t)].astype(f32)+own[at(t),mine].astype(f32)).astype(bf16)
        c=t-skew*z
        @pl.when((c>=0)&(c<nc))
        def _():
            @pl.when(z>0)
            def _(): goR(c).wait_recv()
            @pl.when(z<n-1)
            def _():
                @pl.when(z==0)
                def _(): rst[at(c)]=oth[at(c)]
                @pl.when(z>0)
                def _(): rst[at(c)]=(oth[at(c)].astype(f32)+rb[at(c)].astype(f32)).astype(bf16)
                goR(c).start()
        e=t-skew*(n-1-z)
        @pl.when((e>=0)&(e<nc))
        def _():
            @pl.when(z<n-1)
            def _(): goL(e).wait_recv()
            @pl.when(z>0)
            def _():
                @pl.when(z==n-1)
                def _(): lst[at(e)]=oth[at(e)]
                @pl.when(z<n-1)
                def _(): lst[at(e)]=(oth[at(e)].astype(f32)+lb[at(e)].astype(f32)).astype(bf16)
                goL(e).start()
        g=t-last
        @pl.when((g>=0)&(g<nc))
        def _():
            @pl.when(z==0)
            def _(): out[at(g),mine]=(oth[at(g)].astype(f32)+lb[at(g)].astype(f32)).astype(bf16)
            @pl.when(z==n-1)
            def _(): out[at(g),mine]=(oth[at(g)].astype(f32)+rb[at(g)].astype(f32)).astype(bf16)
            @pl.when((z>0)&(z<n-1))
            def _(): out[at(g),mine]=(oth[at(g)].astype(f32)+rb[at(g)].astype(f32)+lb[at(g)].astype(f32)).astype(bf16)
            give(g).start()
        return carry
    lax.fori_loop(0,nc+skew*(n-1),step,0)
    def drain(c,carry):
        give(c).wait()
        swap(c).wait_send()
        @pl.when(z<n-1)
        def _(): goR(c).wait_send()
        @pl.when(z>0)
        def _(): goL(c).wait_send()
        return carry
    lax.fori_loop(0,nc,drain,0)

def sum_rows(own,chunk,cid,skew=2):
    rows,wd=own.shape; nc=rows//chunk
    buf=pltpu.VMEM((rows,wd//2),bf16)
    return pl.pallas_call(functools.partial(scan_kernel,chunk=chunk,skew=skew),
        in_specs=[VM()],out_specs=VM(),out_shape=jax.ShapeDtypeStruct((rows,wd),bf16),
        scratch_shapes=[buf]*5+[DMA((nc,))]*4+[DMA((2,nc))]*2,
        compiler_params=pltpu.CompilerParams(collective_id=cid,has_side_effects=True,vmem_limit_bytes=60<<20),name="sum_rows")(own)


class Spread:
    def __init__(self, src, dst, first, second, ss, rs, base):
        self.h, self.d = lax.axis_index("head"), lax.axis_index("dp")
        self.src, self.dst, self.first, self.second = src, dst, first, second
        self.ss, self.rs, self.base, self.n = ss, rs, base, len(first)

    def copy(self, src, dst, to, k):
        return pltpu.make_async_remote_copy(
            src, dst, self.ss.at[to - 1, self.base + k], self.rs.at[to - 1, self.base + k],
            device_id=(jnp.bitwise_xor(self.h, to), self.d), device_id_type=MESH,
        )

    def direct(self, to, i):
        rows = (self.first + self.second)[i]
        return self.copy(self.src(rows), self.dst(rows, self.h), to, i)

    def passed(self, to, i):
        rows = (self.second if to == 1 else self.first)[i]
        ref = self.dst(rows, jnp.bitwise_xor(self.h, 3 - to))
        return self.copy(ref, ref, to, 2 * self.n + i)

    def start(self):
        n = self.n
        for i in range(2 * n):
            self.direct(1, i).start()
            self.direct(2, (i + n) % (2 * n)).start()

    def forward(self, i):
        self.direct(1, i).wait_recv()
        self.passed(2, i).start()
        self.direct(2, self.n + i).wait_recv()
        self.passed(1, i).start()

    def arrived(self):
        for i in range(self.n):
            self.direct(1, self.n + i).wait_recv()
            self.direct(2, i).wait_recv()
            self.passed(1, i).wait_recv()
            self.passed(2, i).wait_recv()

    def sent(self):
        for to in (1, 2):
            for i in range(2 * self.n):
                self.direct(to, i).wait_send()
            for i in range(self.n):
                self.passed(to, i).wait_send()


def fwd_conv(x_ref, lg_ref, taps_ref, q_s, k_s, p_s, g_s, r_s, t_s, l_w, heads, chunks):
    i, j = masks()
    low = j <= i
    slow = j < i
    xr = jnp.bitwise_xor(i, j)
    zero8 = jnp.zeros((8, DK), f32)
    for c in range(chunks):
        for h in range(heads):
            rows = slice(c * C, (c + 1) * C)
            pre = {}
            for n, off in (("q", 0), ("k", heads * DK), ("v", 2 * heads * DK)):
                cols = slice(off + h * DK, off + (h + 1) * DK)
                x = x_ref[rows, cols]
                prev = zero8 if c == 0 else x_ref[c * C - 8 : c * C, cols]
                conv, sg = conv_silu(x, prev, taps_ref[:, cols])
                pre[n] = conv * sg
            q, k = pre["q"], pre["k"]
            q = q * (lax.rsqrt(jnp.sum(q * q, -1, keepdims=True) + norm_eps) * DK**-0.5)
            k = k * lax.rsqrt(jnp.sum(k * k, -1, keepdims=True) + norm_eps)
            qb, kb = q.astype(bf16), k.astype(bf16)
            beta = jax.nn.sigmoid(lg_ref[rows, h : h + 1])
            sc = dot_t(jnp.concatenate([qb, kb], 0), kb)
            G = sc[C:]
            Lw = jnp.where(slow, G * beta, 0.0).astype(bf16)
            q_s[h, rows] = qb
            k_s[h, rows] = kb
            p_s[h, rows] = jnp.where(low, sc[0:C], 0.0).astype(bf16)
            g_s[h, rows] = G.astype(bf16)
            r_s[h, rows] = pre["v"].astype(bf16)
            l_w[h, rows] = Lw
            t_s[h, rows] = jnp.where(xr == 0, 1.0, jnp.where(xr == 1, -Lw.astype(f32), 0.0)).astype(bf16)


def fwd_inverse(t_s, l_w, heads, chunks):
    i, j = masks()
    xr = jnp.bitwise_xor(i, j)
    every = [(c, h) for c in range(chunks) for h in range(heads)]
    s = 2
    while s < C:
        part = (xr >= s) & (xr < 2 * s)
        half = [
            dot(t_s[h, c * C : (c + 1) * C], jnp.where(part, l_w[h, c * C : (c + 1) * C], jnp.zeros((C, C), bf16))).astype(bf16)
            for c, h in every
        ]
        for (c, h), y in zip(every, half):
            rows = slice(c * C, (c + 1) * C)
            X = t_s[h, rows]
            t_s[h, rows] = X - dot(y, X).astype(bf16)
        s *= 2


def fwd_states(lg_ref, gain_ref, a_ref, q_s, k_s, u_s, t_s, p_s, r_s, s_s, o_s, heads, chunks):
    S = [jnp.zeros((DK, DK), f32) for _ in range(heads)]
    for c in range(chunks):
        rows = slice(c * C, (c + 1) * C)
        Sb = [S[h].astype(bf16) for h in range(heads)]
        m = [dot(jnp.concatenate([k_s[h, rows], q_s[h, rows]], 0), Sb[h]) for h in range(heads)]
        R = [r_s[h, rows].astype(f32) - m[h][0:C] for h in range(heads)]
        beta = [jax.nn.sigmoid(lg_ref[rows, h : h + 1]) for h in range(heads)]
        ub = [dot(t_s[h, rows], (R[h] * beta[h]).astype(bf16)).astype(bf16) for h in range(heads)]
        S = [S[h] + tdot(k_s[h, rows], ub[h]) for h in range(heads)]
        for h in range(heads):
            s_s[h, rows] = Sb[h]
            r_s[h, rows] = R[h].astype(bf16)
            u_s[h, rows] = ub[h]
            o = m[h][C:] + dot(p_s[h, rows], ub[h])
            o_s[h, rows] = o
            a = o * lax.rsqrt(jnp.mean(o * o, -1, keepdims=True) + norm_eps) * gain_ref[0:1, h * DK : (h + 1) * DK]
            a_ref[rows, h * DK : (h + 1) * DK] = a.astype(bf16)


CH = 128
SKEW = 2


def front_kernel(
    order, gain, lengths, owners, slots, x, cot,
    w, xf, cf, af, of, qkv_o, lg_o, q_o, k_o, u_o, t_o, p_o, g_o, r_o, s_o, o_o,
    own, oth, rb, lb, wv, xv, qv, lv, tp, av, q_s, k_s, u_s, t_s, p_s, g_s, r_s, s_s, o_s, l_w, cv, go, slots_v, table, order_w,
    xs, xr_, gl, fs, fr, ss, rs, as_, ar_, ls, sv,
    *, seqs, heads, lead, at_out, at_gate, hl, small, capacity,
):
    h = lax.axis_index("head")
    d = lax.axis_index("dp")
    n = lax.axis_size("dp") // 2
    z = d // 2
    core = lax.rem(d, 2)
    mate = (h, jnp.bitwise_xor(d, 1))
    h1, h2 = jnp.bitwise_xor(h, 1), jnp.bitwise_xor(h, 2)
    T, Wd = x.shape
    L = T // seqs
    rows_all, width = own.shape
    half = width // 2
    nc = rows_all // CH
    early = wv.shape[0] // CH
    chunks = L // C

    load_t = pltpu.make_async_copy(slots, slots_v.at[pl.ds(0, capacity)], ls.at[6])
    load_t.start()
    b = pltpu.get_barrier_semaphore()
    for p in (mate, (h1, d), (h2, d)):
        pl.semaphore_signal(b, inc=1, device_id=p, device_id_type=MESH)
    @pl.when(z > 0)
    def _():
        pl.semaphore_signal(b, inc=1, device_id=(h, d - 2), device_id_type=MESH)
    @pl.when(z < n - 1)
    def _():
        pl.semaphore_signal(b, inc=1, device_id=(h, d + 2), device_id_type=MESH)
    pl.semaphore_wait(b, 3 + (z > 0).astype(jnp.int32) + (z < n - 1).astype(jnp.int32))

    def col(i, size=Wd):
        return pl.ds(pl.multiple_of(i * size, size), size)

    def at(c):
        return pl.ds(pl.multiple_of(c * CH, CH), CH)

    parts = 3
    R = T // (2 * parts)
    A = [pl.ds(i * R, R) for i in range(parts)]
    B = [pl.ds((i + parts) * R, R) for i in range(parts)]
    spread_x = Spread(lambda r: x.at[r], lambda r, i: xv.at[r, col(i)], A, B, as_, ar_, 0)
    spread_c = Spread(lambda r: cv.at[r], lambda r, i: cf.at[r, col(i)], A, B, as_, ar_, 9)
    spread_a = [
        Spread(
            lambda r: av.at[r], lambda r, i: af.at[r, col(i)],
            [pl.ds(s * L, L // 2)], [pl.ds(s * L + L // 2, L // 2)], as_, ar_, 18 + 3 * s,
        )
        for s in range(seqs)
    ]
    hw = at_gate - at_out
    spread_o = Spread(
        lambda r: w.at[pl.ds(at_out + r[0], r[1])],
        lambda r, i: of.at[pl.ds(pl.multiple_of(i * hw, hw) + r[0], r[1])],
        [(0, hw // 2)], [(hw // 2, hw // 2)], as_, ar_, 18 + 3 * seqs,
    )
    spread_x.start()
    own_x = pltpu.make_async_copy(x, xv.at[:, col(h)], ls.at[0])
    own_x.start()
    load_c = pltpu.make_async_copy(cot, cv, ls.at[5])
    load_c.start()

    mine, other = col(core, half), col(1 - core, half)

    def remote(src, dst, s, r, dev):
        return pltpu.make_async_remote_copy(src, dst, s, r, device_id=dev, device_id_type=MESH)

    def swap(c):
        return remote(own.at[at(c), other], oth.at[at(c)], xs.at[c], xr_.at[c], mate)

    def to_right(c):
        return remote(rb.at[at(c)], rb.at[at(c)], ss.at[0, c], rs.at[0, c], (h, d + 2))

    def to_left(c):
        return remote(lb.at[at(c)], lb.at[at(c)], ss.at[1, c], rs.at[1, c], (h, d - 2))

    def give(c, dst):
        return remote(oth.at[at(c)], dst.at[at(c), mine], fs.at[c], fr.at[c], mate)

    def keep(c, dst):
        return pltpu.make_async_copy(oth.at[at(c)], dst.at[at(c), mine], gl.at[c])

    def pick(c):
        place = lax.broadcasted_iota(jnp.int32, (table.shape[0], CH), 0) + base
        hot = jnp.where(order_w[pl.ds(c, 1)] == place, 1.0, 0.0).astype(bf16)
        own[at(c)] = tdot(hot, table[...]).astype(bf16)
        swap(c).start()

    head = order[0:1]
    lane0 = lax.broadcasted_iota(jnp.int32, head.shape, 1)
    for k in range(small):
        head = jnp.where(lane0 == k, owners[owners.shape[0] - small + k], head)
    order_w[...] = order[...]
    order_w[0:1] = head
    base = d * capacity
    spare = slots_v.shape[0] - capacity
    if spare:
        slots_v[pl.ds(capacity, spare)] = jnp.zeros((spare, 8, width // 8), f32)
    load_t.wait()
    for j in range(8):
        table[:, j * (width // 8) : (j + 1) * (width // 8)] = slots_v[:, j, :].astype(bf16)
    pick(0)
    pick(1)
    last = SKEW * jnp.maximum(z, n - 1 - z)

    def step(t, carry):
        @pl.when(t + 2 < nc)
        def _():
            pick(t + 2)

        @pl.when(t < nc)
        def _():
            swap(t).wait_recv()
            oth[at(t)] = oth[at(t)] + own[at(t), mine]

        c = t - SKEW * z
        @pl.when((c >= 0) & (c < nc))
        def _():
            @pl.when(z > 0)
            def _():
                to_right(c).wait_recv()
                rb[at(c)] = rb[at(c)] + oth[at(c)]
            @pl.when(z == 0)
            def _():
                rb[at(c)] = oth[at(c)]
            @pl.when(z < n - 1)
            def _():
                to_right(c).start()

        e = t - SKEW * (n - 1 - z)
        @pl.when((e >= 0) & (e < nc))
        def _():
            @pl.when(z < n - 1)
            def _():
                to_left(e).wait_recv()
                lb[at(e)] = lb[at(e)] + oth[at(e)]
            @pl.when(z == n - 1)
            def _():
                lb[at(e)] = oth[at(e)]
            @pl.when(z > 0)
            def _():
                to_left(e).start()

        g = t - last
        @pl.when((g >= 0) & (g < nc))
        def _():
            oth[at(g)] = rb[at(g)] + lb[at(g)] - oth[at(g)]
            @pl.when(g < early)
            def _():
                give(g, wv).start()
                keep(g, wv).start()
            @pl.when(g >= early)
            def _():
                give(g, w).start()
                keep(g, w).start()
        return carry

    def steps(lo, hi):
        lax.fori_loop(lo, hi, step, 0)

    steps(0, 1)
    load_c.wait()
    place = lax.broadcasted_iota(jnp.int32, (L, Wd), 0)
    for s in range(seqs):
        r = pl.ds(s * L, L)
        cv[r] = jnp.where(place < lengths[s], cv[r], jnp.zeros((L, Wd), bf16))
    steps(1, 2)
    for i in range(parts):
        spread_x.forward(i)
        steps(2 + i, 3 + i)
    spread_c.start()
    own_c = pltpu.make_async_copy(cv, cf.at[:, col(h)], ls.at[1])
    own_c.start()
    t = early + SKEW * (n - 1)
    steps(2 + parts, t)
    for c in range(early):
        keep(c, wv).wait()
        give(c, wv).wait_recv()
    save_w = pltpu.make_async_copy(wv, w.at[pl.ds(0, early * CH)], ls.at[2])
    save_w.start()
    spread_x.arrived()
    own_x.wait()
    save_x = pltpu.make_async_copy(xv, xf, ls.at[3])
    save_x.start()

    taps3 = wv[0:16].astype(f32)
    flat = [taps3[hl + i : hl + i + 1] for i in range(small - hl)]
    line = 3 * heads * DK
    joined = jnp.concatenate(flat, 1)
    for j in range(KCONV):
        tp[j : j + 1] = joined[:, j * line : (j + 1) * line]

    go[0:1] = gain[2:3, col(h)]
    saves = []
    for s in range(seqs):
        rows = pl.ds(s * L, L)
        for i in range(2):
            r = pl.ds(s * L + i * (L // 2), L // 2)
            xx = xv[r].astype(f32)
            n1 = (xx * lax.rsqrt(jnp.mean(xx * xx, -1, keepdims=True) + norm_eps) * gain[0:1]).astype(bf16)
            lv[r] = dot_t(n1, wv[0:lead])
            qv[r] = dot_t(n1, wv[lead:at_out])
        if s == 0:
            spread_c.forward(0)
        steps(t, t + 1)
        sub = lambda ref: ref.at[:, rows]
        fwd_conv(qv.at[rows], lv.at[rows], tp, sub(q_s), sub(k_s), sub(p_s), sub(g_s), sub(r_s), sub(t_s), l_w, heads, chunks)
        if s == 0:
            spread_c.forward(1)
        else:
            spread_a[s - 1].forward(0)
        steps(t + 1, t + 2)
        fwd_inverse(sub(t_s), l_w, heads, chunks)
        if s == 0:
            spread_c.forward(2)
        steps(t + 2, t + 3)
        fwd_states(lv.at[rows], go, av.at[rows], sub(q_s), sub(k_s), sub(u_s), sub(t_s), sub(p_s), sub(r_s), sub(s_s), sub(o_s), heads, chunks)
        spread_a[s].start()
        saves.append(pltpu.make_async_copy(av.at[rows], af.at[rows, col(h)], sv.at[s, 0]))
        pairs = [(qv.at[rows], qkv_o.at[rows]), (lv.at[rows], lg_o.at[rows])]
        for src, dst in ((q_s, q_o), (k_s, k_o), (u_s, u_o), (t_s, t_o), (p_s, p_o), (g_s, g_o), (r_s, r_o), (s_s, s_o), (o_s, o_o)):
            pairs.append((src.at[:, rows], dst.at[:, rows]))
        for k, (src, dst) in enumerate(pairs):
            saves.append(pltpu.make_async_copy(src, dst, sv.at[s, 1 + k]))
        for cp in saves[-12:]:
            cp.start()
        steps(t + 3, t + 4)
        t += 4
        if s == 1:
            save_w.wait()
            for c in range(early, -(-at_gate // CH)):
                keep(c, w).wait()
                give(c, w).wait_recv()
            spread_o.start()
            own_o = pltpu.make_async_copy(w.at[pl.ds(at_out, hw)], of.at[col(h, hw)], ls.at[4])
            own_o.start()
    steps(t, t + 2)
    spread_a[seqs - 1].forward(0)
    spread_o.forward(0)
    steps(t + 2, nc + SKEW * (n - 1))

    own_c.wait()
    own_o.wait()
    save_x.wait()
    for cp in saves:
        cp.wait()
    for sp in [spread_c, *spread_a, spread_o]:
        sp.arrived()
    for sp in [spread_x, spread_c, *spread_a, spread_o]:
        sp.sent()

    def drain(c, carry):
        swap(c).wait_send()
        @pl.when(c < early)
        def _():
            give(c, wv).wait_send()
        @pl.when(c >= early)
        def _():
            give(c, w).wait_send()
        @pl.when(c >= -(-at_gate // CH))
        def _():
            keep(c, w).wait()
            give(c, w).wait_recv()
        @pl.when(z < n - 1)
        def _():
            to_right(c).wait_send()
        @pl.when(z > 0)
        def _():
            to_left(c).wait_send()
        return carry

    lax.fori_loop(0, nc, drain, 0)


def front(slots, order, gain, lengths, owners, x, cot, seqs, heads, lead, at_out, at_gate, hl, small, capacity, cid):
    T, Wd = x.shape
    rows = order.shape[0] * order.shape[1]
    width = slots.shape[1] * slots.shape[2]
    padded = -(-capacity // 128) * 128
    half = width // 2
    nc = rows // CH
    early = -(-at_out // CH)
    L = T // seqs
    hbm = pl.BlockSpec(memory_space=pl.ANY)
    S = jax.ShapeDtypeStruct
    sav = [S((heads, T, DK), bf16)] * 8 + [S((heads, T, DK), f32)]
    outs = [
        S((rows, width), bf16), S((T, width), bf16), S((T, width), bf16), S((T, width), bf16),
        S((4 * (at_gate - at_out), width), bf16), S((T, at_out - lead), f32), S((T, lead), f32), *sav,
    ]
    V = pltpu.VMEM
    piece = V((rows, half), bf16)
    return pl.pallas_call(
        functools.partial(
            front_kernel, seqs=seqs, heads=heads, lead=lead, at_out=at_out, at_gate=at_gate, hl=hl, small=small, capacity=capacity
        ),
        in_specs=[VM()] * 2 + [pl.BlockSpec(memory_space=pltpu.SMEM)] * 2 + [hbm] * 3,
        out_specs=[hbm] * len(outs),
        out_shape=outs,
        scratch_shapes=[
            V((rows, width), bf16), piece, piece, piece, V((early * CH, width), bf16), V((T, width), bf16),
            V((T, at_out - lead), f32), V((T, lead), f32), V((8, at_out - lead), f32), V((T, heads * DK), bf16),
            *[V((heads, T, DK), bf16)] * 8, V((heads, T, DK), f32), V((heads, L, DK), bf16), V((T, Wd), bf16), V((8, Wd), f32),
            V((padded, 8, width // 8), f32), V((padded, width), bf16), V(order.shape, jnp.int32),
            DMA((nc,)), DMA((nc,)), DMA((nc,)), DMA((nc,)), DMA((nc,)), DMA((2, nc)), DMA((2, nc)),
            DMA((2, 21 + 3 * seqs)), DMA((2, 21 + 3 * seqs)), DMA((7,)), DMA((seqs, 12)),
        ],
        compiler_params=pltpu.CompilerParams(collective_id=cid, has_side_effects=True, vmem_limit_bytes=60 << 20),
        name="front",
    )(order, gain, lengths, owners, slots, x, cot)


def bwd_blocks(da_ref, gain_ref, o_s, q_s, k_s, u_s, p_s, s_s, dg_ref, do_w, w_w, dq_w, dk_w, qd_w, heads, chunks):
    i, j = masks()
    low = j <= i
    for c in range(chunks):
        for h in range(heads):
            rows = slice(c * C, (c + 1) * C)
            hc = slice(h * DK, (h + 1) * DK)
            o = o_s[h, rows]
            ro = lax.rsqrt(jnp.mean(o * o, -1, keepdims=True) + norm_eps)
            da = da_ref[rows, hc]
            on = o * ro
            dg_ref[0:1, hc] += jnp.sum(da * on, 0, keepdims=True)
            t = da * gain_ref[0:1, hc]
            do = (ro * (t - on * jnp.mean(t * on, -1, keepdims=True))).astype(bf16)
            qb, kb = q_s[h, rows], k_s[h, rows]
            dP = jnp.where(low, dot_t(do, u_s[h, rows]), 0.0).astype(bf16)
            do_w[h, rows] = do
            w_w[h, rows] = tdot(p_s[h, rows], do)
            dq_w[h, rows] = dot_t(do, s_s[h, rows]) + dot(dP, kb)
            dk_w[h, rows] = tdot(dP, qb)
            qd_w[h, rows] = tdot(qb, do)


def bwd_states(lg_ref, k_s, t_s, w_w, qd_w, ds_w, heads, chunks):
    dS = [jnp.zeros((DK, DK), f32) for _ in range(heads)]
    for c in reversed(range(chunks)):
        rows = slice(c * C, (c + 1) * C)
        kb = [k_s[h, rows] for h in range(heads)]
        dSb = [dS[h].astype(bf16) for h in range(heads)]
        du = [(w_w[h, rows] + dot(kb[h], dSb[h])).astype(bf16) for h in range(heads)]
        e = [tdot(t_s[h, rows], du[h]) for h in range(heads)]
        beta = [jax.nn.sigmoid(lg_ref[rows, h : h + 1]) for h in range(heads)]
        dS = [dS[h] + qd_w[h, rows] - tdot(kb[h], (beta[h] * e[h]).astype(bf16)) for h in range(heads)]
        for h in range(heads):
            w_w[h, rows] = e[h]
            ds_w[h, rows] = dSb[h]


def bwd_conv(x_ref, lg_ref, taps_ref, q_s, k_s, u_s, g_s, r_s, s_s, w_w, dq_w, dk_w, ds_w, dc, dx_ref, dlg_ref, dt_ref, heads, chunks):
    i, j = masks()
    slow = j < i
    zero8 = jnp.zeros((8, DK), f32)
    W = heads * DK
    lane = lax.broadcasted_iota(jnp.int32, (C, dlg_ref.shape[1]), 1)
    row8 = lax.broadcasted_iota(jnp.int32, (8, DK), 0)
    dc[chunks * C : chunks * C + 8] = jnp.zeros((8, 3 * W), f32)
    for c in reversed(range(chunks)):
        rows = slice(c * C, (c + 1) * C)
        dlg = jnp.zeros(lane.shape, f32)
        for h in range(heads):
            e = w_w[h, rows]
            eb = e.astype(bf16)
            beta = jax.nn.sigmoid(lg_ref[rows, h : h + 1])
            be = beta * e
            ub, kb = u_s[h, rows], k_s[h, rows]
            dL = jnp.where(slow, -dot_t(eb, ub), 0.0)
            dGb = (beta * dL).astype(bf16)
            dk = (
                dk_w[h, rows] + dot_t(ub, ds_w[h, rows]) - dot_t(be.astype(bf16), s_s[h, rows])
                + dot(dGb, kb) + tdot(dGb, kb)
            )
            db = jnp.sum(e * r_s[h, rows].astype(f32) + dL * g_s[h, rows].astype(f32), -1, keepdims=True)
            dlg = jnp.where(lane == h, db * beta * (1.0 - beta), dlg)
            for n, off in (("q", 0), ("k", W), ("v", 2 * W)):
                cols = slice(off + h * DK, off + (h + 1) * DK)
                tp = taps_ref[:, cols]
                x = x_ref[rows, cols]
                prev = zero8 if c == 0 else x_ref[c * C - 8 : c * C, cols]
                moved = [shifted(x, prev, 3 - jj) for jj in range(4)]
                conv = tp[3:4] * moved[3]
                for jj in range(3):
                    conv = conv + tp[jj : jj + 1] * moved[jj]
                sg = jax.nn.sigmoid(conv)
                act = conv * sg
                if n == "v":
                    dd = be
                else:
                    r = lax.rsqrt(jnp.sum(act * act, -1, keepdims=True) + norm_eps)
                    g = dq_w[h, rows] * DK**-0.5 if n == "q" else dk
                    an = act * r
                    dd = r * (g - an * jnp.sum(g * an, -1, keepdims=True))
                dconv = dd * (sg + act * (1.0 - sg))
                dc[rows, cols] = dconv
                for jj in range(4):
                    dt_ref[jj : jj + 1, cols] += jnp.sum(dconv * moved[jj], 0, keepdims=True)
                nxt = dc[(c + 1) * C : (c + 1) * C + 8, cols]
                dx = tp[3:4] * dconv
                for jj in range(1, 4):
                    r = pltpu.roll(dconv, C - jj, 0)
                    bot = jnp.where(row8 >= 8 - jj, pltpu.roll(nxt, 8 - jj, 0), r[C - 8 :])
                    dx = dx + tp[3 - jj : 4 - jj] * jnp.concatenate([r[: C - 8], bot], 0)
                dx_ref[rows, cols] = dx.astype(bf16)
        dlg_ref[rows] = dlg.astype(bf16)


class Scatter:
    def __init__(self, part, beside, rows, bufs, slot, ss, rs, base):
        self.h, self.d = lax.axis_index("head"), lax.axis_index("dp")
        self.part, self.beside, self.slot = part, beside, slot
        self.fb, self.db, self.cb = bufs
        self.half = rows.size // 2
        self.rows = [pl.ds(rows.start + i * self.half, self.half) for i in range(2)]
        self.ss, self.rs, self.base = ss, rs, base

    def col(self, k):
        w = self.part.shape[1] // 4
        return pl.ds(pl.multiple_of(jnp.bitwise_xor(self.h, k) * w, w), w)

    def copy(self, src, dst, to, k):
        return pltpu.make_async_remote_copy(
            src, dst, self.ss.at[to - 1, self.base + k], self.rs.at[to - 1, self.base + k],
            device_id=(jnp.bitwise_xor(self.h, to), self.d), device_id_type=MESH,
        )

    def far(self, side):
        return self.copy(self.part.at[self.rows[side], self.col(3)], self.fb.at[self.slot, side], side + 1, 0)

    def near(self, side):
        return self.copy(self.part.at[self.rows[side], self.col(side + 1)], self.db.at[self.slot, side], side + 1, 1)

    def both(self, side):
        return self.copy(self.fb.at[self.slot, side], self.cb.at[self.slot, side], 2 - side, 2)

    def one(self):
        for side in (0, 1):
            self.far(side).start()
        for side in (0, 1):
            self.near(side).start()

    def two(self):
        for side in (0, 1):
            self.far(side).wait_recv()
            got = self.fb[self.slot, side].astype(f32) + self.beside(side).astype(f32)
            self.fb[self.slot, side] = got.astype(bf16)
            self.both(side).start()

    def three(self):
        got = []
        for side in (0, 1):
            self.near(side).wait_recv()
            self.both(side).wait_recv()
            got.append(self.db[self.slot, side].astype(f32) + self.cb[self.slot, side].astype(f32))
            self.far(side).wait_send()
            self.near(side).wait_send()
            self.both(side).wait_send()
        return got


RING = 4
SLOTS = 4


def back_kernel(
    gain, stat_in, order, lengths, owners,
    h1_part, mlp_part, da_in, dh_own, mlp_own, h1_own, xf, af, w, g_ffn, qkv, lg, q_i, k_i, u_i, t_i, p_i, g_i, r_i, s_i, o_i,
    y_o, ig_o, stat_o, own_o,
    own, oth, rb, lb, rst, lst, qv, lv, q_s, k_s, u_s, t_s, p_s, g_s, r_s, s_s, o_s,
    do_w, w_w, dq_w, dk_w, qd_w, ds_w, dc, xv, wv, nb, da_f, dh_f, mlp_f, h1_f, xp, fb, db, cb, gq, gs, n1_w, dx_w, dlg_w, dt_w, dg_w, g1_w, st_w, go_w, tp, gout, av, acc, order_w,
    xs, xr_, gl, fs, fr, ss, rs, as_, ar_, ls, lds, a2s, a2r, sts, str_, igs, avs,
    *, seqs, heads, lead, n_ffn, hl, small, capacity,
):
    h = lax.axis_index("head")
    d = lax.axis_index("dp")
    n = lax.axis_size("dp") // 2
    z = d // 2
    core = lax.rem(d, 2)
    mate = (h, jnp.bitwise_xor(d, 1))
    T = xf.shape[0]
    L = T // seqs
    rows_all, width = own.shape
    half = width // 2
    Wd = width // 4
    nc = rows_all // CH
    chunks = L // C
    hd = heads * DK
    at_qkv, at_out, at_ffn = lead, lead + 3 * hd, lead + 4 * hd

    def col(i, size=Wd):
        return pl.ds(pl.multiple_of(i * size, size), size)

    def at(c):
        return pl.ds(pl.multiple_of((nc - 1 - c) * CH, CH), CH)

    seq_rows = [pl.ds(s * L, L) for s in range(seqs)]
    bufs = (fb, db, cb)
    jobs = []
    kinds = []
    for kind, part in enumerate((h1_part, mlp_part, xp)):
        for s in range(EARLY if kind == 0 else 0, seqs):
            kinds.append((kind, s))
            if kind < 2:
                def beside(side, kind=kind, s=s):
                    return nb[kind, s, side]
            else:
                def beside(side, s=s):
                    r = pl.ds(s * L + side * (L // 2), L // 2)
                    return xp[r, col(jnp.bitwise_xor(h, 2 - side))]
            k = len(jobs)
            jobs.append(Scatter(part, beside, seq_rows[s], bufs, k % SLOTS, as_, ar_, 3 * k))
    def load(src, dst, k):
        cp = pltpu.make_async_copy(src, dst, ls.at[k])
        cp.start()
        return cp

    first = load(g_ffn, own.at[pl.ds(at_ffn, n_ffn)], 0)
    nbs = []
    for kind, part in enumerate((h1_part, mlp_part)):
        for s in range(EARLY if kind == 0 else 0, seqs):
            for side in (0, 1):
                r = pl.ds(s * L + side * (L // 2), L // 2)
                nbs.append(load(part.at[r, col(jnp.bitwise_xor(h, 2 - side))], nb.at[kind, s, side], 8 + len(nbs)))
    load_da = load(da_in, da_f, 1)
    ins = (q_i, k_i, u_i, t_i, p_i, g_i, r_i, s_i, o_i)
    scr = (q_s, k_s, u_s, t_s, p_s, g_s, r_s, s_s, o_s)

    def fetch(s):
        sl = s % 2
        cps = [pltpu.make_async_copy(qkv.at[seq_rows[s]], qv.at[sl], lds.at[sl, 9]),
               pltpu.make_async_copy(lg.at[seq_rows[s]], lv.at[sl], lds.at[sl, 10])]
        for k, (i, o) in enumerate(zip(ins, scr)):
            cps.append(pltpu.make_async_copy(i.at[:, seq_rows[s]], o.at[sl], lds.at[sl, k]))
        return cps

    for cp in fetch(0):
        cp.start()
    load_w = load(w.at[pl.ds(0, lead + 3 * hd)], wv, 2)
    load_x = load(xf, xv, 3)
    load_dh = load(dh_own, dh_f, 4)
    load_m = load(mlp_own, mlp_f, 5)
    load_h = load(h1_own, h1_f, 6)

    bits = []
    k = 2
    while k < 2 * n:
        bits.append(k)
        k *= 2
    b = pltpu.get_barrier_semaphore()
    peers = [mate] + [(jnp.bitwise_xor(h, k), d) for k in (1, 2, 3)] + [(h, jnp.bitwise_xor(d, k)) for k in bits]
    for p in peers:
        pl.semaphore_signal(b, inc=1, device_id=p, device_id_type=MESH)
    @pl.when(z > 0)
    def _():
        pl.semaphore_signal(b, inc=1, device_id=(h, d - 2), device_id_type=MESH)
    @pl.when(z < n - 1)
    def _():
        pl.semaphore_signal(b, inc=1, device_id=(h, d + 2), device_id_type=MESH)
    pl.semaphore_wait(b, len(peers) + (z > 0).astype(jnp.int32) + (z < n - 1).astype(jnp.int32))

    jobs[0].one()

    mine, other = col(core, half), col(1 - core, half)

    def remote(src, dst, s, r, dev):
        return pltpu.make_async_remote_copy(src, dst, s, r, device_id=dev, device_id_type=MESH)

    def ring(c):
        return pl.ds(pl.multiple_of(lax.rem(c, RING) * CH, CH), CH)

    def swap(c):
        return remote(own.at[at(c), other], oth.at[at(c)], xs.at[c], xr_.at[c], mate)

    def to_right(c):
        return remote(rst.at[ring(c)], rb.at[at(c)], ss.at[0, c], rs.at[0, c], (h, d + 2))

    def to_left(c):
        return remote(lst.at[ring(c)], lb.at[at(c)], ss.at[1, c], rs.at[1, c], (h, d - 2))

    padded = acc.shape[0] // 2

    def place(first, count):
        rows = pl.ds(pl.multiple_of(first * CH, CH), count * CH)

        def block(i, carry):
            low = i * padded
            slot = lax.broadcasted_iota(jnp.int32, (padded, CH), 0) + low
            slot = jnp.where(slot < padded, slot + d * capacity, slot - padded + jnp.bitwise_xor(d, 1) * capacity)
            hot = [jnp.where(order_w[pl.ds(first + k, 1)] == slot, 1.0, 0.0).astype(bf16) for k in range(count)]
            hot = jnp.concatenate(hot, 1) if count > 1 else hot[0]
            here = pl.ds(pl.multiple_of(low, padded), padded)
            acc[here] += dot(hot, oth[rows]).astype(bf16)
            return carry

        lax.fori_loop(0, 2, block, 0)

    def swaps(lo, hi):
        def body(c, carry):
            swap(c).start()
            return carry
        lax.fori_loop(lo, hi, body, 0)

    last = SKEW * jnp.maximum(z, n - 1 - z)

    def step(t, carry):
        @pl.when(t < nc)
        def _():
            swap(t).wait_recv()
            oth[at(t)] = oth[at(t)] + own[at(t), mine]

        c = t - SKEW * z
        @pl.when((c >= 0) & (c < nc))
        def _():
            @pl.when(z > 0)
            def _():
                to_right(c).wait_recv()
            @pl.when(z < n - 1)
            def _():
                @pl.when(c >= RING)
                def _():
                    to_right(c - RING).wait_send()
                @pl.when(z == 0)
                def _():
                    rst[ring(c)] = oth[at(c)]
                @pl.when(z > 0)
                def _():
                    rst[ring(c)] = oth[at(c)] + rb[at(c)]
                to_right(c).start()

        e = t - SKEW * (n - 1 - z)
        @pl.when((e >= 0) & (e < nc))
        def _():
            @pl.when(z < n - 1)
            def _():
                to_left(e).wait_recv()
            @pl.when(z > 0)
            def _():
                @pl.when(e >= RING)
                def _():
                    to_left(e - RING).wait_send()
                @pl.when(z == n - 1)
                def _():
                    lst[ring(e)] = oth[at(e)]
                @pl.when(z < n - 1)
                def _():
                    lst[ring(e)] = oth[at(e)] + lb[at(e)]
                to_left(e).start()

        g = t - last
        @pl.when((g >= 0) & (g < nc))
        def _():
            @pl.when(z == 0)
            def _():
                oth[at(g)] = oth[at(g)] + lb[at(g)]
            @pl.when(z == n - 1)
            def _():
                oth[at(g)] = oth[at(g)] + rb[at(g)]
            @pl.when((z > 0) & (z < n - 1))
            def _():
                oth[at(g)] = (oth[at(g)].astype(f32) + rb[at(g)].astype(f32) + lb[at(g)].astype(f32)).astype(bf16)
            @pl.when(lax.rem(g, 2) == 1)
            def _():
                place(nc - 1 - g, 2)
        return carry

    now = [0]
    end = nc + SKEW * (n - 1)

    def advance(k):
        hi = min(now[0] + k, end)
        if hi > now[0]:
            lax.fori_loop(now[0], hi, step, 0)
        now[0] = hi

    head = order[0:1]
    lane0 = lax.broadcasted_iota(jnp.int32, head.shape, 1)
    for k in range(small):
        head = jnp.where(lane0 == k, owners[owners.shape[0] - small + k], head)
    order_w[...] = order[...]
    order_w[0:1] = head
    first.wait()
    swaps(0, n_ffn // CH)
    for ref in (dt_w, dg_w, g1_w, gq, gs, acc):
        ref[...] = jnp.zeros_like(ref)
    advance(1)
    for cp in nbs:
        cp.wait()
    jobs[0].two()
    jobs[1].one()
    advance(1)
    load_da.wait()

    def save_ig(s):
        return pltpu.make_async_copy(da_f.at[seq_rows[s]], ig_o.at[seq_rows[s]], igs.at[s])

    def finish(k):
        kind, s = kinds[k]
        got = jobs[k].three()
        for side in (0, 1):
            r = pl.ds(s * L + side * (L // 2), L // 2)
            if kind == 0:
                dh_f[r] += got[side]
            elif kind == 1:
                m = mlp_f[r] + got[side]
                y = h1_f[r] + m
                y_o[r] = y.astype(bf16)
                place = lax.broadcasted_iota(jnp.int32, (L // 2, Wd), 0) + side * (L // 2)
                keep_ = place < lengths[s]
                lane = lax.broadcasted_iota(jnp.int32, (1, width), 1)
                sy = jnp.sum(jnp.sum(jnp.where(keep_, y * y, 0.0), -1, keepdims=True), 0, keepdims=True)
                sm = jnp.sum(jnp.sum(jnp.where(keep_, m * m, 0.0), -1, keepdims=True), 0, keepdims=True)
                st_w[0, 3:4] += jnp.where(lane == 0, sy, jnp.where(lane == 2, sm, 0.0))
            else:
                da_f[r] = dh_f[r] + xp[r, col(h)].astype(f32) + got[side]
                if side == 1:
                    save_ig(s).start()

    turn = [1]
    done = [0]

    def relay():
        k = turn[0]
        if k + 1 < len(jobs) and kinds[k + 1][0] == 2:
            assert kinds[k + 1][1] < done[0]
        if k < len(jobs):
            jobs[k].two()
        if k + 1 < len(jobs):
            jobs[k + 1].one()
        if k - 1 < len(jobs):
            finish(k - 1)
        turn[0] += 1

    st_w[0] = stat_in[...]
    load_w.wait()
    taps3 = wv[0:16].astype(f32)
    joined = jnp.concatenate([taps3[hl + i : hl + i + 1] for i in range(small - hl)], 1)
    for j in range(KCONV):
        tp[j : j + 1] = joined[:, j * 3 * hd : (j + 1) * 3 * hd]
    gout[0:1] = gain[2:3, col(h)]
    ex = []
    turns = [jnp.bitwise_xor(h, k) for k in (1, 2, 3, 0)]

    def heads_of(i):
        return pltpu.make_async_copy(af.at[:, col(turns[i])], av.at[i % 2], avs.at[i % 2])

    for i in (0, 1):
        heads_of(i).start()

    def output_rows():
        if ex or turn[0] < 1 + sum(kind == 0 for kind, _ in kinds):
            return
        for i, p in enumerate(turns):
            heads_of(i).wait()
            go_w[col(p, hd)] = tdot(av[i % 2], dh_f[...].astype(bf16)).astype(bf16)
            if i < 2:
                heads_of(i + 2).start()
            if i < 3:
                cp = remote(go_w.at[col(p, hd)], own.at[pl.ds(at_out, hd), col(h)], a2s.at[i], a2r.at[i], (p, d))
                cp.start()
                ex.append(cp)
        own[pl.ds(at_out, hd), col(h)] = go_w[col(h, hd)]

    for s in range(seqs):
        sl = s % 2
        for cp in fetch(s):
            cp.wait()
        if s + 1 < seqs:
            for cp in fetch(s + 1):
                cp.start()
        if s == 0:
            for cp in (load_x, load_dh, load_m, load_h):
                cp.wait()
        sub = [ref.at[sl] for ref in scr]
        q_, k_, u_, t_, p_, g_, r_, s_, o_ = sub
        x_, l_ = qv.at[sl], lv.at[sl]
        bwd_blocks(da_f.at[seq_rows[s]], gout, o_, q_, k_, u_, p_, s_, dg_w, do_w, w_w, dq_w, dk_w, qd_w, heads, chunks)
        advance(1)
        bwd_states(l_, k_, t_, w_w, qd_w, ds_w, heads, chunks)
        if s > 0:
            relay()
            output_rows()
        advance(1)
        bwd_conv(x_, l_, tp, q_, k_, u_, g_, r_, s_, w_w, dq_w, dk_w, ds_w, dc, dx_w, dlg_w, dt_w, heads, chunks)
        advance(1)
        if s == 0:
            relay()
            output_rows()
        for i in range(2):
            lo = i * (L // 2)
            r = pl.ds(s * L + lo, L // 2)
            here = pl.ds(lo, L // 2)
            xx = xv[r].astype(f32)
            r1 = lax.rsqrt(jnp.mean(xx * xx, -1, keepdims=True) + norm_eps)
            xn = xx * r1
            n1_w[here] = (xn * gain[0:1]).astype(bf16)
            dn = dot(dx_w[here], wv[lead:]) + dot(dlg_w[here], wv[0:lead])
            g1_w[0:1] += jnp.sum(dn * xn, 0, keepdims=True)
            gd = dn * gain[0:1]
            xp[r] = (r1 * (gd - xn * jnp.mean(gd * xn, -1, keepdims=True))).astype(bf16)
            if i == 0:
                advance(1)
        done[0] += 1
        gq[...] += tdot(dx_w[...], n1_w[...])
        gs[...] += tdot(dlg_w[...], n1_w[...])
        if 0 < s < seqs - 1:
            relay()
            output_rows()
        if s + 1 < seqs:
            advance(1)
    line = 3 * hd
    dt = jnp.concatenate([dt_w[j : j + 1] for j in range(KCONV)], 1)
    row = lax.broadcasted_iota(jnp.int32, (lead, width), 0)
    tail = gs[...]
    for i in range(small - hl):
        tail = jnp.where(row == hl + i, dt[:, i * width : (i + 1) * width], tail)
    tail = jnp.where(row < small, tail, 0.0)
    own[pl.ds(0, lead)] = tail.astype(bf16)
    own[pl.ds(at_qkv, 3 * hd)] = gq[...].astype(bf16)
    for cp in ex:
        cp.wait()
    assert now[0] <= n_ffn // CH
    swaps(n_ffn // CH, nc)
    lane = lax.broadcasted_iota(jnp.int32, (1, width), 1)
    three = jnp.concatenate([dg_w[0:1]] * 4, 1)
    st_w[0, 0:1] = g1_w[0:1]
    st_w[0, 2:3] = jnp.where((lane >= h * Wd) & (lane < (h + 1) * Wd), three, 0.0)
    assert ex
    advance(1)
    while turn[0] <= len(jobs) - seqs:
        relay()
        advance(3)
    rounds = [(jnp.bitwise_xor(h, k), d) for k in (1, 2)] + [mate] + [(h, jnp.bitwise_xor(d, k)) for k in bits]
    sent = []
    for i, p in enumerate(rounds):
        cp = remote(st_w.at[i], str_.at[i], sts.at[0, i], sts.at[1, i], p)
        cp.start()
        sent.append(cp)
        if turn[0] <= len(jobs) and i % 2 == 1:
            relay()
        advance(2)
        cp.wait_recv()
        st_w[i + 1] = st_w[i] + str_[i]
    stat_o[...] = st_w[len(rounds)]
    while turn[0] <= len(jobs):
        relay()
        advance(2)
    advance(end)
    if nc % 2:
        place(0, 1)
    give = remote(acc.at[pl.ds(padded, padded)], own_o.at[:, mine], fs.at[0], fr.at[0], mate)
    keep = pltpu.make_async_copy(acc.at[pl.ds(0, padded)], own_o.at[:, mine], gl.at[0])
    give.start()
    keep.start()
    for cp in sent:
        cp.wait_send()

    def drain(c, carry):
        swap(c).wait_send()
        @pl.when(c >= nc - RING)
        def _():
            @pl.when(z < n - 1)
            def _():
                to_right(c).wait_send()
            @pl.when(z > 0)
            def _():
                to_left(c).wait_send()
        return carry

    lax.fori_loop(0, nc, drain, 0)
    give.wait()
    keep.wait()
    for s in range(seqs):
        save_ig(s).wait()


def back(gain, stat_in, order, lengths, owners, h1_part, mlp_part, owns, xf, af, w, g_ffn, qkv, lg, saved, seqs, heads, lead, hl, small, capacity, cid):
    T, width = xf.shape
    Wd = width // 4
    half = width // 2
    L = T // seqs
    hd = heads * DK
    n_ffn = g_ffn.shape[0]
    rows = n_ffn + 4 * hd + lead
    nc = rows // CH
    hbm = pl.BlockSpec(memory_space=pl.ANY)
    S = jax.ShapeDtypeStruct
    V = pltpu.VMEM
    n = lax.axis_size("dp") // 2
    rounds = 2 + 1 + max(n.bit_length() - 1, 0)
    piece, ringbuf = V((rows, half), bf16), V((RING * CH, half), bf16)
    blk = lambda dt: V((2, heads, L, DK), dt)
    wk = lambda dt: V((heads, L, DK), dt)
    rsb = V((SLOTS, 2, L // 2, Wd), bf16)
    njobs = 3 * seqs - EARLY
    padded = -(-capacity // 128) * 128
    return pl.pallas_call(
        functools.partial(back_kernel, seqs=seqs, heads=heads, lead=lead, n_ffn=n_ffn, hl=hl, small=small, capacity=capacity),
        in_specs=[VM()] * 3 + [pl.BlockSpec(memory_space=pltpu.SMEM)] * 2 + [hbm] * 21,
        out_specs=[VM(), hbm, VM(), hbm],
        out_shape=[S((T, Wd), bf16), S((T, Wd), f32), S((8, width), f32), S((padded, width), bf16)],
        scratch_shapes=[
            V((rows, width), bf16), piece, piece, piece, ringbuf, ringbuf,
            V((2, L, 3 * hd), f32), V((2, L, lead), f32), *[blk(bf16)] * 8, blk(f32),
            wk(bf16), wk(f32), wk(f32), wk(f32), wk(f32), wk(bf16), V((L + 8, 3 * hd), f32),
            V((T, width), bf16), V((lead + 3 * hd, width), bf16), V((2, seqs, 2, L // 2, Wd), bf16),
            V((T, Wd), f32), V((T, Wd), f32), V((T, Wd), f32), V((T, Wd), f32), V((T, width), bf16), rsb, rsb, rsb,
            V((3 * hd, width), f32), V((lead, width), f32), V((L, width), bf16), V((L, 3 * hd), bf16), V((L, lead), bf16),
            V((8, 3 * hd), f32), V((8, hd), f32), V((8, width), f32), V((rounds + 1, 8, width), f32), V((4 * hd, Wd), bf16),
            V((8, 3 * hd), f32), V((8, Wd), f32), V((2, T, Wd), bf16), V((2 * padded, half), bf16), V(order.shape, jnp.int32),
            DMA((nc,)), DMA((nc,)), DMA((1,)), DMA((1,)), DMA((1,)), DMA((2, nc)), DMA((2, nc)),
            DMA((2, 3 * njobs)), DMA((2, 3 * njobs)), DMA((8 + 4 * seqs,)), DMA((2, 11)), DMA((3,)), DMA((3,)),
            DMA((2, rounds)), V((rounds, 8, width), f32), DMA((seqs,)), DMA((2,)),
        ],
        compiler_params=pltpu.CompilerParams(collective_id=cid, has_side_effects=True, vmem_limit_bytes=63 << 20),
        name="back",
    )(gain, stat_in, order, lengths, owners, h1_part, mlp_part, *owns, xf, af, w, g_ffn, qkv, lg, *saved)


RT = 256
RC = 32
EARLY = 0


def ffn_kernel(
    gain, lengths, af, xf, cf, of, w,
    mlp_o, h1p_o, da_o, dh_o, mo_o, h1_o, g_o, stat_o,
    ov, wgu, wd, wo, a_v, x_v, c_v, n2_s, hid_s, dgu_s, h1_w, t_w, g2_w, r2_w, gate_w, up_w, dh_w, mlp_s, h1p_s, da_s, fb, db, cb, hb, kb, lb, dav, dhv, mov, h1v, gv,
    lw, lt, sv, as_, ar_, hs, hr_, og,
    *, seqs, at_out, at_gate,
):
    h = lax.axis_index("head")
    d = lax.axis_index("dp")
    T, width = xf.shape
    Wd = width // 4
    L = T // seqs
    ffl, ffp = wd.shape[0], wgu.shape[0] // 2
    n = T // RT
    def col(k):
        return pl.ds(pl.multiple_of(jnp.bitwise_xor(h, k) * Wd, Wd), Wd)

    def rows(i):
        return pl.ds(pl.multiple_of(i * RT, RT), RT)

    def slot(i):
        return lax.rem(i, 2)

    def fetch(i):
        return [
            pltpu.make_async_copy(src.at[rows(i)], dst.at[slot(i)], lt.at[slot(i), k])
            for k, (src, dst) in enumerate(((af, a_v), (xf, x_v)))
        ]

    loads = [pltpu.make_async_copy(of, ov, lw.at[0])]
    dsts = (wgu.at[pl.ds(0, ffl)], wgu.at[pl.ds(ffp, ffl)], wd, wo)
    for k, (lo, dst) in enumerate(zip((at_gate, at_gate + ffl, at_gate + 2 * ffl, at_out), dsts)):
        loads.append(pltpu.make_async_copy(w.at[pl.ds(lo, dst.shape[0])], dst, lw.at[1 + k]))
    loads.append(pltpu.make_async_copy(cf, c_v, lw.at[5]))
    loads[0].start()
    for cp in fetch(0):
        cp.start()
    for cp in loads[1:]:
        cp.start()
    b = pltpu.get_barrier_semaphore()
    for k in (1, 2):
        pl.semaphore_signal(b, inc=1, device_id=(jnp.bitwise_xor(h, k), d), device_id_type=MESH)
    pl.semaphore_wait(b, 2)

    stat_o[...] = jnp.zeros_like(stat_o)
    for lo in (ffl, ffp + ffl):
        wgu[pl.ds(lo, ffp - ffl)] = jnp.zeros((ffp - ffl, width), bf16)
        dgu_s[:, lo : lo + ffp - ffl] = jnp.zeros((T, ffp - ffl), bf16)

    def job(i):
        def beside(side):
            start = pl.multiple_of(i * RT + side * (RT // 2), RT // 2)
            return da_s[pl.ds(start, RT // 2), col(2 - side)]

        return Scatter(da_s, beside, rows(i), (fb, db, cb), lax.rem(i, SLOTS), as_, ar_, 3 * i)

    more = EARLY * L // RT

    def job2(i):
        def beside(side):
            start = pl.multiple_of(i * RT + side * (RT // 2), RT // 2)
            return h1p_s[pl.ds(start, RT // 2), col(2 - side)]

        return Scatter(h1p_s, beside, rows(i), (hb, kb, lb), lax.rem(i, SLOTS), hs, hr_, 3 * i)

    def out(k, i):
        src, dst = ((dav, da_o), (dhv, dh_o), (mov, mo_o), (h1v, h1_o))[k]
        return pltpu.make_async_copy(src.at[rows(i)], dst.at[rows(i)], og.at[k, i])

    def finish(i):
        got = job(i).three()
        for side in (0, 1):
            start = pl.multiple_of(i * RT + side * (RT // 2), RT // 2)
            dav[pl.ds(start, RT // 2)] += got[side]
        out(0, i).start()

    def finish2(i):
        got = job2(i).three()
        for side in (0, 1):
            start = pl.multiple_of(i * RT + side * (RT // 2), RT // 2)
            dhv[pl.ds(start, RT // 2)] += got[side]
        out(1, i).start()

    def saves(i):
        return [
            pltpu.make_async_copy(mlp_s.at[slot(i)], mlp_o.at[rows(i)], sv.at[slot(i), 0]),
            pltpu.make_async_copy(h1p_s.at[rows(i)], h1p_o.at[rows(i)], sv.at[slot(i), 1]),
        ]

    loads[0].wait()

    def tile(i, carry):
        @pl.when(i + 1 < n)
        def _():
            for cp in fetch(i + 1):
                cp.start()

        @pl.when(i >= 2)
        def _():
            for cp in saves(i - 2):
                cp.wait()

        for cp in fetch(i):
            cp.wait()
        r, s = rows(i), slot(i)

        def part_of(k):
            return pl.ds(pl.multiple_of(i * RT + k, RC), RC), slice(k, k + RC)

        t_w[...] = dot(a_v[s], ov[...])
        place = lax.broadcasted_iota(jnp.int32, (RT, Wd), 0) + lax.rem(i * RT, L)
        good = place < lengths[i * RT // L]
        lane = lax.broadcasted_iota(jnp.int32, (1, width), 1)
        attn = t_w[:, col(0)]
        sa = jnp.sum(jnp.sum(jnp.where(good, attn * attn, 0.0), 0, keepdims=True), -1, keepdims=True)
        count = jnp.sum(jnp.sum(jnp.where(good, 1.0, 0.0), 0, keepdims=True), -1, keepdims=True)
        stat_o[3:4] += jnp.where(lane == 1, sa, jnp.where(lane == 3, count, 0.0))
        for k in range(0, RT, RC):
            rk, k_ = part_of(k)
            h1 = x_v[s, k_].astype(f32) + t_w[k_]
            h1_w[k_] = h1
            r2 = lax.rsqrt(jnp.mean(h1 * h1, -1, keepdims=True) + norm_eps)
            r2_w[k_] = jnp.broadcast_to(r2, (RC, 128))
            n2_s[rk] = (h1 * r2 * gain[1:2]).astype(bf16)
        h1v[r] = h1_w[:, col(0)]
        out(3, i).start()

        @pl.when(i == 0)
        def _():
            for cp in loads[1:]:
                cp.wait()

        cot = c_v[r]
        gate_w[...] = dot_t(n2_s[r], wgu[0:ffl])
        up_w[...] = dot_t(n2_s[r], wgu[ffp : ffp + ffl])
        dh_w[...] = dot_t(cot, wd[...])
        for k in range(0, RT, RC):
            rk, k_ = part_of(k)
            gate, up, dh = gate_w[k_], up_w[k_], dh_w[k_]
            sig = jax.nn.sigmoid(gate)
            act = gate * sig
            hid_s[rk] = (act * up).astype(bf16)
            dgu_s[rk, 0:ffl] = (dh * up * (sig + act * (1.0 - sig))).astype(bf16)
            dgu_s[rk, ffp : ffp + ffl] = (dh * act).astype(bf16)
        t_w[...] = dot(hid_s[r], wd[...])
        mov[r] = t_w[:, col(0)]
        out(2, i).start()
        mlp_s[s] = t_w[...].astype(bf16)
        t_w[...] = dot(dgu_s[r], wgu[...])
        for k in range(0, RT, RC):
            rk, k_ = part_of(k)
            h1, dn2 = h1_w[k_], t_w[k_]
            r2 = r2_w[k_, 0:1]
            hr = h1 * r2
            g2_w[k_] = dn2 * hr
            gd = dn2 * gain[1:2]
            t_w[k_] = r2 * (gd - hr * jnp.mean(gd * hr, -1, keepdims=True))
        stat_o[1:2] += jnp.sum(g2_w[...], 0, keepdims=True)
        dhv[r] = t_w[:, col(0)] + c_v[r, col(0)].astype(f32)
        low = t_w[...].astype(bf16)
        h1p_s[r] = low
        for cp in saves(i):
            cp.start()
        t_w[...] = dot_t(low, ov[...])
        da_s[r] = t_w[...].astype(bf16)
        dav[r] = t_w[:, col(0)] + dot_t(cot, wo[...])

        @pl.when(i >= 2)
        def _():
            finish(i - 2)

        @pl.when((i >= 2) & (i - 2 < more))
        def _():
            finish2(i - 2)

        @pl.when(i >= 1)
        def _():
            job(i - 1).two()

        @pl.when((i >= 1) & (i - 1 < more))
        def _():
            job2(i - 1).two()

        job(i).one()

        @pl.when(i < more)
        def _():
            job2(i).one()

        @pl.when(i >= more)
        def _():
            out(1, i).start()

        return carry

    lax.fori_loop(0, n, tile, 0)

    def grad(k, value):
        gv[pl.ds(k * ffl, ffl)] = value.astype(bf16)
        return pltpu.make_async_copy(gv.at[pl.ds(k * ffl, ffl)], g_o.at[pl.ds(k * ffl, ffl)], lw.at[k])

    g2 = grad(2, tdot(hid_s[...], c_v[...]))
    g2.start()
    job(n - 1).two()
    finish(n - 2)
    g1 = grad(1, tdot(dgu_s[:, ffp:], n2_s[...])[0:ffl])
    g1.start()
    g0 = grad(0, tdot(dgu_s[:, 0:ffp], n2_s[...])[0:ffl])
    g0.start()
    finish(n - 1)
    for cp in (g0, g1, g2):
        cp.wait()
    for i in (n - 2, n - 1):
        for cp in saves(i):
            cp.wait()
    for i in range(n):
        for k in range(4):
            out(k, i).wait()


def ffn(gain, lengths, af, xf, cf, of, w, seqs, at_out, at_gate, ffl, cid):
    T, width = xf.shape
    Wd = width // 4
    hd = at_gate - at_out
    n = T // RT
    ffp = -(-ffl // 128) * 128
    hbm = pl.BlockSpec(memory_space=pl.ANY)
    S = jax.ShapeDtypeStruct
    V = pltpu.VMEM
    slots = V((SLOTS, 2, RT // 2, Wd), bf16)
    pair = V((2, RT, width), bf16)
    own = S((T, Wd), f32)
    return pl.pallas_call(
        functools.partial(ffn_kernel, seqs=seqs, at_out=at_out, at_gate=at_gate),
        in_specs=[VM(), pl.BlockSpec(memory_space=pltpu.SMEM)] + [hbm] * 5,
        out_specs=[hbm] * 7 + [VM()],
        out_shape=[
            S((T, width), bf16), S((T, width), bf16), own, own, own, own,
            S((3 * ffl, width), bf16), S((8, width), f32),
        ],
        scratch_shapes=[
            V((width, width), bf16), V((2 * ffp, width), bf16), V((ffl, width), bf16), V((hd, width), bf16),
            pair, pair, V((T, width), bf16), V((T, width), bf16), V((T, ffl), bf16), V((T, 2 * ffp), bf16),
            V((RT, width), f32), V((RT, width), f32), V((RT, width), f32), V((RT, 128), f32), *[V((RT, ffl), f32)] * 3, pair, V((T, width), bf16), V((T, width), bf16),
            *[slots] * 6, *[V((T, Wd), f32)] * 4, V((3 * ffl, width), bf16),
            DMA((6,)), DMA((2, 2)), DMA((2, 2)), *[DMA((2, 3 * n))] * 4, DMA((4, n)),
        ],
        compiler_params=pltpu.CompilerParams(collective_id=cid, has_side_effects=True, vmem_limit_bytes=63 << 20),
        name="feed_forward",
    )(gain, lengths, af, xf, cf, of, w)


SB = 128


def tail_kernel(g, stats, gain, gain_m, gain_v, y, ig, p, m, v, p_o, m_o, v_o, gain_o, gm_o, gv_o, rms_o, y_o, ig_o, w, yv, iv, sem):
    i = pl.program_id(0)
    come = [pltpu.make_async_copy(a, b, sem.at[0, k]) for k, (a, b) in enumerate(((y, yv), (ig, iv)))]
    go = [pltpu.make_async_copy(a, b, sem.at[1, k]) for k, (a, b) in enumerate(((yv, y_o), (iv, ig_o)))]

    @pl.when(i == 0)
    def _():
        for cp in come:
            cp.start()

    width = g.shape[1] // 8
    for j in range(8):
        w[:, j, :] = g[:, j * width : (j + 1) * width].astype(f32)
    p_o[...], m_o[...], v_o[...] = adam_step(p[...], m[...], v[...], w[...], weight_rate, weight_decay)

    @pl.when(i == 0)
    def _():
        gain_o[...], gm_o[...], gv_o[...] = adam_step(gain[...], gain_m[...], gain_v[...], stats[0:3], gain_rate, 0.0)
        lane = lax.broadcasted_iota(jnp.int32, (1, 128), 1)
        rms = jnp.sqrt(stats[3:4, 0:128] / stats[3:4, 3:4])
        for k in range(3):
            rms_o[k] = jnp.sum(jnp.where(lane == k, rms, 0.0))

    @pl.when(i == pl.num_programs(0) - 1)
    def _():
        for cp in come:
            cp.wait()
        for cp in go:
            cp.start()
        for cp in go:
            cp.wait()


def tail(g, stats, gain, gain_m, gain_v, y, ig, p, m, v):
    capacity = p.shape[0]
    S = jax.ShapeDtypeStruct
    V = pltpu.VMEM
    hbm = pl.BlockSpec(memory_space=pl.ANY)
    whole = lambda a: pl.BlockSpec(a.shape, lambda i: (0,) * a.ndim)
    blk = pl.BlockSpec((SB, *p.shape[1:]), lambda i: (i, 0, 0))
    like = S(p.shape, f32)
    small = S(gain.shape, f32)
    return pl.pallas_call(
        tail_kernel,
        grid=(-(-capacity // SB),),
        in_specs=[pl.BlockSpec((SB, g.shape[1]), lambda i: (i, 0))] + [whole(a) for a in (stats, gain, gain_m, gain_v)] + [hbm] * 2 + [blk] * 3,
        out_specs=[blk] * 3 + [whole(gain)] * 3 + [pl.BlockSpec(memory_space=pltpu.SMEM), hbm, hbm],
        out_shape=[like] * 3 + [small] * 3 + [S((3,), f32), S(y.shape, y.dtype), S(ig.shape, ig.dtype)],
        scratch_shapes=[V((SB, *p.shape[1:]), f32), V(y.shape, y.dtype), V(ig.shape, ig.dtype), DMA((2, 2))],
        compiler_params=pltpu.CompilerParams(vmem_limit_bytes=56 << 20),
        name="owners_step",
    )(g, stats, gain, gain_m, gain_v, y, ig, p, m, v)


def adam_step(param, first, second_moment, grad, rate, decay):
    first = beta_one * first + (1.0 - beta_one) * grad
    second_moment = beta_two * second_moment + (1.0 - beta_two) * grad * grad
    denom = jnp.sqrt(second_moment / (1.0 - beta_two**STEP)) + adam_eps
    param = param - rate / (1.0 - beta_one**STEP) * first / denom - rate * decay * param
    return (param, first, second_moment)


def on_device(
    inputs, cotangent, lengths, owner_slots, table, table_m, table_v, gains, gains_m, gains_v
):
    shards = lax.axis_size("head")
    seqs = lengths.shape[0]
    hd = HEADS * DK // shards
    ffl = FF // shards
    hl = HEADS // shards
    taps_rows = KCONV * 3 * hd // MODEL_WIDTH
    capacity = table.shape[1]
    small = hl + taps_rows
    lead = 64
    at_out = lead + 3 * hd
    at_gate = at_out + hd
    n_body = 4 * hd + 3 * ffl
    order = lax.pad(owner_slots, jnp.int32(-1), [(lead, n_body - owner_slots.shape[0], 0)]).reshape(-1, CH)
    split = lambda t: t[0].reshape(capacity, 8, MODEL_WIDTH // 8)
    weights, x_full, cot_full, a_full, out_full, qkv, logit, *saved = front(
        split(table), order, gains, lengths, owner_slots, inputs, cotangent, seqs, hl, lead, at_out, at_gate, hl, small, capacity, 0
    )
    mlp_part, h1_part, da, dh_own, mlp_own, h1_own, g_ffn, stat_in = ffn(
        gains, lengths, a_full, x_full, cot_full, out_full, weights, seqs, at_out, at_gate, ffl, 1
    )
    y, input_grad, stats, owned = back(
        gains, stat_in, order, lengths, owner_slots, h1_part, mlp_part, [da, dh_own, mlp_own, h1_own],
        x_full, a_full, weights, g_ffn, qkv, logit, saved, seqs, hl, lead, hl, small, capacity, 2,
    )
    table_new, table_m_new, table_v_new, gains_new, gains_m_new, gains_v_new, rms, y, input_grad = tail(
        owned, stats, gains, gains_m, gains_v, y, input_grad, split(table), split(table_m), split(table_v)
    )
    return (
        y,
        input_grad,
        table_new.reshape(table.shape),
        table_m_new.reshape(table.shape),
        table_v_new.reshape(table.shape),
        gains_new,
        gains_m_new,
        gains_v_new,
        rms,
    )


def solution(mesh):
    tok, tab = P("dp", "head"), P("head", "dp", None)
    return jax.shard_map(
        on_device,
        mesh=mesh,
        in_specs=(tok, tok, P("dp"), P(), tab, tab, tab, P(), P(), P()),
        out_specs=(tok, tok, tab, tab, tab, P(), P(), P(), P()),
        check_vma=False,
    )
```
